32 devices in a mesh: ctx: 8 (over z, y), head: 4 (over x, core).
Axes of the slice: x: 2, y: 2, z: 4, core: 2. Of those that a mesh axis runs over, the one named last changes fastest.
Arguments:
- queries: bfloat16 [2048, 32, 128], P('ctx', 'head'), may hold values from -6 to 6
- key_states: bfloat16 [2048, 4, 128], P('ctx', 'head'), may hold values from -6 to 6
- value_states: bfloat16 [2048, 4, 128], P('ctx', 'head'), may hold values from -6 to 6
- doc_lengths: int32 [8], replicated, may hold values from 1 to 1792, 2048 in all
- grad_attended: bfloat16 [2048, 4096], P(('ctx', 'head')), may hold values from -6 to 6
Outputs:
- attended: bfloat16 [2048, 4096], P(('ctx', 'head'))
- grad_queries: bfloat16 [2048, 32, 128], P('ctx', 'head')
- grad_keys: bfloat16 [2048, 4, 128], P('ctx', 'head')
- grad_values: bfloat16 [2048, 4, 128], P('ctx', 'head')
The draws below stay inside these ranges and needn't reach their ends.
All inputs are finite; a program needn't handle non-finite values.
Results may differ from the reference program's by a relative error of at most 0.022.
Values may be sent and summed in bfloat16 or wider, within the bound.
No kernel may reach another device: no remote copies, remote signals or barrier semaphores. Data moves between devices by JAX's collectives and lax.ppermute only.
A program may use at most 64 MiB of HBM per device.

```python
import math
import jax
import jax.numpy as jnp
import numpy as np
from jax import lax

HEAD_DIM = 128
Q_HEADS = 32
KV_HEADS = 4
TOK_DEV = 256
DOC_MOST = 1792
SEQ_LEN = 2048
DOCS = 8


def draw_queries(key, part):
    key = jax.random.fold_in(key, 11)
    drawn = jnp.clip(jax.random.normal(key, (SEQ_LEN, Q_HEADS, HEAD_DIM), jnp.float32), -4.0, 4.0)
    return drawn.astype(jnp.bfloat16)


def draw_key_states(key, part):
    key = jax.random.fold_in(key, 23)
    drawn = jnp.clip(jax.random.normal(key, (SEQ_LEN, KV_HEADS, HEAD_DIM), jnp.float32), -4.0, 4.0)
    return drawn.astype(jnp.bfloat16)


def steps_of(key, dims, cuts, least, high):
    factor_of, own = 1.0, jax.random.fold_in(key, 6)
    for position, blocks in cuts:
        heights = jnp.exp(jax.random.uniform(jax.random.fold_in(own, position), (blocks,), jnp.float32, least / len(cuts), high / len(cuts)))
        factor_of = factor_of * jnp.repeat(heights, dims[position] // blocks).reshape([-1 if axis == position else 1 for axis in range(len(dims))])
    return factor_of


def split_up(count, total, reach, skew):
    loads = [(1 << 20) // math.isqrt(rank ** skew) + 1 for rank in range(2, count + 1)]
    spare, holding = total - reach - (count - 1), [1] * (count - 1)
    while spare > 0:
        free = [i for i in range(count - 1) if holding[i] < reach]
        mass, left = sum([loads[i] for i in free]), spare
        for i in free:
            more = min(reach - holding[i], max(1, left * loads[i] // mass), spare)
            holding[i] = holding[i] + more
            spare = spare - more
    return np.array([reach] + holding)


def uneven_parts(stream_key, number_of, total, limit, lean):
    if number_of == 2:
        one = jax.random.randint(stream_key, (), max(1, total - limit), min(limit, total - 1) + 1)
        return jnp.stack([one, total - one])
    sizes = jnp.asarray(split_up(number_of, total, limit, lean), jnp.int32)
    twos = (number_of - 1) // 2
    donor, taker = sizes[1:1 + 2 * twos:2], sizes[2:2 + 2 * twos:2]
    slack = jnp.minimum(donor - 1, limit - taker)
    passed = jax.random.randint(jax.random.fold_in(stream_key, 1), (twos,), 0, 1 << 20) % (slack + 1)
    sizes = sizes.at[1:1 + 2 * twos:2].set(donor - passed).at[2:2 + 2 * twos:2].set(taker + passed)
    return sizes[jax.random.permutation(jax.random.fold_in(stream_key, 2), number_of)]


def scatter_about(stream_key, extent, width, bound, cuts=(), kind=jnp.bfloat16):
    array = jax.random.normal(stream_key, extent, jnp.float32) * width
    if len(cuts) > 0:
        array = steps_of(stream_key, extent, cuts, -0.22, 0.18) * array
    return jnp.clip(array, min=-bound, max=bound).astype(kind)


def setup_inputs(seed: int = 0) -> dict:
    splits = jax.random.split(jax.random.key(seed), 6)
    queries = draw_queries(jax.random.fold_in(splits[5], 71), 0)
    key_states = draw_key_states(jax.random.fold_in(splits[5], 71), 0)
    value_states = scatter_about(splits[2], (SEQ_LEN, KV_HEADS, HEAD_DIM), 1.0, 6.0, ((0, 8), (1, 4)))
    doc_lengths = uneven_parts(splits[3], DOCS, SEQ_LEN, DOC_MOST, 2).astype(jnp.int32)
    grad_attended = scatter_about(splits[4], (SEQ_LEN, Q_HEADS * HEAD_DIM), 1.0, 6.0, ((0, 32),))
    return {"queries": queries, "key_states": key_states, "value_states": value_states, "doc_lengths": doc_lengths, "grad_attended": grad_attended}


NEG_FILL = -1e+30

def doc_index(doc_ends, positions):
    counted = lax.optimization_barrier(jnp.sum((positions[:, None] >= doc_ends[None, :]).astype(jnp.int32), axis=1))
    return jnp.where(positions >= 0, counted, -1).astype(jnp.int32)

def to_bf16(values):
    return lax.optimization_barrier(values.astype(jnp.bfloat16)).astype(jnp.float32)

def reference(queries, key_states, value_states, doc_lengths, grad_attended):
    scale_factor = 1.0 / math.sqrt(HEAD_DIM)
    group_size = Q_HEADS // KV_HEADS
    block_len = TOK_DEV
    window_len = DOC_MOST + block_len
    doc_ends = jnp.cumsum(doc_lengths).astype(jnp.int32)
    zero_front = jnp.zeros((DOC_MOST, KV_HEADS, HEAD_DIM), key_states.dtype)
    padded_keys = jnp.concatenate([zero_front, key_states], axis=0)
    padded_values = jnp.concatenate([zero_front, value_states], axis=0)
    query_rows = queries.reshape(SEQ_LEN, KV_HEADS, group_size, HEAD_DIM)
    grad_rows = grad_attended.reshape(SEQ_LEN, KV_HEADS, group_size, HEAD_DIM)

    def one_block(running, block_index):
        key_total, value_total = running
        block_start = (block_index * block_len).astype(jnp.int32)
        query_block = lax.dynamic_slice_in_dim(query_rows, block_start, block_len, 0).astype(jnp.float32)
        grad_block = lax.dynamic_slice_in_dim(grad_rows, block_start, block_len, 0).astype(jnp.float32)
        key_window = lax.dynamic_slice_in_dim(padded_keys, block_start, window_len, 0).astype(jnp.float32)
        value_window = lax.dynamic_slice_in_dim(padded_values, block_start, window_len, 0).astype(jnp.float32)
        q_positions = block_start + jnp.arange(block_len, dtype=jnp.int32)
        k_positions = block_start - DOC_MOST + jnp.arange(window_len, dtype=jnp.int32)
        live_mask = (doc_index(doc_ends, q_positions)[:, None] == doc_index(doc_ends, k_positions)[None, :]) & (k_positions[None, :] <= q_positions[:, None])
        live_wide = live_mask[:, None, None, :]
        scores = jnp.einsum('tgjd,sgd->tgjs', query_block, key_window) * scale_factor
        row_max = lax.optimization_barrier(jnp.max(jnp.where(live_wide, scores, NEG_FILL), axis=-1))
        raw_weights = jnp.where(live_wide, jnp.exp(scores - row_max[..., None]), 0.0)
        denominator = lax.optimization_barrier(jnp.sum(raw_weights, axis=-1))
        weights = to_bf16(raw_weights)
        output = jnp.einsum('tgjs,sgd->tgjd', weights, value_window) / denominator[..., None]
        output_b = output.astype(jnp.bfloat16)
        log_total = row_max + jnp.log(denominator)
        delta_row = lax.optimization_barrier(jnp.sum(grad_block * output_b.astype(jnp.float32), axis=-1))
        probs = jnp.where(live_wide, jnp.exp(scores - log_total[..., None]), 0.0)
        probs_b = to_bf16(probs)
        value_part = jnp.einsum('tgjs,tgjd->sgd', probs_b, grad_block)
        d_probs = jnp.einsum('tgjd,sgd->tgjs', grad_block, value_window)
        d_scores = to_bf16(probs * (d_probs - delta_row[..., None]))
        query_grad = jnp.einsum('tgjs,sgd->tgjd', d_scores, key_window) * scale_factor
        key_part = jnp.einsum('tgjs,tgjd->sgd', d_scores, query_block) * scale_factor
        key_slab = lax.dynamic_slice_in_dim(key_total, block_start, window_len, 0) + key_part
        value_slab = lax.dynamic_slice_in_dim(value_total, block_start, window_len, 0) + value_part
        key_total = lax.dynamic_update_slice_in_dim(key_total, key_slab, block_start, 0)
        value_total = lax.dynamic_update_slice_in_dim(value_total, value_slab, block_start, 0)
        outputs = (output_b.reshape(block_len, Q_HEADS * HEAD_DIM), query_grad.astype(jnp.bfloat16).reshape(block_len, Q_HEADS, HEAD_DIM))
        return ((key_total, value_total), outputs)
    start_totals = (jnp.zeros((DOC_MOST + SEQ_LEN, KV_HEADS, HEAD_DIM), jnp.float32), jnp.zeros((DOC_MOST + SEQ_LEN, KV_HEADS, HEAD_DIM), jnp.float32))
    block_ids = jnp.arange(SEQ_LEN // block_len, dtype=jnp.int32)
    totals, stacked = lax.scan(one_block, start_totals, block_ids)
    attended = stacked[0].reshape(SEQ_LEN, Q_HEADS * HEAD_DIM)
    grad_queries = stacked[1].reshape(SEQ_LEN, Q_HEADS, HEAD_DIM)
    grad_keys = totals[0][DOC_MOST:].astype(jnp.bfloat16)
    grad_values = totals[1][DOC_MOST:].astype(jnp.bfloat16)
    return (attended, grad_queries, grad_keys, grad_values)
```

```python
import functools
import math

import jax
import jax.numpy as jnp
from jax import lax
from jax.experimental import pallas as pl
from jax.experimental.pallas import tpu as pltpu
from jax.sharding import PartitionSpec as P

DOC_MOST = 1792
NEG_FILL = -1e30
TILE = 256
CHUNK = 128
LOG2_E = 1.4426950408889634


def attention_kernel(
    doc_ref,
    place_ref,
    q_ref,
    kv_ref,
    do_ref,
    o_ref,
    dq_ref,
    dkv_ref,
    q32,
    kt,
    vt,
    scores,
    weights,
    accum,
    dk_acc,
    dv_acc,
    *,
    heads,
    width,
    scale,
):
    tok = q_ref.shape[0]
    rows = heads * CHUNK
    docs = doc_ref.shape[0]
    base = place_ref[0]
    own = place_ref[1]
    q32[...] = q_ref[...].astype(jnp.float32)
    dk_acc[...] = jnp.zeros_like(dk_acc)
    dv_acc[...] = jnp.zeros_like(dv_acc)

    def start_of(position):
        end, found = jnp.int32(0), jnp.int32(0)
        for i in range(docs):
            end = end + doc_ref[i]
            found = jnp.where(end <= position, end, found)
        return found

    first_tile = jnp.maximum(start_of(base + own * TILE) - base, 0) // TILE

    def flip(i, carry):
        at = pl.multiple_of(i * TILE, TILE)
        pair = kv_ref[pl.ds(at, TILE), :].astype(jnp.float32)
        kt[:, pl.ds(at, TILE)] = pair[:, :width].T.astype(jnp.bfloat16)
        vt[0:width, pl.ds(at, TILE)] = pair[:, width:].T.astype(jnp.bfloat16)
        vt[width:, pl.ds(at, TILE)] = jnp.ones((16, TILE), jnp.bfloat16)
        return carry

    lax.fori_loop(first_tile, own + 1, flip, 0)

    for chunk in range(tok // CHUNK):
        t_first = base + own * TILE + chunk * CHUNK
        t_last = t_first + CHUNK - 1
        t_row = t_first + lax.broadcasted_iota(jnp.int32, (1, CHUNK), 1)
        end = jnp.int32(0)
        start_row = jnp.zeros((1, CHUNK), jnp.int32)
        for i in range(docs):
            end = end + doc_ref[i]
            start_row = jnp.where(t_row >= end, end, start_row)
        start_first = start_of(t_first)
        start_last = start_of(t_last)
        low = jnp.maximum(start_first - base, 0) // TILE

        q_parts = [
            q32[pl.ds(chunk * CHUNK, CHUNK), j, :].astype(jnp.bfloat16) for j in range(heads)
        ]
        q_rows = jnp.concatenate(q_parts, axis=0)
        q_cols = jnp.concatenate([p.astype(jnp.float32).T for p in q_parts], axis=1).astype(
            jnp.bfloat16
        )

        def score_tile(i, peak):
            at = pl.multiple_of(i * TILE, TILE)
            s_first = base + at
            product = jnp.dot(
                kv_ref[pl.ds(at, TILE), 0:width], q_cols, preferred_element_type=jnp.float32
            )
            inside = (s_first >= start_last) & (s_first + TILE - 1 <= t_first)

            @pl.when(inside)
            def _():
                scores[pl.ds(at, TILE), :] = product

            @pl.when(jnp.logical_not(inside))
            def _():
                s_col = s_first + lax.broadcasted_iota(jnp.int32, (TILE, CHUNK), 0)
                live = (s_col >= start_row) & (s_col <= t_row)
                for j in range(heads):
                    scores[pl.ds(at, TILE), j * CHUNK : (j + 1) * CHUNK] = jnp.where(
                        live, product[:, j * CHUNK : (j + 1) * CHUNK], NEG_FILL
                    )

            tile = scores[pl.ds(at, TILE), :]
            return jnp.maximum(peak, jnp.max(tile.reshape(TILE // 8, 8, rows), axis=0))

        peak = lax.fori_loop(
            low, own + 1, score_tile, jnp.full((8, rows), NEG_FILL, jnp.float32)
        )
        top = jnp.max(peak, axis=0, keepdims=True) * (scale * LOG2_E)

        accum[...] = jnp.zeros_like(accum)

        def weigh_tile(i, carry):
            at = pl.multiple_of(i * TILE, TILE)
            tile = jnp.exp2(scores[pl.ds(at, TILE), :] * (scale * LOG2_E) - top).astype(
                jnp.bfloat16
            )
            weights[pl.ds(at, TILE), :] = tile
            accum[...] += jnp.dot(
                vt[:, pl.ds(at, TILE)], tile, preferred_element_type=jnp.float32
            )
            return carry

        lax.fori_loop(low, own + 1, weigh_tile, 0)
        inverse = 1.0 / accum[width : width + 1, :]
        out_cols = accum[0:width, :] * inverse
        do_cols = jnp.concatenate(
            [
                do_ref[pl.ds(chunk * CHUNK, CHUNK), j * width : (j + 1) * width]
                .astype(jnp.float32)
                .T
                for j in range(heads)
            ],
            axis=1,
        )
        for j in range(heads):
            o_ref[pl.ds(chunk * CHUNK, CHUNK), j * width : (j + 1) * width] = (
                out_cols[:, j * CHUNK : (j + 1) * CHUNK].T.astype(jnp.bfloat16)
            )
        delta = (
            jnp.sum(
                do_cols * out_cols.astype(jnp.bfloat16).astype(jnp.float32), axis=0, keepdims=True
            )
            * inverse
        )
        do_scaled = do_cols * inverse
        do_cols_b = do_scaled.astype(jnp.bfloat16)
        do_rows_b = jnp.concatenate(
            [do_scaled[:, j * CHUNK : (j + 1) * CHUNK].T for j in range(heads)], axis=0
        ).astype(jnp.bfloat16)
        accum[...] = jnp.zeros_like(accum)

        def back_tile(i, carry):
            at = pl.multiple_of(i * TILE, TILE)
            tile = weights[pl.ds(at, TILE), :]
            d_probs = jnp.dot(
                kv_ref[pl.ds(at, TILE), width:], do_cols_b, preferred_element_type=jnp.float32
            )
            d_scores = (tile.astype(jnp.float32) * (d_probs - delta)).astype(jnp.bfloat16)
            dv_acc[pl.ds(at, TILE), :] += jnp.dot(
                tile, do_rows_b, preferred_element_type=jnp.float32
            )
            dk_acc[pl.ds(at, TILE), :] += jnp.dot(
                d_scores, q_rows, preferred_element_type=jnp.float32
            )
            accum[0:width, :] += jnp.dot(
                kt[:, pl.ds(at, TILE)], d_scores, preferred_element_type=jnp.float32
            )
            return carry

        lax.fori_loop(low, own + 1, back_tile, 0)
        for j in range(heads):
            q32[pl.ds(chunk * CHUNK, CHUNK), j, :] = (
                accum[0:width, j * CHUNK : (j + 1) * CHUNK].T * scale
            )

    dq_ref[...] = q32[...].astype(jnp.bfloat16)
    dkv_ref[:, 0:width] = (dk_acc[...] * scale).astype(jnp.bfloat16)
    dkv_ref[:, width:] = dv_acc[...].astype(jnp.bfloat16)


def attend(doc_lengths, place, queries, kv_window, grad_rows):
    tok, heads, width = queries.shape
    span = kv_window.shape[0]
    rows = heads * CHUNK
    vmem = pl.BlockSpec(memory_space=pltpu.VMEM)
    smem = pl.BlockSpec(memory_space=pltpu.SMEM)
    return pl.pallas_call(
        functools.partial(
            attention_kernel, heads=heads, width=width, scale=1.0 / math.sqrt(width)
        ),
        out_shape=(
            jax.ShapeDtypeStruct((tok, heads * width), jnp.bfloat16),
            jax.ShapeDtypeStruct((tok, heads, width), jnp.bfloat16),
            jax.ShapeDtypeStruct((span, 2 * width), jnp.bfloat16),
        ),
        in_specs=[smem, smem, vmem, vmem, vmem],
        out_specs=(vmem, vmem, vmem),
        scratch_shapes=[
            pltpu.VMEM((tok, heads, width), jnp.float32),
            pltpu.VMEM((width, span), jnp.bfloat16),
            pltpu.VMEM((width + 16, span), jnp.bfloat16),
            pltpu.VMEM((span, rows), jnp.float32),
            pltpu.VMEM((span, rows), jnp.bfloat16),
            pltpu.VMEM((width + 16, rows), jnp.float32),
            pltpu.VMEM((span, width), jnp.float32),
            pltpu.VMEM((span, width), jnp.float32),
        ],
        compiler_params=pltpu.CompilerParams(vmem_limit_bytes=48 * 1024 * 1024),
        cost_estimate=pl.CostEstimate(
            flops=14 * tok * heads * width * span,
            bytes_accessed=4 * tok * heads * width * 2 + 4 * span * width * 2,
            transcendentals=tok * heads * span,
        ),
        name="attention",
    )(doc_lengths, place, queries, kv_window, grad_rows)


def body(queries, key_states, value_states, doc_lengths, grad_attended):
    tok, heads, width = queries.shape
    ctx_count = lax.axis_size("ctx")
    ctx = lax.axis_index("ctx")
    reach = min((DOC_MOST + tok - 2) // tok, ctx_count - 1)
    blocks = reach + 1
    own_kv = jnp.concatenate(
        [key_states.reshape(tok, width), value_states.reshape(tok, width)], axis=1
    )
    kv_all = lax.all_gather(own_kv, "ctx", axis=0, tiled=True)
    grad_rows = lax.all_to_all(grad_attended, "head", split_axis=1, concat_axis=0, tiled=True)
    first = jnp.maximum(ctx - reach, 0)
    if blocks == ctx_count:
        kv_window = kv_all
    else:
        kv_window = lax.dynamic_slice_in_dim(kv_all, first * tok, blocks * tok, 0)
    place = jnp.stack([first * tok, ctx - first]).astype(jnp.int32)
    attended, grad_queries, d_kv = attend(doc_lengths, place, queries, kv_window, grad_rows)
    attended = lax.all_to_all(attended, "head", split_axis=0, concat_axis=1, tiled=True)
    if blocks != ctx_count:
        d_kv = lax.dynamic_update_slice_in_dim(
            jnp.zeros((ctx_count * tok, 2 * width), d_kv.dtype), d_kv, first * tok, 0
        )
    d_kv = lax.psum_scatter(d_kv, "ctx", scatter_dimension=0, tiled=True)
    grad_keys = d_kv[:, :width].reshape(tok, 1, width)
    grad_values = d_kv[:, width:].reshape(tok, 1, width)
    return attended, grad_queries, grad_keys, grad_values


def solution(mesh):
    in_specs = (
        P("ctx", "head", None),
        P("ctx", "head", None),
        P("ctx", "head", None),
        P(),
        P(("ctx", "head"), None),
    )
    out_specs = (
        P(("ctx", "head"), None),
        P("ctx", "head", None),
        P("ctx", "head", None),
        P("ctx", "head", None),
    )
    return jax.shard_map(body, mesh=mesh, in_specs=in_specs, out_specs=out_specs, check_vma=False)
```

```python
import functools
import math

import jax
import jax.numpy as jnp
from jax import lax
from jax.experimental import pallas as pl
from jax.experimental.pallas import tpu as pltpu
from jax.sharding import PartitionSpec as P

DOC_MOST = 1792
NEG_FILL = -1e30
TILE = 256
CHUNK = 128
LOG2_E = 1.4426950408889634


def dot(a, b):
    return jnp.dot(a, b, preferred_element_type=jnp.float32)


def dot_nt(a, b):
    return lax.dot_general(a, b, (((1,), (1,)), ((), ())), preferred_element_type=jnp.float32)


def attention_kernel(
    doc_ref,
    place_ref,
    q_ref,
    mine_ref,
    other_ref,
    do_ref,
    o_ref,
    dq_ref,
    dmine_ref,
    dother_ref,
    q32,
    kv,
    kt,
    vt,
    scores,
    weights,
    accum,
    dk_acc,
    dv_acc,
    *,
    heads,
    width,
    scale,
):
    tok = q_ref.shape[0]
    pairs = mine_ref.shape[0] // tok
    rows = heads * CHUNK
    docs = doc_ref.shape[0]
    base = place_ref[0]
    own = place_ref[1]
    parity = place_ref[2]
    eye = (
        lax.broadcasted_iota(jnp.int32, (width, width), 0)
        == lax.broadcasted_iota(jnp.int32, (width, width), 1)
    ).astype(jnp.bfloat16)
    for pair in range(pairs):
        src = pl.ds(pair * tok, tok)
        kv[pl.ds(pl.multiple_of((2 * pair + parity) * tok, tok), tok), :] = mine_ref[src, :]
        kv[pl.ds(pl.multiple_of((2 * pair + 1 - parity) * tok, tok), tok), :] = other_ref[src, :]
    q32[...] = q_ref[...].astype(jnp.float32)
    dk_acc[...] = jnp.zeros_like(dk_acc)
    dv_acc[...] = jnp.zeros_like(dv_acc)

    def start_of(position):
        end, found = jnp.int32(0), jnp.int32(0)
        for i in range(docs):
            end = end + doc_ref[i]
            found = jnp.where(end <= position, end, found)
        return found

    first_tile = jnp.maximum(start_of(base + own * TILE) - base, 0) // TILE

    def flip(i, carry):
        at = pl.multiple_of(i * TILE, TILE)
        kt[:, pl.ds(at, TILE)] = dot_nt(eye, kv[pl.ds(at, TILE), 0:width]).astype(jnp.bfloat16)
        vt[0:width, pl.ds(at, TILE)] = dot_nt(eye, kv[pl.ds(at, TILE), width:]).astype(
            jnp.bfloat16
        )
        vt[width:, pl.ds(at, TILE)] = jnp.ones((16, TILE), jnp.bfloat16)
        return carry

    lax.fori_loop(first_tile, own + 1, flip, 0)

    for chunk in range(tok // CHUNK):
        here = pl.ds(chunk * CHUNK, CHUNK)
        t_first = base + own * TILE + chunk * CHUNK
        t_last = t_first + CHUNK - 1
        t_row = t_first + lax.broadcasted_iota(jnp.int32, (1, CHUNK), 1)
        end = jnp.int32(0)
        start_row = jnp.zeros((1, CHUNK), jnp.int32)
        for i in range(docs):
            end = end + doc_ref[i]
            start_row = jnp.where(t_row >= end, end, start_row)
        low = jnp.maximum(start_of(t_first) - base, 0) // TILE
        clear = jnp.clip((start_of(t_last) - base + TILE - 1) // TILE, low, own)
        last_size = (chunk + 1) * CHUNK

        q_rows = jnp.concatenate(
            [q32[here, j, :].astype(jnp.bfloat16) for j in range(heads)], axis=0
        )
        q_cols = dot_nt(eye, q_rows).astype(jnp.bfloat16)
        do_rows = jnp.concatenate(
            [do_ref[here, j * width : (j + 1) * width] for j in range(heads)], axis=0
        )
        do_cols = dot_nt(eye, do_rows).astype(jnp.bfloat16)

        def score_tile(i, peak, size, masked):
            at = pl.multiple_of(i * TILE, TILE)
            product = dot(kv[pl.ds(at, size), 0:width], q_cols)
            if masked:
                s_col = base + at + lax.broadcasted_iota(jnp.int32, (size, CHUNK), 0)
                live = (s_col >= start_row) & (s_col <= t_row)
                product = jnp.concatenate(
                    [
                        jnp.where(live, product[:, j * CHUNK : (j + 1) * CHUNK], NEG_FILL)
                        for j in range(heads)
                    ],
                    axis=1,
                )
            scores[pl.ds(at, size), :] = product
            return jnp.maximum(peak, jnp.max(product.reshape(size // 8, 8, rows), axis=0))

        def weigh_tile(i, carry, size):
            at = pl.multiple_of(i * TILE, TILE)
            tile = jnp.exp2(scores[pl.ds(at, size), :] * (scale * LOG2_E) - top).astype(
                jnp.bfloat16
            )
            weights[pl.ds(at, size), :] = tile
            accum[...] += dot(vt[:, pl.ds(at, size)], tile)
            return carry

        def back_tile(i, carry, size):
            at = pl.multiple_of(i * TILE, TILE)
            probs = weights[pl.ds(at, size), :].astype(jnp.float32) * inverse
            d_probs = dot(kv[pl.ds(at, size), width:], do_cols)
            d_scores = (probs * (d_probs - delta)).astype(jnp.bfloat16)
            dv_acc[pl.ds(at, size), :] += dot(probs.astype(jnp.bfloat16), do_rows)
            dk_acc[pl.ds(at, size), :] += dot(d_scores, q_rows)
            accum[0:width, :] += dot(kt[:, pl.ds(at, size)], d_scores)
            return carry

        peak = jnp.full((8, rows), NEG_FILL, jnp.float32)
        peak = lax.fori_loop(low, clear, lambda i, p: score_tile(i, p, TILE, True), peak)
        peak = lax.fori_loop(clear, own, lambda i, p: score_tile(i, p, TILE, False), peak)
        peak = score_tile(own, peak, last_size, True)
        top = jnp.max(peak, axis=0, keepdims=True) * (scale * LOG2_E)

        accum[...] = jnp.zeros_like(accum)
        lax.fori_loop(low, own, lambda i, c: weigh_tile(i, c, TILE), 0)
        weigh_tile(own, 0, last_size)
        inverse = 1.0 / accum[width : width + 1, :]
        out_cols = (accum[0:width, :] * inverse).astype(jnp.bfloat16)
        delta = jnp.sum(
            do_cols.astype(jnp.float32) * out_cols.astype(jnp.float32), axis=0, keepdims=True
        )
        for j in range(heads):
            o_ref[here, j * width : (j + 1) * width] = dot_nt(
                eye, out_cols[:, j * CHUNK : (j + 1) * CHUNK]
            ).astype(jnp.bfloat16)

        accum[...] = jnp.zeros_like(accum)
        lax.fori_loop(low, own, lambda i, c: back_tile(i, c, TILE), 0)
        back_tile(own, 0, last_size)
        dq_cols = (accum[0:width, :] * scale).astype(jnp.bfloat16)
        for j in range(heads):
            q32[here, j, :] = dot_nt(eye, dq_cols[:, j * CHUNK : (j + 1) * CHUNK])

    dq_ref[...] = q32[...].astype(jnp.bfloat16)
    for pair in range(pairs):
        dst = pl.ds(pair * tok, tok)
        src = pl.ds(pl.multiple_of((2 * pair + parity) * tok, tok), tok)
        dmine_ref[dst, 0:width] = dk_acc[src, :] * scale
        dmine_ref[dst, width:] = dv_acc[src, :]
        src = pl.ds(pl.multiple_of((2 * pair + 1 - parity) * tok, tok), tok)
        dother_ref[dst, 0:width] = (dk_acc[src, :] * scale).astype(jnp.bfloat16)
        dother_ref[dst, width:] = dv_acc[src, :].astype(jnp.bfloat16)


def attend(doc_lengths, place, queries, mine, other, grad_rows):
    tok, heads, width = queries.shape
    half = mine.shape[0]
    span = 2 * half
    rows = heads * CHUNK
    vmem = pl.BlockSpec(memory_space=pltpu.VMEM)
    smem = pl.BlockSpec(memory_space=pltpu.SMEM)
    return pl.pallas_call(
        functools.partial(
            attention_kernel, heads=heads, width=width, scale=1.0 / math.sqrt(width)
        ),
        out_shape=(
            jax.ShapeDtypeStruct((tok, heads * width), jnp.bfloat16),
            jax.ShapeDtypeStruct((tok, heads, width), jnp.bfloat16),
            jax.ShapeDtypeStruct((half, 2 * width), jnp.float32),
            jax.ShapeDtypeStruct((half, 2 * width), jnp.bfloat16),
        ),
        in_specs=[smem, smem, vmem, vmem, vmem, vmem],
        out_specs=(vmem, vmem, vmem, vmem),
        scratch_shapes=[
            pltpu.VMEM((tok, heads, width), jnp.float32),
            pltpu.VMEM((span, 2 * width), jnp.bfloat16),
            pltpu.VMEM((width, span), jnp.bfloat16),
            pltpu.VMEM((width + 16, span), jnp.bfloat16),
            pltpu.VMEM((span, rows), jnp.float32),
            pltpu.VMEM((span, rows), jnp.bfloat16),
            pltpu.VMEM((width + 16, rows), jnp.float32),
            pltpu.VMEM((span, width), jnp.float32),
            pltpu.VMEM((span, width), jnp.float32),
        ],
        compiler_params=pltpu.CompilerParams(vmem_limit_bytes=48 * 1024 * 1024),
        cost_estimate=pl.CostEstimate(
            flops=14 * tok * heads * width * span,
            bytes_accessed=4 * tok * heads * width * 2 + 4 * span * width * 2,
            transcendentals=tok * heads * span,
        ),
        name="attention",
    )(doc_lengths, place, queries, mine, other, grad_rows)


def shifted(block, by, count):
    pairs = [(i, i + by) for i in range(count) if 0 <= i + by < count]
    return lax.ppermute(block, "ctx", pairs)


def exchanged(block, count):
    return lax.ppermute(block, "ctx", [(i, i ^ 1) for i in range(count)])


def body(queries, key_states, value_states, doc_lengths, grad_attended):
    tok, heads, width = queries.shape
    count = lax.axis_size("ctx")
    ctx = lax.axis_index("ctx")
    reach = min((DOC_MOST + tok - 2) // tok, count - 1)
    back = min((reach + 1) // 2, count // 2 - 1)
    own_kv = jnp.concatenate(
        [key_states.reshape(tok, width), value_states.reshape(tok, width)], axis=1
    )
    near = exchanged(own_kv, count)
    arrived = [shifted(own_kv, 2 * k, count) for k in range(1, back + 1)]
    first_part = (back + 1) // 2
    near_far = [exchanged(jnp.concatenate(arrived[:first_part], axis=0), count)]
    near_far.append(exchanged(jnp.concatenate(arrived[first_part:], axis=0), count))
    near_far = jnp.concatenate(near_far, axis=0).reshape(back, tok, 2 * width)
    mine = jnp.concatenate(arrived[::-1] + [own_kv], axis=0)
    other = jnp.concatenate([near_far[k] for k in range(back)][::-1] + [near], axis=0)

    grad_rows = lax.all_to_all(grad_attended, "head", split_axis=1, concat_axis=0, tiled=True)
    parity = ctx % 2
    place = jnp.stack([(ctx - parity - 2 * back) * tok, 2 * back + parity, parity])
    attended, grad_queries, d_mine, d_other = attend(
        doc_lengths, place.astype(jnp.int32), queries, mine, other, grad_rows
    )
    d_near = exchanged(d_other, count)
    attended = lax.all_to_all(attended, "head", split_axis=0, concat_axis=1, tiled=True)
    total = (d_mine + d_near.astype(jnp.float32)).reshape(back + 1, tok, 2 * width)
    own_total = total[back]
    for k in range(back, 0, -1):
        own_total = own_total + shifted(
            total[back - k].astype(jnp.bfloat16), -2 * k, count
        ).astype(jnp.float32)
    own_total = own_total.astype(jnp.bfloat16)
    grad_keys = own_total[:, :width].reshape(tok, 1, width)
    grad_values = own_total[:, width:].reshape(tok, 1, width)
    return attended, grad_queries, grad_keys, grad_values


def solution(mesh):
    in_specs = (
        P("ctx", "head", None),
        P("ctx", "head", None),
        P("ctx", "head", None),
        P(),
        P(("ctx", "head"), None),
    )
    out_specs = (
        P(("ctx", "head"), None),
        P("ctx", "head", None),
        P("ctx", "head", None),
        P("ctx", "head", None),
    )
    return jax.shard_map(body, mesh=mesh, in_specs=in_specs, out_specs=out_specs, check_vma=False)
```

```python
import functools
import math

import jax
import jax.numpy as jnp
from jax import lax
from jax.experimental import pallas as pl
from jax.experimental.pallas import tpu as pltpu
from jax.sharding import PartitionSpec as P

DOC_MOST = 1792
NEG_FILL = -1e30
TILE = 256
ONES = 16
LOG2_E = 1.4426950408889634


def dot(a, b):
    return jnp.dot(a, b, preferred_element_type=jnp.float32)


def dot_nt(a, b):
    return lax.dot_general(a, b, (((1,), (1,)), ((), ())), preferred_element_type=jnp.float32)


def unit(size):
    rows = lax.broadcasted_iota(jnp.int32, (size, size), 0)
    return (rows == lax.broadcasted_iota(jnp.int32, (size, size), 1)).astype(jnp.bfloat16)


def less(tile, row8):
    rows, columns = tile.shape
    return (tile.reshape(rows // 8, 8, columns) - row8[None]).reshape(rows, columns)


def attention_kernel(
    doc_ref,
    place_ref,
    q_ref,
    do_ref,
    own_ref,
    near_ref,
    far_ref,
    *refs,
    back,
    heads,
    width,
    scale,
):
    arrived = refs[:back]
    (o_ref, dq_ref, dmine_ref, dother_ref) = refs[back : back + 4]
    (
        q32,
        keys,
        values,
        kt,
        vt,
        q_rows,
        do_rows,
        q_cols,
        do_cols,
        scores,
        probs,
        d_scores,
        accum,
        top,
        delta,
    ) = refs[back + 4 :]
    tok = q_ref.shape[0]
    docs = doc_ref.shape[0]
    base = place_ref[0]
    own = place_ref[1]
    parity = place_ref[2]
    small, large = unit(width), unit(tok)

    for pair in range(back + 1):
        k = back - pair
        mine = own_ref[...] if k == 0 else arrived[k - 1][...]
        other = near_ref[...] if k == 0 else far_ref[2 * tok * (k - 1) : 2 * tok * k, :]
        for block, place in ((mine, 2 * pair + parity), (other, 2 * pair + 1 - parity)):
            at = pl.ds(pl.multiple_of(place * tok, tok), tok)
            keys[at, :] = block[:tok]
            values[at, :] = block[tok:]

    q32[...] = q_ref[...].astype(jnp.float32)
    accum[...] = jnp.zeros_like(accum)
    top[...] = jnp.full_like(top, NEG_FILL)
    for j in range(heads):
        part = pl.ds(j * tok, tok)
        q_part = q32[:, j, :].astype(jnp.bfloat16)
        do_part = do_ref[:, j * width : (j + 1) * width]
        q_rows[part, :] = q_part
        do_rows[part, :] = do_part
        q_cols[:, part] = dot_nt(small, q_part).astype(jnp.bfloat16)
        do_cols[:, part] = dot_nt(small, do_part).astype(jnp.bfloat16)

    t_first = base + own * TILE
    t_row = t_first + lax.broadcasted_iota(jnp.int32, (1, tok), 1)
    end = jnp.int32(0)
    start_first, start_last = jnp.int32(0), jnp.int32(0)
    start_row = jnp.zeros((1, tok), jnp.int32)
    for i in range(docs):
        end = end + doc_ref[i]
        start_first = jnp.where(end <= t_first, end, start_first)
        start_last = jnp.where(end <= t_first + tok - 1, end, start_last)
        start_row = jnp.where(t_row >= end, end, start_row)
    low = jnp.maximum(start_first - base, 0) // TILE
    clear = jnp.clip((start_last - base + TILE - 1) // TILE, low, own)

    def score_tile(i, masked):
        at = pl.ds(pl.multiple_of(i * TILE, TILE), TILE)
        key_tile, value_tile = keys[at, :], values[at, :]
        kt[:, at] = dot_nt(small, key_tile).astype(jnp.bfloat16)
        vt[0:width, at] = dot_nt(small, value_tile).astype(jnp.bfloat16)
        vt[width:, at] = jnp.ones((ONES, TILE), jnp.bfloat16)
        if masked:
            s_col = base + i * TILE + lax.broadcasted_iota(jnp.int32, (TILE, tok), 0)
            live = (s_col >= start_row) & (s_col <= t_row)
        for j in range(heads):
            part = pl.ds(j * tok, tok)
            tile = dot(key_tile, q_cols[:, part]) * (scale * LOG2_E)
            if masked:
                tile = jnp.where(live, tile, NEG_FILL)
            scores[at, part] = tile
            top[:, part] = jnp.maximum(
                top[:, part], jnp.max(tile.reshape(TILE // 8, 8, tok), axis=0)
            )

    def edge_step(n, carry):
        score_tile(jnp.where(n < clear - low, low + n, own), True)
        return carry

    def inner_step(i, carry):
        score_tile(i, False)
        return carry

    lax.fori_loop(0, clear - low + 1, edge_step, 0)
    lax.fori_loop(clear, own, inner_step, 0)
    top[...] = jnp.broadcast_to(jnp.max(top[...], axis=0, keepdims=True), top.shape)

    def weigh_step(i, carry):
        at = pl.ds(pl.multiple_of(i * TILE, TILE), TILE)
        for j in range(heads):
            part = pl.ds(j * tok, tok)
            weights = jnp.exp2(less(scores[at, part], top[:, part])).astype(jnp.bfloat16)
            accum[:, part] += dot(vt[:, at], weights)
        return carry

    lax.fori_loop(low, own + 1, weigh_step, 0)

    for j in range(heads):
        part = pl.ds(j * tok, tok)
        total = accum[width : width + 8, part]
        out = (accum[0:width, part] * (1.0 / total[0:1])).astype(jnp.bfloat16)
        o_ref[:, j * width : (j + 1) * width] = dot_nt(large, out).astype(jnp.bfloat16)
        product = do_cols[:, part].astype(jnp.float32) * out.astype(jnp.float32)
        delta[:, part] = jnp.broadcast_to(jnp.sum(product, axis=0, keepdims=True), (8, tok))
        top[:, part] = top[:, part] + jnp.log2(total)
    accum[...] = jnp.zeros_like(accum)

    def put(i, d_keys, d_values):
        to = pl.ds(pl.multiple_of((i // 2) * tok, tok), tok)

        @pl.when(i % 2 == parity)
        def _():
            dmine_ref[to, 0:width] = d_keys
            dmine_ref[to, width:] = d_values

        @pl.when(i % 2 != parity)
        def _():
            dother_ref[to, 0:width] = d_keys.astype(jnp.bfloat16)
            dother_ref[to, width:] = d_values.astype(jnp.bfloat16)

    def empty_step(i, carry):
        zero = jnp.zeros((tok, width), jnp.float32)
        put(i, zero, zero)
        return carry

    def back_step(i, carry):
        at = pl.ds(pl.multiple_of(i * TILE, TILE), TILE)
        value_tile = values[at, :]
        for j in range(heads):
            part = pl.ds(j * tok, tok)
            tile = jnp.exp2(less(scores[at, part], top[:, part]))
            d_probs = dot(value_tile, do_cols[:, part])
            d_tile = (tile * less(d_probs, delta[:, part])).astype(jnp.bfloat16)
            probs[:, part] = tile.astype(jnp.bfloat16)
            d_scores[:, part] = d_tile
            accum[0:width, part] += dot(kt[:, at], d_tile)
        put(i, dot(d_scores[...], q_rows[...]) * scale, dot(probs[...], do_rows[...]))
        return carry

    lax.fori_loop(0, low, empty_step, 0)
    lax.fori_loop(own + 1, 2 * back + 2, empty_step, 0)
    lax.fori_loop(low, own + 1, back_step, 0)
    for j in range(heads):
        d_part = (accum[0:width, j * tok : (j + 1) * tok] * scale).astype(jnp.bfloat16)
        q32[:, j, :] = dot_nt(large, d_part)
    dq_ref[...] = q32[...].astype(jnp.bfloat16)


def attend(doc_lengths, place, queries, grad_rows, own, near, far, arrived):
    tok, heads, width = queries.shape
    back = len(arrived)
    half = (back + 1) * tok
    span = 2 * half
    rows = heads * tok
    vmem = pl.BlockSpec(memory_space=pltpu.VMEM)
    smem = pl.BlockSpec(memory_space=pltpu.SMEM)
    return pl.pallas_call(
        functools.partial(
            attention_kernel,
            back=back,
            heads=heads,
            width=width,
            scale=1.0 / math.sqrt(width),
        ),
        out_shape=(
            jax.ShapeDtypeStruct((tok, heads * width), jnp.bfloat16),
            jax.ShapeDtypeStruct((tok, heads, width), jnp.bfloat16),
            jax.ShapeDtypeStruct((half, 2 * width), jnp.float32),
            jax.ShapeDtypeStruct((half, 2 * width), jnp.bfloat16),
        ),
        in_specs=[smem, smem] + [vmem] * (5 + back),
        out_specs=(vmem, vmem, vmem, vmem),
        scratch_shapes=[
            pltpu.VMEM((tok, heads, width), jnp.float32),
            pltpu.VMEM((span, width), jnp.bfloat16),
            pltpu.VMEM((span, width), jnp.bfloat16),
            pltpu.VMEM((width, span), jnp.bfloat16),
            pltpu.VMEM((width + ONES, span), jnp.bfloat16),
            pltpu.VMEM((rows, width), jnp.bfloat16),
            pltpu.VMEM((rows, width), jnp.bfloat16),
            pltpu.VMEM((width, rows), jnp.bfloat16),
            pltpu.VMEM((width, rows), jnp.bfloat16),
            pltpu.VMEM((span, rows), jnp.float32),
            pltpu.VMEM((TILE, rows), jnp.bfloat16),
            pltpu.VMEM((TILE, rows), jnp.bfloat16),
            pltpu.VMEM((width + ONES, rows), jnp.float32),
            pltpu.VMEM((8, rows), jnp.float32),
            pltpu.VMEM((8, rows), jnp.float32),
        ],
        compiler_params=pltpu.CompilerParams(vmem_limit_bytes=50 * 1024 * 1024),
        cost_estimate=pl.CostEstimate(
            flops=14 * tok * heads * width * span,
            bytes_accessed=4 * tok * heads * width * 2 + 4 * span * width * 2,
            transcendentals=tok * heads * span,
        ),
        name="attention",
    )(doc_lengths, place, queries, grad_rows, own, near, far, *arrived)


def shifted(block, by, count):
    pairs = [(i, i + by) for i in range(count) if 0 <= i + by < count]
    return lax.ppermute(block, "ctx", pairs)


def exchanged(block, count):
    return lax.ppermute(block, "ctx", [(i, i ^ 1) for i in range(count)])


def body(queries, key_states, value_states, doc_lengths, grad_attended):
    tok, heads, width = queries.shape
    count = lax.axis_size("ctx")
    ctx = lax.axis_index("ctx")
    reach = min((DOC_MOST + tok - 2) // tok, count - 1)
    back = min((reach + 1) // 2, count // 2 - 1)
    own = jnp.concatenate(
        [key_states.reshape(tok, width), value_states.reshape(tok, width)], axis=0
    )
    near = exchanged(own, count)
    arrived = [shifted(own, 2 * k, count) for k in range(1, back + 1)]
    near, arrived, grad_attended = lax.optimization_barrier((near, arrived, grad_attended))
    far = exchanged(jnp.concatenate(arrived, axis=0), count)
    grad_rows = lax.all_to_all(grad_attended, "head", split_axis=1, concat_axis=0, tiled=True)
    parity = ctx % 2
    place = jnp.stack([(ctx - parity - 2 * back) * tok, 2 * back + parity, parity])
    attended, grad_queries, d_mine, d_other = attend(
        doc_lengths, place.astype(jnp.int32), queries, grad_rows, own, near, far, arrived
    )
    d_near = exchanged(d_other, count)
    attended = lax.all_to_all(attended, "head", split_axis=0, concat_axis=1, tiled=True)
    total = (d_mine + d_near.astype(jnp.float32)).reshape(back + 1, tok, 2 * width)
    own_total = total[back]
    for k in range(back, 0, -1):
        own_total = own_total + shifted(
            total[back - k].astype(jnp.bfloat16), -2 * k, count
        ).astype(jnp.float32)
    own_total = own_total.astype(jnp.bfloat16)
    grad_keys = own_total[:, :width].reshape(tok, 1, width)
    grad_values = own_total[:, width:].reshape(tok, 1, width)
    return attended, grad_queries, grad_keys, grad_values


def solution(mesh):
    in_specs = (
        P("ctx", "head", None),
        P("ctx", "head", None),
        P("ctx", "head", None),
        P(),
        P(("ctx", "head"), None),
    )
    out_specs = (
        P(("ctx", "head"), None),
        P("ctx", "head", None),
        P("ctx", "head", None),
        P("ctx", "head", None),
    )
    return jax.shard_map(body, mesh=mesh, in_specs=in_specs, out_specs=out_specs, check_vma=False)
```

```python
import functools
import math

import jax
import jax.numpy as jnp
from jax import lax
from jax.experimental import pallas as pl
from jax.experimental.pallas import tpu as pltpu
from jax.sharding import PartitionSpec as P

DOC_MOST = 1792
NEG_FILL = -1e30
TILE = 256
CHUNK = 128
LOG2_E = 1.4426950408889634


def dot(a, b):
    return jnp.dot(a, b, preferred_element_type=jnp.float32)


def dot_nt(a, b):
    return lax.dot_general(a, b, (((1,), (1,)), ((), ())), preferred_element_type=jnp.float32)


def unit(size):
    rows = lax.broadcasted_iota(jnp.int32, (size, size), 0)
    return (rows == lax.broadcasted_iota(jnp.int32, (size, size), 1)).astype(jnp.bfloat16)


def twice(column):
    return jnp.concatenate([column, column], axis=1)


def attention_kernel(
    doc_ref,
    place_ref,
    q_ref,
    do_ref,
    own_ref,
    near_ref,
    far_ref,
    *refs,
    back,
    heads,
    width,
    scale,
):
    arrived = refs[:back]
    (o_ref, dq_ref, dmine_ref, dother_ref) = refs[back : back + 4]
    (
        q32,
        keys,
        values,
        q_rows,
        do_rows,
        q_cols,
        do_cols,
        scores,
        accum,
        dq_acc,
        top,
        delta,
        d_blocks,
    ) = refs[back + 4 :]
    tok = q_ref.shape[0]
    docs = doc_ref.shape[0]
    base = place_ref[0]
    own = place_ref[1]
    parity = place_ref[2]
    small = unit(width)
    ones = jnp.ones((width, width), jnp.bfloat16)

    values[:, width:] = jnp.ones_like(values[:, width:])
    for pair in range(back + 1):
        k = back - pair
        mine = own_ref if k == 0 else arrived[k - 1]
        for ref, first, place in (
            (mine, 0, 2 * pair + parity),
            (near_ref, 0, 2 * pair + 1 - parity)
            if k == 0
            else (far_ref, 2 * tok * (k - 1), 2 * pair + 1 - parity),
        ):
            at = pl.ds(pl.multiple_of(place * tok, tok), tok)
            keys[at, :] = ref[first : first + tok, :]
            values[at, 0:width] = ref[first + tok : first + 2 * tok, :]

    q32[...] = q_ref[...].astype(jnp.float32)
    d_blocks[...] = jnp.zeros_like(d_blocks)

    def chunk_step(chunk, carry):
        here = pl.ds(pl.multiple_of(chunk * CHUNK, CHUNK), CHUNK)
        for j in range(heads):
            part = pl.ds(j * CHUNK, CHUNK)
            q_rows[part, :] = q32[here, j, :].astype(jnp.bfloat16)
            do_rows[part, :] = do_ref[here, j * width : (j + 1) * width]
        q_cols[...] = dot_nt(small, q_rows[...]).astype(jnp.bfloat16)
        do_cols[...] = dot_nt(small, do_rows[...]).astype(jnp.bfloat16)
        top[...] = jnp.full_like(top, NEG_FILL)

        t_first = base + own * TILE + chunk * CHUNK
        t_last = t_first + CHUNK - 1
        t_col = t_first + lax.broadcasted_iota(jnp.int32, (CHUNK, width), 0)
        end = jnp.int32(0)
        start_first, start_last = jnp.int32(0), jnp.int32(0)
        start_col = jnp.zeros((CHUNK, width), jnp.int32)
        for i in range(docs):
            end = end + doc_ref[i]
            start_first = jnp.where(end <= t_first, end, start_first)
            start_last = jnp.where(end <= t_last, end, start_last)
            start_col = jnp.where(t_col >= end, end, start_col)
        low = jnp.maximum(start_first - base, 0) // TILE
        clear = jnp.clip((start_last - base + TILE - 1) // TILE, low, own)

        def score_tile(i, masked):
            at = pl.ds(pl.multiple_of(i * TILE, TILE), TILE)
            tile = dot_nt(q_rows[...], keys[at, :]) * (scale * LOG2_E)
            if masked:
                s_row = base + i * TILE + lax.broadcasted_iota(jnp.int32, (CHUNK, TILE), 1)
                live = (s_row >= twice(start_col)) & (s_row <= twice(t_col))
                tile = jnp.concatenate(
                    [
                        jnp.where(live, tile[j * CHUNK : (j + 1) * CHUNK], NEG_FILL)
                        for j in range(heads)
                    ],
                    axis=0,
                )
            scores[i] = tile
            top[...] = jnp.maximum(top[...], jnp.maximum(tile[:, :width], tile[:, width:]))

        def edge_step(n, carry):
            score_tile(jnp.where(n < clear - low, low + n, own), True)
            return carry

        def inner_step(i, carry):
            score_tile(i, False)
            return carry

        lax.fori_loop(0, clear - low + 1, edge_step, 0)
        lax.fori_loop(clear, own, inner_step, 0)
        top[...] = jnp.broadcast_to(jnp.max(top[...], axis=1, keepdims=True), top.shape)
        accum[...] = jnp.zeros_like(accum)

        def weigh_step(i, carry):
            at = pl.ds(pl.multiple_of(i * TILE, TILE), TILE)
            weights = jnp.exp2(scores[i] - twice(top[...])).astype(jnp.bfloat16)
            accum[...] += dot(weights, values[at, :])
            return carry

        lax.fori_loop(low, own + 1, weigh_step, 0)
        total = accum[:, width:]
        out = (accum[:, 0:width] / total).astype(jnp.bfloat16)
        for j in range(heads):
            o_ref[here, j * width : (j + 1) * width] = out[j * CHUNK : (j + 1) * CHUNK]
        top[...] = top[...] + jnp.log2(total)
        product = do_rows[...].astype(jnp.float32) * out.astype(jnp.float32)
        coarse = product.astype(jnp.bfloat16)
        fine = (product - coarse.astype(jnp.float32)).astype(jnp.bfloat16)
        delta[...] = dot(coarse, ones) + dot(fine, ones)
        dq_acc[...] = jnp.zeros_like(dq_acc)

        def back_step(i, carry):
            at = pl.ds(pl.multiple_of(i * TILE, TILE), TILE)
            probs = jnp.exp2(scores[i] - twice(top[...]))
            d_probs = dot_nt(do_rows[...], values[at, 0:width])
            d_scores = (probs * (d_probs - twice(delta[...]))).astype(jnp.bfloat16)
            dq_acc[...] += dot(d_scores, keys[at, :])
            d_blocks[i, 0:width, :] += dot(q_cols[...], d_scores)
            d_blocks[i, width:, :] += dot(do_cols[...], probs.astype(jnp.bfloat16))
            return carry

        lax.fori_loop(low, own + 1, back_step, 0)
        for j in range(heads):
            q32[here, j, :] = dq_acc[j * CHUNK : (j + 1) * CHUNK, :] * scale
        return carry

    lax.fori_loop(0, tok // CHUNK, chunk_step, 0)
    dq_ref[...] = q32[...].astype(jnp.bfloat16)
    for pair in range(back + 1):
        mine, other = 2 * pair + parity, 2 * pair + 1 - parity
        dmine_ref[pair, 0:width, :] = d_blocks[mine, 0:width, :] * scale
        dmine_ref[pair, width:, :] = d_blocks[mine, width:, :]
        dother_ref[pair, 0:width, :] = (d_blocks[other, 0:width, :] * scale).astype(jnp.bfloat16)
        dother_ref[pair, width:, :] = d_blocks[other, width:, :].astype(jnp.bfloat16)


def attend(doc_lengths, place, queries, grad_rows, own, near, far, arrived):
    tok, heads, width = queries.shape
    back = len(arrived)
    tiles = 2 * (back + 1)
    span = tiles * tok
    rows = heads * CHUNK
    vmem = pl.BlockSpec(memory_space=pltpu.VMEM)
    smem = pl.BlockSpec(memory_space=pltpu.SMEM)
    return pl.pallas_call(
        functools.partial(
            attention_kernel,
            back=back,
            heads=heads,
            width=width,
            scale=1.0 / math.sqrt(width),
        ),
        out_shape=(
            jax.ShapeDtypeStruct((tok, heads * width), jnp.bfloat16),
            jax.ShapeDtypeStruct((tok, heads, width), jnp.bfloat16),
            jax.ShapeDtypeStruct((back + 1, 2 * width, tok), jnp.float32),
            jax.ShapeDtypeStruct((back + 1, 2 * width, tok), jnp.bfloat16),
        ),
        in_specs=[smem, smem] + [vmem] * (5 + back),
        out_specs=(vmem, vmem, vmem, vmem),
        scratch_shapes=[
            pltpu.VMEM((tok, heads, width), jnp.float32),
            pltpu.VMEM((span, width), jnp.bfloat16),
            pltpu.VMEM((span, 2 * width), jnp.bfloat16),
            pltpu.VMEM((rows, width), jnp.bfloat16),
            pltpu.VMEM((rows, width), jnp.bfloat16),
            pltpu.VMEM((width, rows), jnp.bfloat16),
            pltpu.VMEM((width, rows), jnp.bfloat16),
            pltpu.VMEM((tiles, rows, TILE), jnp.float32),
            pltpu.VMEM((rows, 2 * width), jnp.float32),
            pltpu.VMEM((rows, width), jnp.float32),
            pltpu.VMEM((rows, width), jnp.float32),
            pltpu.VMEM((rows, width), jnp.float32),
            pltpu.VMEM((tiles, 2 * width, tok), jnp.float32),
        ],
        compiler_params=pltpu.CompilerParams(vmem_limit_bytes=40 * 1024 * 1024),
        cost_estimate=pl.CostEstimate(
            flops=14 * tok * heads * width * span,
            bytes_accessed=4 * tok * heads * width * 2 + 4 * span * width * 2,
            transcendentals=tok * heads * span,
        ),
        name="attention",
    )(doc_lengths, place, queries, grad_rows, own, near, far, *arrived)


def finish_kernel(own_ref, *refs):
    arrived = refs[:-2]
    dk_ref, dv_ref = refs[-2:]
    total = own_ref[...]
    for ref in arrived:
        total = total + ref[...].astype(jnp.float32)
    total = total.astype(jnp.bfloat16)
    width = dk_ref.shape[1]
    large = unit(dk_ref.shape[0])
    dk_ref[...] = dot_nt(large, total[:width]).astype(jnp.bfloat16)
    dv_ref[...] = dot_nt(large, total[width:]).astype(jnp.bfloat16)


def finish(own_part, arrived):
    both, tok = own_part.shape
    vmem = pl.BlockSpec(memory_space=pltpu.VMEM)
    shape = jax.ShapeDtypeStruct((tok, both // 2), jnp.bfloat16)
    return pl.pallas_call(
        finish_kernel,
        out_shape=(shape, shape),
        in_specs=[vmem] * (1 + len(arrived)),
        out_specs=(vmem, vmem),
        name="finish",
    )(own_part, *arrived)


def shifted(block, by, count):
    pairs = [(i, i + by) for i in range(count) if 0 <= i + by < count]
    return lax.ppermute(block, "ctx", pairs)


def exchanged(block, count):
    return lax.ppermute(block, "ctx", [(i, i ^ 1) for i in range(count)])


def body(queries, key_states, value_states, doc_lengths, grad_attended):
    tok, heads, width = queries.shape
    count = lax.axis_size("ctx")
    ctx = lax.axis_index("ctx")
    reach = min((DOC_MOST + tok - 2) // tok, count - 1)
    back = min((reach + 1) // 2, count // 2 - 1)
    own = jnp.concatenate(
        [key_states.reshape(tok, width), value_states.reshape(tok, width)], axis=0
    )
    near = exchanged(own, count)
    arrived = [shifted(own, 2 * k, count) for k in range(1, back + 1)]
    near, arrived, grad_attended = lax.optimization_barrier((near, arrived, grad_attended))
    far = exchanged(jnp.concatenate(arrived, axis=0), count)
    grad_rows = lax.all_to_all(grad_attended, "head", split_axis=1, concat_axis=0, tiled=True)
    parity = ctx % 2
    place = jnp.stack([(ctx - parity - 2 * back) * tok, 2 * back + parity, parity])
    attended, grad_queries, d_mine, d_other = attend(
        doc_lengths, place.astype(jnp.int32), queries, grad_rows, own, near, far, arrived
    )
    d_near = exchanged(d_other, count)
    attended = lax.all_to_all(attended, "head", split_axis=0, concat_axis=1, tiled=True)
    total = d_mine + d_near.astype(jnp.float32)
    arrived = [
        shifted(total[back - k].astype(jnp.bfloat16), -2 * k, count) for k in range(back, 0, -1)
    ]
    grad_keys, grad_values = finish(total[back], arrived)
    grad_keys = grad_keys.reshape(tok, 1, width)
    grad_values = grad_values.reshape(tok, 1, width)
    return attended, grad_queries, grad_keys, grad_values


def solution(mesh):
    in_specs = (
        P("ctx", "head", None),
        P("ctx", "head", None),
        P("ctx", "head", None),
        P(),
        P(("ctx", "head"), None),
    )
    out_specs = (
        P(("ctx", "head"), None),
        P("ctx", "head", None),
        P("ctx", "head", None),
        P("ctx", "head", None),
    )
    return jax.shard_map(body, mesh=mesh, in_specs=in_specs, out_specs=out_specs, check_vma=False)
```

```python
import functools
import math

import jax
import jax.numpy as jnp
from jax import lax
from jax.experimental import pallas as pl
from jax.experimental.pallas import tpu as pltpu
from jax.sharding import PartitionSpec as P

DOC_MOST = 1792
NEG_FILL = -1e30
TILE = 256
CHUNK = 128
LOG2_E = 1.4426950408889634


def dot(a, b):
    return jnp.dot(a, b, preferred_element_type=jnp.float32)


def dot_nt(a, b):
    return lax.dot_general(a, b, (((1,), (1,)), ((), ())), preferred_element_type=jnp.float32)


def unit(size):
    rows = lax.broadcasted_iota(jnp.int32, (size, size), 0)
    return (rows == lax.broadcasted_iota(jnp.int32, (size, size), 1)).astype(jnp.bfloat16)


def twice(column):
    return jnp.concatenate([column, column], axis=1)


def attention_kernel(
    doc_ref,
    place_ref,
    q_ref,
    own_ref,
    near_ref,
    *refs,
    back,
    ranks,
    heads,
    width,
    scale,
):
    arrived, far, refs = refs[:back], refs[back : 2 * back], refs[2 * back :]
    grad_parts, refs = refs[:ranks], refs[ranks:]
    out_parts, refs = refs[:ranks], refs[ranks:]
    (
        dq_ref,
        mine_first_ref,
        mine_last_ref,
        other_first_ref,
        other_last_ref,
        do_ref,
        o_ref,
        q32,
        keys,
        values,
        q_rows,
        do_rows,
        q_cols,
        do_cols,
        scores,
        accum,
        dq_acc,
        top,
        delta,
        d_blocks,
    ) = refs
    tok = q_ref.shape[0]
    part_rows = tok // ranks
    docs = doc_ref.shape[0]
    base = place_ref[0]
    own = place_ref[1]
    parity = place_ref[2]
    rank = place_ref[3]
    small = unit(width)
    ones = jnp.ones((width, width), jnp.bfloat16)

    values[:, width:] = jnp.ones_like(values[:, width:])
    for pair in range(back + 1):
        k = back - pair
        mine, other = (own_ref, near_ref) if k == 0 else (arrived[k - 1], far[k - 1])
        for ref, place in ((mine, 2 * pair + parity), (other, 2 * pair + 1 - parity)):
            at = pl.ds(pl.multiple_of(place * tok, tok), tok)
            keys[at, :] = ref[0:tok, :]
            values[at, 0:width] = ref[tok:, :]
    for k in range(ranks):
        at = pl.ds(pl.multiple_of((rank ^ k) * part_rows, part_rows), part_rows)
        do_ref[at, :] = grad_parts[k][...]

    q32[...] = q_ref[...].astype(jnp.float32)
    d_blocks[...] = jnp.zeros_like(d_blocks)

    def chunk_step(chunk, carry):
        here = pl.ds(pl.multiple_of(chunk * CHUNK, CHUNK), CHUNK)
        for j in range(heads):
            part = pl.ds(j * CHUNK, CHUNK)
            q_rows[part, :] = q32[here, j, :].astype(jnp.bfloat16)
            do_rows[part, :] = do_ref[here, j * width : (j + 1) * width]
        q_cols[...] = dot_nt(small, q_rows[...]).astype(jnp.bfloat16)
        do_cols[...] = dot_nt(small, do_rows[...]).astype(jnp.bfloat16)
        top[...] = jnp.full_like(top, NEG_FILL)

        t_first = base + own * TILE + chunk * CHUNK
        t_last = t_first + CHUNK - 1
        t_col = t_first + lax.broadcasted_iota(jnp.int32, (CHUNK, width), 0)
        end = jnp.int32(0)
        start_first, start_last = jnp.int32(0), jnp.int32(0)
        start_col = jnp.zeros((CHUNK, width), jnp.int32)
        for i in range(docs):
            end = end + doc_ref[i]
            start_first = jnp.where(end <= t_first, end, start_first)
            start_last = jnp.where(end <= t_last, end, start_last)
            start_col = jnp.where(t_col >= end, end, start_col)
        low = jnp.maximum(start_first - base, 0) // TILE
        clear = jnp.clip((start_last - base + TILE - 1) // TILE, low, own)

        def score_tile(i, masked):
            at = pl.ds(pl.multiple_of(i * TILE, TILE), TILE)
            tile = dot_nt(q_rows[...], keys[at, :]) * (scale * LOG2_E)
            if masked:
                s_row = base + i * TILE + lax.broadcasted_iota(jnp.int32, (CHUNK, TILE), 1)
                live = (s_row >= twice(start_col)) & (s_row <= twice(t_col))
                tile = jnp.concatenate(
                    [
                        jnp.where(live, tile[j * CHUNK : (j + 1) * CHUNK], NEG_FILL)
                        for j in range(heads)
                    ],
                    axis=0,
                )
            scores[i] = tile
            top[...] = jnp.maximum(top[...], jnp.maximum(tile[:, :width], tile[:, width:]))

        def edge_step(n, carry):
            score_tile(jnp.where(n < clear - low, low + n, own), True)
            return carry

        def inner_step(i, carry):
            score_tile(i, False)
            return carry

        lax.fori_loop(0, clear - low + 1, edge_step, 0)
        lax.fori_loop(clear, own, inner_step, 0)
        top[...] = jnp.broadcast_to(jnp.max(top[...], axis=1, keepdims=True), top.shape)
        accum[...] = jnp.zeros_like(accum)

        def weigh_step(i, carry):
            at = pl.ds(pl.multiple_of(i * TILE, TILE), TILE)
            weights = jnp.exp2(scores[i] - twice(top[...])).astype(jnp.bfloat16)
            accum[...] += dot(weights, values[at, :])
            return carry

        lax.fori_loop(low, own + 1, weigh_step, 0)
        total = accum[:, width:]
        out = (accum[:, 0:width] / total).astype(jnp.bfloat16)
        for j in range(heads):
            o_ref[here, j * width : (j + 1) * width] = out[j * CHUNK : (j + 1) * CHUNK]
        top[...] = top[...] + jnp.log2(total)
        product = do_rows[...].astype(jnp.float32) * out.astype(jnp.float32)
        coarse = product.astype(jnp.bfloat16)
        fine = (product - coarse.astype(jnp.float32)).astype(jnp.bfloat16)
        delta[...] = dot(coarse, ones) + dot(fine, ones)
        dq_acc[...] = jnp.zeros_like(dq_acc)

        def back_step(i, carry):
            at = pl.ds(pl.multiple_of(i * TILE, TILE), TILE)
            probs = jnp.exp2(scores[i] - twice(top[...]))
            d_probs = dot_nt(do_rows[...], values[at, 0:width])
            d_scores = (probs * (d_probs - twice(delta[...]))).astype(jnp.bfloat16)
            dq_acc[...] += dot(d_scores, keys[at, :])
            d_blocks[i, 0:width, :] += dot(q_cols[...], d_scores)
            d_blocks[i, width:, :] += dot(do_cols[...], probs.astype(jnp.bfloat16))
            return carry

        lax.fori_loop(low, own + 1, back_step, 0)
        for j in range(heads):
            q32[here, j, :] = dq_acc[j * CHUNK : (j + 1) * CHUNK, :] * scale
        return carry

    lax.fori_loop(0, tok // CHUNK, chunk_step, 0)
    for k in range(ranks):
        at = pl.ds(pl.multiple_of((rank ^ k) * part_rows, part_rows), part_rows)
        out_parts[k][...] = o_ref[at, :]
    dq_ref[...] = q32[...].astype(jnp.bfloat16)
    for pair in range(back + 1):
        mine, other = 2 * pair + parity, 2 * pair + 1 - parity
        first = mine_first_ref.shape[0]
        early = pair < first
        to = pair if early else pair - first
        ref = mine_first_ref if early else mine_last_ref
        ref[to, 0:width, :] = d_blocks[mine, 0:width, :] * scale
        ref[to, width:, :] = d_blocks[mine, width:, :]
        ref = other_first_ref if early else other_last_ref
        ref[to, 0:width, :] = (d_blocks[other, 0:width, :] * scale).astype(jnp.bfloat16)
        ref[to, width:, :] = d_blocks[other, width:, :].astype(jnp.bfloat16)


def attend(doc_lengths, place, queries, own, near, arrived, far, grad_parts):
    tok, heads, width = queries.shape
    back = len(arrived)
    ranks = len(grad_parts)
    first = (back + 1) // 2
    tiles = 2 * (back + 1)
    span = tiles * tok
    rows = heads * CHUNK
    vmem = pl.BlockSpec(memory_space=pltpu.VMEM)
    smem = pl.BlockSpec(memory_space=pltpu.SMEM)
    out_part = jax.ShapeDtypeStruct((tok // ranks, heads * width), jnp.bfloat16)
    return pl.pallas_call(
        functools.partial(
            attention_kernel,
            back=back,
            ranks=ranks,
            heads=heads,
            width=width,
            scale=1.0 / math.sqrt(width),
        ),
        out_shape=[out_part] * ranks
        + [
            jax.ShapeDtypeStruct((tok, heads, width), jnp.bfloat16),
        ]
        + [
            jax.ShapeDtypeStruct((size, 2 * width, tok), dtype)
            for dtype in (jnp.float32, jnp.bfloat16)
            for size in (first, back + 1 - first)
        ],
        in_specs=[smem, smem] + [vmem] * (3 + 2 * back + ranks),
        out_specs=[vmem] * (ranks + 5),
        scratch_shapes=[
            pltpu.VMEM((tok, heads * width), jnp.bfloat16),
            pltpu.VMEM((tok, heads * width), jnp.bfloat16),
            pltpu.VMEM((tok, heads, width), jnp.float32),
            pltpu.VMEM((span, width), jnp.bfloat16),
            pltpu.VMEM((span, 2 * width), jnp.bfloat16),
            pltpu.VMEM((rows, width), jnp.bfloat16),
            pltpu.VMEM((rows, width), jnp.bfloat16),
            pltpu.VMEM((width, rows), jnp.bfloat16),
            pltpu.VMEM((width, rows), jnp.bfloat16),
            pltpu.VMEM((tiles, rows, TILE), jnp.float32),
            pltpu.VMEM((rows, 2 * width), jnp.float32),
            pltpu.VMEM((rows, width), jnp.float32),
            pltpu.VMEM((rows, width), jnp.float32),
            pltpu.VMEM((rows, width), jnp.float32),
            pltpu.VMEM((tiles, 2 * width, tok), jnp.float32),
        ],
        compiler_params=pltpu.CompilerParams(vmem_limit_bytes=40 * 1024 * 1024),
        cost_estimate=pl.CostEstimate(
            flops=14 * tok * heads * width * span,
            bytes_accessed=4 * tok * heads * width * 2 + 4 * span * width * 2,
            transcendentals=tok * heads * span,
        ),
        name="attention",
    )(doc_lengths, place, queries, own, near, *arrived, *far, *grad_parts)


def pack_kernel(key_ref, value_ref, own_ref):
    tok = key_ref.shape[0]
    own_ref[0:tok, :] = key_ref[...]
    own_ref[tok:, :] = value_ref[...]


def pack(keys, values):
    tok, width = keys.shape
    vmem = pl.BlockSpec(memory_space=pltpu.VMEM)
    return pl.pallas_call(
        pack_kernel,
        out_shape=jax.ShapeDtypeStruct((2 * tok, width), keys.dtype),
        in_specs=[vmem, vmem],
        out_specs=vmem,
        name="pack",
    )(keys, values)


def split_kernel(place_ref, grad_ref, *part_refs):
    size = part_refs[0].shape[1]
    for k, ref in enumerate(part_refs):
        at = pl.multiple_of((place_ref[3] ^ k) * size, size)
        ref[...] = grad_ref[:, pl.ds(at, size)]


def split(place, grad_attended, ranks):
    rows, columns = grad_attended.shape
    vmem = pl.BlockSpec(memory_space=pltpu.VMEM)
    part = jax.ShapeDtypeStruct((rows, columns // ranks), grad_attended.dtype)
    return pl.pallas_call(
        split_kernel,
        out_shape=[part] * ranks,
        in_specs=[pl.BlockSpec(memory_space=pltpu.SMEM), vmem],
        out_specs=[vmem] * ranks,
        name="split",
    )(place, grad_attended)


def join_kernel(place_ref, *refs):
    out_ref = refs[-1]
    size = refs[0].shape[1]
    for k, ref in enumerate(refs[:-1]):
        at = pl.multiple_of((place_ref[3] ^ k) * size, size)
        out_ref[:, pl.ds(at, size)] = ref[...]


def join(place, parts):
    rows, size = parts[0].shape
    vmem = pl.BlockSpec(memory_space=pltpu.VMEM)
    return pl.pallas_call(
        join_kernel,
        out_shape=jax.ShapeDtypeStruct((rows, size * len(parts)), parts[0].dtype),
        in_specs=[pl.BlockSpec(memory_space=pltpu.SMEM)] + [vmem] * len(parts),
        out_specs=vmem,
        name="join",
    )(place, *parts)


def merge_kernel(mine_ref, other_ref, *block_refs):
    for k, ref in enumerate(block_refs):
        ref[...] = (mine_ref[k] + other_ref[k].astype(jnp.float32)).astype(ref.dtype)


def merge(mine, other, dtypes):
    vmem = pl.BlockSpec(memory_space=pltpu.VMEM)
    return pl.pallas_call(
        merge_kernel,
        out_shape=[jax.ShapeDtypeStruct(mine.shape[1:], dtype) for dtype in dtypes],
        in_specs=[vmem, vmem],
        out_specs=[vmem] * len(dtypes),
        name="merge",
    )(mine, other)


def finish_kernel(own_ref, *refs):
    arrived = refs[:-2]
    dk_ref, dv_ref = refs[-2:]
    total = own_ref[...]
    for ref in arrived:
        total = total + ref[...].astype(jnp.float32)
    total = total.astype(jnp.bfloat16)
    width = dk_ref.shape[1]
    large = unit(dk_ref.shape[0])
    dk_ref[...] = dot_nt(large, total[:width]).astype(jnp.bfloat16)
    dv_ref[...] = dot_nt(large, total[width:]).astype(jnp.bfloat16)


def finish(own_part, arrived):
    both, tok = own_part.shape
    vmem = pl.BlockSpec(memory_space=pltpu.VMEM)
    shape = jax.ShapeDtypeStruct((tok, both // 2), jnp.bfloat16)
    return pl.pallas_call(
        finish_kernel,
        out_shape=(shape, shape),
        in_specs=[vmem] * (1 + len(arrived)),
        out_specs=(vmem, vmem),
        name="finish",
    )(own_part, *arrived)


def shifted(block, by, count):
    pairs = [(i, i + by) for i in range(count) if 0 <= i + by < count]
    return lax.ppermute(block, "ctx", pairs)


def exchanged(block, axis, by):
    return lax.ppermute(block, axis, [(i, i ^ by) for i in range(lax.axis_size(axis))])


def body(queries, key_states, value_states, doc_lengths, grad_attended):
    tok, heads, width = queries.shape
    count = lax.axis_size("ctx")
    ranks = lax.axis_size("head")
    ctx = lax.axis_index("ctx")
    reach = min((DOC_MOST + tok - 2) // tok, count - 1)
    back = min((reach + 1) // 2, count // 2 - 1)
    parity = ctx % 2
    place = jnp.stack(
        [(ctx - parity - 2 * back) * tok, 2 * back + parity, parity, lax.axis_index("head")]
    ).astype(jnp.int32)
    own = pack(key_states.reshape(tok, width), value_states.reshape(tok, width))
    arrived = [shifted(own, 2 * k, count) for k in range(back, 0, -1)][::-1]
    far = []
    for block in arrived:
        if far:
            block, far[-1] = lax.optimization_barrier((block, far[-1]))
        far.append(exchanged(block, "ctx", 1))
    near = exchanged(own, "ctx", 1)
    grad_parts = split(place, grad_attended, ranks)
    grad_parts = [part if k == 0 else exchanged(part, "head", k) for k, part in enumerate(grad_parts)]
    *out_parts, grad_queries, mine_first, mine_last, other_first, other_last = attend(
        doc_lengths, place, queries, own, near, arrived, far, grad_parts
    )
    first = mine_first.shape[0]
    out_parts = [part if k == 0 else exchanged(part, "head", k) for k, part in enumerate(out_parts)]
    other_first = exchanged(other_first, "ctx", 1)
    other_last = exchanged(other_last, "ctx", 1)
    blocks = merge(mine_first, other_first, [jnp.bfloat16] * first)
    arrived = [shifted(block, 2 * (pair - back), count) for pair, block in enumerate(blocks)]
    *blocks, own_block = merge(
        mine_last, other_last, [jnp.bfloat16] * (back - first) + [jnp.float32]
    )
    arrived += [
        shifted(block, 2 * (first + k - back), count) for k, block in enumerate(blocks)
    ]
    grad_keys, grad_values = finish(own_block, arrived)
    attended = join(place, out_parts)
    grad_keys = grad_keys.reshape(tok, 1, width)
    grad_values = grad_values.reshape(tok, 1, width)
    return attended, grad_queries, grad_keys, grad_values


def solution(mesh):
    in_specs = (
        P("ctx", "head", None),
        P("ctx", "head", None),
        P("ctx", "head", None),
        P(),
        P(("ctx", "head"), None),
    )
    out_specs = (
        P(("ctx", "head"), None),
        P("ctx", "head", None),
        P("ctx", "head", None),
        P("ctx", "head", None),
    )
    return jax.shard_map(body, mesh=mesh, in_specs=in_specs, out_specs=out_specs, check_vma=False)
```

```python
import functools
import math

import jax
import jax.numpy as jnp
from jax import lax
from jax.experimental import pallas as pl
from jax.experimental.pallas import tpu as pltpu
from jax.sharding import PartitionSpec as P

DOC_MOST = 1792
NEG_FILL = -1e30
TILE = 256
CHUNK = 128
LOG2_E = 1.4426950408889634
SMALL_VMEM = 8 * 1024 * 1024


def dot(a, b):
    return jnp.dot(a, b, preferred_element_type=jnp.float32)


def dot_nt(a, b):
    return lax.dot_general(a, b, (((1,), (1,)), ((), ())), preferred_element_type=jnp.float32)


def unit(size):
    rows = lax.broadcasted_iota(jnp.int32, (size, size), 0)
    return (rows == lax.broadcasted_iota(jnp.int32, (size, size), 1)).astype(jnp.bfloat16)


def twice(column):
    return jnp.concatenate([column, column], axis=1)


def attention_kernel(
    doc_ref,
    q_ref,
    own_ref,
    near_ref,
    *refs,
    back,
    ranks,
    heads,
    width,
    scale,
):
    arrived, far, refs = refs[:back], refs[back : 2 * back], refs[2 * back :]
    grad_parts, refs = refs[:ranks], refs[ranks:]
    out_parts, refs = refs[:ranks], refs[ranks:]
    (
        dq_ref,
        mine_first_ref,
        mine_last_ref,
        other_first_ref,
        other_last_ref,
        do_ref,
        o_ref,
        q32,
        keys,
        values,
        q_rows,
        do_rows,
        q_cols,
        do_cols,
        scores,
        accum,
        dq_acc,
        top,
        delta,
        d_blocks,
    ) = refs
    tok = q_ref.shape[0]
    part_rows = tok // ranks
    docs = doc_ref.shape[0]
    ctx = lax.axis_index("ctx")
    rank = lax.axis_index("head")
    parity = lax.rem(ctx, 2)
    base = (ctx - parity - 2 * back) * tok
    own = 2 * back + parity
    small = unit(width)
    ones = jnp.ones((width, width), jnp.bfloat16)

    values[:, width:] = jnp.ones_like(values[:, width:])
    for pair in range(back + 1):
        k = back - pair
        mine, other = (own_ref, near_ref) if k == 0 else (arrived[k - 1], far[k - 1])
        for ref, place in ((mine, 2 * pair + parity), (other, 2 * pair + 1 - parity)):
            at = pl.ds(pl.multiple_of(place * tok, tok), tok)
            keys[at, :] = ref[0:tok, :]
            values[at, 0:width] = ref[tok:, :]
    for k in range(ranks):
        at = pl.ds(pl.multiple_of((rank ^ k) * part_rows, part_rows), part_rows)
        do_ref[at, :] = grad_parts[k][...]

    q32[...] = q_ref[...].astype(jnp.float32)
    d_blocks[...] = jnp.zeros_like(d_blocks)

    def chunk_step(chunk, carry):
        here = pl.ds(pl.multiple_of(chunk * CHUNK, CHUNK), CHUNK)
        for j in range(heads):
            part = pl.ds(j * CHUNK, CHUNK)
            q_rows[part, :] = q32[here, j, :].astype(jnp.bfloat16)
            do_rows[part, :] = do_ref[here, j * width : (j + 1) * width]
        q_cols[...] = dot_nt(small, q_rows[...]).astype(jnp.bfloat16)
        do_cols[...] = dot_nt(small, do_rows[...]).astype(jnp.bfloat16)
        top[...] = jnp.full_like(top, NEG_FILL)

        t_first = base + own * TILE + chunk * CHUNK
        t_last = t_first + CHUNK - 1
        t_col = t_first + lax.broadcasted_iota(jnp.int32, (CHUNK, width), 0)
        end = jnp.int32(0)
        start_first, start_last = jnp.int32(0), jnp.int32(0)
        start_col = jnp.zeros((CHUNK, width), jnp.int32)
        for i in range(docs):
            end = end + doc_ref[i]
            start_first = jnp.where(end <= t_first, end, start_first)
            start_last = jnp.where(end <= t_last, end, start_last)
            start_col = jnp.where(t_col >= end, end, start_col)
        low = jnp.maximum(start_first - base, 0) // TILE
        clear = jnp.clip((start_last - base + TILE - 1) // TILE, low, own)

        def score_tile(i, masked):
            at = pl.ds(pl.multiple_of(i * TILE, TILE), TILE)
            tile = dot_nt(q_rows[...], keys[at, :]) * (scale * LOG2_E)
            if masked:
                s_row = base + i * TILE + lax.broadcasted_iota(jnp.int32, (CHUNK, TILE), 1)
                live = (s_row >= twice(start_col)) & (s_row <= twice(t_col))
                tile = jnp.concatenate(
                    [
                        jnp.where(live, tile[j * CHUNK : (j + 1) * CHUNK], NEG_FILL)
                        for j in range(heads)
                    ],
                    axis=0,
                )
            scores[i] = tile
            top[...] = jnp.maximum(top[...], jnp.maximum(tile[:, :width], tile[:, width:]))

        def edge_step(n, carry):
            score_tile(jnp.where(n < clear - low, low + n, own), True)
            return carry

        def inner_step(i, carry):
            score_tile(i, False)
            return carry

        lax.fori_loop(0, clear - low + 1, edge_step, 0)
        lax.fori_loop(clear, own, inner_step, 0)
        top[...] = jnp.broadcast_to(jnp.max(top[...], axis=1, keepdims=True), top.shape)
        accum[...] = jnp.zeros_like(accum)

        def weigh_step(i, carry):
            at = pl.ds(pl.multiple_of(i * TILE, TILE), TILE)
            weights = jnp.exp2(scores[i] - twice(top[...])).astype(jnp.bfloat16)
            accum[...] += dot(weights, values[at, :])
            return carry

        lax.fori_loop(low, own + 1, weigh_step, 0)
        total = accum[:, width:]
        out = (accum[:, 0:width] / total).astype(jnp.bfloat16)
        for j in range(heads):
            o_ref[here, j * width : (j + 1) * width] = out[j * CHUNK : (j + 1) * CHUNK]
        top[...] = top[...] + jnp.log2(total)
        product = do_rows[...].astype(jnp.float32) * out.astype(jnp.float32)
        coarse = product.astype(jnp.bfloat16)
        fine = (product - coarse.astype(jnp.float32)).astype(jnp.bfloat16)
        delta[...] = dot(coarse, ones) + dot(fine, ones)
        dq_acc[...] = jnp.zeros_like(dq_acc)

        def back_step(i, carry):
            at = pl.ds(pl.multiple_of(i * TILE, TILE), TILE)
            probs = jnp.exp2(scores[i] - twice(top[...]))
            d_probs = dot_nt(do_rows[...], values[at, 0:width])
            d_scores = (probs * (d_probs - twice(delta[...]))).astype(jnp.bfloat16)
            dq_acc[...] += dot(d_scores, keys[at, :])
            d_blocks[i, 0:width, :] += dot(q_cols[...], d_scores)
            d_blocks[i, width:, :] += dot(do_cols[...], probs.astype(jnp.bfloat16))
            return carry

        lax.fori_loop(low, own + 1, back_step, 0)
        for j in range(heads):
            q32[here, j, :] = dq_acc[j * CHUNK : (j + 1) * CHUNK, :] * scale
        return carry

    lax.fori_loop(0, tok // CHUNK, chunk_step, 0)
    for k in range(ranks):
        at = pl.ds(pl.multiple_of((rank ^ k) * part_rows, part_rows), part_rows)
        out_parts[k][...] = o_ref[at, :]
    dq_ref[...] = q32[...].astype(jnp.bfloat16)
    for pair in range(back + 1):
        mine, other = 2 * pair + parity, 2 * pair + 1 - parity
        first = mine_first_ref.shape[0]
        early = pair < first
        to = pair if early else pair - first
        ref = mine_first_ref if early else mine_last_ref
        ref[to, 0:width, :] = d_blocks[mine, 0:width, :] * scale
        ref[to, width:, :] = d_blocks[mine, width:, :]
        ref = other_first_ref if early else other_last_ref
        ref[to, 0:width, :] = (d_blocks[other, 0:width, :] * scale).astype(jnp.bfloat16)
        ref[to, width:, :] = d_blocks[other, width:, :].astype(jnp.bfloat16)


def attend(doc_lengths, queries, own, near, arrived, far, grad_parts):
    tok, heads, width = queries.shape
    back = len(arrived)
    ranks = len(grad_parts)
    first = (back + 1) // 2
    tiles = 2 * (back + 1)
    span = tiles * tok
    rows = heads * CHUNK
    vmem = pl.BlockSpec(memory_space=pltpu.VMEM)
    smem = pl.BlockSpec(memory_space=pltpu.SMEM)
    out_part = jax.ShapeDtypeStruct((tok // ranks, heads * width), jnp.bfloat16)
    return pl.pallas_call(
        functools.partial(
            attention_kernel,
            back=back,
            ranks=ranks,
            heads=heads,
            width=width,
            scale=1.0 / math.sqrt(width),
        ),
        out_shape=[out_part] * ranks
        + [
            jax.ShapeDtypeStruct((tok, heads, width), jnp.bfloat16),
        ]
        + [
            jax.ShapeDtypeStruct((size, 2 * width, tok), dtype)
            for dtype in (jnp.float32, jnp.bfloat16)
            for size in (first, back + 1 - first)
        ],
        in_specs=[smem] + [vmem] * (3 + 2 * back + ranks),
        out_specs=[vmem] * (ranks + 5),
        scratch_shapes=[
            pltpu.VMEM((tok, heads * width), jnp.bfloat16),
            pltpu.VMEM((tok, heads * width), jnp.bfloat16),
            pltpu.VMEM((tok, heads, width), jnp.float32),
            pltpu.VMEM((span, width), jnp.bfloat16),
            pltpu.VMEM((span, 2 * width), jnp.bfloat16),
            pltpu.VMEM((rows, width), jnp.bfloat16),
            pltpu.VMEM((rows, width), jnp.bfloat16),
            pltpu.VMEM((width, rows), jnp.bfloat16),
            pltpu.VMEM((width, rows), jnp.bfloat16),
            pltpu.VMEM((tiles, rows, TILE), jnp.float32),
            pltpu.VMEM((rows, 2 * width), jnp.float32),
            pltpu.VMEM((rows, width), jnp.float32),
            pltpu.VMEM((rows, width), jnp.float32),
            pltpu.VMEM((rows, width), jnp.float32),
            pltpu.VMEM((tiles, 2 * width, tok), jnp.float32),
        ],
        compiler_params=pltpu.CompilerParams(vmem_limit_bytes=40 * 1024 * 1024),
        cost_estimate=pl.CostEstimate(
            flops=14 * tok * heads * width * span,
            bytes_accessed=4 * tok * heads * width * 2 + 4 * span * width * 2,
            transcendentals=tok * heads * span,
        ),
        name="attention",
    )(doc_lengths, queries, own, near, *arrived, *far, *grad_parts)


def pack_kernel(key_ref, value_ref, own_ref):
    tok = key_ref.shape[0]
    own_ref[0:tok, :] = key_ref[...]
    own_ref[tok:, :] = value_ref[...]


def pack(keys, values):
    tok, width = keys.shape
    vmem = pl.BlockSpec(memory_space=pltpu.VMEM)
    return pl.pallas_call(
        pack_kernel,
        out_shape=jax.ShapeDtypeStruct((2 * tok, width), keys.dtype),
        in_specs=[vmem, vmem],
        out_specs=vmem,
        compiler_params=pltpu.CompilerParams(vmem_limit_bytes=SMALL_VMEM),
        name="pack",
    )(keys, values)


def split_kernel(grad_ref, *part_refs):
    size = part_refs[0].shape[1]
    for k, ref in enumerate(part_refs):
        at = pl.multiple_of((lax.axis_index("head") ^ k) * size, size)
        ref[...] = grad_ref[:, pl.ds(at, size)]


def split(grad_attended, ranks):
    rows, columns = grad_attended.shape
    vmem = pl.BlockSpec(memory_space=pltpu.VMEM)
    part = jax.ShapeDtypeStruct((rows, columns // ranks), grad_attended.dtype)
    return pl.pallas_call(
        split_kernel,
        out_shape=[part] * ranks,
        in_specs=[vmem],
        out_specs=[vmem] * ranks,
        compiler_params=pltpu.CompilerParams(vmem_limit_bytes=SMALL_VMEM),
        name="split",
    )(grad_attended)


def join_kernel(*refs):
    out_ref = refs[-1]
    size = refs[0].shape[1]
    for k, ref in enumerate(refs[:-1]):
        at = pl.multiple_of((lax.axis_index("head") ^ k) * size, size)
        out_ref[:, pl.ds(at, size)] = ref[...]


def join(parts):
    rows, size = parts[0].shape
    vmem = pl.BlockSpec(memory_space=pltpu.VMEM)
    return pl.pallas_call(
        join_kernel,
        out_shape=jax.ShapeDtypeStruct((rows, size * len(parts)), parts[0].dtype),
        in_specs=[vmem] * len(parts),
        out_specs=vmem,
        compiler_params=pltpu.CompilerParams(vmem_limit_bytes=SMALL_VMEM),
        name="join",
    )(*parts)


def merge_kernel(mine_ref, other_ref, *block_refs):
    for k, ref in enumerate(block_refs):
        ref[...] = (mine_ref[k] + other_ref[k].astype(jnp.float32)).astype(ref.dtype)


def merge(mine, other, dtypes):
    vmem = pl.BlockSpec(memory_space=pltpu.VMEM)
    return pl.pallas_call(
        merge_kernel,
        out_shape=[jax.ShapeDtypeStruct(mine.shape[1:], dtype) for dtype in dtypes],
        in_specs=[vmem, vmem],
        out_specs=[vmem] * len(dtypes),
        compiler_params=pltpu.CompilerParams(vmem_limit_bytes=SMALL_VMEM),
        name="merge",
    )(mine, other)


def finish_kernel(own_ref, *refs):
    arrived = refs[:-2]
    dk_ref, dv_ref = refs[-2:]
    total = own_ref[...]
    for ref in arrived:
        total = total + ref[...].astype(jnp.float32)
    total = total.astype(jnp.bfloat16)
    width = dk_ref.shape[1]
    large = unit(dk_ref.shape[0])
    dk_ref[...] = dot_nt(large, total[:width]).astype(jnp.bfloat16)
    dv_ref[...] = dot_nt(large, total[width:]).astype(jnp.bfloat16)


def finish(own_part, arrived):
    both, tok = own_part.shape
    vmem = pl.BlockSpec(memory_space=pltpu.VMEM)
    shape = jax.ShapeDtypeStruct((tok, both // 2), jnp.bfloat16)
    return pl.pallas_call(
        finish_kernel,
        out_shape=(shape, shape),
        in_specs=[vmem] * (1 + len(arrived)),
        out_specs=(vmem, vmem),
        compiler_params=pltpu.CompilerParams(vmem_limit_bytes=SMALL_VMEM),
        name="finish",
    )(own_part, *arrived)


def shifted(block, by, count):
    pairs = [(i, i + by) for i in range(count) if 0 <= i + by < count]
    return lax.ppermute(block, "ctx", pairs)


def exchanged(block, axis, by):
    return lax.ppermute(block, axis, [(i, i ^ by) for i in range(lax.axis_size(axis))])


def body(queries, key_states, value_states, doc_lengths, grad_attended):
    tok, heads, width = queries.shape
    count = lax.axis_size("ctx")
    ranks = lax.axis_size("head")
    reach = min((DOC_MOST + tok - 2) // tok, count - 1)
    back = min((reach + 1) // 2, count // 2 - 1)
    own = pack(key_states.reshape(tok, width), value_states.reshape(tok, width))
    arrived = [shifted(own, 2 * k, count) for k in range(1, back + 1)]
    near = exchanged(own, "ctx", 1)
    grad_parts = split(grad_attended, ranks)
    grad_parts = [part if k == 0 else exchanged(part, "head", k) for k, part in enumerate(grad_parts)]
    far = []
    for k, block in enumerate(arrived):
        if k + 1 < ranks:
            block, grad_parts[k + 1] = lax.optimization_barrier((block, grad_parts[k + 1]))
        if far:
            block, far[-1] = lax.optimization_barrier((block, far[-1]))
        far.append(exchanged(block, "ctx", 1))
    *out_parts, grad_queries, mine_first, mine_last, other_first, other_last = attend(
        doc_lengths, queries, own, near, arrived, far, grad_parts
    )
    first = mine_first.shape[0]
    out_parts = [part if k == 0 else exchanged(part, "head", k) for k, part in enumerate(out_parts)]
    other_first = exchanged(other_first, "ctx", 1)
    other_last = exchanged(other_last, "ctx", 1)
    blocks = merge(mine_first, other_first, [jnp.bfloat16] * first)
    arrived = [shifted(block, 2 * (pair - back), count) for pair, block in enumerate(blocks)]
    other_last, arrived[0] = lax.optimization_barrier((other_last, arrived[0]))
    *blocks, own_block = merge(
        mine_last, other_last, [jnp.bfloat16] * (back - first) + [jnp.float32]
    )
    arrived += [
        shifted(block, 2 * (first + k - back), count) for k, block in enumerate(blocks)
    ]
    grad_keys, grad_values = finish(own_block, arrived)
    attended = join(out_parts)
    grad_keys = grad_keys.reshape(tok, 1, width)
    grad_values = grad_values.reshape(tok, 1, width)
    return attended, grad_queries, grad_keys, grad_values


def solution(mesh):
    in_specs = (
        P("ctx", "head", None),
        P("ctx", "head", None),
        P("ctx", "head", None),
        P(),
        P(("ctx", "head"), None),
    )
    out_specs = (
        P(("ctx", "head"), None),
        P("ctx", "head", None),
        P("ctx", "head", None),
        P("ctx", "head", None),
    )
    return jax.shard_map(body, mesh=mesh, in_specs=in_specs, out_specs=out_specs, check_vma=False)
```

```python
import functools
import math

import jax
import jax.numpy as jnp
from jax import lax
from jax.experimental import pallas as pl
from jax.experimental.pallas import tpu as pltpu
from jax.sharding import PartitionSpec as P

DOC_MOST = 1792
NEG_FILL = -1e30
TILE = 256
CHUNK = 128
LOG2_E = 1.4426950408889634
SMALL_VMEM = 8 * 1024 * 1024


def dot(a, b):
    return jnp.dot(a, b, preferred_element_type=jnp.float32)


def dot_nt(a, b):
    return lax.dot_general(a, b, (((1,), (1,)), ((), ())), preferred_element_type=jnp.float32)


def unit(size):
    rows = lax.broadcasted_iota(jnp.int32, (size, size), 0)
    return (rows == lax.broadcasted_iota(jnp.int32, (size, size), 1)).astype(jnp.bfloat16)


def twice(column):
    return jnp.concatenate([column, column], axis=1)


def attention_kernel(
    doc_ref,
    q_ref,
    own_ref,
    near_ref,
    *refs,
    back,
    ranks,
    heads,
    width,
    scale,
):
    arrived, far, refs = refs[:back], refs[back : 2 * back], refs[2 * back :]
    grad_parts, refs = refs[:ranks], refs[ranks:]
    out_parts, refs = refs[:ranks], refs[ranks:]
    (
        dq_ref,
        mine_first_ref,
        mine_last_ref,
        other_first_ref,
        other_last_ref,
        do_ref,
        o_ref,
        q32,
        keys,
        values,
        q_rows,
        do_rows,
        q_cols,
        do_cols,
        scores,
        accum,
        dq_acc,
        top,
        delta,
        d_blocks,
    ) = refs
    tok = q_ref.shape[0]
    part_rows = tok // ranks
    docs = doc_ref.shape[0]
    ctx = lax.axis_index("ctx")
    rank = lax.axis_index("head")
    parity = lax.rem(ctx, 2)
    base = (ctx - parity - 2 * back) * tok
    own = 2 * back + parity
    small = unit(width)
    ones = jnp.ones((width, width), jnp.bfloat16)

    values[:, width:] = jnp.ones_like(values[:, width:])
    for pair in range(back + 1):
        k = back - pair
        mine, other = (own_ref, near_ref) if k == 0 else (arrived[k - 1], far[k - 1])
        for ref, place in ((mine, 2 * pair + parity), (other, 2 * pair + 1 - parity)):
            at = pl.ds(pl.multiple_of(place * tok, tok), tok)
            keys[at, :] = ref[0:tok, :]
            values[at, 0:width] = ref[tok:, :]
    for k in range(ranks):
        at = pl.ds(pl.multiple_of((rank ^ k) * part_rows, part_rows), part_rows)
        do_ref[at, :] = grad_parts[k][...]

    q32[...] = q_ref[...].astype(jnp.float32)
    d_blocks[...] = jnp.zeros_like(d_blocks)

    def chunk_step(chunk, carry):
        here = pl.ds(pl.multiple_of(chunk * CHUNK, CHUNK), CHUNK)
        for j in range(heads):
            part = pl.ds(j * CHUNK, CHUNK)
            q_rows[part, :] = q32[here, j, :].astype(jnp.bfloat16)
            do_rows[part, :] = do_ref[here, j * width : (j + 1) * width]
        q_cols[...] = dot_nt(small, q_rows[...]).astype(jnp.bfloat16)
        do_cols[...] = dot_nt(small, do_rows[...]).astype(jnp.bfloat16)
        top[...] = jnp.full_like(top, NEG_FILL)

        t_first = base + own * TILE + chunk * CHUNK
        t_last = t_first + CHUNK - 1
        t_col = t_first + lax.broadcasted_iota(jnp.int32, (CHUNK, width), 0)
        end = jnp.int32(0)
        start_first, start_last = jnp.int32(0), jnp.int32(0)
        start_col = jnp.zeros((CHUNK, width), jnp.int32)
        for i in range(docs):
            end = end + doc_ref[i]
            start_first = jnp.where(end <= t_first, end, start_first)
            start_last = jnp.where(end <= t_last, end, start_last)
            start_col = jnp.where(t_col >= end, end, start_col)
        low = jnp.maximum(start_first - base, 0) // TILE
        clear = jnp.clip((start_last - base + TILE - 1) // TILE, low, own)

        def score_tile(i, masked):
            at = pl.ds(pl.multiple_of(i * TILE, TILE), TILE)
            tile = dot_nt(q_rows[...], keys[at, :]) * (scale * LOG2_E)
            if masked:
                s_row = base + i * TILE + lax.broadcasted_iota(jnp.int32, (CHUNK, TILE), 1)
                live = (s_row >= twice(start_col)) & (s_row <= twice(t_col))
                tile = jnp.concatenate(
                    [
                        jnp.where(live, tile[j * CHUNK : (j + 1) * CHUNK], NEG_FILL)
                        for j in range(heads)
                    ],
                    axis=0,
                )
            scores[i] = tile
            top[...] = jnp.maximum(top[...], jnp.maximum(tile[:, :width], tile[:, width:]))

        def edge_step(n, carry):
            score_tile(jnp.where(n < clear - low, low + n, own), True)
            return carry

        def inner_step(i, carry):
            score_tile(i, False)
            return carry

        lax.fori_loop(0, clear - low + 1, edge_step, 0)
        lax.fori_loop(clear, own, inner_step, 0)
        top[...] = jnp.broadcast_to(jnp.max(top[...], axis=1, keepdims=True), top.shape)
        accum[...] = jnp.zeros_like(accum)

        def weigh_step(i, carry):
            at = pl.ds(pl.multiple_of(i * TILE, TILE), TILE)
            weights = jnp.exp2(scores[i] - twice(top[...])).astype(jnp.bfloat16)
            accum[...] += dot(weights, values[at, :])
            return carry

        lax.fori_loop(low, own + 1, weigh_step, 0)
        total = accum[:, width:]
        out = (accum[:, 0:width] / total).astype(jnp.bfloat16)
        for j in range(heads):
            o_ref[here, j * width : (j + 1) * width] = out[j * CHUNK : (j + 1) * CHUNK]
        top[...] = top[...] + jnp.log2(total)
        product = do_rows[...].astype(jnp.float32) * out.astype(jnp.float32)
        coarse = product.astype(jnp.bfloat16)
        fine = (product - coarse.astype(jnp.float32)).astype(jnp.bfloat16)
        delta[...] = dot(coarse, ones) + dot(fine, ones)
        dq_acc[...] = jnp.zeros_like(dq_acc)

        def back_step(i, carry):
            at = pl.ds(pl.multiple_of(i * TILE, TILE), TILE)
            probs = jnp.exp2(scores[i] - twice(top[...]))
            d_probs = dot_nt(do_rows[...], values[at, 0:width])
            d_scores = (probs * (d_probs - twice(delta[...]))).astype(jnp.bfloat16)
            dq_acc[...] += dot(d_scores, keys[at, :])
            d_blocks[i, 0:width, :] += dot(q_cols[...], d_scores)
            d_blocks[i, width:, :] += dot(do_cols[...], probs.astype(jnp.bfloat16))
            return carry

        lax.fori_loop(low, own + 1, back_step, 0)
        for j in range(heads):
            q32[here, j, :] = dq_acc[j * CHUNK : (j + 1) * CHUNK, :] * scale
        return carry

    lax.fori_loop(0, tok // CHUNK, chunk_step, 0)
    for k in range(ranks):
        at = pl.ds(pl.multiple_of((rank ^ k) * part_rows, part_rows), part_rows)
        out_parts[k][...] = o_ref[at, :]
    dq_ref[...] = q32[...].astype(jnp.bfloat16)
    for pair in range(back + 1):
        mine, other = 2 * pair + parity, 2 * pair + 1 - parity
        first = mine_first_ref.shape[0]
        early = pair < first
        to = pair if early else pair - first
        ref = mine_first_ref if early else mine_last_ref
        ref[to, 0:width, :] = d_blocks[mine, 0:width, :] * scale
        ref[to, width:, :] = d_blocks[mine, width:, :]
        ref = other_first_ref if early else other_last_ref
        ref[to, 0:width, :] = (d_blocks[other, 0:width, :] * scale).astype(jnp.bfloat16)
        ref[to, width:, :] = d_blocks[other, width:, :].astype(jnp.bfloat16)


def attend(doc_lengths, queries, own, near, arrived, far, grad_parts):
    tok, heads, width = queries.shape
    back = len(arrived)
    ranks = len(grad_parts)
    first = (back + 1) // 2
    tiles = 2 * (back + 1)
    span = tiles * tok
    rows = heads * CHUNK
    vmem = pl.BlockSpec(memory_space=pltpu.VMEM)
    smem = pl.BlockSpec(memory_space=pltpu.SMEM)
    out_part = jax.ShapeDtypeStruct((tok // ranks, heads * width), jnp.bfloat16)
    return pl.pallas_call(
        functools.partial(
            attention_kernel,
            back=back,
            ranks=ranks,
            heads=heads,
            width=width,
            scale=1.0 / math.sqrt(width),
        ),
        out_shape=[out_part] * ranks
        + [
            jax.ShapeDtypeStruct((tok, heads, width), jnp.bfloat16),
        ]
        + [
            jax.ShapeDtypeStruct((size, 2 * width, tok), dtype)
            for dtype in (jnp.float32, jnp.bfloat16)
            for size in (first, back + 1 - first)
        ],
        in_specs=[smem] + [vmem] * (3 + 2 * back + ranks),
        out_specs=[vmem] * (ranks + 5),
        scratch_shapes=[
            pltpu.VMEM((tok, heads * width), jnp.bfloat16),
            pltpu.VMEM((tok, heads * width), jnp.bfloat16),
            pltpu.VMEM((tok, heads, width), jnp.float32),
            pltpu.VMEM((span, width), jnp.bfloat16),
            pltpu.VMEM((span, 2 * width), jnp.bfloat16),
            pltpu.VMEM((rows, width), jnp.bfloat16),
            pltpu.VMEM((rows, width), jnp.bfloat16),
            pltpu.VMEM((width, rows), jnp.bfloat16),
            pltpu.VMEM((width, rows), jnp.bfloat16),
            pltpu.VMEM((tiles, rows, TILE), jnp.float32),
            pltpu.VMEM((rows, 2 * width), jnp.float32),
            pltpu.VMEM((rows, width), jnp.float32),
            pltpu.VMEM((rows, width), jnp.float32),
            pltpu.VMEM((rows, width), jnp.float32),
            pltpu.VMEM((tiles, 2 * width, tok), jnp.float32),
        ],
        compiler_params=pltpu.CompilerParams(vmem_limit_bytes=40 * 1024 * 1024),
        cost_estimate=pl.CostEstimate(
            flops=14 * tok * heads * width * span,
            bytes_accessed=4 * tok * heads * width * 2 + 4 * span * width * 2,
            transcendentals=tok * heads * span,
        ),
        name="attention",
    )(doc_lengths, queries, own, near, *arrived, *far, *grad_parts)


def split_kernel(grad_ref, *part_refs):
    size = part_refs[0].shape[1]
    for k, ref in enumerate(part_refs):
        at = pl.multiple_of((lax.axis_index("head") ^ k) * size, size)
        ref[...] = grad_ref[:, pl.ds(at, size)]


def split(grad_attended, ranks):
    rows, columns = grad_attended.shape
    vmem = pl.BlockSpec(memory_space=pltpu.VMEM)
    part = jax.ShapeDtypeStruct((rows, columns // ranks), grad_attended.dtype)
    return pl.pallas_call(
        split_kernel,
        out_shape=[part] * ranks,
        in_specs=[vmem],
        out_specs=[vmem] * ranks,
        compiler_params=pltpu.CompilerParams(vmem_limit_bytes=SMALL_VMEM),
        name="split",
    )(grad_attended)


def join_kernel(*refs):
    out_ref = refs[-1]
    size = refs[0].shape[1]
    for k, ref in enumerate(refs[:-1]):
        at = pl.multiple_of((lax.axis_index("head") ^ k) * size, size)
        out_ref[:, pl.ds(at, size)] = ref[...]


def join(parts):
    rows, size = parts[0].shape
    vmem = pl.BlockSpec(memory_space=pltpu.VMEM)
    return pl.pallas_call(
        join_kernel,
        out_shape=jax.ShapeDtypeStruct((rows, size * len(parts)), parts[0].dtype),
        in_specs=[vmem] * len(parts),
        out_specs=vmem,
        compiler_params=pltpu.CompilerParams(vmem_limit_bytes=SMALL_VMEM),
        name="join",
    )(*parts)


def merge_kernel(mine_ref, other_ref, *block_refs):
    for k, ref in enumerate(block_refs):
        ref[...] = (mine_ref[k] + other_ref[k].astype(jnp.float32)).astype(ref.dtype)


def merge(mine, other, dtypes):
    vmem = pl.BlockSpec(memory_space=pltpu.VMEM)
    return pl.pallas_call(
        merge_kernel,
        out_shape=[jax.ShapeDtypeStruct(mine.shape[1:], dtype) for dtype in dtypes],
        in_specs=[vmem, vmem],
        out_specs=[vmem] * len(dtypes),
        compiler_params=pltpu.CompilerParams(vmem_limit_bytes=SMALL_VMEM),
        name="merge",
    )(mine, other)


def finish_kernel(own_ref, *refs):
    arrived = refs[:-2]
    dk_ref, dv_ref = refs[-2:]
    total = own_ref[...]
    for ref in arrived:
        total = total + ref[...].astype(jnp.float32)
    total = total.astype(jnp.bfloat16)
    width = dk_ref.shape[1]
    large = unit(dk_ref.shape[0])
    dk_ref[...] = dot_nt(large, total[:width]).astype(jnp.bfloat16)
    dv_ref[...] = dot_nt(large, total[width:]).astype(jnp.bfloat16)


def finish(own_part, arrived):
    both, tok = own_part.shape
    vmem = pl.BlockSpec(memory_space=pltpu.VMEM)
    shape = jax.ShapeDtypeStruct((tok, both // 2), jnp.bfloat16)
    return pl.pallas_call(
        finish_kernel,
        out_shape=(shape, shape),
        in_specs=[vmem] * (1 + len(arrived)),
        out_specs=(vmem, vmem),
        compiler_params=pltpu.CompilerParams(vmem_limit_bytes=SMALL_VMEM),
        name="finish",
    )(own_part, *arrived)


def shifted(block, by, count):
    pairs = [(i, i + by) for i in range(count) if 0 <= i + by < count]
    return lax.ppermute(block, "ctx", pairs)


def exchanged(block, axis, by):
    return lax.ppermute(block, axis, [(i, i ^ by) for i in range(lax.axis_size(axis))])


def body(queries, key_states, value_states, doc_lengths, grad_attended):
    tok, heads, width = queries.shape
    count = lax.axis_size("ctx")
    ranks = lax.axis_size("head")
    reach = min((DOC_MOST + tok - 2) // tok, count - 1)
    back = min((reach + 1) // 2, count // 2 - 1)
    own = jnp.concatenate(
        [key_states.reshape(tok, width), value_states.reshape(tok, width)], axis=0
    )
    near = exchanged(own, "ctx", 1)
    grad_parts = split(grad_attended, ranks)
    grad_parts = [part if k == 0 else exchanged(part, "head", k) for k, part in enumerate(grad_parts)]
    arrived, far = [shifted(own, 2, count)], []
    for k in range(1, back):
        block = arrived[-1]
        if k < ranks:
            block, grad_parts[k] = lax.optimization_barrier((block, grad_parts[k]))
        if k == 1:
            block, near = lax.optimization_barrier((block, near))
        else:
            block, far[-1] = lax.optimization_barrier((block, far[-1]))
        far.append(exchanged(block, "ctx", 1))
        arrived.append(shifted(block, 2, count))
    block, far[-1] = lax.optimization_barrier((arrived[-1], far[-1]))
    far.append(exchanged(block, "ctx", 1))
    *out_parts, grad_queries, mine_first, mine_last, other_first, other_last = attend(
        doc_lengths, queries, own, near, arrived, far, grad_parts
    )
    first = mine_first.shape[0]
    out_parts = [part if k == 0 else exchanged(part, "head", k) for k, part in enumerate(out_parts)]
    other_first = exchanged(other_first, "ctx", 1)
    other_last = exchanged(other_last, "ctx", 1)
    other_first, out_parts[:3] = lax.optimization_barrier((other_first, out_parts[:3]))
    blocks = merge(mine_first, other_first, [jnp.bfloat16] * first)
    arrived = [shifted(block, 2 * (pair - back), count) for pair, block in enumerate(blocks)]
    other_last, arrived[0] = lax.optimization_barrier((other_last, arrived[0]))
    *blocks, own_block = merge(
        mine_last, other_last, [jnp.bfloat16] * (back - first) + [jnp.float32]
    )
    arrived += [
        shifted(block, 2 * (first + k - back), count) for k, block in enumerate(blocks)
    ]
    grad_keys, grad_values = finish(own_block, arrived)
    attended = join(out_parts)
    grad_keys = grad_keys.reshape(tok, 1, width)
    grad_values = grad_values.reshape(tok, 1, width)
    return attended, grad_queries, grad_keys, grad_values


def solution(mesh):
    in_specs = (
        P("ctx", "head", None),
        P("ctx", "head", None),
        P("ctx", "head", None),
        P(),
        P(("ctx", "head"), None),
    )
    out_specs = (
        P(("ctx", "head"), None),
        P("ctx", "head", None),
        P("ctx", "head", None),
        P("ctx", "head", None),
    )
    return jax.shard_map(body, mesh=mesh, in_specs=in_specs, out_specs=out_specs, check_vma=False)
```

```python
import functools
import math

import jax
import jax.numpy as jnp
from jax import lax
from jax.experimental import pallas as pl
from jax.experimental.pallas import tpu as pltpu
from jax.sharding import PartitionSpec as P

DOC_MOST = 1792
NEG_FILL = -1e30
TILE = 256
CHUNK = 128
LOG2_E = 1.4426950408889634
SMALL_VMEM = 8 * 1024 * 1024


def dot(a, b):
    return jnp.dot(a, b, preferred_element_type=jnp.float32)


def dot_nt(a, b):
    return lax.dot_general(a, b, (((1,), (1,)), ((), ())), preferred_element_type=jnp.float32)


def unit(size):
    rows = lax.broadcasted_iota(jnp.int32, (size, size), 0)
    return (rows == lax.broadcasted_iota(jnp.int32, (size, size), 1)).astype(jnp.bfloat16)


def twice(column):
    return jnp.concatenate([column, column], axis=1)


def attention_kernel(
    doc_ref,
    q_ref,
    own_ref,
    near_ref,
    *refs,
    back,
    whole,
    ranks,
    heads,
    width,
    scale,
):
    arrived, far, refs = refs[:back], refs[back : 2 * back], refs[2 * back :]
    grad_parts, refs = refs[:ranks], refs[ranks:]
    out_parts, refs = refs[:ranks], refs[ranks:]
    (
        dq_ref,
        *refs,
    ) = refs
    d_refs, refs = refs[:4], refs[4:]
    (
        do_ref,
        o_ref,
        q32,
        keys,
        values,
        q_rows,
        do_rows,
        q_cols,
        do_cols,
        scores,
        accum,
        dq_acc,
        top,
        delta,
        d_blocks,
    ) = refs
    tok = q_ref.shape[0]
    part_rows = tok // ranks
    docs = doc_ref.shape[0]
    ctx = lax.axis_index("ctx")
    rank = lax.axis_index("head")
    parity = lax.rem(ctx, 2)
    base = 0 if whole else (ctx - parity - 2 * back) * tok
    own = ctx if whole else 2 * back + parity

    def pair_of(k):
        return (ctx // 2) ^ k if whole else back - k

    small = unit(width)
    ones = jnp.ones((width, width), jnp.bfloat16)

    values[:, width:] = jnp.ones_like(values[:, width:])
    for k in range(back + 1):
        pair = pair_of(k)
        mine, other = (own_ref, near_ref) if k == 0 else (arrived[k - 1], far[k - 1])
        for ref, place in ((mine, 2 * pair + parity), (other, 2 * pair + 1 - parity)):
            at = pl.ds(pl.multiple_of(place * tok, tok), tok)
            keys[at, :] = ref[0:tok, :]
            values[at, 0:width] = ref[tok:, :]
    for k in range(ranks):
        at = pl.ds(pl.multiple_of((rank ^ k) * part_rows, part_rows), part_rows)
        do_ref[at, :] = grad_parts[k][...]

    q32[...] = q_ref[...].astype(jnp.float32)
    d_blocks[...] = jnp.zeros_like(d_blocks)

    def chunk_step(chunk, carry):
        here = pl.ds(pl.multiple_of(chunk * CHUNK, CHUNK), CHUNK)
        for j in range(heads):
            part = pl.ds(j * CHUNK, CHUNK)
            q_rows[part, :] = q32[here, j, :].astype(jnp.bfloat16)
            do_rows[part, :] = do_ref[here, j * width : (j + 1) * width]
        q_cols[...] = dot_nt(small, q_rows[...]).astype(jnp.bfloat16)
        do_cols[...] = dot_nt(small, do_rows[...]).astype(jnp.bfloat16)
        top[...] = jnp.full_like(top, NEG_FILL)

        t_first = base + own * TILE + chunk * CHUNK
        t_last = t_first + CHUNK - 1
        t_col = t_first + lax.broadcasted_iota(jnp.int32, (CHUNK, width), 0)
        end = jnp.int32(0)
        start_first, start_last = jnp.int32(0), jnp.int32(0)
        start_col = jnp.zeros((CHUNK, width), jnp.int32)
        for i in range(docs):
            end = end + doc_ref[i]
            start_first = jnp.where(end <= t_first, end, start_first)
            start_last = jnp.where(end <= t_last, end, start_last)
            start_col = jnp.where(t_col >= end, end, start_col)
        low = jnp.maximum(start_first - base, 0) // TILE
        clear = jnp.clip((start_last - base + TILE - 1) // TILE, low, own)

        def score_tile(i, masked):
            at = pl.ds(pl.multiple_of(i * TILE, TILE), TILE)
            tile = dot_nt(q_rows[...], keys[at, :]) * (scale * LOG2_E)
            if masked:
                s_row = base + i * TILE + lax.broadcasted_iota(jnp.int32, (CHUNK, TILE), 1)
                live = (s_row >= twice(start_col)) & (s_row <= twice(t_col))
                tile = jnp.concatenate(
                    [
                        jnp.where(live, tile[j * CHUNK : (j + 1) * CHUNK], NEG_FILL)
                        for j in range(heads)
                    ],
                    axis=0,
                )
            scores[i] = tile
            top[...] = jnp.maximum(top[...], jnp.maximum(tile[:, :width], tile[:, width:]))

        def edge_step(n, carry):
            score_tile(jnp.where(n < clear - low, low + n, own), True)
            return carry

        def inner_step(i, carry):
            score_tile(i, False)
            return carry

        lax.fori_loop(0, clear - low + 1, edge_step, 0)
        lax.fori_loop(clear, own, inner_step, 0)
        top[...] = jnp.broadcast_to(jnp.max(top[...], axis=1, keepdims=True), top.shape)
        accum[...] = jnp.zeros_like(accum)

        def weigh_step(i, carry):
            at = pl.ds(pl.multiple_of(i * TILE, TILE), TILE)
            weights = jnp.exp2(scores[i] - twice(top[...])).astype(jnp.bfloat16)
            accum[...] += dot(weights, values[at, :])
            return carry

        lax.fori_loop(low, own + 1, weigh_step, 0)
        total = accum[:, width:]
        out = (accum[:, 0:width] / total).astype(jnp.bfloat16)
        for j in range(heads):
            o_ref[here, j * width : (j + 1) * width] = out[j * CHUNK : (j + 1) * CHUNK]
        top[...] = top[...] + jnp.log2(total)
        product = do_rows[...].astype(jnp.float32) * out.astype(jnp.float32)
        coarse = product.astype(jnp.bfloat16)
        fine = (product - coarse.astype(jnp.float32)).astype(jnp.bfloat16)
        delta[...] = dot(coarse, ones) + dot(fine, ones)
        dq_acc[...] = jnp.zeros_like(dq_acc)

        def back_step(i, carry):
            at = pl.ds(pl.multiple_of(i * TILE, TILE), TILE)
            probs = jnp.exp2(scores[i] - twice(top[...]))
            d_probs = dot_nt(do_rows[...], values[at, 0:width])
            d_scores = (probs * (d_probs - twice(delta[...]))).astype(jnp.bfloat16)
            dq_acc[...] += dot(d_scores, keys[at, :])
            d_blocks[i, 0:width, :] += dot(q_cols[...], d_scores)
            d_blocks[i, width:, :] += dot(do_cols[...], probs.astype(jnp.bfloat16))
            return carry

        lax.fori_loop(low, own + 1, back_step, 0)
        for j in range(heads):
            q32[here, j, :] = dq_acc[j * CHUNK : (j + 1) * CHUNK, :] * scale
        return carry

    lax.fori_loop(0, tok // CHUNK, chunk_step, 0)
    for k in range(ranks):
        at = pl.ds(pl.multiple_of((rank ^ k) * part_rows, part_rows), part_rows)
        out_parts[k][...] = o_ref[at, :]
    dq_ref[...] = q32[...].astype(jnp.bfloat16)
    for k in range(back + 1):
        mine, other = 2 * pair_of(k) + parity, 2 * pair_of(k) + 1 - parity
        which, to = (0, back - k) if k > 1 else (2, k)
        d_refs[which][to, 0:width, :] = d_blocks[mine, 0:width, :] * scale
        d_refs[which][to, width:, :] = d_blocks[mine, width:, :]
        d_refs[which + 1][to, 0:width, :] = (d_blocks[other, 0:width, :] * scale).astype(
            jnp.bfloat16
        )
        d_refs[which + 1][to, width:, :] = d_blocks[other, width:, :].astype(jnp.bfloat16)


def attend(doc_lengths, queries, own, near, arrived, far, grad_parts, whole):
    tok, heads, width = queries.shape
    back = len(arrived)
    ranks = len(grad_parts)
    tiles = 2 * (back + 1)
    span = tiles * tok
    rows = heads * CHUNK
    vmem = pl.BlockSpec(memory_space=pltpu.VMEM)
    smem = pl.BlockSpec(memory_space=pltpu.SMEM)
    out_part = jax.ShapeDtypeStruct((tok // ranks, heads * width), jnp.bfloat16)
    return pl.pallas_call(
        functools.partial(
            attention_kernel,
            back=back,
            whole=whole,
            ranks=ranks,
            heads=heads,
            width=width,
            scale=1.0 / math.sqrt(width),
        ),
        out_shape=[out_part] * ranks
        + [
            jax.ShapeDtypeStruct((tok, heads, width), jnp.bfloat16),
        ]
        + [
            jax.ShapeDtypeStruct((size, 2 * width, tok), dtype)
            for size in (back - 1, 2)
            for dtype in (jnp.float32, jnp.bfloat16)
        ],
        in_specs=[smem] + [vmem] * (3 + 2 * back + ranks),
        out_specs=[vmem] * (ranks + 5),
        scratch_shapes=[
            pltpu.VMEM((tok, heads * width), jnp.bfloat16),
            pltpu.VMEM((tok, heads * width), jnp.bfloat16),
            pltpu.VMEM((tok, heads, width), jnp.float32),
            pltpu.VMEM((span, width), jnp.bfloat16),
            pltpu.VMEM((span, 2 * width), jnp.bfloat16),
            pltpu.VMEM((rows, width), jnp.bfloat16),
            pltpu.VMEM((rows, width), jnp.bfloat16),
            pltpu.VMEM((width, rows), jnp.bfloat16),
            pltpu.VMEM((width, rows), jnp.bfloat16),
            pltpu.VMEM((tiles, rows, TILE), jnp.float32),
            pltpu.VMEM((rows, 2 * width), jnp.float32),
            pltpu.VMEM((rows, width), jnp.float32),
            pltpu.VMEM((rows, width), jnp.float32),
            pltpu.VMEM((rows, width), jnp.float32),
            pltpu.VMEM((tiles, 2 * width, tok), jnp.float32),
        ],
        compiler_params=pltpu.CompilerParams(vmem_limit_bytes=40 * 1024 * 1024),
        cost_estimate=pl.CostEstimate(
            flops=14 * tok * heads * width * span,
            bytes_accessed=4 * tok * heads * width * 2 + 4 * span * width * 2,
            transcendentals=tok * heads * span,
        ),
        name="attention",
    )(doc_lengths, queries, own, near, *arrived, *far, *grad_parts)


def split_kernel(grad_ref, *part_refs):
    size = part_refs[0].shape[1]
    for k, ref in enumerate(part_refs):
        at = pl.multiple_of((lax.axis_index("head") ^ k) * size, size)
        ref[...] = grad_ref[:, pl.ds(at, size)]


def split(grad_attended, ranks):
    rows, columns = grad_attended.shape
    vmem = pl.BlockSpec(memory_space=pltpu.VMEM)
    part = jax.ShapeDtypeStruct((rows, columns // ranks), grad_attended.dtype)
    return pl.pallas_call(
        split_kernel,
        out_shape=[part] * ranks,
        in_specs=[vmem],
        out_specs=[vmem] * ranks,
        compiler_params=pltpu.CompilerParams(vmem_limit_bytes=SMALL_VMEM),
        name="split",
    )(grad_attended)


def join_kernel(*refs):
    out_ref = refs[-1]
    size = refs[0].shape[1]
    for k, ref in enumerate(refs[:-1]):
        at = pl.multiple_of((lax.axis_index("head") ^ k) * size, size)
        out_ref[:, pl.ds(at, size)] = ref[...]


def join(parts):
    rows, size = parts[0].shape
    vmem = pl.BlockSpec(memory_space=pltpu.VMEM)
    return pl.pallas_call(
        join_kernel,
        out_shape=jax.ShapeDtypeStruct((rows, size * len(parts)), parts[0].dtype),
        in_specs=[vmem] * len(parts),
        out_specs=vmem,
        compiler_params=pltpu.CompilerParams(vmem_limit_bytes=SMALL_VMEM),
        name="join",
    )(*parts)


def merge_kernel(mine_ref, other_ref, *block_refs):
    for k, ref in enumerate(block_refs):
        ref[...] = (mine_ref[k] + other_ref[k].astype(jnp.float32)).astype(ref.dtype)


def merge(mine, other, dtypes):
    vmem = pl.BlockSpec(memory_space=pltpu.VMEM)
    return pl.pallas_call(
        merge_kernel,
        out_shape=[jax.ShapeDtypeStruct(mine.shape[1:], dtype) for dtype in dtypes],
        in_specs=[vmem, vmem],
        out_specs=[vmem] * len(dtypes),
        compiler_params=pltpu.CompilerParams(vmem_limit_bytes=SMALL_VMEM),
        name="merge",
    )(mine, other)


def finish_kernel(own_ref, *refs):
    arrived = refs[:-2]
    dk_ref, dv_ref = refs[-2:]
    total = own_ref[...]
    for ref in arrived:
        total = total + ref[...].astype(jnp.float32)
    total = total.astype(jnp.bfloat16)
    width = dk_ref.shape[1]
    large = unit(dk_ref.shape[0])
    dk_ref[...] = dot_nt(large, total[:width]).astype(jnp.bfloat16)
    dv_ref[...] = dot_nt(large, total[width:]).astype(jnp.bfloat16)


def finish(own_part, arrived):
    both, tok = own_part.shape
    vmem = pl.BlockSpec(memory_space=pltpu.VMEM)
    shape = jax.ShapeDtypeStruct((tok, both // 2), jnp.bfloat16)
    return pl.pallas_call(
        finish_kernel,
        out_shape=(shape, shape),
        in_specs=[vmem] * (1 + len(arrived)),
        out_specs=(vmem, vmem),
        compiler_params=pltpu.CompilerParams(vmem_limit_bytes=SMALL_VMEM),
        name="finish",
    )(own_part, *arrived)


def shifted(block, by, count):
    pairs = [(i, i + by) for i in range(count) if 0 <= i + by < count]
    return lax.ppermute(block, "ctx", pairs)


def exchanged(block, axis, by):
    return lax.ppermute(block, axis, [(i, i ^ by) for i in range(lax.axis_size(axis))])


def after(value, *others):
    return lax.optimization_barrier((value, *others))


def body(queries, key_states, value_states, doc_lengths, grad_attended):
    tok, heads, width = queries.shape
    count = lax.axis_size("ctx")
    ranks = lax.axis_size("head")
    reach = min((DOC_MOST + tok - 2) // tok, count - 1)
    back = min((reach + 1) // 2, count // 2 - 1)
    whole = count == 8 and back == 3
    own = jnp.concatenate(
        [key_states.reshape(tok, width), value_states.reshape(tok, width)], axis=0
    )
    if whole:
        across, beside = exchanged(own, "ctx", 4), exchanged(own, "ctx", 2)
    else:
        arrived = [shifted(own, 2 * k, count) for k in range(1, back + 1)]
    near = exchanged(own, "ctx", 1)
    grads = split(grad_attended, ranks)
    grads = [part if k == 0 else exchanged(part, "head", k) for k, part in enumerate(grads)]
    if whole:
        beside, near = after(beside, near)
        far_beside = exchanged(beside, "ctx", 1)
        across, far_beside, *grads[1:3] = after(across, far_beside, *grads[1:3])
        passed = exchanged(across, "ctx", 2)
        far_across = exchanged(across, "ctx", 1)
        passed, *grads[3:] = after(passed, *grads[3:])
        far_passed = exchanged(passed, "ctx", 1)
        arrived = [beside, across, passed]
        far = [far_beside, far_across, far_passed]
    else:
        far = [exchanged(block, "ctx", 1) for block in arrived]
    outputs = attend(
        doc_lengths, queries, own, near, arrived, far, grads, whole
    )

    def home(block, k):
        return exchanged(block, "ctx", 2 * k) if whole else shifted(block, -2 * k, count)

    outs, grad_queries = list(outputs[:ranks]), outputs[ranks]
    mine_far, other_far, mine_rest, other_rest = outputs[ranks + 1 :]
    other_far = exchanged(other_far, "ctx", 1)
    other_rest = exchanged(other_rest, "ctx", 1)
    outs[1:] = [exchanged(part, "head", k + 1) for k, part in enumerate(outs[1:])]
    other_far, *outs[1:3] = after(other_far, *outs[1:3])
    blocks = merge(mine_far, other_far, [jnp.bfloat16] * (back - 1))
    returned = [home(block, back - n) for n, block in enumerate(blocks)]
    other_rest, returned[0] = after(other_rest, returned[0])
    own_block, block = merge(mine_rest, other_rest, [jnp.float32, jnp.bfloat16])
    returned.append(home(block, 1))
    grad_keys, grad_values = finish(own_block, returned)
    attended = join(outs)
    grad_keys = grad_keys.reshape(tok, 1, width)
    grad_values = grad_values.reshape(tok, 1, width)
    return attended, grad_queries, grad_keys, grad_values


def solution(mesh):
    in_specs = (
        P("ctx", "head", None),
        P("ctx", "head", None),
        P("ctx", "head", None),
        P(),
        P(("ctx", "head"), None),
    )
    out_specs = (
        P(("ctx", "head"), None),
        P("ctx", "head", None),
        P("ctx", "head", None),
        P("ctx", "head", None),
    )
    return jax.shard_map(body, mesh=mesh, in_specs=in_specs, out_specs=out_specs, check_vma=False)
```

```python
import functools
import math

import jax
import jax.numpy as jnp
from jax import lax
from jax.experimental import pallas as pl
from jax.experimental.pallas import tpu as pltpu
from jax.sharding import PartitionSpec as P

DOC_MOST = 1792
NEG_FILL = -1e30
TILE = 256
CHUNK = 128
LOG2_E = 1.4426950408889634
SMALL_VMEM = 8 * 1024 * 1024


def dot(a, b):
    return jnp.dot(a, b, preferred_element_type=jnp.float32)


def dot_nt(a, b):
    return lax.dot_general(a, b, (((1,), (1,)), ((), ())), preferred_element_type=jnp.float32)


def unit(size):
    rows = lax.broadcasted_iota(jnp.int32, (size, size), 0)
    return (rows == lax.broadcasted_iota(jnp.int32, (size, size), 1)).astype(jnp.bfloat16)


def twice(column):
    return jnp.concatenate([column, column], axis=1)


def attention_kernel(
    doc_ref,
    q_ref,
    own_ref,
    near_ref,
    *refs,
    back,
    whole,
    ranks,
    heads,
    width,
    scale,
):
    arrived, far, refs = refs[:back], refs[back : 2 * back], refs[2 * back :]
    grad_parts, refs = refs[:ranks], refs[ranks:]
    out_parts, refs = refs[:ranks], refs[ranks:]
    (
        dq_ref,
        *refs,
    ) = refs
    d_refs, refs = refs[: 2 * back + 2], refs[2 * back + 2 :]
    (
        do_ref,
        o_ref,
        q32,
        keys,
        values,
        q_rows,
        do_rows,
        q_cols,
        do_cols,
        scores,
        accum,
        dq_acc,
        top,
        delta,
        d_blocks,
    ) = refs
    tok = q_ref.shape[0]
    part_rows = tok // ranks
    docs = doc_ref.shape[0]
    ctx = lax.axis_index("ctx")
    rank = lax.axis_index("head")
    parity = lax.rem(ctx, 2)
    base = 0 if whole else (ctx - parity - 2 * back) * tok
    own = ctx if whole else 2 * back + parity

    def pair_of(k):
        return (ctx // 2) ^ k if whole else back - k

    small = unit(width)
    ones = jnp.ones((width, width), jnp.bfloat16)

    values[:, width:] = jnp.ones_like(values[:, width:])
    for k in range(back + 1):
        pair = pair_of(k)
        mine, other = (own_ref, near_ref) if k == 0 else (arrived[k - 1], far[k - 1])
        for ref, place in ((mine, 2 * pair + parity), (other, 2 * pair + 1 - parity)):
            at = pl.ds(pl.multiple_of(place * tok, tok), tok)
            keys[at, :] = ref[0:tok, :]
            values[at, 0:width] = ref[tok:, :]
    for k in range(ranks):
        at = pl.ds(pl.multiple_of((rank ^ k) * part_rows, part_rows), part_rows)
        do_ref[at, :] = grad_parts[k][...]

    q32[...] = q_ref[...].astype(jnp.float32)
    d_blocks[...] = jnp.zeros_like(d_blocks)

    def chunk_step(chunk, carry):
        here = pl.ds(pl.multiple_of(chunk * CHUNK, CHUNK), CHUNK)
        for j in range(heads):
            part = pl.ds(j * CHUNK, CHUNK)
            q_rows[part, :] = q32[here, j, :].astype(jnp.bfloat16)
            do_rows[part, :] = do_ref[here, j * width : (j + 1) * width]
        q_cols[...] = dot_nt(small, q_rows[...]).astype(jnp.bfloat16)
        do_cols[...] = dot_nt(small, do_rows[...]).astype(jnp.bfloat16)
        top[...] = jnp.full_like(top, NEG_FILL)

        t_first = base + own * TILE + chunk * CHUNK
        t_last = t_first + CHUNK - 1
        t_col = t_first + lax.broadcasted_iota(jnp.int32, (CHUNK, width), 0)
        end = jnp.int32(0)
        start_first, start_last = jnp.int32(0), jnp.int32(0)
        start_col = jnp.zeros((CHUNK, width), jnp.int32)
        for i in range(docs):
            end = end + doc_ref[i]
            start_first = jnp.where(end <= t_first, end, start_first)
            start_last = jnp.where(end <= t_last, end, start_last)
            start_col = jnp.where(t_col >= end, end, start_col)
        low = jnp.maximum(start_first - base, 0) // TILE
        clear = jnp.clip((start_last - base + TILE - 1) // TILE, low, own)

        def score_tile(i, masked):
            at = pl.ds(pl.multiple_of(i * TILE, TILE), TILE)
            tile = dot_nt(q_rows[...], keys[at, :]) * (scale * LOG2_E)
            if masked:
                s_row = base + i * TILE + lax.broadcasted_iota(jnp.int32, (CHUNK, TILE), 1)
                live = (s_row >= twice(start_col)) & (s_row <= twice(t_col))
                tile = jnp.concatenate(
                    [
                        jnp.where(live, tile[j * CHUNK : (j + 1) * CHUNK], NEG_FILL)
                        for j in range(heads)
                    ],
                    axis=0,
                )
            scores[i] = tile
            top[...] = jnp.maximum(top[...], jnp.maximum(tile[:, :width], tile[:, width:]))

        def edge_step(n, carry):
            score_tile(jnp.where(n < clear - low, low + n, own), True)
            return carry

        def inner_step(i, carry):
            score_tile(i, False)
            return carry

        lax.fori_loop(0, clear - low + 1, edge_step, 0)
        lax.fori_loop(clear, own, inner_step, 0)
        top[...] = jnp.broadcast_to(jnp.max(top[...], axis=1, keepdims=True), top.shape)
        accum[...] = jnp.zeros_like(accum)

        def weigh_step(i, carry):
            at = pl.ds(pl.multiple_of(i * TILE, TILE), TILE)
            weights = jnp.exp2(scores[i] - twice(top[...])).astype(jnp.bfloat16)
            accum[...] += dot(weights, values[at, :])
            return carry

        lax.fori_loop(low, own + 1, weigh_step, 0)
        total = accum[:, width:]
        out = (accum[:, 0:width] / total).astype(jnp.bfloat16)
        for j in range(heads):
            o_ref[here, j * width : (j + 1) * width] = out[j * CHUNK : (j + 1) * CHUNK]
        top[...] = top[...] + jnp.log2(total)
        product = do_rows[...].astype(jnp.float32) * out.astype(jnp.float32)
        coarse = product.astype(jnp.bfloat16)
        fine = (product - coarse.astype(jnp.float32)).astype(jnp.bfloat16)
        delta[...] = dot(coarse, ones) + dot(fine, ones)
        dq_acc[...] = jnp.zeros_like(dq_acc)

        def back_step(i, carry):
            at = pl.ds(pl.multiple_of(i * TILE, TILE), TILE)
            probs = jnp.exp2(scores[i] - twice(top[...]))
            d_probs = dot_nt(do_rows[...], values[at, 0:width])
            d_scores = (probs * (d_probs - twice(delta[...]))).astype(jnp.bfloat16)
            dq_acc[...] += dot(d_scores, keys[at, :])
            d_blocks[i, 0:width, :] += dot(q_cols[...], d_scores)
            d_blocks[i, width:, :] += dot(do_cols[...], probs.astype(jnp.bfloat16))
            return carry

        lax.fori_loop(low, own + 1, back_step, 0)
        for j in range(heads):
            q32[here, j, :] = dq_acc[j * CHUNK : (j + 1) * CHUNK, :] * scale
        return carry

    lax.fori_loop(0, tok // CHUNK, chunk_step, 0)
    for k in range(ranks):
        at = pl.ds(pl.multiple_of((rank ^ k) * part_rows, part_rows), part_rows)
        out_parts[k][...] = o_ref[at, :]
    dq_ref[...] = q32[...].astype(jnp.bfloat16)
    for k in range(back + 1):
        mine, other = 2 * pair_of(k) + parity, 2 * pair_of(k) + 1 - parity
        mine_ref, other_ref = d_refs[2 * k], d_refs[2 * k + 1]
        mine_ref[0:width, :] = d_blocks[mine, 0:width, :] * scale
        mine_ref[width:, :] = d_blocks[mine, width:, :]
        other_ref[0:width, :] = (d_blocks[other, 0:width, :] * scale).astype(jnp.bfloat16)
        other_ref[width:, :] = d_blocks[other, width:, :].astype(jnp.bfloat16)


def attend(doc_lengths, queries, own, near, arrived, far, grad_parts, whole):
    tok, heads, width = queries.shape
    back = len(arrived)
    ranks = len(grad_parts)
    tiles = 2 * (back + 1)
    span = tiles * tok
    rows = heads * CHUNK
    vmem = pl.BlockSpec(memory_space=pltpu.VMEM)
    smem = pl.BlockSpec(memory_space=pltpu.SMEM)
    out_part = jax.ShapeDtypeStruct((tok // ranks, heads * width), jnp.bfloat16)
    return pl.pallas_call(
        functools.partial(
            attention_kernel,
            back=back,
            whole=whole,
            ranks=ranks,
            heads=heads,
            width=width,
            scale=1.0 / math.sqrt(width),
        ),
        out_shape=[out_part] * ranks
        + [
            jax.ShapeDtypeStruct((tok, heads, width), jnp.bfloat16),
        ]
        + [
            jax.ShapeDtypeStruct((2 * width, tok), dtype)
            for _ in range(back + 1)
            for dtype in (jnp.float32, jnp.bfloat16)
        ],
        in_specs=[smem] + [vmem] * (3 + 2 * back + ranks),
        out_specs=[vmem] * (ranks + 2 * back + 3),
        scratch_shapes=[
            pltpu.VMEM((tok, heads * width), jnp.bfloat16),
            pltpu.VMEM((tok, heads * width), jnp.bfloat16),
            pltpu.VMEM((tok, heads, width), jnp.float32),
            pltpu.VMEM((span, width), jnp.bfloat16),
            pltpu.VMEM((span, 2 * width), jnp.bfloat16),
            pltpu.VMEM((rows, width), jnp.bfloat16),
            pltpu.VMEM((rows, width), jnp.bfloat16),
            pltpu.VMEM((width, rows), jnp.bfloat16),
            pltpu.VMEM((width, rows), jnp.bfloat16),
            pltpu.VMEM((tiles, rows, TILE), jnp.float32),
            pltpu.VMEM((rows, 2 * width), jnp.float32),
            pltpu.VMEM((rows, width), jnp.float32),
            pltpu.VMEM((rows, width), jnp.float32),
            pltpu.VMEM((rows, width), jnp.float32),
            pltpu.VMEM((tiles, 2 * width, tok), jnp.float32),
        ],
        compiler_params=pltpu.CompilerParams(vmem_limit_bytes=40 * 1024 * 1024),
        cost_estimate=pl.CostEstimate(
            flops=14 * tok * heads * width * span,
            bytes_accessed=4 * tok * heads * width * 2 + 4 * span * width * 2,
            transcendentals=tok * heads * span,
        ),
        name="attention",
    )(doc_lengths, queries, own, near, *arrived, *far, *grad_parts)


def split_kernel(grad_ref, *part_refs):
    size = part_refs[0].shape[1]
    for k, ref in enumerate(part_refs):
        at = pl.multiple_of((lax.axis_index("head") ^ k) * size, size)
        ref[...] = grad_ref[:, pl.ds(at, size)]


def split(grad_attended, ranks):
    rows, columns = grad_attended.shape
    vmem = pl.BlockSpec(memory_space=pltpu.VMEM)
    part = jax.ShapeDtypeStruct((rows, columns // ranks), grad_attended.dtype)
    return pl.pallas_call(
        split_kernel,
        out_shape=[part] * ranks,
        in_specs=[vmem],
        out_specs=[vmem] * ranks,
        compiler_params=pltpu.CompilerParams(vmem_limit_bytes=SMALL_VMEM),
        name="split",
    )(grad_attended)


def join_kernel(*refs):
    out_ref = refs[-1]
    size = refs[0].shape[1]
    for k, ref in enumerate(refs[:-1]):
        at = pl.multiple_of((lax.axis_index("head") ^ k) * size, size)
        out_ref[:, pl.ds(at, size)] = ref[...]


def join(parts):
    rows, size = parts[0].shape
    vmem = pl.BlockSpec(memory_space=pltpu.VMEM)
    return pl.pallas_call(
        join_kernel,
        out_shape=jax.ShapeDtypeStruct((rows, size * len(parts)), parts[0].dtype),
        in_specs=[vmem] * len(parts),
        out_specs=vmem,
        compiler_params=pltpu.CompilerParams(vmem_limit_bytes=SMALL_VMEM),
        name="join",
    )(*parts)


def merge_kernel(*refs):
    total = refs[0][...]
    for ref in refs[1:-1]:
        total = total + ref[...].astype(jnp.float32)
    refs[-1][...] = total.astype(jnp.bfloat16)


def merge(*blocks):
    vmem = pl.BlockSpec(memory_space=pltpu.VMEM)
    return pl.pallas_call(
        merge_kernel,
        out_shape=jax.ShapeDtypeStruct(blocks[0].shape, jnp.bfloat16),
        in_specs=[vmem] * len(blocks),
        out_specs=vmem,
        compiler_params=pltpu.CompilerParams(vmem_limit_bytes=SMALL_VMEM),
        name="merge",
    )(*blocks)


def finish_kernel(own_ref, *refs):
    arrived = refs[:-2]
    dk_ref, dv_ref = refs[-2:]
    total = own_ref[...]
    for ref in arrived:
        total = total + ref[...].astype(jnp.float32)
    total = total.astype(jnp.bfloat16)
    width = dk_ref.shape[1]
    large = unit(dk_ref.shape[0])
    dk_ref[...] = dot_nt(large, total[:width]).astype(jnp.bfloat16)
    dv_ref[...] = dot_nt(large, total[width:]).astype(jnp.bfloat16)


def finish(own_part, arrived):
    both, tok = own_part.shape
    vmem = pl.BlockSpec(memory_space=pltpu.VMEM)
    shape = jax.ShapeDtypeStruct((tok, both // 2), jnp.bfloat16)
    return pl.pallas_call(
        finish_kernel,
        out_shape=(shape, shape),
        in_specs=[vmem] * (1 + len(arrived)),
        out_specs=(vmem, vmem),
        compiler_params=pltpu.CompilerParams(vmem_limit_bytes=SMALL_VMEM),
        name="finish",
    )(own_part, *arrived)


def shifted(block, by, count):
    pairs = [(i, i + by) for i in range(count) if 0 <= i + by < count]
    return lax.ppermute(block, "ctx", pairs)


def exchanged(block, axis, by):
    return lax.ppermute(block, axis, [(i, i ^ by) for i in range(lax.axis_size(axis))])


def after(value, *others):
    return lax.optimization_barrier((value, *others))


def body(queries, key_states, value_states, doc_lengths, grad_attended):
    tok, heads, width = queries.shape
    count = lax.axis_size("ctx")
    ranks = lax.axis_size("head")
    reach = min((DOC_MOST + tok - 2) // tok, count - 1)
    back = min((reach + 1) // 2, count // 2 - 1)
    whole = count == 8 and back == 3 and ranks == 4
    own = jnp.concatenate(
        [key_states.reshape(tok, width), value_states.reshape(tok, width)], axis=0
    )
    near = exchanged(own, "ctx", 1)
    if whole:
        beside = exchanged(own, "ctx", 2)
        across = exchanged(own, "ctx", 4)
    else:
        arrived = [shifted(own, 2 * k, count) for k in range(1, back + 1)]
    grads = split(grad_attended, ranks)
    grads = [part if k == 0 else exchanged(part, "head", k) for k, part in enumerate(grads)]
    if whole:
        beside, near = after(beside, near)
        far_beside = exchanged(beside, "ctx", 1)
        across, grads[1] = after(across, grads[1])
        passed = exchanged(across, "ctx", 2)
        across, far_beside, grads[2] = after(across, far_beside, grads[2])
        far_across = exchanged(across, "ctx", 1)
        passed, grads[3] = after(passed, grads[3])
        far_passed = exchanged(passed, "ctx", 1)
        arrived = [beside, across, passed]
        far = [far_beside, far_across, far_passed]
    else:
        far = [exchanged(block, "ctx", 1) for block in arrived]
    outputs = attend(
        doc_lengths, queries, own, near, arrived, far, grads, whole
    )

    outs, grad_queries, parts = list(outputs[:ranks]), outputs[ranks], outputs[ranks + 1 :]
    mine, other = list(parts[0::2]), list(parts[1::2])
    outs = [part if k == 0 else exchanged(part, "head", k) for k, part in enumerate(outs)]
    for k in range(back, -1, -1):
        if k < back:
            other[k], other[k + 1] = after(other[k], other[k + 1])
        other[k] = exchanged(other[k], "ctx", 1)
    if whole:
        other[3], outs[1] = after(other[3], outs[1])
        passed = exchanged(merge(mine[3], other[3]), "ctx", 2)
        passed, outs[2] = after(passed, outs[2])
        across = exchanged(merge(mine[2], other[2], passed), "ctx", 4)
        other[1], outs[3] = after(other[1], outs[3])
        beside = exchanged(merge(mine[1], other[1]), "ctx", 2)
        returned = [beside, across]
    else:
        returned = [
            shifted(merge(mine[k], other[k]), -2 * k, count) for k in range(back, 0, -1)
        ]
    grad_keys, grad_values = finish(mine[0], [other[0]] + returned)
    attended = join(outs)
    grad_keys = grad_keys.reshape(tok, 1, width)
    grad_values = grad_values.reshape(tok, 1, width)
    return attended, grad_queries, grad_keys, grad_values


def solution(mesh):
    in_specs = (
        P("ctx", "head", None),
        P("ctx", "head", None),
        P("ctx", "head", None),
        P(),
        P(("ctx", "head"), None),
    )
    out_specs = (
        P(("ctx", "head"), None),
        P("ctx", "head", None),
        P("ctx", "head", None),
        P("ctx", "head", None),
    )
    return jax.shard_map(body, mesh=mesh, in_specs=in_specs, out_specs=out_specs, check_vma=False)
```

```python
import functools
import math

import jax
import jax.numpy as jnp
from jax import lax
from jax.experimental import pallas as pl
from jax.experimental.pallas import tpu as pltpu
from jax.sharding import PartitionSpec as P

DOC_MOST = 1792
NEG_FILL = -1e30
TILE = 256
CHUNK = 128
LOG2_E = 1.4426950408889634
SMALL_VMEM = 8 * 1024 * 1024


def dot(a, b):
    return jnp.dot(a, b, preferred_element_type=jnp.float32)


def dot_nt(a, b):
    return lax.dot_general(a, b, (((1,), (1,)), ((), ())), preferred_element_type=jnp.float32)


def unit(size):
    rows = lax.broadcasted_iota(jnp.int32, (size, size), 0)
    return (rows == lax.broadcasted_iota(jnp.int32, (size, size), 1)).astype(jnp.bfloat16)


def twice(column):
    return jnp.concatenate([column, column], axis=1)


def attention_kernel(
    doc_ref,
    q_rows,
    q_cols,
    do_rows,
    do_cols,
    own_ref,
    near_ref,
    *refs,
    back,
    whole,
    ranks,
    heads,
    width,
    scale,
):
    arrived, far, refs = refs[:back], refs[back : 2 * back], refs[2 * back :]
    out_parts, dq_acc, refs = refs[:ranks], refs[ranks], refs[ranks + 1 :]
    d_refs, refs = refs[: 2 * back + 2], refs[2 * back + 2 :]
    (o_ref, keys, values, scores, accum, top, delta, d_blocks) = refs
    tok = own_ref.shape[0] // 2
    part_rows = tok // ranks
    docs = doc_ref.shape[0]
    ctx = lax.axis_index("ctx")
    rank = lax.axis_index("head")
    parity = lax.rem(ctx, 2)
    base = 0 if whole else (ctx - parity - 2 * back) * tok
    own = ctx if whole else 2 * back + parity
    ones = jnp.ones((width, width), jnp.bfloat16)

    def pair_of(k):
        return (ctx // 2) ^ k if whole else back - k

    values[:, width:] = jnp.ones_like(values[:, width:])
    for k in range(back + 1):
        pair = pair_of(k)
        mine, other = (own_ref, near_ref) if k == 0 else (arrived[k - 1], far[k - 1])
        for ref, place in ((mine, 2 * pair + parity), (other, 2 * pair + 1 - parity)):
            at = pl.ds(pl.multiple_of(place * tok, tok), tok)
            keys[at, :] = ref[0:tok, :]
            values[at, 0:width] = ref[tok:, :]
    d_blocks[...] = jnp.zeros_like(d_blocks)

    def chunk_step(chunk, carry):
        here = pl.ds(pl.multiple_of(chunk * CHUNK, CHUNK), CHUNK)
        top[...] = jnp.full_like(top, NEG_FILL)

        t_first = base + own * TILE + chunk * CHUNK
        t_last = t_first + CHUNK - 1
        t_col = t_first + lax.broadcasted_iota(jnp.int32, (CHUNK, width), 0)
        end = jnp.int32(0)
        start_first, start_last = jnp.int32(0), jnp.int32(0)
        start_col = jnp.zeros((CHUNK, width), jnp.int32)
        for i in range(docs):
            end = end + doc_ref[i]
            start_first = jnp.where(end <= t_first, end, start_first)
            start_last = jnp.where(end <= t_last, end, start_last)
            start_col = jnp.where(t_col >= end, end, start_col)
        low = jnp.maximum(start_first - base, 0) // TILE
        clear = jnp.clip((start_last - base + TILE - 1) // TILE, low, own)

        def score_tile(i, masked):
            at = pl.ds(pl.multiple_of(i * TILE, TILE), TILE)
            tile = dot_nt(q_rows[chunk], keys[at, :]) * (scale * LOG2_E)
            if masked:
                s_row = base + i * TILE + lax.broadcasted_iota(jnp.int32, (CHUNK, TILE), 1)
                live = (s_row >= twice(start_col)) & (s_row <= twice(t_col))
                tile = jnp.concatenate(
                    [
                        jnp.where(live, tile[j * CHUNK : (j + 1) * CHUNK], NEG_FILL)
                        for j in range(heads)
                    ],
                    axis=0,
                )
            scores[i] = tile
            top[...] = jnp.maximum(top[...], jnp.maximum(tile[:, :width], tile[:, width:]))

        def edge_step(n, carry):
            score_tile(jnp.where(n < clear - low, low + n, own), True)
            return carry

        def inner_step(i, carry):
            score_tile(i, False)
            return carry

        lax.fori_loop(0, clear - low + 1, edge_step, 0)
        lax.fori_loop(clear, own, inner_step, 0)
        top[...] = jnp.broadcast_to(jnp.max(top[...], axis=1, keepdims=True), top.shape)
        accum[...] = jnp.zeros_like(accum)

        def weigh_step(i, carry):
            at = pl.ds(pl.multiple_of(i * TILE, TILE), TILE)
            weights = jnp.exp2(scores[i] - twice(top[...])).astype(jnp.bfloat16)
            accum[...] += dot(weights, values[at, :])
            return carry

        lax.fori_loop(low, own + 1, weigh_step, 0)
        total = accum[:, width:]
        out = (accum[:, 0:width] / total).astype(jnp.bfloat16)
        for j in range(heads):
            o_ref[here, j * width : (j + 1) * width] = out[j * CHUNK : (j + 1) * CHUNK]
        top[...] = top[...] + jnp.log2(total)
        product = do_rows[chunk].astype(jnp.float32) * out.astype(jnp.float32)
        coarse = product.astype(jnp.bfloat16)
        fine = (product - coarse.astype(jnp.float32)).astype(jnp.bfloat16)
        delta[...] = dot(coarse, ones) + dot(fine, ones)
        dq_acc[chunk] = jnp.zeros(dq_acc.shape[1:], jnp.float32)

        def back_step(i, carry):
            at = pl.ds(pl.multiple_of(i * TILE, TILE), TILE)
            probs = jnp.exp2(scores[i] - twice(top[...]))
            d_probs = dot_nt(do_rows[chunk], values[at, 0:width])
            d_scores = (probs * (d_probs - twice(delta[...]))).astype(jnp.bfloat16)
            dq_acc[chunk] += dot(d_scores, keys[at, :])
            d_blocks[i, 0:width, :] += dot(q_cols[chunk], d_scores)
            d_blocks[i, width:, :] += dot(do_cols[chunk], probs.astype(jnp.bfloat16))
            return carry

        lax.fori_loop(low, own + 1, back_step, 0)
        return carry

    lax.fori_loop(0, tok // CHUNK, chunk_step, 0)
    for k in range(ranks):
        at = pl.ds(pl.multiple_of((rank ^ k) * part_rows, part_rows), part_rows)
        out_parts[k][...] = o_ref[at, :]
    for k in range(back + 1):
        pair = jnp.maximum(ctx // 2 - k, 0) if whole else back - k
        mine, other = 2 * pair + parity, 2 * pair + 1 - parity
        mine_ref, other_ref = d_refs[2 * k], d_refs[2 * k + 1]
        mine_ref[0:width, :] = d_blocks[mine, 0:width, :] * scale
        mine_ref[width:, :] = d_blocks[mine, width:, :]
        other_ref[0:width, :] = (d_blocks[other, 0:width, :] * scale).astype(jnp.bfloat16)
        other_ref[width:, :] = d_blocks[other, width:, :].astype(jnp.bfloat16)


def attend(doc_lengths, prepared, own, near, arrived, far, ranks, whole):
    chunks, rows, width = prepared[0].shape
    tok = chunks * CHUNK
    heads = rows // CHUNK
    back = len(arrived)
    tiles = 2 * (back + 1)
    span = tiles * tok
    vmem = pl.BlockSpec(memory_space=pltpu.VMEM)
    smem = pl.BlockSpec(memory_space=pltpu.SMEM)
    out_part = jax.ShapeDtypeStruct((tok // ranks, heads * width), jnp.bfloat16)
    return pl.pallas_call(
        functools.partial(
            attention_kernel,
            back=back,
            whole=whole,
            ranks=ranks,
            heads=heads,
            width=width,
            scale=1.0 / math.sqrt(width),
        ),
        out_shape=[out_part] * ranks
        + [
            jax.ShapeDtypeStruct((chunks, rows, width), jnp.float32),
        ]
        + [
            jax.ShapeDtypeStruct((2 * width, tok), dtype)
            for _ in range(back + 1)
            for dtype in (jnp.float32, jnp.bfloat16)
        ],
        in_specs=[smem] + [vmem] * (6 + 2 * back),
        out_specs=[vmem] * (ranks + 2 * back + 3),
        scratch_shapes=[
            pltpu.VMEM((tok, heads * width), jnp.bfloat16),
            pltpu.VMEM((span, width), jnp.bfloat16),
            pltpu.VMEM((span, 2 * width), jnp.bfloat16),
            pltpu.VMEM((tiles, rows, TILE), jnp.float32),
            pltpu.VMEM((rows, 2 * width), jnp.float32),
            pltpu.VMEM((rows, width), jnp.float32),
            pltpu.VMEM((rows, width), jnp.float32),
            pltpu.VMEM((tiles, 2 * width, tok), jnp.float32),
        ],
        compiler_params=pltpu.CompilerParams(vmem_limit_bytes=32 * 1024 * 1024),
        cost_estimate=pl.CostEstimate(
            flops=14 * tok * heads * width * span,
            bytes_accessed=4 * tok * heads * width * 2 + 4 * span * width * 2,
            transcendentals=tok * heads * span,
        ),
        name="attention",
    )(doc_lengths, *prepared, own, near, *arrived, *far)


def split_kernel(grad_ref, *part_refs):
    size = part_refs[0].shape[1]
    for k, ref in enumerate(part_refs):
        at = pl.multiple_of((lax.axis_index("head") ^ k) * size, size)
        ref[...] = grad_ref[:, pl.ds(at, size)]


def split(grad_attended, ranks):
    rows, columns = grad_attended.shape
    vmem = pl.BlockSpec(memory_space=pltpu.VMEM)
    part = jax.ShapeDtypeStruct((rows, columns // ranks), grad_attended.dtype)
    return pl.pallas_call(
        split_kernel,
        out_shape=[part] * ranks,
        in_specs=[vmem],
        out_specs=[vmem] * ranks,
        compiler_params=pltpu.CompilerParams(vmem_limit_bytes=SMALL_VMEM),
        name="split",
    )(grad_attended)


def arrange_kernel(q_ref, rows_ref, cols_ref, wide):
    small = unit(q_ref.shape[2])
    wide[...] = q_ref[...].astype(jnp.float32)
    for chunk in range(rows_ref.shape[0]):
        for j in range(q_ref.shape[1]):
            rows_ref[chunk, j * CHUNK : (j + 1) * CHUNK, :] = wide[
                chunk * CHUNK : (chunk + 1) * CHUNK, j, :
            ].astype(jnp.bfloat16)
        cols_ref[chunk] = dot_nt(small, rows_ref[chunk]).astype(jnp.bfloat16)


def arrange_grads_kernel(*refs):
    parts, (rows_ref, cols_ref, grads) = refs[:-3], refs[-3:]
    width = rows_ref.shape[2]
    small = unit(width)
    size = parts[0].shape[0]
    for k, ref in enumerate(parts):
        at = pl.multiple_of((lax.axis_index("head") ^ k) * size, size)
        grads[pl.ds(at, size), :] = ref[...]
    for chunk in range(rows_ref.shape[0]):
        for j in range(rows_ref.shape[1] // CHUNK):
            rows_ref[chunk, j * CHUNK : (j + 1) * CHUNK, :] = grads[
                chunk * CHUNK : (chunk + 1) * CHUNK, j * width : (j + 1) * width
            ]
        cols_ref[chunk] = dot_nt(small, rows_ref[chunk]).astype(jnp.bfloat16)


def arrange(kernel, arrays, shape, scratch):
    tok, heads, width = shape
    vmem = pl.BlockSpec(memory_space=pltpu.VMEM)
    chunks, rows = tok // CHUNK, heads * CHUNK
    return pl.pallas_call(
        kernel,
        out_shape=[
            jax.ShapeDtypeStruct((chunks, rows, width), jnp.bfloat16),
            jax.ShapeDtypeStruct((chunks, width, rows), jnp.bfloat16),
        ],
        in_specs=[vmem] * len(arrays),
        out_specs=[vmem, vmem],
        scratch_shapes=[scratch],
        compiler_params=pltpu.CompilerParams(vmem_limit_bytes=SMALL_VMEM),
        name="arrange",
    )(*arrays)


def join_kernel(*refs):
    parts, (rows_ref, out_ref, dq_ref, wide) = refs[:-4], refs[-4:]
    size = parts[0].shape[1]
    for k, ref in enumerate(parts):
        at = pl.multiple_of((lax.axis_index("head") ^ k) * size, size)
        out_ref[:, pl.ds(at, size)] = ref[...]
    scale = 1.0 / math.sqrt(rows_ref.shape[2])
    for chunk in range(rows_ref.shape[0]):
        for j in range(dq_ref.shape[1]):
            wide[chunk * CHUNK : (chunk + 1) * CHUNK, j, :] = (
                rows_ref[chunk, j * CHUNK : (j + 1) * CHUNK, :] * scale
            )
    dq_ref[...] = wide[...].astype(jnp.bfloat16)


def join(parts, dq_rows, shape):
    rows, size = parts[0].shape
    vmem = pl.BlockSpec(memory_space=pltpu.VMEM)
    return pl.pallas_call(
        join_kernel,
        out_shape=(
            jax.ShapeDtypeStruct((rows, size * len(parts)), parts[0].dtype),
            jax.ShapeDtypeStruct(shape, jnp.bfloat16),
        ),
        in_specs=[vmem] * (len(parts) + 1),
        out_specs=(vmem, vmem),
        scratch_shapes=[pltpu.VMEM(shape, jnp.float32)],
        compiler_params=pltpu.CompilerParams(vmem_limit_bytes=SMALL_VMEM),
        name="join",
    )(*parts, dq_rows)


def merge_kernel(*refs):
    total = refs[0][...]
    for ref in refs[1:-1]:
        total = total + ref[...].astype(jnp.float32)
    refs[-1][...] = total.astype(jnp.bfloat16)


def merge(*blocks):
    vmem = pl.BlockSpec(memory_space=pltpu.VMEM)
    return pl.pallas_call(
        merge_kernel,
        out_shape=jax.ShapeDtypeStruct(blocks[0].shape, jnp.bfloat16),
        in_specs=[vmem] * len(blocks),
        out_specs=vmem,
        compiler_params=pltpu.CompilerParams(vmem_limit_bytes=SMALL_VMEM),
        name="merge",
    )(*blocks)


def finish_kernel(own_ref, *refs):
    arrived = refs[:-2]
    dk_ref, dv_ref = refs[-2:]
    total = own_ref[...]
    for ref in arrived:
        total = total + ref[...].astype(jnp.float32)
    total = total.astype(jnp.bfloat16)
    width = dk_ref.shape[1]
    large = unit(dk_ref.shape[0])
    dk_ref[...] = dot_nt(large, total[:width]).astype(jnp.bfloat16)
    dv_ref[...] = dot_nt(large, total[width:]).astype(jnp.bfloat16)


def finish(own_part, arrived):
    both, tok = own_part.shape
    vmem = pl.BlockSpec(memory_space=pltpu.VMEM)
    shape = jax.ShapeDtypeStruct((tok, both // 2), jnp.bfloat16)
    return pl.pallas_call(
        finish_kernel,
        out_shape=(shape, shape),
        in_specs=[vmem] * (1 + len(arrived)),
        out_specs=(vmem, vmem),
        compiler_params=pltpu.CompilerParams(vmem_limit_bytes=SMALL_VMEM),
        name="finish",
    )(own_part, *arrived)


def shifted(block, by, count):
    pairs = [(i, i + by) for i in range(count) if 0 <= i + by < count]
    return lax.ppermute(block, "ctx", pairs)


def exchanged(block, axis, by):
    return lax.ppermute(block, axis, [(i, i ^ by) for i in range(lax.axis_size(axis))])


def after(value, *others):
    return lax.optimization_barrier((value, *others))


def body(queries, key_states, value_states, doc_lengths, grad_attended):
    tok, heads, width = queries.shape
    count = lax.axis_size("ctx")
    ranks = lax.axis_size("head")
    reach = min((DOC_MOST + tok - 2) // tok, count - 1)
    back = min((reach + 1) // 2, count // 2 - 1)
    whole = count == 8 and back == 3 and ranks == 4
    own = jnp.concatenate(
        [key_states.reshape(tok, width), value_states.reshape(tok, width)], axis=0
    )
    near = exchanged(own, "ctx", 1)
    if whole:
        beside = exchanged(own, "ctx", 2)
        across = exchanged(own, "ctx", 4)
    else:
        arrived = [shifted(own, 2 * k, count) for k in range(1, back + 1)]
    grads = split(grad_attended, ranks)
    grads = [part if k == 0 else exchanged(part, "head", k) for k, part in enumerate(grads)]
    prepared = arrange(
        arrange_kernel, [queries], queries.shape, pltpu.VMEM(queries.shape, jnp.float32)
    )
    if whole:
        beside, near = after(beside, near)
        far_beside = exchanged(beside, "ctx", 1)
        across, grads[1], *prepared = after(across, grads[1], *prepared)
        passed = exchanged(across, "ctx", 2)
        across, far_beside, grads[2] = after(across, far_beside, grads[2])
        far_across = exchanged(across, "ctx", 1)
    prepared = [*prepared, *arrange(
        arrange_grads_kernel,
        grads,
        queries.shape,
        pltpu.VMEM((tok, heads * width), jnp.bfloat16),
    )]
    if whole:
        passed, *prepared = after(passed, *prepared)
        far_passed = exchanged(passed, "ctx", 1)
        arrived = [beside, across, passed]
        far = [far_beside, far_across, far_passed]
    else:
        far = [exchanged(block, "ctx", 1) for block in arrived]
    outputs = attend(doc_lengths, prepared, own, near, arrived, far, ranks, whole)
    outs, dq_rows, parts = list(outputs[:ranks]), outputs[ranks], outputs[ranks + 1 :]
    mine, other = list(parts[0::2]), list(parts[1::2])
    outs = [part if k == 0 else exchanged(part, "head", k) for k, part in enumerate(outs)]
    for k in range(back, -1, -1):
        if k == 0:
            other[0], other[1] = after(other[0], other[1])
        other[k] = exchanged(other[k], "ctx", 1)
    other[back], *outs[1:3] = after(other[back], *outs[1:3])
    returned = []
    for k in range(back, 0, -1):
        if k == 1:
            other[1], returned[0] = after(other[1], returned[0])
        returned.append(shifted(merge(mine[k], other[k]), -2 * k, count))
    grad_keys, grad_values = finish(mine[0], [other[0]] + returned)
    attended, grad_queries = join(outs, dq_rows, queries.shape)
    grad_keys = grad_keys.reshape(tok, 1, width)
    grad_values = grad_values.reshape(tok, 1, width)
    return attended, grad_queries, grad_keys, grad_values


def solution(mesh):
    in_specs = (
        P("ctx", "head", None),
        P("ctx", "head", None),
        P("ctx", "head", None),
        P(),
        P(("ctx", "head"), None),
    )
    out_specs = (
        P(("ctx", "head"), None),
        P("ctx", "head", None),
        P("ctx", "head", None),
        P("ctx", "head", None),
    )
    return jax.shard_map(body, mesh=mesh, in_specs=in_specs, out_specs=out_specs, check_vma=False)
```

```python
import functools
import math

import jax
import jax.numpy as jnp
from jax import lax
from jax.experimental import pallas as pl
from jax.experimental.pallas import tpu as pltpu
from jax.sharding import PartitionSpec as P

DOC_MOST = 1792
NEG_FILL = -1e30
TILE = 256
CHUNK = 128
LOG2_E = 1.4426950408889634
SMALL_VMEM = 8 * 1024 * 1024


def dot(a, b):
    return jnp.dot(a, b, preferred_element_type=jnp.float32)


def dot_nt(a, b):
    return lax.dot_general(a, b, (((1,), (1,)), ((), ())), preferred_element_type=jnp.float32)


def unit(size):
    rows = lax.broadcasted_iota(jnp.int32, (size, size), 0)
    return (rows == lax.broadcasted_iota(jnp.int32, (size, size), 1)).astype(jnp.bfloat16)


def twice(column):
    return jnp.concatenate([column, column], axis=1)


def attention_kernel(
    doc_ref,
    q_rows,
    q_cols,
    do_rows,
    do_cols,
    own_ref,
    near_ref,
    *refs,
    back,
    whole,
    ranks,
    heads,
    width,
    scale,
):
    arrived, far, refs = refs[:back], refs[back : 2 * back], refs[2 * back :]
    out_parts, dq_acc, refs = refs[:ranks], refs[ranks], refs[ranks + 1 :]
    d_refs, refs = refs[: 2 * back + 2], refs[2 * back + 2 :]
    (o_ref, keys, values, scores, accum, top, delta, d_blocks) = refs
    tok = own_ref.shape[0] // 2
    part_rows = tok // ranks
    docs = doc_ref.shape[0]
    ctx = lax.axis_index("ctx")
    rank = lax.axis_index("head")
    parity = lax.rem(ctx, 2)
    base = 0 if whole else (ctx - parity - 2 * back) * tok
    own = ctx if whole else 2 * back + parity
    ones = jnp.ones((width, width), jnp.bfloat16)

    def pair_of(k):
        return (ctx // 2) ^ k if whole else back - k

    values[:, width:] = jnp.ones_like(values[:, width:])
    for k in range(back + 1):
        pair = pair_of(k)
        mine, other = (own_ref, near_ref) if k == 0 else (arrived[k - 1], far[k - 1])
        for ref, place in ((mine, 2 * pair + parity), (other, 2 * pair + 1 - parity)):
            at = pl.ds(pl.multiple_of(place * tok, tok), tok)
            keys[at, :] = ref[0:tok, :]
            values[at, 0:width] = ref[tok:, :]
    d_blocks[...] = jnp.zeros_like(d_blocks)

    def chunk_step(chunk, carry):
        here = pl.ds(pl.multiple_of(chunk * CHUNK, CHUNK), CHUNK)
        top[...] = jnp.full_like(top, NEG_FILL)

        t_first = base + own * TILE + chunk * CHUNK
        t_last = t_first + CHUNK - 1
        t_col = t_first + lax.broadcasted_iota(jnp.int32, (CHUNK, width), 0)
        end = jnp.int32(0)
        start_first, start_last = jnp.int32(0), jnp.int32(0)
        start_col = jnp.zeros((CHUNK, width), jnp.int32)
        for i in range(docs):
            end = end + doc_ref[i]
            start_first = jnp.where(end <= t_first, end, start_first)
            start_last = jnp.where(end <= t_last, end, start_last)
            start_col = jnp.where(t_col >= end, end, start_col)
        low = jnp.maximum(start_first - base, 0) // TILE
        clear = jnp.clip((start_last - base + TILE - 1) // TILE, low, own)

        def score_tile(i, masked):
            at = pl.ds(pl.multiple_of(i * TILE, TILE), TILE)
            tile = dot_nt(q_rows[chunk], keys[at, :]) * (scale * LOG2_E)
            if masked:
                s_row = base + i * TILE + lax.broadcasted_iota(jnp.int32, (CHUNK, TILE), 1)
                live = (s_row >= twice(start_col)) & (s_row <= twice(t_col))
                tile = jnp.concatenate(
                    [
                        jnp.where(live, tile[j * CHUNK : (j + 1) * CHUNK], NEG_FILL)
                        for j in range(heads)
                    ],
                    axis=0,
                )
            scores[i] = tile
            top[...] = jnp.maximum(top[...], jnp.maximum(tile[:, :width], tile[:, width:]))

        def edge_step(n, carry):
            score_tile(jnp.where(n < clear - low, low + n, own), True)
            return carry

        def inner_step(i, carry):
            score_tile(i, False)
            return carry

        lax.fori_loop(0, clear - low + 1, edge_step, 0)
        lax.fori_loop(clear, own, inner_step, 0)
        top[...] = jnp.broadcast_to(jnp.max(top[...], axis=1, keepdims=True), top.shape)
        accum[...] = jnp.zeros_like(accum)

        def weigh_step(i, carry):
            at = pl.ds(pl.multiple_of(i * TILE, TILE), TILE)
            weights = jnp.exp2(scores[i] - twice(top[...])).astype(jnp.bfloat16)
            accum[...] += dot(weights, values[at, :])
            return carry

        lax.fori_loop(low, own + 1, weigh_step, 0)
        total = accum[:, width:]
        out = (accum[:, 0:width] / total).astype(jnp.bfloat16)
        for j in range(heads):
            o_ref[here, j * width : (j + 1) * width] = out[j * CHUNK : (j + 1) * CHUNK]
        top[...] = top[...] + jnp.log2(total)
        product = do_rows[chunk].astype(jnp.float32) * out.astype(jnp.float32)
        coarse = product.astype(jnp.bfloat16)
        fine = (product - coarse.astype(jnp.float32)).astype(jnp.bfloat16)
        delta[...] = dot(coarse, ones) + dot(fine, ones)
        dq_acc[chunk] = jnp.zeros(dq_acc.shape[1:], jnp.float32)

        def back_step(i, carry):
            at = pl.ds(pl.multiple_of(i * TILE, TILE), TILE)
            probs = jnp.exp2(scores[i] - twice(top[...]))
            d_probs = dot_nt(do_rows[chunk], values[at, 0:width])
            d_scores = (probs * (d_probs - twice(delta[...]))).astype(jnp.bfloat16)
            dq_acc[chunk] += dot(d_scores, keys[at, :])
            d_blocks[i, 0:width, :] += dot(q_cols[chunk], d_scores)
            d_blocks[i, width:, :] += dot(do_cols[chunk], probs.astype(jnp.bfloat16))
            return carry

        lax.fori_loop(low, own + 1, back_step, 0)
        return carry

    lax.fori_loop(0, tok // CHUNK, chunk_step, 0)
    for k in range(ranks):
        at = pl.ds(pl.multiple_of((rank ^ k) * part_rows, part_rows), part_rows)
        out_parts[k][...] = o_ref[at, :]
    for k in range(back + 1):
        pair = jnp.maximum(ctx // 2 - k, 0) if whole else back - k
        mine, other = 2 * pair + parity, 2 * pair + 1 - parity
        mine_ref, other_ref = d_refs[2 * k], d_refs[2 * k + 1]
        mine_ref[0:width, :] = d_blocks[mine, 0:width, :] * scale
        mine_ref[width:, :] = d_blocks[mine, width:, :]
        other_ref[0:width, :] = (d_blocks[other, 0:width, :] * scale).astype(jnp.bfloat16)
        other_ref[width:, :] = d_blocks[other, width:, :].astype(jnp.bfloat16)


def attend(doc_lengths, prepared, own, near, arrived, far, ranks, whole):
    chunks, rows, width = prepared[0].shape
    tok = chunks * CHUNK
    heads = rows // CHUNK
    back = len(arrived)
    tiles = 2 * (back + 1)
    span = tiles * tok
    vmem = pl.BlockSpec(memory_space=pltpu.VMEM)
    smem = pl.BlockSpec(memory_space=pltpu.SMEM)
    out_part = jax.ShapeDtypeStruct((tok // ranks, heads * width), jnp.bfloat16)
    return pl.pallas_call(
        functools.partial(
            attention_kernel,
            back=back,
            whole=whole,
            ranks=ranks,
            heads=heads,
            width=width,
            scale=1.0 / math.sqrt(width),
        ),
        out_shape=[out_part] * ranks
        + [
            jax.ShapeDtypeStruct((chunks, rows, width), jnp.float32),
        ]
        + [
            jax.ShapeDtypeStruct((2 * width, tok), dtype)
            for _ in range(back + 1)
            for dtype in (jnp.float32, jnp.bfloat16)
        ],
        in_specs=[smem] + [vmem] * (6 + 2 * back),
        out_specs=[vmem] * (ranks + 2 * back + 3),
        scratch_shapes=[
            pltpu.VMEM((tok, heads * width), jnp.bfloat16),
            pltpu.VMEM((span, width), jnp.bfloat16),
            pltpu.VMEM((span, 2 * width), jnp.bfloat16),
            pltpu.VMEM((tiles, rows, TILE), jnp.float32),
            pltpu.VMEM((rows, 2 * width), jnp.float32),
            pltpu.VMEM((rows, width), jnp.float32),
            pltpu.VMEM((rows, width), jnp.float32),
            pltpu.VMEM((tiles, 2 * width, tok), jnp.float32),
        ],
        compiler_params=pltpu.CompilerParams(vmem_limit_bytes=32 * 1024 * 1024),
        cost_estimate=pl.CostEstimate(
            flops=14 * tok * heads * width * span,
            bytes_accessed=4 * tok * heads * width * 2 + 4 * span * width * 2,
            transcendentals=tok * heads * span,
        ),
        name="attention",
    )(doc_lengths, *prepared, own, near, *arrived, *far)


def split_kernel(grad_ref, *part_refs):
    size = part_refs[0].shape[1]
    for k, ref in enumerate(part_refs):
        at = pl.multiple_of((lax.axis_index("head") ^ k) * size, size)
        ref[...] = grad_ref[:, pl.ds(at, size)]


def split(grad_attended, ranks):
    rows, columns = grad_attended.shape
    vmem = pl.BlockSpec(memory_space=pltpu.VMEM)
    part = jax.ShapeDtypeStruct((rows, columns // ranks), grad_attended.dtype)
    return pl.pallas_call(
        split_kernel,
        out_shape=[part] * ranks,
        in_specs=[vmem],
        out_specs=[vmem] * ranks,
        compiler_params=pltpu.CompilerParams(vmem_limit_bytes=SMALL_VMEM),
        name="split",
    )(grad_attended)


def arrange_kernel(q_ref, rows_ref, cols_ref, wide):
    small = unit(q_ref.shape[2])
    wide[...] = q_ref[...].astype(jnp.float32)
    for chunk in range(rows_ref.shape[0]):
        for j in range(q_ref.shape[1]):
            rows_ref[chunk, j * CHUNK : (j + 1) * CHUNK, :] = wide[
                chunk * CHUNK : (chunk + 1) * CHUNK, j, :
            ].astype(jnp.bfloat16)
        cols_ref[chunk] = dot_nt(small, rows_ref[chunk]).astype(jnp.bfloat16)


def arrange_grads_kernel(*refs):
    parts, (rows_ref, cols_ref, grads) = refs[:-3], refs[-3:]
    width = rows_ref.shape[2]
    small = unit(width)
    size = parts[0].shape[0]
    for k, ref in enumerate(parts):
        at = pl.multiple_of((lax.axis_index("head") ^ k) * size, size)
        grads[pl.ds(at, size), :] = ref[...]
    for chunk in range(rows_ref.shape[0]):
        for j in range(rows_ref.shape[1] // CHUNK):
            rows_ref[chunk, j * CHUNK : (j + 1) * CHUNK, :] = grads[
                chunk * CHUNK : (chunk + 1) * CHUNK, j * width : (j + 1) * width
            ]
        cols_ref[chunk] = dot_nt(small, rows_ref[chunk]).astype(jnp.bfloat16)


def arrange(kernel, arrays, shape, scratch):
    tok, heads, width = shape
    vmem = pl.BlockSpec(memory_space=pltpu.VMEM)
    chunks, rows = tok // CHUNK, heads * CHUNK
    return pl.pallas_call(
        kernel,
        out_shape=[
            jax.ShapeDtypeStruct((chunks, rows, width), jnp.bfloat16),
            jax.ShapeDtypeStruct((chunks, width, rows), jnp.bfloat16),
        ],
        in_specs=[vmem] * len(arrays),
        out_specs=[vmem, vmem],
        scratch_shapes=[scratch],
        compiler_params=pltpu.CompilerParams(vmem_limit_bytes=SMALL_VMEM),
        name="arrange",
    )(*arrays)


def join_kernel(*refs):
    parts, (rows_ref, out_ref, dq_ref, wide) = refs[:-4], refs[-4:]
    size = parts[0].shape[1]
    for k, ref in enumerate(parts):
        at = pl.multiple_of((lax.axis_index("head") ^ k) * size, size)
        out_ref[:, pl.ds(at, size)] = ref[...]
    scale = 1.0 / math.sqrt(rows_ref.shape[2])
    for chunk in range(rows_ref.shape[0]):
        for j in range(dq_ref.shape[1]):
            wide[chunk * CHUNK : (chunk + 1) * CHUNK, j, :] = (
                rows_ref[chunk, j * CHUNK : (j + 1) * CHUNK, :] * scale
            )
    dq_ref[...] = wide[...].astype(jnp.bfloat16)


def join(parts, dq_rows, shape):
    rows, size = parts[0].shape
    vmem = pl.BlockSpec(memory_space=pltpu.VMEM)
    return pl.pallas_call(
        join_kernel,
        out_shape=(
            jax.ShapeDtypeStruct((rows, size * len(parts)), parts[0].dtype),
            jax.ShapeDtypeStruct(shape, jnp.bfloat16),
        ),
        in_specs=[vmem] * (len(parts) + 1),
        out_specs=(vmem, vmem),
        scratch_shapes=[pltpu.VMEM(shape, jnp.float32)],
        compiler_params=pltpu.CompilerParams(vmem_limit_bytes=SMALL_VMEM),
        name="join",
    )(*parts, dq_rows)


def merge_kernel(*refs):
    total = refs[0][...]
    for ref in refs[1:-1]:
        total = total + ref[...].astype(jnp.float32)
    refs[-1][...] = total.astype(jnp.bfloat16)


def merge(*blocks):
    vmem = pl.BlockSpec(memory_space=pltpu.VMEM)
    return pl.pallas_call(
        merge_kernel,
        out_shape=jax.ShapeDtypeStruct(blocks[0].shape, jnp.bfloat16),
        in_specs=[vmem] * len(blocks),
        out_specs=vmem,
        compiler_params=pltpu.CompilerParams(vmem_limit_bytes=SMALL_VMEM),
        name="merge",
    )(*blocks)


def finish_kernel(own_ref, *refs):
    arrived = refs[:-2]
    dk_ref, dv_ref = refs[-2:]
    total = own_ref[...]
    for ref in arrived:
        total = total + ref[...].astype(jnp.float32)
    total = total.astype(jnp.bfloat16)
    width = dk_ref.shape[1]
    large = unit(dk_ref.shape[0])
    dk_ref[...] = dot_nt(large, total[:width]).astype(jnp.bfloat16)
    dv_ref[...] = dot_nt(large, total[width:]).astype(jnp.bfloat16)


def finish(own_part, arrived):
    both, tok = own_part.shape
    vmem = pl.BlockSpec(memory_space=pltpu.VMEM)
    shape = jax.ShapeDtypeStruct((tok, both // 2), jnp.bfloat16)
    return pl.pallas_call(
        finish_kernel,
        out_shape=(shape, shape),
        in_specs=[vmem] * (1 + len(arrived)),
        out_specs=(vmem, vmem),
        compiler_params=pltpu.CompilerParams(vmem_limit_bytes=SMALL_VMEM),
        name="finish",
    )(own_part, *arrived)


def shifted(block, by, count):
    pairs = [(i, i + by) for i in range(count) if 0 <= i + by < count]
    return lax.ppermute(block, "ctx", pairs)


def exchanged(block, axis, by):
    return lax.ppermute(block, axis, [(i, i ^ by) for i in range(lax.axis_size(axis))])


def after(value, *others):
    return lax.optimization_barrier((value, *others))


def body(queries, key_states, value_states, doc_lengths, grad_attended):
    tok, heads, width = queries.shape
    count = lax.axis_size("ctx")
    ranks = lax.axis_size("head")
    reach = min((DOC_MOST + tok - 2) // tok, count - 1)
    back = min((reach + 1) // 2, count // 2 - 1)
    whole = count == 8 and back == 3 and ranks == 4
    own = jnp.concatenate(
        [key_states.reshape(tok, width), value_states.reshape(tok, width)], axis=0
    )
    near = exchanged(own, "ctx", 1)
    if whole:
        beside = exchanged(own, "ctx", 2)
        across = exchanged(own, "ctx", 4)
    else:
        arrived = [shifted(own, 2 * k, count) for k in range(1, back + 1)]
    grads = split(grad_attended, ranks)
    grads = [part if k == 0 else exchanged(part, "head", k) for k, part in enumerate(grads)]
    prepared = arrange(
        arrange_kernel, [queries], queries.shape, pltpu.VMEM(queries.shape, jnp.float32)
    )
    if whole:
        beside, near = after(beside, near)
        far_beside = exchanged(beside, "ctx", 1)
        across, grads[1], *prepared = after(across, grads[1], *prepared)
        passed = exchanged(across, "ctx", 2)
        far_across = exchanged(across, "ctx", 1)
    prepared = [*prepared, *arrange(
        arrange_grads_kernel,
        grads,
        queries.shape,
        pltpu.VMEM((tok, heads * width), jnp.bfloat16),
    )]
    if whole:
        passed, far_beside, *prepared = after(passed, far_beside, *prepared)
        far_passed = exchanged(passed, "ctx", 1)
        arrived = [beside, across, passed]
        far = [far_beside, far_across, far_passed]
    else:
        far = [exchanged(block, "ctx", 1) for block in arrived]
    outputs = attend(doc_lengths, prepared, own, near, arrived, far, ranks, whole)
    outs, dq_rows, parts = list(outputs[:ranks]), outputs[ranks], outputs[ranks + 1 :]
    mine, other = list(parts[0::2]), list(parts[1::2])
    outs = [part if k == 0 else exchanged(part, "head", k) for k, part in enumerate(outs)]
    for k in range(back, 1, -1):
        other[k] = exchanged(other[k], "ctx", 1)
    other[back], *outs[1:2] = after(other[back], *outs[1:2])
    returned = []
    for k in range(back, 0, -1):
        if k == back - 1:
            other[k], *outs[2:3] = after(other[k], *outs[2:3])
        block = merge(mine[k], other[k])
        if k == back:
            block, other[1] = after(block, other[1])
            other[1] = exchanged(other[1], "ctx", 1)
            other[0], other[1] = after(other[0], other[1])
            other[0] = exchanged(other[0], "ctx", 1)
        returned.append(shifted(block, -2 * k, count))
    grad_keys, grad_values = finish(mine[0], [other[0]] + returned)
    attended, grad_queries = join(outs, dq_rows, queries.shape)
    grad_keys = grad_keys.reshape(tok, 1, width)
    grad_values = grad_values.reshape(tok, 1, width)
    return attended, grad_queries, grad_keys, grad_values


def solution(mesh):
    in_specs = (
        P("ctx", "head", None),
        P("ctx", "head", None),
        P("ctx", "head", None),
        P(),
        P(("ctx", "head"), None),
    )
    out_specs = (
        P(("ctx", "head"), None),
        P("ctx", "head", None),
        P("ctx", "head", None),
        P("ctx", "head", None),
    )
    return jax.shard_map(body, mesh=mesh, in_specs=in_specs, out_specs=out_specs, check_vma=False)
```

```python
import functools
import math

import jax
import jax.numpy as jnp
from jax import lax
from jax.experimental import pallas as pl
from jax.experimental.pallas import tpu as pltpu
from jax.sharding import PartitionSpec as P

DOC_MOST = 1792
NEG_FILL = -1e30
TILE = 256
CHUNK = 128
LOG2_E = 1.4426950408889634
SMALL_VMEM = 8 * 1024 * 1024
KERNEL_VMEM = 16 * 1024 * 1024


def dot(a, b):
    return jnp.dot(a, b, preferred_element_type=jnp.float32)


def dot_nt(a, b):
    return lax.dot_general(a, b, (((1,), (1,)), ((), ())), preferred_element_type=jnp.float32)


def unit(size):
    rows = lax.broadcasted_iota(jnp.int32, (size, size), 0)
    return (rows == lax.broadcasted_iota(jnp.int32, (size, size), 1)).astype(jnp.bfloat16)


def twice(column):
    return jnp.concatenate([column, column], axis=1)


def starts_in(doc_ref, positions):
    end, found = jnp.int32(0), jnp.zeros_like(positions)
    for i in range(doc_ref.shape[0]):
        end = end + doc_ref[i]
        found = jnp.where(positions >= end, end, found)
    return found


def here(tok, back, whole):
    ctx = lax.axis_index("ctx")
    parity = lax.rem(ctx, 2)
    last = ctx // 2 if whole else back
    base = 0 if whole else (ctx - parity - 2 * back) * tok
    return parity, last, base, 2 * last + parity


def back_tile(i, slot, chunk, width, refs):
    q_cols, do_rows, do_cols, keys, values, scores, top, delta, dq_acc, d_blocks = refs
    at = pl.ds(pl.multiple_of(i * TILE, TILE), TILE)
    probs = jnp.exp2(scores[chunk, i] - twice(top[chunk]))
    d_probs = dot_nt(do_rows[chunk], values[at, 0:width])
    d_scores = (probs * (d_probs - twice(delta[chunk]))).astype(jnp.bfloat16)
    dq_acc[chunk] += dot(d_scores, keys[at, :])
    d_blocks[slot, 0:width, :] += dot(q_cols[chunk], d_scores)
    d_blocks[slot, width:, :] += dot(do_cols[chunk], probs.astype(jnp.bfloat16))


def put(d_blocks, mine, other, mine_ref, other_ref, width, scale):
    mine_ref[0:width, :] = d_blocks[mine, 0:width, :] * scale
    mine_ref[width:, :] = d_blocks[mine, width:, :]
    other_ref[0:width, :] = (d_blocks[other, 0:width, :] * scale).astype(jnp.bfloat16)
    other_ref[width:, :] = d_blocks[other, width:, :].astype(jnp.bfloat16)


def attention_kernel(
    doc_ref,
    q_rows,
    q_cols,
    do_rows,
    do_cols,
    own_ref,
    near_ref,
    *refs,
    back,
    whole,
    ranks,
    heads,
    width,
    scale,
):
    arrived, far, refs = refs[:back], refs[back : 2 * back], refs[2 * back :]
    out_parts, refs = refs[:ranks], refs[ranks:]
    (scores, top, delta, keys, values, dq_acc), refs = refs[:6], refs[6:]
    d_refs, (o_ref, accum, d_blocks) = refs[:-3], refs[-3:]
    tok = own_ref.shape[0] // 2
    part_rows = tok // ranks
    rank = lax.axis_index("head")
    parity, last, base, own = here(tok, back, whole)
    cut = 2 * (last - 1)
    ones = jnp.ones((width, width), jnp.bfloat16)

    values[:, width:] = jnp.ones_like(values[:, width:])
    for k in range(back + 1):
        pair = last ^ k if whole else last - k
        mine, other = (own_ref, near_ref) if k == 0 else (arrived[k - 1], far[k - 1])
        for ref, place in ((mine, 2 * pair + parity), (other, 2 * pair + 1 - parity)):
            at = pl.ds(pl.multiple_of(place * tok, tok), tok)
            keys[at, :] = ref[0:tok, :]
            values[at, 0:width] = ref[tok:, :]
    d_blocks[...] = jnp.zeros_like(d_blocks)
    top[...] = jnp.full_like(top, NEG_FILL)
    dq_acc[...] = jnp.zeros_like(dq_acc)

    def chunk_step(chunk, carry):
        rows_at = pl.ds(pl.multiple_of(chunk * CHUNK, CHUNK), CHUNK)
        t_first = base + own * TILE + chunk * CHUNK
        t_last = t_first + CHUNK - 1
        t_col = t_first + lax.broadcasted_iota(jnp.int32, (CHUNK, width), 0)
        start_col = starts_in(doc_ref, t_col)
        low = jnp.maximum(starts_in(doc_ref, t_first) - base, 0) // TILE
        clear = jnp.clip((starts_in(doc_ref, t_last) - base + TILE - 1) // TILE, low, own)

        def score_tile(i, masked):
            at = pl.ds(pl.multiple_of(i * TILE, TILE), TILE)
            tile = dot_nt(q_rows[chunk], keys[at, :]) * (scale * LOG2_E)
            if masked:
                s_row = base + i * TILE + lax.broadcasted_iota(jnp.int32, (CHUNK, TILE), 1)
                live = (s_row >= twice(start_col)) & (s_row <= twice(t_col))
                tile = jnp.concatenate(
                    [
                        jnp.where(live, tile[j * CHUNK : (j + 1) * CHUNK], NEG_FILL)
                        for j in range(heads)
                    ],
                    axis=0,
                )
            scores[chunk, i] = tile
            top[chunk] = jnp.maximum(top[chunk], jnp.maximum(tile[:, :width], tile[:, width:]))

        def edge_step(n, carry):
            score_tile(jnp.where(n < clear - low, low + n, own), True)
            return carry

        def inner_step(i, carry):
            score_tile(i, False)
            return carry

        lax.fori_loop(0, clear - low + 1, edge_step, 0)
        lax.fori_loop(clear, own, inner_step, 0)
        top[chunk] = jnp.broadcast_to(jnp.max(top[chunk], axis=1, keepdims=True), top.shape[1:])
        accum[...] = jnp.zeros_like(accum)

        def weigh_step(i, carry):
            at = pl.ds(pl.multiple_of(i * TILE, TILE), TILE)
            weights = jnp.exp2(scores[chunk, i] - twice(top[chunk])).astype(jnp.bfloat16)
            accum[...] += dot(weights, values[at, :])
            return carry

        lax.fori_loop(low, own + 1, weigh_step, 0)
        total = accum[:, width:]
        out = (accum[:, 0:width] / total).astype(jnp.bfloat16)
        for j in range(heads):
            o_ref[rows_at, j * width : (j + 1) * width] = out[j * CHUNK : (j + 1) * CHUNK]
        top[chunk] = top[chunk] + jnp.log2(total)
        product = do_rows[chunk].astype(jnp.float32) * out.astype(jnp.float32)
        coarse = product.astype(jnp.bfloat16)
        fine = (product - coarse.astype(jnp.float32)).astype(jnp.bfloat16)
        delta[chunk] = dot(coarse, ones) + dot(fine, ones)

        def back_step(i, carry):
            refs = (
                q_cols, do_rows, do_cols, keys, values, scores, top, delta, dq_acc, d_blocks
            )
            back_tile(i, i, chunk, width, refs)
            return carry

        lax.fori_loop(low, cut, back_step, 0)
        return carry

    lax.fori_loop(0, tok // CHUNK, chunk_step, 0)
    for k in range(ranks):
        at = pl.ds(pl.multiple_of((rank ^ k) * part_rows, part_rows), part_rows)
        out_parts[k][...] = o_ref[at, :]
    for k in range(2, back + 1):
        pair = jnp.maximum(last - k, 0)
        mine, other = 2 * pair + parity, 2 * pair + 1 - parity
        put(d_blocks, mine, other, d_refs[2 * k - 4], d_refs[2 * k - 3], width, scale)


def attend(doc_lengths, prepared, own, near, arrived, far, ranks, whole):
    chunks, rows, width = prepared[0].shape
    tok = chunks * CHUNK
    heads = rows // CHUNK
    back = len(arrived)
    tiles = 2 * (back + 1)
    span = tiles * tok
    vmem = pl.BlockSpec(memory_space=pltpu.VMEM)
    smem = pl.BlockSpec(memory_space=pltpu.SMEM)
    out_part = jax.ShapeDtypeStruct((tok // ranks, heads * width), jnp.bfloat16)
    row_state = jax.ShapeDtypeStruct((chunks, rows, width), jnp.float32)
    outputs = pl.pallas_call(
        functools.partial(
            attention_kernel,
            back=back,
            whole=whole,
            ranks=ranks,
            heads=heads,
            width=width,
            scale=1.0 / math.sqrt(width),
        ),
        out_shape=[out_part] * ranks
        + [
            jax.ShapeDtypeStruct((chunks, tiles, rows, TILE), jnp.float32),
            row_state,
            row_state,
            jax.ShapeDtypeStruct((span, width), jnp.bfloat16),
            jax.ShapeDtypeStruct((span, 2 * width), jnp.bfloat16),
            row_state,
        ]
        + [
            jax.ShapeDtypeStruct((2 * width, tok), dtype)
            for _ in range(back - 1)
            for dtype in (jnp.float32, jnp.bfloat16)
        ],
        in_specs=[smem] + [vmem] * (6 + 2 * back),
        out_specs=[vmem] * (ranks + 4 + 2 * back),
        scratch_shapes=[
            pltpu.VMEM((tok, heads * width), jnp.bfloat16),
            pltpu.VMEM((rows, 2 * width), jnp.float32),
            pltpu.VMEM((tiles, 2 * width, tok), jnp.float32),
        ],
        compiler_params=pltpu.CompilerParams(vmem_limit_bytes=KERNEL_VMEM),
        cost_estimate=pl.CostEstimate(
            flops=14 * tok * heads * width * span,
            bytes_accessed=4 * tok * heads * width * 2 + 4 * span * width * 2,
            transcendentals=tok * heads * span,
        ),
        name="attention",
    )(doc_lengths, *prepared, own, near, *arrived, *far)
    return outputs[:ranks], outputs[ranks : ranks + 6], outputs[ranks + 6 :]


def near_kernel(
    doc_ref,
    q_cols,
    do_rows,
    do_cols,
    scores,
    top,
    delta,
    keys,
    values,
    dq_far,
    dq_acc,
    mine1_ref,
    other1_ref,
    mine0_ref,
    other0_ref,
    d_blocks,
    *,
    back,
    whole,
    width,
    scale,
):
    tok = mine1_ref.shape[1]
    parity, last, base, own = here(tok, back, whole)
    cut = 2 * (last - 1)
    d_blocks[...] = jnp.zeros_like(d_blocks)
    dq_acc[...] = dq_far[...]

    def chunk_step(chunk, carry):
        t_first = base + own * TILE + chunk * CHUNK
        low = jnp.maximum(starts_in(doc_ref, t_first) - base, 0) // TILE

        def back_step(i, carry):
            refs = (
                q_cols, do_rows, do_cols, keys, values, scores, top, delta, dq_acc, d_blocks
            )
            back_tile(i, i - cut, chunk, width, refs)
            return carry

        lax.fori_loop(jnp.maximum(low, cut), own + 1, back_step, 0)
        return carry

    lax.fori_loop(0, tok // CHUNK, chunk_step, 0)
    put(d_blocks, parity, 1 - parity, mine1_ref, other1_ref, width, scale)
    put(d_blocks, 2 + parity, 3 - parity, mine0_ref, other0_ref, width, scale)


def attend_near(doc_lengths, prepared, state, back, whole):
    _, q_cols, do_rows, do_cols = prepared
    chunks, rows, width = do_rows.shape
    tok = chunks * CHUNK
    vmem = pl.BlockSpec(memory_space=pltpu.VMEM)
    smem = pl.BlockSpec(memory_space=pltpu.SMEM)
    return pl.pallas_call(
        functools.partial(
            near_kernel, back=back, whole=whole, width=width, scale=1.0 / math.sqrt(width)
        ),
        out_shape=[jax.ShapeDtypeStruct((chunks, rows, width), jnp.float32)]
        + [
            jax.ShapeDtypeStruct((2 * width, tok), dtype)
            for _ in range(2)
            for dtype in (jnp.float32, jnp.bfloat16)
        ],
        in_specs=[smem] + [vmem] * 9,
        out_specs=[vmem] * 5,
        scratch_shapes=[pltpu.VMEM((4, 2 * width, tok), jnp.float32)],
        compiler_params=pltpu.CompilerParams(vmem_limit_bytes=KERNEL_VMEM),
        cost_estimate=pl.CostEstimate(
            flops=8 * chunks * rows * width * 4 * tok,
            bytes_accessed=4 * chunks * rows * width * 2,
            transcendentals=4 * chunks * rows * tok,
        ),
        name="near",
    )(doc_lengths, q_cols, do_rows, do_cols, *state)


def split_kernel(grad_ref, *part_refs):
    size = part_refs[0].shape[1]
    for k, ref in enumerate(part_refs):
        at = pl.multiple_of((lax.axis_index("head") ^ k) * size, size)
        ref[...] = grad_ref[:, pl.ds(at, size)]


def split(grad_attended, ranks):
    rows, columns = grad_attended.shape
    vmem = pl.BlockSpec(memory_space=pltpu.VMEM)
    part = jax.ShapeDtypeStruct((rows, columns // ranks), grad_attended.dtype)
    return pl.pallas_call(
        split_kernel,
        out_shape=[part] * ranks,
        in_specs=[vmem],
        out_specs=[vmem] * ranks,
        compiler_params=pltpu.CompilerParams(vmem_limit_bytes=SMALL_VMEM),
        name="split",
    )(grad_attended)


def arrange_kernel(q_ref, rows_ref, cols_ref, wide):
    small = unit(q_ref.shape[2])
    wide[...] = q_ref[...].astype(jnp.float32)
    for chunk in range(rows_ref.shape[0]):
        for j in range(q_ref.shape[1]):
            rows_ref[chunk, j * CHUNK : (j + 1) * CHUNK, :] = wide[
                chunk * CHUNK : (chunk + 1) * CHUNK, j, :
            ].astype(jnp.bfloat16)
        cols_ref[chunk] = dot_nt(small, rows_ref[chunk]).astype(jnp.bfloat16)


def arrange_grads_kernel(*refs):
    parts, (rows_ref, cols_ref, grads) = refs[:-3], refs[-3:]
    width = rows_ref.shape[2]
    small = unit(width)
    size = parts[0].shape[0]
    for k, ref in enumerate(parts):
        at = pl.multiple_of((lax.axis_index("head") ^ k) * size, size)
        grads[pl.ds(at, size), :] = ref[...]
    for chunk in range(rows_ref.shape[0]):
        for j in range(rows_ref.shape[1] // CHUNK):
            rows_ref[chunk, j * CHUNK : (j + 1) * CHUNK, :] = grads[
                chunk * CHUNK : (chunk + 1) * CHUNK, j * width : (j + 1) * width
            ]
        cols_ref[chunk] = dot_nt(small, rows_ref[chunk]).astype(jnp.bfloat16)


def arrange(kernel, arrays, shape, scratch):
    tok, heads, width = shape
    vmem = pl.BlockSpec(memory_space=pltpu.VMEM)
    chunks, rows = tok // CHUNK, heads * CHUNK
    return pl.pallas_call(
        kernel,
        out_shape=[
            jax.ShapeDtypeStruct((chunks, rows, width), jnp.bfloat16),
            jax.ShapeDtypeStruct((chunks, width, rows), jnp.bfloat16),
        ],
        in_specs=[vmem] * len(arrays),
        out_specs=[vmem, vmem],
        scratch_shapes=[scratch],
        compiler_params=pltpu.CompilerParams(vmem_limit_bytes=SMALL_VMEM),
        name="arrange",
    )(*arrays)


def join_kernel(*refs):
    parts, (rows_ref, out_ref, dq_ref, wide) = refs[:-4], refs[-4:]
    size = parts[0].shape[1]
    for k, ref in enumerate(parts):
        at = pl.multiple_of((lax.axis_index("head") ^ k) * size, size)
        out_ref[:, pl.ds(at, size)] = ref[...]
    scale = 1.0 / math.sqrt(rows_ref.shape[2])
    for chunk in range(rows_ref.shape[0]):
        for j in range(dq_ref.shape[1]):
            wide[chunk * CHUNK : (chunk + 1) * CHUNK, j, :] = (
                rows_ref[chunk, j * CHUNK : (j + 1) * CHUNK, :] * scale
            )
    dq_ref[...] = wide[...].astype(jnp.bfloat16)


def join(parts, dq_rows, shape):
    rows, size = parts[0].shape
    vmem = pl.BlockSpec(memory_space=pltpu.VMEM)
    return pl.pallas_call(
        join_kernel,
        out_shape=(
            jax.ShapeDtypeStruct((rows, size * len(parts)), parts[0].dtype),
            jax.ShapeDtypeStruct(shape, jnp.bfloat16),
        ),
        in_specs=[vmem] * (len(parts) + 1),
        out_specs=(vmem, vmem),
        scratch_shapes=[pltpu.VMEM(shape, jnp.float32)],
        compiler_params=pltpu.CompilerParams(vmem_limit_bytes=SMALL_VMEM),
        name="join",
    )(*parts, dq_rows)


def merge_kernel(*refs):
    total = refs[0][...]
    for ref in refs[1:-1]:
        total = total + ref[...].astype(jnp.float32)
    refs[-1][...] = total.astype(jnp.bfloat16)


def merge(*blocks):
    vmem = pl.BlockSpec(memory_space=pltpu.VMEM)
    return pl.pallas_call(
        merge_kernel,
        out_shape=jax.ShapeDtypeStruct(blocks[0].shape, jnp.bfloat16),
        in_specs=[vmem] * len(blocks),
        out_specs=vmem,
        compiler_params=pltpu.CompilerParams(vmem_limit_bytes=SMALL_VMEM),
        name="merge",
    )(*blocks)


def finish_kernel(own_ref, *refs):
    arrived = refs[:-2]
    dk_ref, dv_ref = refs[-2:]
    total = own_ref[...]
    for ref in arrived:
        total = total + ref[...].astype(jnp.float32)
    total = total.astype(jnp.bfloat16)
    width = dk_ref.shape[1]
    large = unit(dk_ref.shape[0])
    dk_ref[...] = dot_nt(large, total[:width]).astype(jnp.bfloat16)
    dv_ref[...] = dot_nt(large, total[width:]).astype(jnp.bfloat16)


def finish(own_part, arrived):
    both, tok = own_part.shape
    vmem = pl.BlockSpec(memory_space=pltpu.VMEM)
    shape = jax.ShapeDtypeStruct((tok, both // 2), jnp.bfloat16)
    return pl.pallas_call(
        finish_kernel,
        out_shape=(shape, shape),
        in_specs=[vmem] * (1 + len(arrived)),
        out_specs=(vmem, vmem),
        compiler_params=pltpu.CompilerParams(vmem_limit_bytes=SMALL_VMEM),
        name="finish",
    )(own_part, *arrived)


def shifted(block, by, count):
    pairs = [(i, i + by) for i in range(count) if 0 <= i + by < count]
    return lax.ppermute(block, "ctx", pairs)


def exchanged(block, axis, by):
    return lax.ppermute(block, axis, [(i, i ^ by) for i in range(lax.axis_size(axis))])


def after(value, *others):
    return lax.optimization_barrier((value, *others))


def body(queries, key_states, value_states, doc_lengths, grad_attended):
    tok, heads, width = queries.shape
    count = lax.axis_size("ctx")
    ranks = lax.axis_size("head")
    reach = min((DOC_MOST + tok - 2) // tok, count - 1)
    back = min((reach + 1) // 2, count // 2 - 1)
    whole = count == 8 and back == 3 and ranks == 4
    own = jnp.concatenate(
        [key_states.reshape(tok, width), value_states.reshape(tok, width)], axis=0
    )
    near = exchanged(own, "ctx", 1)
    if whole:
        beside = exchanged(own, "ctx", 2)
        across = exchanged(own, "ctx", 4)
    else:
        arrived = [shifted(own, 2 * k, count) for k in range(1, back + 1)]
    grads = split(grad_attended, ranks)
    grads = [part if k == 0 else exchanged(part, "head", k) for k, part in enumerate(grads)]
    prepared = arrange(
        arrange_kernel, [queries], queries.shape, pltpu.VMEM(queries.shape, jnp.float32)
    )
    if whole:
        beside, near = after(beside, near)
        far_beside = exchanged(beside, "ctx", 1)
        across, grads[1], *prepared = after(across, grads[1], *prepared)
        passed = exchanged(across, "ctx", 2)
        far_across = exchanged(across, "ctx", 1)
    prepared = [*prepared, *arrange(
        arrange_grads_kernel,
        grads,
        queries.shape,
        pltpu.VMEM((tok, heads * width), jnp.bfloat16),
    )]
    if whole:
        passed, far_beside, *prepared = after(passed, far_beside, *prepared)
        far_passed = exchanged(passed, "ctx", 1)
        arrived = [beside, across, passed]
        far = [far_beside, far_across, far_passed]
    else:
        far = [exchanged(block, "ctx", 1) for block in arrived]
    outs, state, parts = attend(doc_lengths, prepared, own, near, arrived, far, ranks, whole)
    outs, far_parts = list(outs), list(parts)
    dq_rows, mine1, other1, mine0, other0 = attend_near(
        doc_lengths, prepared, state, back, whole
    )
    outs = [part if k == 0 else exchanged(part, "head", k) for k, part in enumerate(outs)]
    mine = [mine0, mine1] + far_parts[0::2]
    other = [other0, other1] + [exchanged(part, "ctx", 1) for part in far_parts[1::2]]
    other[back], *outs[1:2] = after(other[back], *outs[1:2])
    returned = []
    for k in range(back, 0, -1):
        if k == back - 1:
            other[k], *outs[2:3] = after(other[k], *outs[2:3])
        block = merge(mine[k], other[k])
        if k == back:
            block, other[1] = after(block, other[1])
            other[1] = exchanged(other[1], "ctx", 1)
            other[0], other[1] = after(other[0], other[1])
            other[0] = exchanged(other[0], "ctx", 1)
        returned.append(shifted(block, -2 * k, count))
    grad_keys, grad_values = finish(mine[0], [other[0]] + returned)
    attended, grad_queries = join(outs, dq_rows, queries.shape)
    grad_keys = grad_keys.reshape(tok, 1, width)
    grad_values = grad_values.reshape(tok, 1, width)
    return attended, grad_queries, grad_keys, grad_values


def solution(mesh):
    in_specs = (
        P("ctx", "head", None),
        P("ctx", "head", None),
        P("ctx", "head", None),
        P(),
        P(("ctx", "head"), None),
    )
    out_specs = (
        P(("ctx", "head"), None),
        P("ctx", "head", None),
        P("ctx", "head", None),
        P("ctx", "head", None),
    )
    return jax.shard_map(body, mesh=mesh, in_specs=in_specs, out_specs=out_specs, check_vma=False)
```

```python
import functools
import math

import jax
import jax.numpy as jnp
from jax import lax
from jax.experimental import pallas as pl
from jax.experimental.pallas import tpu as pltpu
from jax.sharding import PartitionSpec as P

DOC_MOST = 1792
NEG_FILL = -1e30
TILE = 256
CHUNK = 128
LOG2_E = 1.4426950408889634
SMALL_VMEM = 8 * 1024 * 1024
KERNEL_VMEM = 16 * 1024 * 1024


def dot(a, b):
    return jnp.dot(a, b, preferred_element_type=jnp.float32)


def dot_nt(a, b):
    return lax.dot_general(a, b, (((1,), (1,)), ((), ())), preferred_element_type=jnp.float32)


def unit(size):
    rows = lax.broadcasted_iota(jnp.int32, (size, size), 0)
    return (rows == lax.broadcasted_iota(jnp.int32, (size, size), 1)).astype(jnp.bfloat16)


def twice(column):
    return jnp.concatenate([column, column], axis=1)


def starts_in(doc_ref, positions):
    end, found = jnp.int32(0), jnp.zeros_like(positions)
    for i in range(doc_ref.shape[0]):
        end = end + doc_ref[i]
        found = jnp.where(positions >= end, end, found)
    return found


def here(tok, back, whole):
    ctx = lax.axis_index("ctx")
    parity = lax.rem(ctx, 2)
    last = ctx // 2 if whole else back
    base = 0 if whole else (ctx - parity - 2 * back) * tok
    return parity, last, base, 2 * last + parity


def back_tile(i, slot, chunk, width, refs):
    q_cols, do_rows, do_cols, keys, values, scores, top, delta, dq_acc, d_blocks = refs
    at = pl.ds(pl.multiple_of(i * TILE, TILE), TILE)
    probs = jnp.exp2(scores[chunk, i] - twice(top[chunk]))
    d_probs = dot_nt(do_rows[chunk], values[at, 0:width])
    d_scores = (probs * (d_probs - twice(delta[chunk]))).astype(jnp.bfloat16)
    dq_acc[chunk] += dot(d_scores, keys[at, :])
    d_blocks[slot, 0:width, :] += dot(q_cols[chunk], d_scores)
    d_blocks[slot, width:, :] += dot(do_cols[chunk], probs.astype(jnp.bfloat16))


def put(d_blocks, mine, other, mine_ref, other_ref, width, scale):
    mine_ref[0:width, :] = d_blocks[mine, 0:width, :] * scale
    mine_ref[width:, :] = d_blocks[mine, width:, :]
    other_ref[0:width, :] = (d_blocks[other, 0:width, :] * scale).astype(jnp.bfloat16)
    other_ref[width:, :] = d_blocks[other, width:, :].astype(jnp.bfloat16)


def attention_kernel(
    doc_ref,
    q_rows,
    q_cols,
    do_rows,
    do_cols,
    own_ref,
    near_ref,
    *refs,
    back,
    whole,
    ranks,
    heads,
    width,
    scale,
):
    arrived, far, refs = refs[:back], refs[back : 2 * back], refs[2 * back :]
    out_parts, refs = refs[:ranks], refs[ranks:]
    (scores, top, delta, keys, values, dq_acc), refs = refs[:6], refs[6:]
    d_refs, (o_ref, accum, d_blocks) = refs[:-3], refs[-3:]
    tok = own_ref.shape[0] // 2
    part_rows = tok // ranks
    rank = lax.axis_index("head")
    parity, last, base, own = here(tok, back, whole)
    cut = 2 * (last - 1)
    ones = jnp.ones((width, width), jnp.bfloat16)

    values[:, width:] = jnp.ones_like(values[:, width:])
    for k in range(back + 1):
        pair = last ^ k if whole else last - k
        mine, other = (own_ref, near_ref) if k == 0 else (arrived[k - 1], far[k - 1])
        for ref, place in ((mine, 2 * pair + parity), (other, 2 * pair + 1 - parity)):
            at = pl.ds(pl.multiple_of(place * tok, tok), tok)
            keys[at, :] = ref[0:tok, :]
            values[at, 0:width] = ref[tok:, :]
    d_blocks[...] = jnp.zeros_like(d_blocks)
    top[...] = jnp.full_like(top, NEG_FILL)
    dq_acc[...] = jnp.zeros_like(dq_acc)

    def chunk_step(chunk, carry):
        rows_at = pl.ds(pl.multiple_of(chunk * CHUNK, CHUNK), CHUNK)
        t_first = base + own * TILE + chunk * CHUNK
        t_last = t_first + CHUNK - 1
        t_col = t_first + lax.broadcasted_iota(jnp.int32, (CHUNK, width), 0)
        start_col = starts_in(doc_ref, t_col)
        low = jnp.maximum(starts_in(doc_ref, t_first) - base, 0) // TILE
        clear = jnp.clip((starts_in(doc_ref, t_last) - base + TILE - 1) // TILE, low, own)

        def score_tile(i, masked):
            at = pl.ds(pl.multiple_of(i * TILE, TILE), TILE)
            tile = dot_nt(q_rows[chunk], keys[at, :]) * (scale * LOG2_E)
            if masked:
                s_row = base + i * TILE + lax.broadcasted_iota(jnp.int32, (CHUNK, TILE), 1)
                live = (s_row >= twice(start_col)) & (s_row <= twice(t_col))
                tile = jnp.concatenate(
                    [
                        jnp.where(live, tile[j * CHUNK : (j + 1) * CHUNK], NEG_FILL)
                        for j in range(heads)
                    ],
                    axis=0,
                )
            scores[chunk, i] = tile
            top[chunk] = jnp.maximum(top[chunk], jnp.maximum(tile[:, :width], tile[:, width:]))

        def edge_step(n, carry):
            score_tile(jnp.where(n < clear - low, low + n, own), True)
            return carry

        def inner_step(i, carry):
            score_tile(i, False)
            return carry

        lax.fori_loop(0, clear - low + 1, edge_step, 0)
        lax.fori_loop(clear, own, inner_step, 0)
        top[chunk] = jnp.broadcast_to(jnp.max(top[chunk], axis=1, keepdims=True), top.shape[1:])
        accum[...] = jnp.zeros_like(accum)

        def weigh_step(i, carry):
            at = pl.ds(pl.multiple_of(i * TILE, TILE), TILE)
            weights = jnp.exp2(scores[chunk, i] - twice(top[chunk])).astype(jnp.bfloat16)
            accum[...] += dot(weights, values[at, :])
            return carry

        lax.fori_loop(low, own + 1, weigh_step, 0)
        total = accum[:, width:]
        out = (accum[:, 0:width] / total).astype(jnp.bfloat16)
        for j in range(heads):
            o_ref[rows_at, j * width : (j + 1) * width] = out[j * CHUNK : (j + 1) * CHUNK]
        top[chunk] = top[chunk] + jnp.log2(total)
        product = do_rows[chunk].astype(jnp.float32) * out.astype(jnp.float32)
        coarse = product.astype(jnp.bfloat16)
        fine = (product - coarse.astype(jnp.float32)).astype(jnp.bfloat16)
        delta[chunk] = dot(coarse, ones) + dot(fine, ones)

        def back_step(i, carry):
            refs = (
                q_cols, do_rows, do_cols, keys, values, scores, top, delta, dq_acc, d_blocks
            )
            back_tile(i, i, chunk, width, refs)
            return carry

        lax.fori_loop(low, cut, back_step, 0)
        return carry

    lax.fori_loop(0, tok // CHUNK, chunk_step, 0)
    for k in range(ranks):
        at = pl.ds(pl.multiple_of((rank ^ k) * part_rows, part_rows), part_rows)
        out_parts[k][...] = o_ref[at, :]
    for k in range(2, back + 1):
        pair = jnp.maximum(last - k, 0)
        mine, other = 2 * pair + parity, 2 * pair + 1 - parity
        mine_ref, other_ref = (ref.at[k - 2] for ref in d_refs)
        put(d_blocks, mine, other, mine_ref, other_ref, width, scale)


def attend(doc_lengths, prepared, own, near, arrived, far, ranks, whole):
    chunks, rows, width = prepared[0].shape
    tok = chunks * CHUNK
    heads = rows // CHUNK
    back = len(arrived)
    tiles = 2 * (back + 1)
    span = tiles * tok
    vmem = pl.BlockSpec(memory_space=pltpu.VMEM)
    smem = pl.BlockSpec(memory_space=pltpu.SMEM)
    out_part = jax.ShapeDtypeStruct((tok // ranks, heads * width), jnp.bfloat16)
    row_state = jax.ShapeDtypeStruct((chunks, rows, width), jnp.float32)
    outputs = pl.pallas_call(
        functools.partial(
            attention_kernel,
            back=back,
            whole=whole,
            ranks=ranks,
            heads=heads,
            width=width,
            scale=1.0 / math.sqrt(width),
        ),
        out_shape=[out_part] * ranks
        + [
            jax.ShapeDtypeStruct((chunks, tiles, rows, TILE), jnp.float32),
            row_state,
            row_state,
            jax.ShapeDtypeStruct((span, width), jnp.bfloat16),
            jax.ShapeDtypeStruct((span, 2 * width), jnp.bfloat16),
            row_state,
        ]
        + [
            jax.ShapeDtypeStruct((back - 1, 2 * width, tok), dtype)
            for dtype in (jnp.float32, jnp.bfloat16)
        ],
        in_specs=[smem] + [vmem] * (6 + 2 * back),
        out_specs=[vmem] * (ranks + 8),
        scratch_shapes=[
            pltpu.VMEM((tok, heads * width), jnp.bfloat16),
            pltpu.VMEM((rows, 2 * width), jnp.float32),
            pltpu.VMEM((tiles, 2 * width, tok), jnp.float32),
        ],
        compiler_params=pltpu.CompilerParams(vmem_limit_bytes=KERNEL_VMEM),
        cost_estimate=pl.CostEstimate(
            flops=14 * tok * heads * width * span,
            bytes_accessed=4 * tok * heads * width * 2 + 4 * span * width * 2,
            transcendentals=tok * heads * span,
        ),
        name="attention",
    )(doc_lengths, *prepared, own, near, *arrived, *far)
    return outputs[:ranks], outputs[ranks : ranks + 6], outputs[ranks + 6 :]


def near_kernel(
    doc_ref,
    q_cols,
    do_rows,
    do_cols,
    scores,
    top,
    delta,
    keys,
    values,
    dq_far,
    dq_acc,
    mine1_ref,
    other1_ref,
    mine0_ref,
    other0_ref,
    d_blocks,
    *,
    back,
    whole,
    width,
    scale,
):
    tok = mine0_ref.shape[1]
    parity, last, base, own = here(tok, back, whole)
    cut = 2 * (last - 1)
    d_blocks[...] = jnp.zeros_like(d_blocks)
    dq_acc[...] = dq_far[...]

    def chunk_step(chunk, carry):
        t_first = base + own * TILE + chunk * CHUNK
        low = jnp.maximum(starts_in(doc_ref, t_first) - base, 0) // TILE

        def back_step(i, carry):
            refs = (
                q_cols, do_rows, do_cols, keys, values, scores, top, delta, dq_acc, d_blocks
            )
            back_tile(i, i - cut, chunk, width, refs)
            return carry

        lax.fori_loop(jnp.maximum(low, cut), own + 1, back_step, 0)
        return carry

    lax.fori_loop(0, tok // CHUNK, chunk_step, 0)
    put(d_blocks, parity, 1 - parity, mine1_ref.at[0], other1_ref.at[0], width, scale)
    put(d_blocks, 2 + parity, 3 - parity, mine0_ref, other0_ref, width, scale)


def attend_near(doc_lengths, prepared, state, back, whole):
    _, q_cols, do_rows, do_cols = prepared
    chunks, rows, width = do_rows.shape
    tok = chunks * CHUNK
    vmem = pl.BlockSpec(memory_space=pltpu.VMEM)
    smem = pl.BlockSpec(memory_space=pltpu.SMEM)
    return pl.pallas_call(
        functools.partial(
            near_kernel, back=back, whole=whole, width=width, scale=1.0 / math.sqrt(width)
        ),
        out_shape=[jax.ShapeDtypeStruct((chunks, rows, width), jnp.float32)]
        + [
            jax.ShapeDtypeStruct(shape, dtype)
            for shape in ((1, 2 * width, tok), (2 * width, tok))
            for dtype in (jnp.float32, jnp.bfloat16)
        ],
        in_specs=[smem] + [vmem] * 9,
        out_specs=[vmem] * 5,
        scratch_shapes=[pltpu.VMEM((4, 2 * width, tok), jnp.float32)],
        compiler_params=pltpu.CompilerParams(vmem_limit_bytes=KERNEL_VMEM),
        cost_estimate=pl.CostEstimate(
            flops=8 * chunks * rows * width * 4 * tok,
            bytes_accessed=4 * chunks * rows * width * 2,
            transcendentals=4 * chunks * rows * tok,
        ),
        name="near",
    )(doc_lengths, q_cols, do_rows, do_cols, *state)


def split_kernel(grad_ref, *part_refs):
    size = part_refs[0].shape[1]
    for k, ref in enumerate(part_refs):
        at = pl.multiple_of((lax.axis_index("head") ^ k) * size, size)
        ref[...] = grad_ref[:, pl.ds(at, size)]


def split(grad_attended, ranks):
    rows, columns = grad_attended.shape
    vmem = pl.BlockSpec(memory_space=pltpu.VMEM)
    part = jax.ShapeDtypeStruct((rows, columns // ranks), grad_attended.dtype)
    return pl.pallas_call(
        split_kernel,
        out_shape=[part] * ranks,
        in_specs=[vmem],
        out_specs=[vmem] * ranks,
        compiler_params=pltpu.CompilerParams(vmem_limit_bytes=SMALL_VMEM),
        name="split",
    )(grad_attended)


def arrange_kernel(doc_ref, q_ref, lengths_ref, rows_ref, cols_ref, wide):
    for i in range(doc_ref.shape[0]):
        lengths_ref[i] = doc_ref[i]
    small = unit(q_ref.shape[2])
    wide[...] = q_ref[...].astype(jnp.float32)
    for chunk in range(rows_ref.shape[0]):
        for j in range(q_ref.shape[1]):
            rows_ref[chunk, j * CHUNK : (j + 1) * CHUNK, :] = wide[
                chunk * CHUNK : (chunk + 1) * CHUNK, j, :
            ].astype(jnp.bfloat16)
        cols_ref[chunk] = dot_nt(small, rows_ref[chunk]).astype(jnp.bfloat16)


def arrange_grads_kernel(*refs):
    parts, (rows_ref, cols_ref, grads) = refs[:-3], refs[-3:]
    width = rows_ref.shape[2]
    small = unit(width)
    size = parts[0].shape[0]
    for k, ref in enumerate(parts):
        at = pl.multiple_of((lax.axis_index("head") ^ k) * size, size)
        grads[pl.ds(at, size), :] = ref[...]
    for chunk in range(rows_ref.shape[0]):
        for j in range(rows_ref.shape[1] // CHUNK):
            rows_ref[chunk, j * CHUNK : (j + 1) * CHUNK, :] = grads[
                chunk * CHUNK : (chunk + 1) * CHUNK, j * width : (j + 1) * width
            ]
        cols_ref[chunk] = dot_nt(small, rows_ref[chunk]).astype(jnp.bfloat16)


def arrange(kernel, arrays, shape, scratch, lengths=()):
    tok, heads, width = shape
    vmem = pl.BlockSpec(memory_space=pltpu.VMEM)
    smem = pl.BlockSpec(memory_space=pltpu.SMEM)
    chunks, rows = tok // CHUNK, heads * CHUNK
    return pl.pallas_call(
        kernel,
        out_shape=[jax.ShapeDtypeStruct(length.shape, length.dtype) for length in lengths]
        + [
            jax.ShapeDtypeStruct((chunks, rows, width), jnp.bfloat16),
            jax.ShapeDtypeStruct((chunks, width, rows), jnp.bfloat16),
        ],
        in_specs=[smem] * len(lengths) + [vmem] * len(arrays),
        out_specs=[smem] * len(lengths) + [vmem, vmem],
        scratch_shapes=[scratch],
        compiler_params=pltpu.CompilerParams(vmem_limit_bytes=SMALL_VMEM),
        name="arrange",
    )(*lengths, *arrays)


def join_kernel(*refs):
    parts, (rows_ref, out_ref, dq_ref, wide) = refs[:-4], refs[-4:]
    size = parts[0].shape[1]
    for k, ref in enumerate(parts):
        at = pl.multiple_of((lax.axis_index("head") ^ k) * size, size)
        out_ref[:, pl.ds(at, size)] = ref[...]
    scale = 1.0 / math.sqrt(rows_ref.shape[2])
    for chunk in range(rows_ref.shape[0]):
        for j in range(dq_ref.shape[1]):
            wide[chunk * CHUNK : (chunk + 1) * CHUNK, j, :] = (
                rows_ref[chunk, j * CHUNK : (j + 1) * CHUNK, :] * scale
            )
    dq_ref[...] = wide[...].astype(jnp.bfloat16)


def join(parts, dq_rows, shape):
    rows, size = parts[0].shape
    vmem = pl.BlockSpec(memory_space=pltpu.VMEM)
    return pl.pallas_call(
        join_kernel,
        out_shape=(
            jax.ShapeDtypeStruct((rows, size * len(parts)), parts[0].dtype),
            jax.ShapeDtypeStruct(shape, jnp.bfloat16),
        ),
        in_specs=[vmem] * (len(parts) + 1),
        out_specs=(vmem, vmem),
        scratch_shapes=[pltpu.VMEM(shape, jnp.float32)],
        compiler_params=pltpu.CompilerParams(vmem_limit_bytes=SMALL_VMEM),
        name="join",
    )(*parts, dq_rows)


def merge_kernel(mine_ref, other_ref, *block_refs):
    for k, ref in enumerate(block_refs):
        ref[...] = (mine_ref[k] + other_ref[k].astype(jnp.float32)).astype(ref.dtype)


def merge(mine, other):
    vmem = pl.BlockSpec(memory_space=pltpu.VMEM)
    block = jax.ShapeDtypeStruct(mine.shape[1:], jnp.bfloat16)
    return pl.pallas_call(
        merge_kernel,
        out_shape=[block] * mine.shape[0],
        in_specs=[vmem, vmem],
        out_specs=[vmem] * mine.shape[0],
        compiler_params=pltpu.CompilerParams(vmem_limit_bytes=SMALL_VMEM),
        name="merge",
    )(mine, other)


def finish_kernel(own_ref, *refs):
    arrived = refs[:-2]
    dk_ref, dv_ref = refs[-2:]
    total = own_ref[...]
    for ref in arrived:
        total = total + ref[...].astype(jnp.float32)
    total = total.astype(jnp.bfloat16)
    width = dk_ref.shape[1]
    large = unit(dk_ref.shape[0])
    dk_ref[...] = dot_nt(large, total[:width]).astype(jnp.bfloat16)
    dv_ref[...] = dot_nt(large, total[width:]).astype(jnp.bfloat16)


def finish(own_part, arrived):
    both, tok = own_part.shape
    vmem = pl.BlockSpec(memory_space=pltpu.VMEM)
    shape = jax.ShapeDtypeStruct((tok, both // 2), jnp.bfloat16)
    return pl.pallas_call(
        finish_kernel,
        out_shape=(shape, shape),
        in_specs=[vmem] * (1 + len(arrived)),
        out_specs=(vmem, vmem),
        compiler_params=pltpu.CompilerParams(vmem_limit_bytes=SMALL_VMEM),
        name="finish",
    )(own_part, *arrived)


def shifted(block, by, count):
    pairs = [(i, i + by) for i in range(count) if 0 <= i + by < count]
    return lax.ppermute(block, "ctx", pairs)


def exchanged(block, axis, by):
    return lax.ppermute(block, axis, [(i, i ^ by) for i in range(lax.axis_size(axis))])


def after(value, *others):
    return lax.optimization_barrier((value, *others))


def body(queries, key_states, value_states, doc_lengths, grad_attended):
    tok, heads, width = queries.shape
    count = lax.axis_size("ctx")
    ranks = lax.axis_size("head")
    reach = min((DOC_MOST + tok - 2) // tok, count - 1)
    back = min((reach + 1) // 2, count // 2 - 1)
    whole = count == 8 and back == 3 and ranks == 4
    own = jnp.concatenate(
        [key_states.reshape(tok, width), value_states.reshape(tok, width)], axis=0
    )
    near = exchanged(own, "ctx", 1)
    if whole:
        beside = exchanged(own, "ctx", 2)
        across = exchanged(own, "ctx", 4)
    else:
        arrived = [shifted(own, 2 * k, count) for k in range(1, back + 1)]
    grads = split(grad_attended, ranks)
    grads = [part if k == 0 else exchanged(part, "head", k) for k, part in enumerate(grads)]
    doc_lengths, *prepared = arrange(
        arrange_kernel,
        [queries],
        queries.shape,
        pltpu.VMEM(queries.shape, jnp.float32),
        [doc_lengths],
    )
    if whole:
        beside, near, across = after(beside, near, across)
        far_beside = exchanged(beside, "ctx", 1)
        across, grads[1], *prepared = after(across, grads[1], *prepared)
        passed = exchanged(across, "ctx", 2)
        far_across = exchanged(across, "ctx", 1)
    prepared = [*prepared, *arrange(
        arrange_grads_kernel,
        grads,
        queries.shape,
        pltpu.VMEM((tok, heads * width), jnp.bfloat16),
    )]
    if whole:
        passed, far_beside, *prepared = after(passed, far_beside, *prepared)
        far_passed = exchanged(passed, "ctx", 1)
        arrived = [beside, across, passed]
        far = [far_beside, far_across, far_passed]
    else:
        far = [exchanged(block, "ctx", 1) for block in arrived]
    outs, state, parts = attend(doc_lengths, prepared, own, near, arrived, far, ranks, whole)
    outs, (mine_far, other_far) = list(outs), parts
    dq_rows, mine1, other1, mine0, other0 = attend_near(
        doc_lengths, prepared, state, back, whole
    )
    other_far = exchanged(other_far, "ctx", 1)
    outs[1:2] = [exchanged(part, "head", 1) for part in outs[1:2]]
    other_far, mine0, *outs[1:2] = after(other_far, mine0, *outs[1:2])
    blocks = list(merge(mine_far, other_far))
    other1, blocks[0], *outs[2:] = after(other1, blocks[0], *outs[2:])
    other1 = exchanged(other1, "ctx", 1)
    outs[2:] = [exchanged(part, "head", k + 2) for k, part in enumerate(outs[2:])]
    returned = [shifted(block, -2 * (k + 2), count) for k, block in enumerate(blocks)]
    other0, returned[0] = after(other0, returned[0])
    other0 = exchanged(other0, "ctx", 1)
    (block,) = merge(mine1, other1)
    returned.append(shifted(block, -2, count))
    grad_keys, grad_values = finish(mine0, [other0] + returned)
    attended, grad_queries = join(outs, dq_rows, queries.shape)
    grad_keys = grad_keys.reshape(tok, 1, width)
    grad_values = grad_values.reshape(tok, 1, width)
    return attended, grad_queries, grad_keys, grad_values


def solution(mesh):
    in_specs = (
        P("ctx", "head", None),
        P("ctx", "head", None),
        P("ctx", "head", None),
        P(),
        P(("ctx", "head"), None),
    )
    out_specs = (
        P(("ctx", "head"), None),
        P("ctx", "head", None),
        P("ctx", "head", None),
        P("ctx", "head", None),
    )
    return jax.shard_map(body, mesh=mesh, in_specs=in_specs, out_specs=out_specs, check_vma=False)
```

```python
import functools
import math

import jax
import jax.numpy as jnp
from jax import lax
from jax.experimental import pallas as pl
from jax.experimental.pallas import tpu as pltpu
from jax.sharding import PartitionSpec as P

DOC_MOST = 1792
NEG_FILL = -1e30
TILE = 256
CHUNK = 128
LOG2_E = 1.4426950408889634
SMALL_VMEM = 8 * 1024 * 1024
KERNEL_VMEM = 16 * 1024 * 1024


def dot(a, b):
    return jnp.dot(a, b, preferred_element_type=jnp.float32)


def dot_nt(a, b):
    return lax.dot_general(a, b, (((1,), (1,)), ((), ())), preferred_element_type=jnp.float32)


def unit(size):
    rows = lax.broadcasted_iota(jnp.int32, (size, size), 0)
    return (rows == lax.broadcasted_iota(jnp.int32, (size, size), 1)).astype(jnp.bfloat16)


def twice(column):
    return jnp.concatenate([column, column], axis=1)


def starts_in(doc_ref, positions):
    end, found = jnp.int32(0), jnp.zeros_like(positions)
    for i in range(doc_ref.shape[0]):
        end = end + doc_ref[i]
        found = jnp.where(positions >= end, end, found)
    return found


def here(tok, back, whole):
    ctx = lax.axis_index("ctx")
    parity = lax.rem(ctx, 2)
    last = ctx // 2 if whole else back
    base = 0 if whole else (ctx - parity - 2 * back) * tok
    return parity, last, base, 2 * last + parity


def back_tile(i, slot, chunk, width, refs):
    q_cols, do_rows, do_cols, keys, values, scores, top, delta, dq_acc, d_blocks = refs
    at = pl.ds(pl.multiple_of(i * TILE, TILE), TILE)
    probs = jnp.exp2(scores[chunk, i] - twice(top[chunk]))
    d_probs = dot_nt(do_rows[chunk], values[at, 0:width])
    d_scores = (probs * (d_probs - twice(delta[chunk]))).astype(jnp.bfloat16)
    dq_acc[chunk] += dot(d_scores, keys[at, :])
    d_blocks[slot, 0:width, :] += dot(q_cols[chunk], d_scores)
    d_blocks[slot, width:, :] += dot(do_cols[chunk], probs.astype(jnp.bfloat16))


def put(d_blocks, mine, other, mine_ref, other_ref, width, scale):
    mine_ref[0:width, :] = d_blocks[mine, 0:width, :] * scale
    mine_ref[width:, :] = d_blocks[mine, width:, :]
    other_ref[0:width, :] = (d_blocks[other, 0:width, :] * scale).astype(jnp.bfloat16)
    other_ref[width:, :] = d_blocks[other, width:, :].astype(jnp.bfloat16)


def attention_kernel(
    doc_ref,
    q_rows,
    q_cols,
    do_rows,
    do_cols,
    own_ref,
    near_ref,
    *refs,
    back,
    whole,
    ranks,
    heads,
    width,
    scale,
):
    arrived, far, refs = refs[:back], refs[back : 2 * back], refs[2 * back :]
    out_parts, refs = refs[:ranks], refs[ranks:]
    (scores, top, delta, keys, values, dq_acc), refs = refs[:6], refs[6:]
    d_refs, (o_ref, accum, d_blocks) = refs[:-3], refs[-3:]
    tok = own_ref.shape[0] // 2
    part_rows = tok // ranks
    rank = lax.axis_index("head")
    parity, last, base, own = here(tok, back, whole)
    cut = 2 * (last - 1)
    ones = jnp.ones((width, width), jnp.bfloat16)

    values[:, width:] = jnp.ones_like(values[:, width:])
    for k in range(back + 1):
        pair = last ^ k if whole else last - k
        mine, other = (own_ref, near_ref) if k == 0 else (arrived[k - 1], far[k - 1])
        for ref, place in ((mine, 2 * pair + parity), (other, 2 * pair + 1 - parity)):
            at = pl.ds(pl.multiple_of(place * tok, tok), tok)
            keys[at, :] = ref[0:tok, :]
            values[at, 0:width] = ref[tok:, :]
    d_blocks[...] = jnp.zeros_like(d_blocks)
    top[...] = jnp.full_like(top, NEG_FILL)
    dq_acc[...] = jnp.zeros_like(dq_acc)

    def chunk_step(chunk, carry):
        rows_at = pl.ds(pl.multiple_of(chunk * CHUNK, CHUNK), CHUNK)
        t_first = base + own * TILE + chunk * CHUNK
        t_last = t_first + CHUNK - 1
        t_col = t_first + lax.broadcasted_iota(jnp.int32, (CHUNK, width), 0)
        start_col = starts_in(doc_ref, t_col)
        low = jnp.maximum(starts_in(doc_ref, t_first) - base, 0) // TILE
        clear = jnp.clip((starts_in(doc_ref, t_last) - base + TILE - 1) // TILE, low, own)

        def score_tile(i, masked):
            at = pl.ds(pl.multiple_of(i * TILE, TILE), TILE)
            tile = dot_nt(q_rows[chunk], keys[at, :]) * (scale * LOG2_E)
            if masked:
                s_row = base + i * TILE + lax.broadcasted_iota(jnp.int32, (CHUNK, TILE), 1)
                live = (s_row >= twice(start_col)) & (s_row <= twice(t_col))
                tile = jnp.concatenate(
                    [
                        jnp.where(live, tile[j * CHUNK : (j + 1) * CHUNK], NEG_FILL)
                        for j in range(heads)
                    ],
                    axis=0,
                )
            scores[chunk, i] = tile
            top[chunk] = jnp.maximum(top[chunk], jnp.maximum(tile[:, :width], tile[:, width:]))

        def edge_step(n, carry):
            score_tile(jnp.where(n < clear - low, low + n, own), True)
            return carry

        def inner_step(i, carry):
            score_tile(i, False)
            return carry

        lax.fori_loop(0, clear - low + 1, edge_step, 0)
        lax.fori_loop(clear, own, inner_step, 0)
        top[chunk] = jnp.broadcast_to(jnp.max(top[chunk], axis=1, keepdims=True), top.shape[1:])
        accum[...] = jnp.zeros_like(accum)

        def weigh_step(i, carry):
            at = pl.ds(pl.multiple_of(i * TILE, TILE), TILE)
            weights = jnp.exp2(scores[chunk, i] - twice(top[chunk])).astype(jnp.bfloat16)
            accum[...] += dot(weights, values[at, :])
            return carry

        lax.fori_loop(low, own + 1, weigh_step, 0)
        total = accum[:, width:]
        out = (accum[:, 0:width] / total).astype(jnp.bfloat16)
        for j in range(heads):
            o_ref[rows_at, j * width : (j + 1) * width] = out[j * CHUNK : (j + 1) * CHUNK]
        top[chunk] = top[chunk] + jnp.log2(total)
        product = do_rows[chunk].astype(jnp.float32) * out.astype(jnp.float32)
        coarse = product.astype(jnp.bfloat16)
        fine = (product - coarse.astype(jnp.float32)).astype(jnp.bfloat16)
        delta[chunk] = dot(coarse, ones) + dot(fine, ones)

        def back_step(i, carry):
            refs = (
                q_cols, do_rows, do_cols, keys, values, scores, top, delta, dq_acc, d_blocks
            )
            back_tile(i, i, chunk, width, refs)
            return carry

        lax.fori_loop(low, cut, back_step, 0)
        return carry

    lax.fori_loop(0, tok // CHUNK, chunk_step, 0)
    for k in range(ranks):
        at = pl.ds(pl.multiple_of((rank ^ k) * part_rows, part_rows), part_rows)
        out_parts[k][...] = o_ref[at, :]
    for k in range(2, back + 1):
        pair = jnp.maximum(last - k, 0)
        mine, other = 2 * pair + parity, 2 * pair + 1 - parity
        mine_ref, other_ref = (ref.at[k - 2] for ref in d_refs)
        put(d_blocks, mine, other, mine_ref, other_ref, width, scale)


def attend(doc_lengths, prepared, own, near, arrived, far, ranks, whole):
    chunks, rows, width = prepared[0].shape
    tok = chunks * CHUNK
    heads = rows // CHUNK
    back = len(arrived)
    tiles = 2 * (back + 1)
    span = tiles * tok
    vmem = pl.BlockSpec(memory_space=pltpu.VMEM)
    smem = pl.BlockSpec(memory_space=pltpu.SMEM)
    out_part = jax.ShapeDtypeStruct((tok // ranks, heads * width), jnp.bfloat16)
    row_state = jax.ShapeDtypeStruct((chunks, rows, width), jnp.float32)
    outputs = pl.pallas_call(
        functools.partial(
            attention_kernel,
            back=back,
            whole=whole,
            ranks=ranks,
            heads=heads,
            width=width,
            scale=1.0 / math.sqrt(width),
        ),
        out_shape=[out_part] * ranks
        + [
            jax.ShapeDtypeStruct((chunks, tiles, rows, TILE), jnp.float32),
            row_state,
            row_state,
            jax.ShapeDtypeStruct((span, width), jnp.bfloat16),
            jax.ShapeDtypeStruct((span, 2 * width), jnp.bfloat16),
            row_state,
        ]
        + [
            jax.ShapeDtypeStruct((back - 1, 2 * width, tok), dtype)
            for dtype in (jnp.float32, jnp.bfloat16)
        ],
        in_specs=[smem] + [vmem] * (6 + 2 * back),
        out_specs=[vmem] * (ranks + 8),
        scratch_shapes=[
            pltpu.VMEM((tok, heads * width), jnp.bfloat16),
            pltpu.VMEM((rows, 2 * width), jnp.float32),
            pltpu.VMEM((tiles, 2 * width, tok), jnp.float32),
        ],
        compiler_params=pltpu.CompilerParams(vmem_limit_bytes=KERNEL_VMEM),
        cost_estimate=pl.CostEstimate(
            flops=14 * tok * heads * width * span,
            bytes_accessed=4 * tok * heads * width * 2 + 4 * span * width * 2,
            transcendentals=tok * heads * span,
        ),
        name="attention",
    )(doc_lengths, *prepared, own, near, *arrived, *far)
    return outputs[:ranks], outputs[ranks : ranks + 6], outputs[ranks + 6 :]


def near_kernel(
    doc_ref,
    q_cols,
    do_rows,
    do_cols,
    scores,
    top,
    delta,
    keys,
    values,
    dq_far,
    dq_acc,
    mine1_ref,
    other1_ref,
    mine0_ref,
    other0_ref,
    d_blocks,
    *,
    back,
    whole,
    width,
    scale,
):
    tok = mine0_ref.shape[1]
    parity, last, base, own = here(tok, back, whole)
    cut = 2 * (last - 1)
    d_blocks[...] = jnp.zeros_like(d_blocks)
    dq_acc[...] = dq_far[...]

    def chunk_step(chunk, carry):
        t_first = base + own * TILE + chunk * CHUNK
        low = jnp.maximum(starts_in(doc_ref, t_first) - base, 0) // TILE

        def back_step(i, carry):
            refs = (
                q_cols, do_rows, do_cols, keys, values, scores, top, delta, dq_acc, d_blocks
            )
            back_tile(i, i - cut, chunk, width, refs)
            return carry

        lax.fori_loop(jnp.maximum(low, cut), own + 1, back_step, 0)
        return carry

    lax.fori_loop(0, tok // CHUNK, chunk_step, 0)
    put(d_blocks, parity, 1 - parity, mine1_ref.at[0], other1_ref.at[0], width, scale)
    put(d_blocks, 2 + parity, 3 - parity, mine0_ref, other0_ref, width, scale)


def attend_near(doc_lengths, prepared, state, back, whole):
    _, q_cols, do_rows, do_cols = prepared
    chunks, rows, width = do_rows.shape
    tok = chunks * CHUNK
    vmem = pl.BlockSpec(memory_space=pltpu.VMEM)
    smem = pl.BlockSpec(memory_space=pltpu.SMEM)
    return pl.pallas_call(
        functools.partial(
            near_kernel, back=back, whole=whole, width=width, scale=1.0 / math.sqrt(width)
        ),
        out_shape=[jax.ShapeDtypeStruct((chunks, rows, width), jnp.float32)]
        + [
            jax.ShapeDtypeStruct(shape, dtype)
            for shape in ((1, 2 * width, tok), (2 * width, tok))
            for dtype in (jnp.float32, jnp.bfloat16)
        ],
        in_specs=[smem] + [vmem] * 9,
        out_specs=[vmem] * 5,
        scratch_shapes=[pltpu.VMEM((4, 2 * width, tok), jnp.float32)],
        compiler_params=pltpu.CompilerParams(vmem_limit_bytes=KERNEL_VMEM),
        cost_estimate=pl.CostEstimate(
            flops=8 * chunks * rows * width * 4 * tok,
            bytes_accessed=4 * chunks * rows * width * 2,
            transcendentals=4 * chunks * rows * tok,
        ),
        name="near",
    )(doc_lengths, q_cols, do_rows, do_cols, *state)


def split_kernel(doc_ref, grad_ref, lengths_ref, *part_refs):
    for i in range(doc_ref.shape[0]):
        lengths_ref[i] = doc_ref[i]
    size = part_refs[0].shape[1]
    for k, ref in enumerate(part_refs):
        at = pl.multiple_of((lax.axis_index("head") ^ k) * size, size)
        ref[...] = grad_ref[:, pl.ds(at, size)]


def split(doc_lengths, grad_attended, ranks):
    rows, columns = grad_attended.shape
    vmem = pl.BlockSpec(memory_space=pltpu.VMEM)
    smem = pl.BlockSpec(memory_space=pltpu.SMEM)
    part = jax.ShapeDtypeStruct((rows, columns // ranks), grad_attended.dtype)
    return pl.pallas_call(
        split_kernel,
        out_shape=[jax.ShapeDtypeStruct(doc_lengths.shape, doc_lengths.dtype)] + [part] * ranks,
        in_specs=[smem, vmem],
        out_specs=[smem] + [vmem] * ranks,
        compiler_params=pltpu.CompilerParams(vmem_limit_bytes=SMALL_VMEM),
        name="split",
    )(doc_lengths, grad_attended)


def arrange_kernel(q_ref, rows_ref, cols_ref, wide):
    small = unit(q_ref.shape[2])
    wide[...] = q_ref[...].astype(jnp.float32)
    for chunk in range(rows_ref.shape[0]):
        for j in range(q_ref.shape[1]):
            rows_ref[chunk, j * CHUNK : (j + 1) * CHUNK, :] = wide[
                chunk * CHUNK : (chunk + 1) * CHUNK, j, :
            ].astype(jnp.bfloat16)
        cols_ref[chunk] = dot_nt(small, rows_ref[chunk]).astype(jnp.bfloat16)


def arrange_grads_kernel(*refs):
    parts, (rows_ref, cols_ref, grads) = refs[:-3], refs[-3:]
    width = rows_ref.shape[2]
    small = unit(width)
    size = parts[0].shape[0]
    for k, ref in enumerate(parts):
        at = pl.multiple_of((lax.axis_index("head") ^ k) * size, size)
        grads[pl.ds(at, size), :] = ref[...]
    for chunk in range(rows_ref.shape[0]):
        for j in range(rows_ref.shape[1] // CHUNK):
            rows_ref[chunk, j * CHUNK : (j + 1) * CHUNK, :] = grads[
                chunk * CHUNK : (chunk + 1) * CHUNK, j * width : (j + 1) * width
            ]
        cols_ref[chunk] = dot_nt(small, rows_ref[chunk]).astype(jnp.bfloat16)


def arrange(kernel, arrays, shape, scratch):
    tok, heads, width = shape
    vmem = pl.BlockSpec(memory_space=pltpu.VMEM)
    chunks, rows = tok // CHUNK, heads * CHUNK
    return pl.pallas_call(
        kernel,
        out_shape=[
            jax.ShapeDtypeStruct((chunks, rows, width), jnp.bfloat16),
            jax.ShapeDtypeStruct((chunks, width, rows), jnp.bfloat16),
        ],
        in_specs=[vmem] * len(arrays),
        out_specs=[vmem, vmem],
        scratch_shapes=[scratch],
        compiler_params=pltpu.CompilerParams(vmem_limit_bytes=SMALL_VMEM),
        name="arrange",
    )(*arrays)


def join_kernel(*refs):
    parts, (rows_ref, out_ref, dq_ref, wide) = refs[:-4], refs[-4:]
    size = parts[0].shape[1]
    for k, ref in enumerate(parts):
        at = pl.multiple_of((lax.axis_index("head") ^ k) * size, size)
        out_ref[:, pl.ds(at, size)] = ref[...]
    scale = 1.0 / math.sqrt(rows_ref.shape[2])
    for chunk in range(rows_ref.shape[0]):
        for j in range(dq_ref.shape[1]):
            wide[chunk * CHUNK : (chunk + 1) * CHUNK, j, :] = (
                rows_ref[chunk, j * CHUNK : (j + 1) * CHUNK, :] * scale
            )
    dq_ref[...] = wide[...].astype(jnp.bfloat16)


def join(parts, dq_rows, shape):
    rows, size = parts[0].shape
    vmem = pl.BlockSpec(memory_space=pltpu.VMEM)
    return pl.pallas_call(
        join_kernel,
        out_shape=(
            jax.ShapeDtypeStruct((rows, size * len(parts)), parts[0].dtype),
            jax.ShapeDtypeStruct(shape, jnp.bfloat16),
        ),
        in_specs=[vmem] * (len(parts) + 1),
        out_specs=(vmem, vmem),
        scratch_shapes=[pltpu.VMEM(shape, jnp.float32)],
        compiler_params=pltpu.CompilerParams(vmem_limit_bytes=SMALL_VMEM),
        name="join",
    )(*parts, dq_rows)


def merge_kernel(mine_ref, other_ref, *block_refs):
    for k, ref in enumerate(block_refs):
        ref[...] = (mine_ref[k] + other_ref[k].astype(jnp.float32)).astype(ref.dtype)


def merge(mine, other):
    vmem = pl.BlockSpec(memory_space=pltpu.VMEM)
    block = jax.ShapeDtypeStruct(mine.shape[1:], jnp.bfloat16)
    return pl.pallas_call(
        merge_kernel,
        out_shape=[block] * mine.shape[0],
        in_specs=[vmem, vmem],
        out_specs=[vmem] * mine.shape[0],
        compiler_params=pltpu.CompilerParams(vmem_limit_bytes=SMALL_VMEM),
        name="merge",
    )(mine, other)


def finish_kernel(own_ref, *refs):
    arrived = refs[:-2]
    dk_ref, dv_ref = refs[-2:]
    total = own_ref[...]
    for ref in arrived:
        total = total + ref[...].astype(jnp.float32)
    total = total.astype(jnp.bfloat16)
    width = dk_ref.shape[1]
    large = unit(dk_ref.shape[0])
    dk_ref[...] = dot_nt(large, total[:width]).astype(jnp.bfloat16)
    dv_ref[...] = dot_nt(large, total[width:]).astype(jnp.bfloat16)


def finish(own_part, arrived):
    both, tok = own_part.shape
    vmem = pl.BlockSpec(memory_space=pltpu.VMEM)
    shape = jax.ShapeDtypeStruct((tok, both // 2), jnp.bfloat16)
    return pl.pallas_call(
        finish_kernel,
        out_shape=(shape, shape),
        in_specs=[vmem] * (1 + len(arrived)),
        out_specs=(vmem, vmem),
        compiler_params=pltpu.CompilerParams(vmem_limit_bytes=SMALL_VMEM),
        name="finish",
    )(own_part, *arrived)


def shifted(block, by, count):
    pairs = [(i, i + by) for i in range(count) if 0 <= i + by < count]
    return lax.ppermute(block, "ctx", pairs)


def exchanged(block, axis, by):
    return lax.ppermute(block, axis, [(i, i ^ by) for i in range(lax.axis_size(axis))])


def after(value, *others):
    return lax.optimization_barrier((value, *others))


def body(queries, key_states, value_states, doc_lengths, grad_attended):
    tok, heads, width = queries.shape
    count = lax.axis_size("ctx")
    ranks = lax.axis_size("head")
    reach = min((DOC_MOST + tok - 2) // tok, count - 1)
    back = min((reach + 1) // 2, count // 2 - 1)
    whole = count == 8 and back == 3 and ranks == 4
    own = jnp.concatenate(
        [key_states.reshape(tok, width), value_states.reshape(tok, width)], axis=0
    )
    near = exchanged(own, "ctx", 1)
    if whole:
        beside = exchanged(own, "ctx", 2)
        across = exchanged(own, "ctx", 4)
    else:
        arrived = [shifted(own, 2 * k, count) for k in range(1, back + 1)]
    doc_lengths, *grads = split(doc_lengths, grad_attended, ranks)
    grads = [part if k == 0 else exchanged(part, "head", k) for k, part in enumerate(grads)]
    if whole:
        far_beside = exchanged(beside, "ctx", 1)
        across, *grads[1:3] = after(across, *grads[1:3])
        passed = exchanged(across, "ctx", 2)
        far_across = exchanged(across, "ctx", 1)
        passed, far_beside, near, grads[3] = after(passed, far_beside, near, grads[3])
        far_passed = exchanged(passed, "ctx", 1)
        arrived = [beside, across, passed]
        far = [far_beside, far_across, far_passed]
    else:
        far = [exchanged(block, "ctx", 1) for block in arrived]
    prepared = arrange(
        arrange_kernel, [queries], queries.shape, pltpu.VMEM(queries.shape, jnp.float32)
    )
    prepared += arrange(
        arrange_grads_kernel,
        grads,
        queries.shape,
        pltpu.VMEM((tok, heads * width), jnp.bfloat16),
    )
    outs, state, parts = attend(doc_lengths, prepared, own, near, arrived, far, ranks, whole)
    outs, (mine_far, other_far) = list(outs), parts
    dq_rows, mine1, other1, mine0, other0 = attend_near(
        doc_lengths, prepared, state, back, whole
    )
    other_far = exchanged(other_far, "ctx", 1)
    outs[1:2] = [exchanged(part, "head", 1) for part in outs[1:2]]
    other_far, mine0, *outs[1:2] = after(other_far, mine0, *outs[1:2])
    blocks = list(merge(mine_far, other_far))
    other1, blocks[0], *outs[2:] = after(other1, blocks[0], *outs[2:])
    other1 = exchanged(other1, "ctx", 1)
    outs[2:] = [exchanged(part, "head", k + 2) for k, part in enumerate(outs[2:])]
    returned = [shifted(block, -2 * (k + 2), count) for k, block in enumerate(blocks)]
    other0, returned[0] = after(other0, returned[0])
    other0 = exchanged(other0, "ctx", 1)
    (block,) = merge(mine1, other1)
    returned.append(shifted(block, -2, count))
    grad_keys, grad_values = finish(mine0, [other0] + returned)
    attended, grad_queries = join(outs, dq_rows, queries.shape)
    grad_keys = grad_keys.reshape(tok, 1, width)
    grad_values = grad_values.reshape(tok, 1, width)
    return attended, grad_queries, grad_keys, grad_values


def solution(mesh):
    in_specs = (
        P("ctx", "head", None),
        P("ctx", "head", None),
        P("ctx", "head", None),
        P(),
        P(("ctx", "head"), None),
    )
    out_specs = (
        P(("ctx", "head"), None),
        P("ctx", "head", None),
        P("ctx", "head", None),
        P("ctx", "head", None),
    )
    return jax.shard_map(body, mesh=mesh, in_specs=in_specs, out_specs=out_specs, check_vma=False)
```

```python
import functools
import math

import jax
import jax.numpy as jnp
from jax import lax
from jax.experimental import pallas as pl
from jax.experimental.pallas import tpu as pltpu
from jax.sharding import PartitionSpec as P

DOC_MOST = 1792
NEG_FILL = -1e30
TILE = 256
CHUNK = 128
LOG2_E = 1.4426950408889634
SMALL_VMEM = 8 * 1024 * 1024
KERNEL_VMEM = 16 * 1024 * 1024


def dot(a, b):
    return jnp.dot(a, b, preferred_element_type=jnp.float32)


def dot_nt(a, b):
    return lax.dot_general(a, b, (((1,), (1,)), ((), ())), preferred_element_type=jnp.float32)


def unit(size):
    rows = lax.broadcasted_iota(jnp.int32, (size, size), 0)
    return (rows == lax.broadcasted_iota(jnp.int32, (size, size), 1)).astype(jnp.bfloat16)


def twice(column):
    return jnp.concatenate([column, column], axis=1)


def starts_in(doc_ref, positions):
    end, found = jnp.int32(0), jnp.zeros_like(positions)
    for i in range(doc_ref.shape[0]):
        end = end + doc_ref[i]
        found = jnp.where(positions >= end, end, found)
    return found


def here(tok, back, whole):
    ctx = lax.axis_index("ctx")
    parity = lax.rem(ctx, 2)
    last = ctx // 2 if whole else back
    base = 0 if whole else (ctx - parity - 2 * back) * tok
    return parity, last, base, 2 * last + parity


def back_tile(i, slot, chunk, width, refs):
    q_cols, do_rows, do_cols, keys, values, scores, top, delta, dq_acc, d_blocks = refs
    at = pl.ds(pl.multiple_of(i * TILE, TILE), TILE)
    probs = jnp.exp2(scores[chunk, i] - twice(top[chunk]))
    d_probs = dot_nt(do_rows[chunk], values[at, 0:width])
    d_scores = (probs * (d_probs - twice(delta[chunk]))).astype(jnp.bfloat16)
    dq_acc[chunk] += dot(d_scores, keys[at, :])
    d_blocks[slot, 0:width, :] += dot(q_cols[chunk], d_scores)
    d_blocks[slot, width:, :] += dot(do_cols[chunk], probs.astype(jnp.bfloat16))


def put(d_blocks, mine, other, mine_ref, other_ref, width, scale):
    mine_ref[0:width, :] = d_blocks[mine, 0:width, :] * scale
    mine_ref[width:, :] = d_blocks[mine, width:, :]
    other_ref[0:width, :] = (d_blocks[other, 0:width, :] * scale).astype(jnp.bfloat16)
    other_ref[width:, :] = d_blocks[other, width:, :].astype(jnp.bfloat16)


def attention_kernel(
    doc_ref,
    q_rows,
    q_cols,
    do_rows,
    do_cols,
    own_ref,
    near_ref,
    *refs,
    back,
    whole,
    ranks,
    heads,
    width,
    scale,
):
    arrived, far, refs = refs[:back], refs[back : 2 * back], refs[2 * back :]
    out_parts, refs = refs[:ranks], refs[ranks:]
    (scores, top, delta, keys, values, dq_acc), refs = refs[:6], refs[6:]
    d_refs, (o_ref, accum, d_blocks) = refs[:-3], refs[-3:]
    tok = own_ref.shape[0] // 2
    part_rows = tok // ranks
    rank = lax.axis_index("head")
    parity, last, base, own = here(tok, back, whole)
    cut = 2 * (last - 1)
    ones = jnp.ones((width, width), jnp.bfloat16)

    values[:, width:] = jnp.ones_like(values[:, width:])
    for k in range(back + 1):
        pair = last ^ k if whole else last - k
        mine, other = (own_ref, near_ref) if k == 0 else (arrived[k - 1], far[k - 1])
        for ref, place in ((mine, 2 * pair + parity), (other, 2 * pair + 1 - parity)):
            at = pl.ds(pl.multiple_of(place * tok, tok), tok)
            keys[at, :] = ref[0:tok, :]
            values[at, 0:width] = ref[tok:, :]
    d_blocks[...] = jnp.zeros_like(d_blocks)
    top[...] = jnp.full_like(top, NEG_FILL)
    dq_acc[...] = jnp.zeros_like(dq_acc)

    def chunk_step(chunk, carry):
        rows_at = pl.ds(pl.multiple_of(chunk * CHUNK, CHUNK), CHUNK)
        t_first = base + own * TILE + chunk * CHUNK
        t_last = t_first + CHUNK - 1
        t_col = t_first + lax.broadcasted_iota(jnp.int32, (CHUNK, width), 0)
        start_col = starts_in(doc_ref, t_col)
        low = jnp.maximum(starts_in(doc_ref, t_first) - base, 0) // TILE
        clear = jnp.clip((starts_in(doc_ref, t_last) - base + TILE - 1) // TILE, low, own)

        def score_tile(i, masked):
            at = pl.ds(pl.multiple_of(i * TILE, TILE), TILE)
            tile = dot_nt(q_rows[chunk], keys[at, :]) * (scale * LOG2_E)
            if masked:
                s_row = base + i * TILE + lax.broadcasted_iota(jnp.int32, (CHUNK, TILE), 1)
                live = (s_row >= twice(start_col)) & (s_row <= twice(t_col))
                tile = jnp.concatenate(
                    [
                        jnp.where(live, tile[j * CHUNK : (j + 1) * CHUNK], NEG_FILL)
                        for j in range(heads)
                    ],
                    axis=0,
                )
            scores[chunk, i] = tile
            top[chunk] = jnp.maximum(top[chunk], jnp.maximum(tile[:, :width], tile[:, width:]))

        def edge_step(n, carry):
            score_tile(jnp.where(n < clear - low, low + n, own), True)
            return carry

        def inner_step(i, carry):
            score_tile(i, False)
            return carry

        lax.fori_loop(0, clear - low + 1, edge_step, 0)
        lax.fori_loop(clear, own, inner_step, 0)
        top[chunk] = jnp.broadcast_to(jnp.max(top[chunk], axis=1, keepdims=True), top.shape[1:])
        accum[...] = jnp.zeros_like(accum)

        def weigh_step(i, carry):
            at = pl.ds(pl.multiple_of(i * TILE, TILE), TILE)
            weights = jnp.exp2(scores[chunk, i] - twice(top[chunk])).astype(jnp.bfloat16)
            accum[...] += dot(weights, values[at, :])
            return carry

        lax.fori_loop(low, own + 1, weigh_step, 0)
        total = accum[:, width:]
        out = (accum[:, 0:width] / total).astype(jnp.bfloat16)
        for j in range(heads):
            o_ref[rows_at, j * width : (j + 1) * width] = out[j * CHUNK : (j + 1) * CHUNK]
        top[chunk] = top[chunk] + jnp.log2(total)
        product = do_rows[chunk].astype(jnp.float32) * out.astype(jnp.float32)
        coarse = product.astype(jnp.bfloat16)
        fine = (product - coarse.astype(jnp.float32)).astype(jnp.bfloat16)
        delta[chunk] = dot(coarse, ones) + dot(fine, ones)

        def back_step(i, carry):
            refs = (
                q_cols, do_rows, do_cols, keys, values, scores, top, delta, dq_acc, d_blocks
            )
            back_tile(i, i, chunk, width, refs)
            return carry

        lax.fori_loop(low, cut, back_step, 0)
        return carry

    lax.fori_loop(0, tok // CHUNK, chunk_step, 0)
    for k in range(ranks):
        at = pl.ds(pl.multiple_of((rank ^ k) * part_rows, part_rows), part_rows)
        out_parts[k][...] = o_ref[at, :]
    for k in range(2, back + 1):
        pair = jnp.maximum(last - k, 0)
        mine, other = 2 * pair + parity, 2 * pair + 1 - parity
        mine_ref, other_ref = (ref.at[k - 2] for ref in d_refs)
        put(d_blocks, mine, other, mine_ref, other_ref, width, scale)


def attend(doc_lengths, prepared, own, near, arrived, far, ranks, whole):
    chunks, rows, width = prepared[0].shape
    tok = chunks * CHUNK
    heads = rows // CHUNK
    back = len(arrived)
    tiles = 2 * (back + 1)
    span = tiles * tok
    vmem = pl.BlockSpec(memory_space=pltpu.VMEM)
    smem = pl.BlockSpec(memory_space=pltpu.SMEM)
    out_part = jax.ShapeDtypeStruct((tok // ranks, heads * width), jnp.bfloat16)
    row_state = jax.ShapeDtypeStruct((chunks, rows, width), jnp.float32)
    outputs = pl.pallas_call(
        functools.partial(
            attention_kernel,
            back=back,
            whole=whole,
            ranks=ranks,
            heads=heads,
            width=width,
            scale=1.0 / math.sqrt(width),
        ),
        out_shape=[out_part] * ranks
        + [
            jax.ShapeDtypeStruct((chunks, tiles, rows, TILE), jnp.float32),
            row_state,
            row_state,
            jax.ShapeDtypeStruct((span, width), jnp.bfloat16),
            jax.ShapeDtypeStruct((span, 2 * width), jnp.bfloat16),
            row_state,
        ]
        + [
            jax.ShapeDtypeStruct((back - 1, 2 * width, tok), dtype)
            for dtype in (jnp.float32, jnp.bfloat16)
        ],
        in_specs=[smem] + [vmem] * (6 + 2 * back),
        out_specs=[vmem] * (ranks + 8),
        scratch_shapes=[
            pltpu.VMEM((tok, heads * width), jnp.bfloat16),
            pltpu.VMEM((rows, 2 * width), jnp.float32),
            pltpu.VMEM((tiles, 2 * width, tok), jnp.float32),
        ],
        compiler_params=pltpu.CompilerParams(vmem_limit_bytes=KERNEL_VMEM),
        cost_estimate=pl.CostEstimate(
            flops=14 * tok * heads * width * span,
            bytes_accessed=4 * tok * heads * width * 2 + 4 * span * width * 2,
            transcendentals=tok * heads * span,
        ),
        name="attention",
    )(doc_lengths, *prepared, own, near, *arrived, *far)
    return outputs[:ranks], outputs[ranks : ranks + 6], outputs[ranks + 6 :]


def near_kernel(
    doc_ref,
    q_cols,
    do_rows,
    do_cols,
    scores,
    top,
    delta,
    keys,
    values,
    dq_far,
    dq_acc,
    mine1_ref,
    other1_ref,
    mine0_ref,
    other0_ref,
    d_blocks,
    *,
    back,
    whole,
    width,
    scale,
):
    tok = mine0_ref.shape[1]
    parity, last, base, own = here(tok, back, whole)
    cut = 2 * (last - 1)
    d_blocks[...] = jnp.zeros_like(d_blocks)
    dq_acc[...] = dq_far[...]

    def chunk_step(chunk, carry):
        t_first = base + own * TILE + chunk * CHUNK
        low = jnp.maximum(starts_in(doc_ref, t_first) - base, 0) // TILE

        def back_step(i, carry):
            refs = (
                q_cols, do_rows, do_cols, keys, values, scores, top, delta, dq_acc, d_blocks
            )
            back_tile(i, i - cut, chunk, width, refs)
            return carry

        lax.fori_loop(jnp.maximum(low, cut), own + 1, back_step, 0)
        return carry

    lax.fori_loop(0, tok // CHUNK, chunk_step, 0)
    put(d_blocks, parity, 1 - parity, mine1_ref.at[0], other1_ref.at[0], width, scale)
    put(d_blocks, 2 + parity, 3 - parity, mine0_ref, other0_ref, width, scale)


def attend_near(doc_lengths, prepared, state, back, whole):
    _, q_cols, do_rows, do_cols = prepared
    chunks, rows, width = do_rows.shape
    tok = chunks * CHUNK
    vmem = pl.BlockSpec(memory_space=pltpu.VMEM)
    smem = pl.BlockSpec(memory_space=pltpu.SMEM)
    return pl.pallas_call(
        functools.partial(
            near_kernel, back=back, whole=whole, width=width, scale=1.0 / math.sqrt(width)
        ),
        out_shape=[jax.ShapeDtypeStruct((chunks, rows, width), jnp.float32)]
        + [
            jax.ShapeDtypeStruct(shape, dtype)
            for shape in ((1, 2 * width, tok), (2 * width, tok))
            for dtype in (jnp.float32, jnp.bfloat16)
        ],
        in_specs=[smem] + [vmem] * 9,
        out_specs=[vmem] * 5,
        scratch_shapes=[pltpu.VMEM((4, 2 * width, tok), jnp.float32)],
        compiler_params=pltpu.CompilerParams(vmem_limit_bytes=KERNEL_VMEM),
        cost_estimate=pl.CostEstimate(
            flops=8 * chunks * rows * width * 4 * tok,
            bytes_accessed=4 * chunks * rows * width * 2,
            transcendentals=4 * chunks * rows * tok,
        ),
        name="near",
    )(doc_lengths, q_cols, do_rows, do_cols, *state)


def split_kernel(grad_ref, *part_refs):
    size = part_refs[0].shape[1]
    for k, ref in enumerate(part_refs):
        at = pl.multiple_of((lax.axis_index("head") ^ k) * size, size)
        ref[...] = grad_ref[:, pl.ds(at, size)]


def split(grad_attended, ranks):
    rows, columns = grad_attended.shape
    vmem = pl.BlockSpec(memory_space=pltpu.VMEM)
    part = jax.ShapeDtypeStruct((rows, columns // ranks), grad_attended.dtype)
    return pl.pallas_call(
        split_kernel,
        out_shape=[part] * ranks,
        in_specs=[vmem],
        out_specs=[vmem] * ranks,
        compiler_params=pltpu.CompilerParams(vmem_limit_bytes=SMALL_VMEM),
        name="split",
    )(grad_attended)


def arrange_kernel(doc_ref, q_ref, lengths_ref, rows_ref, cols_ref, wide):
    for i in range(doc_ref.shape[0]):
        lengths_ref[i] = doc_ref[i]
    small = unit(q_ref.shape[2])
    wide[...] = q_ref[...].astype(jnp.float32)
    for chunk in range(rows_ref.shape[0]):
        for j in range(q_ref.shape[1]):
            rows_ref[chunk, j * CHUNK : (j + 1) * CHUNK, :] = wide[
                chunk * CHUNK : (chunk + 1) * CHUNK, j, :
            ].astype(jnp.bfloat16)
        cols_ref[chunk] = dot_nt(small, rows_ref[chunk]).astype(jnp.bfloat16)


def arrange_grads_kernel(*refs):
    parts, (rows_ref, cols_ref, grads) = refs[:-3], refs[-3:]
    width = rows_ref.shape[2]
    small = unit(width)
    size = parts[0].shape[0]
    for k, ref in enumerate(parts):
        at = pl.multiple_of((lax.axis_index("head") ^ k) * size, size)
        grads[pl.ds(at, size), :] = ref[...]
    for chunk in range(rows_ref.shape[0]):
        for j in range(rows_ref.shape[1] // CHUNK):
            rows_ref[chunk, j * CHUNK : (j + 1) * CHUNK, :] = grads[
                chunk * CHUNK : (chunk + 1) * CHUNK, j * width : (j + 1) * width
            ]
        cols_ref[chunk] = dot_nt(small, rows_ref[chunk]).astype(jnp.bfloat16)


def arrange(kernel, arrays, shape, scratch, lengths=()):
    tok, heads, width = shape
    vmem = pl.BlockSpec(memory_space=pltpu.VMEM)
    smem = pl.BlockSpec(memory_space=pltpu.SMEM)
    chunks, rows = tok // CHUNK, heads * CHUNK
    return pl.pallas_call(
        kernel,
        out_shape=[jax.ShapeDtypeStruct(length.shape, length.dtype) for length in lengths]
        + [
            jax.ShapeDtypeStruct((chunks, rows, width), jnp.bfloat16),
            jax.ShapeDtypeStruct((chunks, width, rows), jnp.bfloat16),
        ],
        in_specs=[smem] * len(lengths) + [vmem] * len(arrays),
        out_specs=[smem] * len(lengths) + [vmem, vmem],
        scratch_shapes=[scratch],
        compiler_params=pltpu.CompilerParams(vmem_limit_bytes=SMALL_VMEM),
        name="arrange",
    )(*lengths, *arrays)


def join_kernel(*refs):
    parts, (rows_ref, out_ref, dq_ref, wide) = refs[:-4], refs[-4:]
    size = parts[0].shape[1]
    for k, ref in enumerate(parts):
        at = pl.multiple_of((lax.axis_index("head") ^ k) * size, size)
        out_ref[:, pl.ds(at, size)] = ref[...]
    scale = 1.0 / math.sqrt(rows_ref.shape[2])
    for chunk in range(rows_ref.shape[0]):
        for j in range(dq_ref.shape[1]):
            wide[chunk * CHUNK : (chunk + 1) * CHUNK, j, :] = (
                rows_ref[chunk, j * CHUNK : (j + 1) * CHUNK, :] * scale
            )
    dq_ref[...] = wide[...].astype(jnp.bfloat16)


def join(parts, dq_rows, shape):
    rows, size = parts[0].shape
    vmem = pl.BlockSpec(memory_space=pltpu.VMEM)
    return pl.pallas_call(
        join_kernel,
        out_shape=(
            jax.ShapeDtypeStruct((rows, size * len(parts)), parts[0].dtype),
            jax.ShapeDtypeStruct(shape, jnp.bfloat16),
        ),
        in_specs=[vmem] * (len(parts) + 1),
        out_specs=(vmem, vmem),
        scratch_shapes=[pltpu.VMEM(shape, jnp.float32)],
        compiler_params=pltpu.CompilerParams(vmem_limit_bytes=SMALL_VMEM),
        name="join",
    )(*parts, dq_rows)


def merge_kernel(mine_ref, other_ref, *block_refs):
    for k, ref in enumerate(block_refs):
        ref[...] = (mine_ref[k] + other_ref[k].astype(jnp.float32)).astype(ref.dtype)


def merge(mine, other):
    vmem = pl.BlockSpec(memory_space=pltpu.VMEM)
    block = jax.ShapeDtypeStruct(mine.shape[1:], jnp.bfloat16)
    return pl.pallas_call(
        merge_kernel,
        out_shape=[block] * mine.shape[0],
        in_specs=[vmem, vmem],
        out_specs=[vmem] * mine.shape[0],
        compiler_params=pltpu.CompilerParams(vmem_limit_bytes=SMALL_VMEM),
        name="merge",
    )(mine, other)


def finish_kernel(own_ref, *refs):
    arrived = refs[:-2]
    dk_ref, dv_ref = refs[-2:]
    total = own_ref[...]
    for ref in arrived:
        total = total + ref[...].astype(jnp.float32)
    total = total.astype(jnp.bfloat16)
    width = dk_ref.shape[1]
    large = unit(dk_ref.shape[0])
    dk_ref[...] = dot_nt(large, total[:width]).astype(jnp.bfloat16)
    dv_ref[...] = dot_nt(large, total[width:]).astype(jnp.bfloat16)


def finish(own_part, arrived):
    both, tok = own_part.shape
    vmem = pl.BlockSpec(memory_space=pltpu.VMEM)
    shape = jax.ShapeDtypeStruct((tok, both // 2), jnp.bfloat16)
    return pl.pallas_call(
        finish_kernel,
        out_shape=(shape, shape),
        in_specs=[vmem] * (1 + len(arrived)),
        out_specs=(vmem, vmem),
        compiler_params=pltpu.CompilerParams(vmem_limit_bytes=SMALL_VMEM),
        name="finish",
    )(own_part, *arrived)


def shifted(block, by, count):
    pairs = [(i, i + by) for i in range(count) if 0 <= i + by < count]
    return lax.ppermute(block, "ctx", pairs)


def exchanged(block, axis, by):
    return lax.ppermute(block, axis, [(i, i ^ by) for i in range(lax.axis_size(axis))])


def after(value, *others):
    return lax.optimization_barrier((value, *others))


def body(queries, key_states, value_states, doc_lengths, grad_attended):
    tok, heads, width = queries.shape
    count = lax.axis_size("ctx")
    ranks = lax.axis_size("head")
    reach = min((DOC_MOST + tok - 2) // tok, count - 1)
    back = min((reach + 1) // 2, count // 2 - 1)
    whole = count == 8 and back == 3 and ranks == 4
    own = jnp.concatenate(
        [key_states.reshape(tok, width), value_states.reshape(tok, width)], axis=0
    )
    near = exchanged(own, "ctx", 1)
    if whole:
        beside = exchanged(own, "ctx", 2)
        across = exchanged(own, "ctx", 4)
    else:
        arrived = [shifted(own, 2 * k, count) for k in range(1, back + 1)]
    grads = split(grad_attended, ranks)
    grads = [part if k == 0 else exchanged(part, "head", k) for k, part in enumerate(grads)]
    doc_lengths, *prepared = arrange(
        arrange_kernel,
        [queries],
        queries.shape,
        pltpu.VMEM(queries.shape, jnp.float32),
        [doc_lengths],
    )
    if whole:
        beside, near = after(beside, near)
        far_beside = exchanged(beside, "ctx", 1)
        across, grads[1], *prepared = after(across, grads[1], *prepared)
        passed = exchanged(across, "ctx", 2)
        far_across = exchanged(across, "ctx", 1)
    prepared = [*prepared, *arrange(
        arrange_grads_kernel,
        grads,
        queries.shape,
        pltpu.VMEM((tok, heads * width), jnp.bfloat16),
    )]
    if whole:
        passed, far_beside, *prepared = after(passed, far_beside, *prepared)
        far_passed = exchanged(passed, "ctx", 1)
        arrived = [beside, across, passed]
        far = [far_beside, far_across, far_passed]
    else:
        far = [exchanged(block, "ctx", 1) for block in arrived]
    outs, state, parts = attend(doc_lengths, prepared, own, near, arrived, far, ranks, whole)
    outs, (mine_far, other_far) = list(outs), parts
    dq_rows, mine1, other1, mine0, other0 = attend_near(
        doc_lengths, prepared, state, back, whole
    )
    other_far = exchanged(other_far, "ctx", 1)
    outs[1:2] = [exchanged(part, "head", 1) for part in outs[1:2]]
    other1 = exchanged(other1, "ctx", 1)
    other_far, mine0, *outs[1:2] = after(other_far, mine0, *outs[1:2])
    blocks = list(merge(mine_far, other_far))
    outs[2:] = [exchanged(part, "head", k + 2) for k, part in enumerate(outs[2:])]
    returned = [shifted(block, -2 * (k + 2), count) for k, block in enumerate(blocks)]
    other1, returned[-1] = after(other1, returned[-1])
    (block,) = merge(mine1, other1)
    block, other0 = after(block, other0)
    other0 = exchanged(other0, "ctx", 1)
    returned.append(shifted(block, -2, count))
    grad_keys, grad_values = finish(mine0, [other0] + returned)
    attended, grad_queries = join(outs, dq_rows, queries.shape)
    grad_keys = grad_keys.reshape(tok, 1, width)
    grad_values = grad_values.reshape(tok, 1, width)
    return attended, grad_queries, grad_keys, grad_values


def solution(mesh):
    in_specs = (
        P("ctx", "head", None),
        P("ctx", "head", None),
        P("ctx", "head", None),
        P(),
        P(("ctx", "head"), None),
    )
    out_specs = (
        P(("ctx", "head"), None),
        P("ctx", "head", None),
        P("ctx", "head", None),
        P("ctx", "head", None),
    )
    return jax.shard_map(body, mesh=mesh, in_specs=in_specs, out_specs=out_specs, check_vma=False)
```

```python
import functools
import math

import jax
import jax.numpy as jnp
from jax import lax
from jax.experimental import pallas as pl
from jax.experimental.pallas import tpu as pltpu
from jax.sharding import PartitionSpec as P

DOC_MOST = 1792
NEG_FILL = -1e30
TILE = 256
CHUNK = 128
LOG2_E = 1.4426950408889634
SMALL_VMEM = 8 * 1024 * 1024
KERNEL_VMEM = 16 * 1024 * 1024


def dot(a, b):
    return jnp.dot(a, b, preferred_element_type=jnp.float32)


def dot_nt(a, b):
    return lax.dot_general(a, b, (((1,), (1,)), ((), ())), preferred_element_type=jnp.float32)


def unit(size):
    rows = lax.broadcasted_iota(jnp.int32, (size, size), 0)
    return (rows == lax.broadcasted_iota(jnp.int32, (size, size), 1)).astype(jnp.bfloat16)


def twice(column):
    return jnp.concatenate([column, column], axis=1)


def starts_in(doc_ref, positions):
    end, found = jnp.int32(0), jnp.zeros_like(positions)
    for i in range(doc_ref.shape[0]):
        end = end + doc_ref[i]
        found = jnp.where(positions >= end, end, found)
    return found


def here(tok, back, whole):
    ctx = lax.axis_index("ctx")
    parity = lax.rem(ctx, 2)
    last = ctx // 2 if whole else back
    base = 0 if whole else (ctx - parity - 2 * back) * tok
    return parity, last, base, 2 * last + parity


def back_tile(i, slot, chunk, width, refs):
    q_cols, do_rows, do_cols, keys, values, scores, top, delta, dq_acc, d_blocks = refs
    at = pl.ds(pl.multiple_of(i * TILE, TILE), TILE)
    probs = jnp.exp2(scores[chunk, i] - twice(top[chunk]))
    d_probs = dot_nt(do_rows[chunk], values[at, 0:width])
    d_scores = (probs * (d_probs - twice(delta[chunk]))).astype(jnp.bfloat16)
    dq_acc[chunk] += dot(d_scores, keys[at, :])
    d_blocks[slot, 0:width, :] += dot(q_cols[chunk], d_scores)
    d_blocks[slot, width:, :] += dot(do_cols[chunk], probs.astype(jnp.bfloat16))


def put(d_blocks, mine, other, mine_ref, other_ref, width, scale):
    mine_ref[0:width, :] = d_blocks[mine, 0:width, :] * scale
    mine_ref[width:, :] = d_blocks[mine, width:, :]
    other_ref[0:width, :] = (d_blocks[other, 0:width, :] * scale).astype(jnp.bfloat16)
    other_ref[width:, :] = d_blocks[other, width:, :].astype(jnp.bfloat16)


def attention_kernel(
    doc_ref,
    q_rows,
    q_cols,
    do_rows,
    do_cols,
    own_ref,
    near_ref,
    *refs,
    back,
    whole,
    ranks,
    heads,
    width,
    scale,
):
    arrived, far, refs = refs[:back], refs[back : 2 * back], refs[2 * back :]
    out_parts, refs = refs[:ranks], refs[ranks:]
    (scores, top, delta, keys, values, dq_acc), refs = refs[:6], refs[6:]
    d_refs, (o_ref, accum, d_blocks) = refs[:-3], refs[-3:]
    tok = own_ref.shape[0] // 2
    part_rows = tok // ranks
    rank = lax.axis_index("head")
    parity, last, base, own = here(tok, back, whole)
    cut = 2 * (last - 1)
    ones = jnp.ones((width, width), jnp.bfloat16)

    values[:, width:] = jnp.ones_like(values[:, width:])
    for k in range(back + 1):
        pair = last ^ k if whole else last - k
        mine, other = (own_ref, near_ref) if k == 0 else (arrived[k - 1], far[k - 1])
        for ref, place in ((mine, 2 * pair + parity), (other, 2 * pair + 1 - parity)):
            at = pl.ds(pl.multiple_of(place * tok, tok), tok)
            keys[at, :] = ref[0:tok, :]
            values[at, 0:width] = ref[tok:, :]
    d_blocks[...] = jnp.zeros_like(d_blocks)
    top[...] = jnp.full_like(top, NEG_FILL)
    dq_acc[...] = jnp.zeros_like(dq_acc)

    def chunk_step(chunk, carry):
        rows_at = pl.ds(pl.multiple_of(chunk * CHUNK, CHUNK), CHUNK)
        t_first = base + own * TILE + chunk * CHUNK
        t_last = t_first + CHUNK - 1
        t_col = t_first + lax.broadcasted_iota(jnp.int32, (CHUNK, width), 0)
        start_col = starts_in(doc_ref, t_col)
        low = jnp.maximum(starts_in(doc_ref, t_first) - base, 0) // TILE
        clear = jnp.clip((starts_in(doc_ref, t_last) - base + TILE - 1) // TILE, low, own)

        def score_tile(i, masked):
            at = pl.ds(pl.multiple_of(i * TILE, TILE), TILE)
            tile = dot_nt(q_rows[chunk], keys[at, :]) * (scale * LOG2_E)
            if masked:
                s_row = base + i * TILE + lax.broadcasted_iota(jnp.int32, (CHUNK, TILE), 1)
                live = (s_row >= twice(start_col)) & (s_row <= twice(t_col))
                tile = jnp.concatenate(
                    [
                        jnp.where(live, tile[j * CHUNK : (j + 1) * CHUNK], NEG_FILL)
                        for j in range(heads)
                    ],
                    axis=0,
                )
            scores[chunk, i] = tile
            top[chunk] = jnp.maximum(top[chunk], jnp.maximum(tile[:, :width], tile[:, width:]))

        def edge_step(n, carry):
            score_tile(jnp.where(n < clear - low, low + n, own), True)
            return carry

        def inner_step(i, carry):
            score_tile(i, False)
            return carry

        lax.fori_loop(0, clear - low + 1, edge_step, 0)
        lax.fori_loop(clear, own, inner_step, 0)
        top[chunk] = jnp.broadcast_to(jnp.max(top[chunk], axis=1, keepdims=True), top.shape[1:])
        accum[...] = jnp.zeros_like(accum)

        def weigh_step(i, carry):
            at = pl.ds(pl.multiple_of(i * TILE, TILE), TILE)
            weights = jnp.exp2(scores[chunk, i] - twice(top[chunk])).astype(jnp.bfloat16)
            accum[...] += dot(weights, values[at, :])
            return carry

        lax.fori_loop(low, own + 1, weigh_step, 0)
        total = accum[:, width:]
        out = (accum[:, 0:width] / total).astype(jnp.bfloat16)
        for j in range(heads):
            o_ref[rows_at, j * width : (j + 1) * width] = out[j * CHUNK : (j + 1) * CHUNK]
        top[chunk] = top[chunk] + jnp.log2(total)
        product = do_rows[chunk].astype(jnp.float32) * out.astype(jnp.float32)
        coarse = product.astype(jnp.bfloat16)
        fine = (product - coarse.astype(jnp.float32)).astype(jnp.bfloat16)
        delta[chunk] = dot(coarse, ones) + dot(fine, ones)

        def back_step(i, carry):
            refs = (
                q_cols, do_rows, do_cols, keys, values, scores, top, delta, dq_acc, d_blocks
            )
            back_tile(i, i, chunk, width, refs)
            return carry

        lax.fori_loop(low, cut, back_step, 0)
        return carry

    lax.fori_loop(0, tok // CHUNK, chunk_step, 0)
    for k in range(ranks):
        at = pl.ds(pl.multiple_of((rank ^ k) * part_rows, part_rows), part_rows)
        out_parts[k][...] = o_ref[at, :]
    for k in range(2, back + 1):
        pair = jnp.maximum(last - k, 0)
        mine, other = 2 * pair + parity, 2 * pair + 1 - parity
        mine_ref, other_ref = (ref.at[k - 2] for ref in d_refs)
        put(d_blocks, mine, other, mine_ref, other_ref, width, scale)


def attend(doc_lengths, prepared, own, near, arrived, far, ranks, whole):
    chunks, rows, width = prepared[0].shape
    tok = chunks * CHUNK
    heads = rows // CHUNK
    back = len(arrived)
    tiles = 2 * (back + 1)
    span = tiles * tok
    vmem = pl.BlockSpec(memory_space=pltpu.VMEM)
    smem = pl.BlockSpec(memory_space=pltpu.SMEM)
    out_part = jax.ShapeDtypeStruct((tok // ranks, heads * width), jnp.bfloat16)
    row_state = jax.ShapeDtypeStruct((chunks, rows, width), jnp.float32)
    outputs = pl.pallas_call(
        functools.partial(
            attention_kernel,
            back=back,
            whole=whole,
            ranks=ranks,
            heads=heads,
            width=width,
            scale=1.0 / math.sqrt(width),
        ),
        out_shape=[out_part] * ranks
        + [
            jax.ShapeDtypeStruct((chunks, tiles, rows, TILE), jnp.float32),
            row_state,
            row_state,
            jax.ShapeDtypeStruct((span, width), jnp.bfloat16),
            jax.ShapeDtypeStruct((span, 2 * width), jnp.bfloat16),
            row_state,
        ]
        + [
            jax.ShapeDtypeStruct((back - 1, 2 * width, tok), dtype)
            for dtype in (jnp.float32, jnp.bfloat16)
        ],
        in_specs=[smem] + [vmem] * (6 + 2 * back),
        out_specs=[vmem] * (ranks + 8),
        scratch_shapes=[
            pltpu.VMEM((tok, heads * width), jnp.bfloat16),
            pltpu.VMEM((rows, 2 * width), jnp.float32),
            pltpu.VMEM((tiles, 2 * width, tok), jnp.float32),
        ],
        compiler_params=pltpu.CompilerParams(vmem_limit_bytes=KERNEL_VMEM),
        cost_estimate=pl.CostEstimate(
            flops=14 * tok * heads * width * span,
            bytes_accessed=4 * tok * heads * width * 2 + 4 * span * width * 2,
            transcendentals=tok * heads * span,
        ),
        name="attention",
    )(doc_lengths, *prepared, own, near, *arrived, *far)
    return outputs[:ranks], outputs[ranks : ranks + 6], outputs[ranks + 6 :]


def near_kernel(
    doc_ref,
    q_cols,
    do_rows,
    do_cols,
    scores,
    top,
    delta,
    keys,
    values,
    dq_far,
    dq_acc,
    mine1_ref,
    other1_ref,
    mine0_ref,
    other0_ref,
    d_blocks,
    *,
    back,
    whole,
    width,
    scale,
):
    tok = mine0_ref.shape[1]
    parity, last, base, own = here(tok, back, whole)
    cut = 2 * (last - 1)
    d_blocks[...] = jnp.zeros_like(d_blocks)
    dq_acc[...] = dq_far[...]

    def chunk_step(chunk, carry):
        t_first = base + own * TILE + chunk * CHUNK
        low = jnp.maximum(starts_in(doc_ref, t_first) - base, 0) // TILE

        def back_step(i, carry):
            refs = (
                q_cols, do_rows, do_cols, keys, values, scores, top, delta, dq_acc, d_blocks
            )
            back_tile(i, i - cut, chunk, width, refs)
            return carry

        lax.fori_loop(jnp.maximum(low, cut), own + 1, back_step, 0)
        return carry

    lax.fori_loop(0, tok // CHUNK, chunk_step, 0)
    put(d_blocks, parity, 1 - parity, mine1_ref.at[0], other1_ref.at[0], width, scale)
    put(d_blocks, 2 + parity, 3 - parity, mine0_ref, other0_ref, width, scale)


def attend_near(doc_lengths, prepared, state, back, whole):
    _, q_cols, do_rows, do_cols = prepared
    chunks, rows, width = do_rows.shape
    tok = chunks * CHUNK
    vmem = pl.BlockSpec(memory_space=pltpu.VMEM)
    smem = pl.BlockSpec(memory_space=pltpu.SMEM)
    return pl.pallas_call(
        functools.partial(
            near_kernel, back=back, whole=whole, width=width, scale=1.0 / math.sqrt(width)
        ),
        out_shape=[jax.ShapeDtypeStruct((chunks, rows, width), jnp.float32)]
        + [
            jax.ShapeDtypeStruct(shape, dtype)
            for shape in ((1, 2 * width, tok), (2 * width, tok))
            for dtype in (jnp.float32, jnp.bfloat16)
        ],
        in_specs=[smem] + [vmem] * 9,
        out_specs=[vmem] * 5,
        scratch_shapes=[pltpu.VMEM((4, 2 * width, tok), jnp.float32)],
        compiler_params=pltpu.CompilerParams(vmem_limit_bytes=KERNEL_VMEM),
        cost_estimate=pl.CostEstimate(
            flops=8 * chunks * rows * width * 4 * tok,
            bytes_accessed=4 * chunks * rows * width * 2,
            transcendentals=4 * chunks * rows * tok,
        ),
        name="near",
    )(doc_lengths, q_cols, do_rows, do_cols, *state)


def split_kernel(grad_ref, *part_refs):
    size = part_refs[0].shape[1]
    for k, ref in enumerate(part_refs):
        at = pl.multiple_of((lax.axis_index("head") ^ k) * size, size)
        ref[...] = grad_ref[:, pl.ds(at, size)]


def split(grad_attended, ranks):
    rows, columns = grad_attended.shape
    vmem = pl.BlockSpec(memory_space=pltpu.VMEM)
    part = jax.ShapeDtypeStruct((rows, columns // ranks), grad_attended.dtype)
    return pl.pallas_call(
        split_kernel,
        out_shape=[part] * ranks,
        in_specs=[vmem],
        out_specs=[vmem] * ranks,
        compiler_params=pltpu.CompilerParams(vmem_limit_bytes=SMALL_VMEM),
        name="split",
    )(grad_attended)


def arrange_kernel(doc_ref, q_ref, lengths_ref, rows_ref, cols_ref, wide):
    for i in range(doc_ref.shape[0]):
        lengths_ref[i] = doc_ref[i]
    small = unit(q_ref.shape[2])
    wide[...] = q_ref[...].astype(jnp.float32)
    for chunk in range(rows_ref.shape[0]):
        for j in range(q_ref.shape[1]):
            rows_ref[chunk, j * CHUNK : (j + 1) * CHUNK, :] = wide[
                chunk * CHUNK : (chunk + 1) * CHUNK, j, :
            ].astype(jnp.bfloat16)
        cols_ref[chunk] = dot_nt(small, rows_ref[chunk]).astype(jnp.bfloat16)


def arrange_grads_kernel(*refs):
    parts, (rows_ref, cols_ref, grads) = refs[:-3], refs[-3:]
    width = rows_ref.shape[2]
    small = unit(width)
    size = parts[0].shape[0]
    for k, ref in enumerate(parts):
        at = pl.multiple_of((lax.axis_index("head") ^ k) * size, size)
        grads[pl.ds(at, size), :] = ref[...]
    for chunk in range(rows_ref.shape[0]):
        for j in range(rows_ref.shape[1] // CHUNK):
            rows_ref[chunk, j * CHUNK : (j + 1) * CHUNK, :] = grads[
                chunk * CHUNK : (chunk + 1) * CHUNK, j * width : (j + 1) * width
            ]
        cols_ref[chunk] = dot_nt(small, rows_ref[chunk]).astype(jnp.bfloat16)


def arrange(kernel, arrays, shape, scratch, lengths=()):
    tok, heads, width = shape
    vmem = pl.BlockSpec(memory_space=pltpu.VMEM)
    smem = pl.BlockSpec(memory_space=pltpu.SMEM)
    chunks, rows = tok // CHUNK, heads * CHUNK
    return pl.pallas_call(
        kernel,
        out_shape=[jax.ShapeDtypeStruct(length.shape, length.dtype) for length in lengths]
        + [
            jax.ShapeDtypeStruct((chunks, rows, width), jnp.bfloat16),
            jax.ShapeDtypeStruct((chunks, width, rows), jnp.bfloat16),
        ],
        in_specs=[smem] * len(lengths) + [vmem] * len(arrays),
        out_specs=[smem] * len(lengths) + [vmem, vmem],
        scratch_shapes=[scratch],
        compiler_params=pltpu.CompilerParams(vmem_limit_bytes=SMALL_VMEM),
        name="arrange",
    )(*lengths, *arrays)


def join_kernel(*refs):
    parts, (rows_ref, out_ref, dq_ref, wide) = refs[:-4], refs[-4:]
    size = parts[0].shape[1]
    for k, ref in enumerate(parts):
        at = pl.multiple_of((lax.axis_index("head") ^ k) * size, size)
        out_ref[:, pl.ds(at, size)] = ref[...]
    scale = 1.0 / math.sqrt(rows_ref.shape[2])
    for chunk in range(rows_ref.shape[0]):
        for j in range(dq_ref.shape[1]):
            wide[chunk * CHUNK : (chunk + 1) * CHUNK, j, :] = (
                rows_ref[chunk, j * CHUNK : (j + 1) * CHUNK, :] * scale
            )
    dq_ref[...] = wide[...].astype(jnp.bfloat16)


def join(parts, dq_rows, shape):
    rows, size = parts[0].shape
    vmem = pl.BlockSpec(memory_space=pltpu.VMEM)
    return pl.pallas_call(
        join_kernel,
        out_shape=(
            jax.ShapeDtypeStruct((rows, size * len(parts)), parts[0].dtype),
            jax.ShapeDtypeStruct(shape, jnp.bfloat16),
        ),
        in_specs=[vmem] * (len(parts) + 1),
        out_specs=(vmem, vmem),
        scratch_shapes=[pltpu.VMEM(shape, jnp.float32)],
        compiler_params=pltpu.CompilerParams(vmem_limit_bytes=SMALL_VMEM),
        name="join",
    )(*parts, dq_rows)


def merge_kernel(mine_ref, other_ref, *block_refs):
    for k, ref in enumerate(block_refs):
        ref[...] = (mine_ref[k] + other_ref[k].astype(jnp.float32)).astype(ref.dtype)


def merge(mine, other):
    vmem = pl.BlockSpec(memory_space=pltpu.VMEM)
    block = jax.ShapeDtypeStruct(mine.shape[1:], jnp.bfloat16)
    return pl.pallas_call(
        merge_kernel,
        out_shape=[block] * mine.shape[0],
        in_specs=[vmem, vmem],
        out_specs=[vmem] * mine.shape[0],
        compiler_params=pltpu.CompilerParams(vmem_limit_bytes=SMALL_VMEM),
        name="merge",
    )(mine, other)


def finish_kernel(own_ref, *refs):
    arrived = refs[:-2]
    dk_ref, dv_ref = refs[-2:]
    total = own_ref[...]
    for ref in arrived:
        total = total + ref[...].astype(jnp.float32)
    total = total.astype(jnp.bfloat16)
    width = dk_ref.shape[1]
    large = unit(dk_ref.shape[0])
    dk_ref[...] = dot_nt(large, total[:width]).astype(jnp.bfloat16)
    dv_ref[...] = dot_nt(large, total[width:]).astype(jnp.bfloat16)


def finish(own_part, arrived):
    both, tok = own_part.shape
    vmem = pl.BlockSpec(memory_space=pltpu.VMEM)
    shape = jax.ShapeDtypeStruct((tok, both // 2), jnp.bfloat16)
    return pl.pallas_call(
        finish_kernel,
        out_shape=(shape, shape),
        in_specs=[vmem] * (1 + len(arrived)),
        out_specs=(vmem, vmem),
        compiler_params=pltpu.CompilerParams(vmem_limit_bytes=SMALL_VMEM),
        name="finish",
    )(own_part, *arrived)


def shifted(block, by, count):
    pairs = [(i, i + by) for i in range(count) if 0 <= i + by < count]
    return lax.ppermute(block, "ctx", pairs)


def exchanged(block, axis, by):
    return lax.ppermute(block, axis, [(i, i ^ by) for i in range(lax.axis_size(axis))])


def after(value, *others):
    return lax.optimization_barrier((value, *others))


def body(queries, key_states, value_states, doc_lengths, grad_attended):
    tok, heads, width = queries.shape
    count = lax.axis_size("ctx")
    ranks = lax.axis_size("head")
    reach = min((DOC_MOST + tok - 2) // tok, count - 1)
    back = min((reach + 1) // 2, count // 2 - 1)
    whole = count == 8 and back == 3 and ranks == 4
    own = jnp.concatenate(
        [key_states.reshape(tok, width), value_states.reshape(tok, width)], axis=0
    )
    near = exchanged(own, "ctx", 1)
    if whole:
        beside = exchanged(own, "ctx", 2)
        across = exchanged(own, "ctx", 4)
    else:
        arrived = [shifted(own, 2 * k, count) for k in range(1, back + 1)]
    grads = split(grad_attended, ranks)
    grads = [part if k == 0 else exchanged(part, "head", k) for k, part in enumerate(grads)]
    if whole:
        far_beside = exchanged(beside, "ctx", 1)
        passed = exchanged(across, "ctx", 2)
        far_across = exchanged(across, "ctx", 1)
        passed, far_beside, near, *grads[1:] = after(passed, far_beside, near, *grads[1:])
        far_passed = exchanged(passed, "ctx", 1)
        arrived = [beside, across, passed]
        far = [far_beside, far_across, far_passed]
    else:
        far = [exchanged(block, "ctx", 1) for block in arrived]
    doc_lengths, *prepared = arrange(
        arrange_kernel,
        [queries],
        queries.shape,
        pltpu.VMEM(queries.shape, jnp.float32),
        [doc_lengths],
    )
    prepared += arrange(
        arrange_grads_kernel,
        grads,
        queries.shape,
        pltpu.VMEM((tok, heads * width), jnp.bfloat16),
    )
    outs, state, parts = attend(doc_lengths, prepared, own, near, arrived, far, ranks, whole)
    outs, (mine_far, other_far) = list(outs), parts
    dq_rows, mine1, other1, mine0, other0 = attend_near(
        doc_lengths, prepared, state, back, whole
    )
    other_far = exchanged(other_far, "ctx", 1)
    outs[1:2] = [exchanged(part, "head", 1) for part in outs[1:2]]
    other_far, mine0, *outs[1:2] = after(other_far, mine0, *outs[1:2])
    blocks = list(merge(mine_far, other_far))
    other1, blocks[-1] = after(other1, blocks[-1])
    other1 = exchanged(other1, "ctx", 1)
    outs[2:] = [exchanged(part, "head", k + 2) for k, part in enumerate(outs[2:])]
    returned = [shifted(block, -2 * (k + 2), count) for k, block in enumerate(blocks)]
    other0, other1 = after(other0, other1)
    other0 = exchanged(other0, "ctx", 1)
    (block,) = merge(mine1, other1)
    returned.append(shifted(block, -2, count))
    grad_keys, grad_values = finish(mine0, [other0] + returned)
    attended, grad_queries = join(outs, dq_rows, queries.shape)
    grad_keys = grad_keys.reshape(tok, 1, width)
    grad_values = grad_values.reshape(tok, 1, width)
    return attended, grad_queries, grad_keys, grad_values


def solution(mesh):
    in_specs = (
        P("ctx", "head", None),
        P("ctx", "head", None),
        P("ctx", "head", None),
        P(),
        P(("ctx", "head"), None),
    )
    out_specs = (
        P(("ctx", "head"), None),
        P("ctx", "head", None),
        P("ctx", "head", None),
        P("ctx", "head", None),
    )
    return jax.shard_map(body, mesh=mesh, in_specs=in_specs, out_specs=out_specs, check_vma=False)
```

```python
import functools
import math

import jax
import jax.numpy as jnp
from jax import lax
from jax.experimental import pallas as pl
from jax.experimental.pallas import tpu as pltpu
from jax.sharding import PartitionSpec as P

DOC_MOST = 1792
NEG_FILL = -1e30
TILE = 256
CHUNK = 128
LOG2_E = 1.4426950408889634
SMALL_VMEM = 8 * 1024 * 1024
KERNEL_VMEM = 16 * 1024 * 1024


def dot(a, b):
    return jnp.dot(a, b, preferred_element_type=jnp.float32)


def dot_nt(a, b):
    return lax.dot_general(a, b, (((1,), (1,)), ((), ())), preferred_element_type=jnp.float32)


def unit(size):
    rows = lax.broadcasted_iota(jnp.int32, (size, size), 0)
    return (rows == lax.broadcasted_iota(jnp.int32, (size, size), 1)).astype(jnp.bfloat16)


def twice(column):
    return jnp.concatenate([column, column], axis=1)


def starts_in(doc_ref, positions):
    found = jnp.zeros_like(positions)
    for i in range(doc_ref.shape[0]):
        found = jnp.where(positions >= doc_ref[i], doc_ref[i], found)
    return found


def here(tok, back, whole):
    ctx = lax.axis_index("ctx")
    parity = lax.rem(ctx, 2)
    last = ctx // 2 if whole else back
    base = 0 if whole else (ctx - parity - 2 * back) * tok
    return parity, last, base, 2 * last + parity


def back_tile(i, slot, chunk, width, refs):
    q_cols, do_rows, do_cols, keys, values, scores, top, delta, dq_acc, d_blocks = refs
    at = pl.ds(pl.multiple_of(i * TILE, TILE), TILE)
    probs = jnp.exp2(scores[chunk, i] - twice(top[chunk]))
    d_probs = dot_nt(do_rows[chunk], values[at, 0:width])
    d_scores = (probs * (d_probs - twice(delta[chunk]))).astype(jnp.bfloat16)
    dq_acc[chunk] += dot(d_scores, keys[at, :])
    d_blocks[slot, 0:width, :] += dot(q_cols[chunk], d_scores)
    d_blocks[slot, width:, :] += dot(do_cols[chunk], probs.astype(jnp.bfloat16))


def put(d_blocks, mine, other, mine_ref, other_ref, width, scale):
    mine_ref[0:width, :] = d_blocks[mine, 0:width, :] * scale
    mine_ref[width:, :] = d_blocks[mine, width:, :]
    other_ref[0:width, :] = (d_blocks[other, 0:width, :] * scale).astype(jnp.bfloat16)
    other_ref[width:, :] = d_blocks[other, width:, :].astype(jnp.bfloat16)


def attention_kernel(
    doc_ref,
    q_rows,
    q_cols,
    do_rows,
    do_cols,
    own_ref,
    near_ref,
    *refs,
    back,
    whole,
    ranks,
    heads,
    width,
    scale,
):
    arrived, far, refs = refs[:back], refs[back : 2 * back], refs[2 * back :]
    out_parts, refs = refs[:ranks], refs[ranks:]
    (lows_ref, scores, top, delta, keys, values, dq_acc), refs = refs[:7], refs[7:]
    d_refs, (o_ref, accum, d_blocks) = refs[:-3], refs[-3:]
    tok = own_ref.shape[0] // 2
    part_rows = tok // ranks
    rank = lax.axis_index("head")
    parity, last, base, own = here(tok, back, whole)
    cut = 2 * (last - 1)
    ones = jnp.ones((width, width), jnp.bfloat16)

    values[:, width:] = jnp.ones_like(values[:, width:])
    for k in range(back + 1):
        pair = last ^ k if whole else last - k
        mine, other = (own_ref, near_ref) if k == 0 else (arrived[k - 1], far[k - 1])
        for ref, place in ((mine, 2 * pair + parity), (other, 2 * pair + 1 - parity)):
            at = pl.ds(pl.multiple_of(place * tok, tok), tok)
            keys[at, :] = ref[0:tok, :]
            values[at, 0:width] = ref[tok:, :]
    d_blocks[...] = jnp.zeros_like(d_blocks)
    top[...] = jnp.full_like(top, NEG_FILL)
    dq_acc[...] = jnp.zeros_like(dq_acc)

    def chunk_step(chunk, carry):
        rows_at = pl.ds(pl.multiple_of(chunk * CHUNK, CHUNK), CHUNK)
        t_first = base + own * TILE + chunk * CHUNK
        t_last = t_first + CHUNK - 1
        t_col = t_first + lax.broadcasted_iota(jnp.int32, (CHUNK, width), 0)
        start_col = starts_in(doc_ref, t_col)
        low = jnp.maximum(starts_in(doc_ref, t_first) - base, 0) // TILE
        lows_ref[chunk] = low
        clear = jnp.clip((starts_in(doc_ref, t_last) - base + TILE - 1) // TILE, low, own)

        def score_tile(i, masked):
            at = pl.ds(pl.multiple_of(i * TILE, TILE), TILE)
            tile = dot_nt(q_rows[chunk], keys[at, :]) * (scale * LOG2_E)
            if masked:
                s_row = base + i * TILE + lax.broadcasted_iota(jnp.int32, (CHUNK, TILE), 1)
                live = (s_row >= twice(start_col)) & (s_row <= twice(t_col))
                tile = jnp.concatenate(
                    [
                        jnp.where(live, tile[j * CHUNK : (j + 1) * CHUNK], NEG_FILL)
                        for j in range(heads)
                    ],
                    axis=0,
                )
            scores[chunk, i] = tile
            top[chunk] = jnp.maximum(top[chunk], jnp.maximum(tile[:, :width], tile[:, width:]))

        def edge_step(n, carry):
            score_tile(jnp.where(n < clear - low, low + n, own), True)
            return carry

        def inner_step(i, carry):
            score_tile(i, False)
            return carry

        lax.fori_loop(0, clear - low + 1, edge_step, 0)
        lax.fori_loop(clear, own, inner_step, 0)
        top[chunk] = jnp.broadcast_to(jnp.max(top[chunk], axis=1, keepdims=True), top.shape[1:])
        accum[...] = jnp.zeros_like(accum)

        def weigh_step(i, carry):
            at = pl.ds(pl.multiple_of(i * TILE, TILE), TILE)
            weights = jnp.exp2(scores[chunk, i] - twice(top[chunk])).astype(jnp.bfloat16)
            accum[...] += dot(weights, values[at, :])
            return carry

        lax.fori_loop(low, own + 1, weigh_step, 0)
        total = accum[:, width:]
        out = (accum[:, 0:width] / total).astype(jnp.bfloat16)
        for j in range(heads):
            o_ref[rows_at, j * width : (j + 1) * width] = out[j * CHUNK : (j + 1) * CHUNK]
        top[chunk] = top[chunk] + jnp.log2(total)
        product = do_rows[chunk].astype(jnp.float32) * out.astype(jnp.float32)
        coarse = product.astype(jnp.bfloat16)
        fine = (product - coarse.astype(jnp.float32)).astype(jnp.bfloat16)
        delta[chunk] = dot(coarse, ones) + dot(fine, ones)

        def back_step(i, carry):
            refs = (
                q_cols, do_rows, do_cols, keys, values, scores, top, delta, dq_acc, d_blocks
            )
            back_tile(i, i, chunk, width, refs)
            return carry

        lax.fori_loop(low, cut, back_step, 0)
        return carry

    lax.fori_loop(0, tok // CHUNK, chunk_step, 0)
    for k in range(ranks):
        at = pl.ds(pl.multiple_of((rank ^ k) * part_rows, part_rows), part_rows)
        out_parts[k][...] = o_ref[at, :]
    for k in range(2, back + 1):
        pair = jnp.maximum(last - k, 0)
        mine, other = 2 * pair + parity, 2 * pair + 1 - parity
        mine_ref, other_ref = (ref.at[k - 2] for ref in d_refs)
        put(d_blocks, mine, other, mine_ref, other_ref, width, scale)


def attend(doc_ends, prepared, own, near, arrived, far, ranks, whole):
    chunks, rows, width = prepared[0].shape
    tok = chunks * CHUNK
    heads = rows // CHUNK
    back = len(arrived)
    tiles = 2 * (back + 1)
    span = tiles * tok
    vmem = pl.BlockSpec(memory_space=pltpu.VMEM)
    smem = pl.BlockSpec(memory_space=pltpu.SMEM)
    out_part = jax.ShapeDtypeStruct((tok // ranks, heads * width), jnp.bfloat16)
    row_state = jax.ShapeDtypeStruct((chunks, rows, width), jnp.float32)
    outputs = pl.pallas_call(
        functools.partial(
            attention_kernel,
            back=back,
            whole=whole,
            ranks=ranks,
            heads=heads,
            width=width,
            scale=1.0 / math.sqrt(width),
        ),
        out_shape=[out_part] * ranks
        + [
            jax.ShapeDtypeStruct((chunks,), jnp.int32),
            jax.ShapeDtypeStruct((chunks, tiles, rows, TILE), jnp.float32),
            row_state,
            row_state,
            jax.ShapeDtypeStruct((span, width), jnp.bfloat16),
            jax.ShapeDtypeStruct((span, 2 * width), jnp.bfloat16),
            row_state,
        ]
        + [
            jax.ShapeDtypeStruct((back - 1, 2 * width, tok), dtype)
            for dtype in (jnp.float32, jnp.bfloat16)
        ],
        in_specs=[smem] + [vmem] * (6 + 2 * back),
        out_specs=[vmem] * ranks + [smem] + [vmem] * 8,
        scratch_shapes=[
            pltpu.VMEM((tok, heads * width), jnp.bfloat16),
            pltpu.VMEM((rows, 2 * width), jnp.float32),
            pltpu.VMEM((tiles, 2 * width, tok), jnp.float32),
        ],
        compiler_params=pltpu.CompilerParams(vmem_limit_bytes=KERNEL_VMEM),
        cost_estimate=pl.CostEstimate(
            flops=14 * tok * heads * width * span,
            bytes_accessed=4 * tok * heads * width * 2 + 4 * span * width * 2,
            transcendentals=tok * heads * span,
        ),
        name="attention",
    )(doc_ends, *prepared, own, near, *arrived, *far)
    return outputs[:ranks], outputs[ranks : ranks + 7], outputs[ranks + 7 :]


def near_kernel(
    q_cols,
    do_rows,
    do_cols,
    lows_ref,
    scores,
    top,
    delta,
    keys,
    values,
    dq_far,
    dq_acc,
    mine1_ref,
    other1_ref,
    mine0_ref,
    other0_ref,
    d_blocks,
    *,
    back,
    whole,
    width,
    scale,
):
    tok = mine0_ref.shape[1]
    parity, last, _, own = here(tok, back, whole)
    cut = 2 * (last - 1)
    d_blocks[...] = jnp.zeros_like(d_blocks)
    dq_acc[...] = dq_far[...]

    def chunk_step(chunk, carry):
        low = lows_ref[chunk]

        def back_step(i, carry):
            refs = (
                q_cols, do_rows, do_cols, keys, values, scores, top, delta, dq_acc, d_blocks
            )
            back_tile(i, i - cut, chunk, width, refs)
            return carry

        lax.fori_loop(jnp.maximum(low, cut), own + 1, back_step, 0)
        return carry

    lax.fori_loop(0, tok // CHUNK, chunk_step, 0)
    put(d_blocks, parity, 1 - parity, mine1_ref.at[0], other1_ref.at[0], width, scale)
    put(d_blocks, 2 + parity, 3 - parity, mine0_ref, other0_ref, width, scale)


def attend_near(prepared, state, back, whole):
    _, q_cols, do_rows, do_cols = prepared
    chunks, rows, width = do_rows.shape
    tok = chunks * CHUNK
    vmem = pl.BlockSpec(memory_space=pltpu.VMEM)
    smem = pl.BlockSpec(memory_space=pltpu.SMEM)
    return pl.pallas_call(
        functools.partial(
            near_kernel, back=back, whole=whole, width=width, scale=1.0 / math.sqrt(width)
        ),
        out_shape=[jax.ShapeDtypeStruct((chunks, rows, width), jnp.float32)]
        + [
            jax.ShapeDtypeStruct(shape, dtype)
            for shape in ((1, 2 * width, tok), (2 * width, tok))
            for dtype in (jnp.float32, jnp.bfloat16)
        ],
        in_specs=[vmem] * 3 + [smem] + [vmem] * 6,
        out_specs=[vmem] * 5,
        scratch_shapes=[pltpu.VMEM((4, 2 * width, tok), jnp.float32)],
        compiler_params=pltpu.CompilerParams(vmem_limit_bytes=KERNEL_VMEM),
        cost_estimate=pl.CostEstimate(
            flops=8 * chunks * rows * width * 4 * tok,
            bytes_accessed=4 * chunks * rows * width * 2,
            transcendentals=4 * chunks * rows * tok,
        ),
        name="near",
    )(q_cols, do_rows, do_cols, *state)


def split_kernel(grad_ref, *part_refs):
    size = part_refs[0].shape[1]
    for k, ref in enumerate(part_refs):
        at = pl.multiple_of((lax.axis_index("head") ^ k) * size, size)
        ref[...] = grad_ref[:, pl.ds(at, size)]


def split(grad_attended, ranks):
    rows, columns = grad_attended.shape
    vmem = pl.BlockSpec(memory_space=pltpu.VMEM)
    part = jax.ShapeDtypeStruct((rows, columns // ranks), grad_attended.dtype)
    return pl.pallas_call(
        split_kernel,
        out_shape=[part] * ranks,
        in_specs=[vmem],
        out_specs=[vmem] * ranks,
        compiler_params=pltpu.CompilerParams(vmem_limit_bytes=SMALL_VMEM),
        name="split",
    )(grad_attended)


def arrange_kernel(q_ref, rows_ref, cols_ref, wide):
    small = unit(q_ref.shape[2])
    wide[...] = q_ref[...].astype(jnp.float32)
    for chunk in range(rows_ref.shape[0]):
        for j in range(q_ref.shape[1]):
            rows_ref[chunk, j * CHUNK : (j + 1) * CHUNK, :] = wide[
                chunk * CHUNK : (chunk + 1) * CHUNK, j, :
            ].astype(jnp.bfloat16)
        cols_ref[chunk] = dot_nt(small, rows_ref[chunk]).astype(jnp.bfloat16)


def arrange_grads_kernel(*refs):
    parts, (rows_ref, cols_ref, grads) = refs[:-3], refs[-3:]
    width = rows_ref.shape[2]
    small = unit(width)
    size = parts[0].shape[0]
    for k, ref in enumerate(parts):
        at = pl.multiple_of((lax.axis_index("head") ^ k) * size, size)
        grads[pl.ds(at, size), :] = ref[...]
    for chunk in range(rows_ref.shape[0]):
        for j in range(rows_ref.shape[1] // CHUNK):
            rows_ref[chunk, j * CHUNK : (j + 1) * CHUNK, :] = grads[
                chunk * CHUNK : (chunk + 1) * CHUNK, j * width : (j + 1) * width
            ]
        cols_ref[chunk] = dot_nt(small, rows_ref[chunk]).astype(jnp.bfloat16)


def arrange(kernel, arrays, shape, scratch):
    tok, heads, width = shape
    vmem = pl.BlockSpec(memory_space=pltpu.VMEM)
    chunks, rows = tok // CHUNK, heads * CHUNK
    return pl.pallas_call(
        kernel,
        out_shape=[
            jax.ShapeDtypeStruct((chunks, rows, width), jnp.bfloat16),
            jax.ShapeDtypeStruct((chunks, width, rows), jnp.bfloat16),
        ],
        in_specs=[vmem] * len(arrays),
        out_specs=[vmem, vmem],
        scratch_shapes=[scratch],
        compiler_params=pltpu.CompilerParams(vmem_limit_bytes=SMALL_VMEM),
        name="arrange",
    )(*arrays)


def join_kernel(*refs):
    parts, (rows_ref, out_ref, dq_ref, wide) = refs[:-4], refs[-4:]
    size = parts[0].shape[1]
    for k, ref in enumerate(parts):
        at = pl.multiple_of((lax.axis_index("head") ^ k) * size, size)
        out_ref[:, pl.ds(at, size)] = ref[...]
    scale = 1.0 / math.sqrt(rows_ref.shape[2])
    for chunk in range(rows_ref.shape[0]):
        for j in range(dq_ref.shape[1]):
            wide[chunk * CHUNK : (chunk + 1) * CHUNK, j, :] = (
                rows_ref[chunk, j * CHUNK : (j + 1) * CHUNK, :] * scale
            )
    dq_ref[...] = wide[...].astype(jnp.bfloat16)


def join(parts, dq_rows, shape):
    rows, size = parts[0].shape
    vmem = pl.BlockSpec(memory_space=pltpu.VMEM)
    return pl.pallas_call(
        join_kernel,
        out_shape=(
            jax.ShapeDtypeStruct((rows, size * len(parts)), parts[0].dtype),
            jax.ShapeDtypeStruct(shape, jnp.bfloat16),
        ),
        in_specs=[vmem] * (len(parts) + 1),
        out_specs=(vmem, vmem),
        scratch_shapes=[pltpu.VMEM(shape, jnp.float32)],
        compiler_params=pltpu.CompilerParams(vmem_limit_bytes=SMALL_VMEM),
        name="join",
    )(*parts, dq_rows)


def merge_kernel(mine_ref, other_ref, *block_refs):
    for k, ref in enumerate(block_refs):
        ref[...] = (mine_ref[k] + other_ref[k].astype(jnp.float32)).astype(ref.dtype)


def merge(mine, other):
    vmem = pl.BlockSpec(memory_space=pltpu.VMEM)
    block = jax.ShapeDtypeStruct(mine.shape[1:], jnp.bfloat16)
    return pl.pallas_call(
        merge_kernel,
        out_shape=[block] * mine.shape[0],
        in_specs=[vmem, vmem],
        out_specs=[vmem] * mine.shape[0],
        compiler_params=pltpu.CompilerParams(vmem_limit_bytes=SMALL_VMEM),
        name="merge",
    )(mine, other)


def finish_kernel(own_ref, *refs):
    arrived = refs[:-2]
    dk_ref, dv_ref = refs[-2:]
    total = own_ref[...]
    for ref in arrived:
        total = total + ref[...].astype(jnp.float32)
    total = total.astype(jnp.bfloat16)
    width = dk_ref.shape[1]
    large = unit(dk_ref.shape[0])
    dk_ref[...] = dot_nt(large, total[:width]).astype(jnp.bfloat16)
    dv_ref[...] = dot_nt(large, total[width:]).astype(jnp.bfloat16)


def finish(own_part, arrived):
    both, tok = own_part.shape
    vmem = pl.BlockSpec(memory_space=pltpu.VMEM)
    shape = jax.ShapeDtypeStruct((tok, both // 2), jnp.bfloat16)
    return pl.pallas_call(
        finish_kernel,
        out_shape=(shape, shape),
        in_specs=[vmem] * (1 + len(arrived)),
        out_specs=(vmem, vmem),
        compiler_params=pltpu.CompilerParams(vmem_limit_bytes=SMALL_VMEM),
        name="finish",
    )(own_part, *arrived)


def shifted(block, by, count):
    pairs = [(i, i + by) for i in range(count) if 0 <= i + by < count]
    return lax.ppermute(block, "ctx", pairs)


def exchanged(block, axis, by):
    return lax.ppermute(block, axis, [(i, i ^ by) for i in range(lax.axis_size(axis))])


def after(value, *others):
    return lax.optimization_barrier((value, *others))


def body(queries, key_states, value_states, doc_lengths, grad_attended):
    tok, heads, width = queries.shape
    count = lax.axis_size("ctx")
    ranks = lax.axis_size("head")
    reach = min((DOC_MOST + tok - 2) // tok, count - 1)
    back = min((reach + 1) // 2, count // 2 - 1)
    whole = count == 8 and back == 3 and ranks == 4
    docs = jnp.arange(doc_lengths.shape[0])
    doc_ends = jnp.sum(jnp.where(docs[None] <= docs[:, None], doc_lengths[None], 0), axis=1)
    own = jnp.concatenate(
        [key_states.reshape(tok, width), value_states.reshape(tok, width)], axis=0
    )
    near = exchanged(own, "ctx", 1)
    if whole:
        beside = exchanged(own, "ctx", 2)
        across = exchanged(own, "ctx", 4)
    else:
        arrived = [shifted(own, 2 * k, count) for k in range(1, back + 1)]
    grads = split(grad_attended, ranks)
    grads = [part if k == 0 else exchanged(part, "head", k) for k, part in enumerate(grads)]
    if whole:
        far_beside = exchanged(beside, "ctx", 1)
        passed = exchanged(across, "ctx", 2)
        far_across = exchanged(across, "ctx", 1)
        passed, doc_ends, far_beside, near, *grads[1:] = after(
            passed, doc_ends, far_beside, near, *grads[1:]
        )
        far_passed = exchanged(passed, "ctx", 1)
        arrived = [beside, across, passed]
        far = [far_beside, far_across, far_passed]
    else:
        far = [exchanged(block, "ctx", 1) for block in arrived]
    prepared = arrange(
        arrange_kernel, [queries], queries.shape, pltpu.VMEM(queries.shape, jnp.float32)
    )
    prepared += arrange(
        arrange_grads_kernel,
        grads,
        queries.shape,
        pltpu.VMEM((tok, heads * width), jnp.bfloat16),
    )
    outs, state, parts = attend(doc_ends, prepared, own, near, arrived, far, ranks, whole)
    outs, (mine_far, other_far) = list(outs), parts
    dq_rows, mine1, other1, mine0, other0 = attend_near(prepared, state, back, whole)
    other_far = exchanged(other_far, "ctx", 1)
    outs[1:2] = [exchanged(part, "head", 1) for part in outs[1:2]]
    other_far, mine0, *outs[1:2] = after(other_far, mine0, *outs[1:2])
    blocks = list(merge(mine_far, other_far))
    other1, blocks[-1] = after(other1, blocks[-1])
    other1 = exchanged(other1, "ctx", 1)
    outs[2:] = [exchanged(part, "head", k + 2) for k, part in enumerate(outs[2:])]
    returned = [shifted(block, -2 * (k + 2), count) for k, block in enumerate(blocks)]
    other0, other1 = after(other0, other1)
    other0 = exchanged(other0, "ctx", 1)
    (block,) = merge(mine1, other1)
    returned.append(shifted(block, -2, count))
    grad_keys, grad_values = finish(mine0, returned + [other0])
    attended, grad_queries = join(outs, dq_rows, queries.shape)
    grad_keys = grad_keys.reshape(tok, 1, width)
    grad_values = grad_values.reshape(tok, 1, width)
    return attended, grad_queries, grad_keys, grad_values


def solution(mesh):
    in_specs = (
        P("ctx", "head", None),
        P("ctx", "head", None),
        P("ctx", "head", None),
        P(),
        P(("ctx", "head"), None),
    )
    out_specs = (
        P(("ctx", "head"), None),
        P("ctx", "head", None),
        P("ctx", "head", None),
        P("ctx", "head", None),
    )
    return jax.shard_map(body, mesh=mesh, in_specs=in_specs, out_specs=out_specs, check_vma=False)
```

```python
import functools
import math

import jax
import jax.numpy as jnp
from jax import lax
from jax.experimental import pallas as pl
from jax.experimental.pallas import tpu as pltpu
from jax.sharding import PartitionSpec as P

DOC_MOST = 1792
NEG_FILL = -1e30
TILE = 256
CHUNK = 128
LOG2_E = 1.4426950408889634
SMALL_VMEM = 8 * 1024 * 1024
KERNEL_VMEM = 16 * 1024 * 1024


def dot(a, b):
    return jnp.dot(a, b, preferred_element_type=jnp.float32)


def dot_nt(a, b):
    return lax.dot_general(a, b, (((1,), (1,)), ((), ())), preferred_element_type=jnp.float32)


def unit(size):
    rows = lax.broadcasted_iota(jnp.int32, (size, size), 0)
    return (rows == lax.broadcasted_iota(jnp.int32, (size, size), 1)).astype(jnp.bfloat16)


def twice(column):
    return jnp.concatenate([column, column], axis=1)


def starts_in(doc_ref, positions):
    found = jnp.zeros_like(positions)
    for i in range(doc_ref.shape[0]):
        found = jnp.where(positions >= doc_ref[i], doc_ref[i], found)
    return found


def here(tok, back, whole):
    ctx = lax.axis_index("ctx")
    parity = lax.rem(ctx, 2)
    last = ctx // 2 if whole else back
    base = 0 if whole else (ctx - parity - 2 * back) * tok
    return parity, last, base, 2 * last + parity


def back_tile(i, slot, chunk, width, refs):
    q_cols, do_rows, do_cols, keys, values, scores, top, delta, dq_acc, d_blocks = refs
    at = pl.ds(pl.multiple_of(i * TILE, TILE), TILE)
    probs = jnp.exp2(scores[chunk, i] - twice(top[chunk]))
    d_probs = dot_nt(do_rows[chunk], values[at, 0:width])
    d_scores = (probs * (d_probs - twice(delta[chunk]))).astype(jnp.bfloat16)
    dq_acc[chunk] += dot(d_scores, keys[at, :])
    d_blocks[slot, 0:width, :] += dot(q_cols[chunk], d_scores)
    d_blocks[slot, width:, :] += dot(do_cols[chunk], probs.astype(jnp.bfloat16))


def put(d_blocks, mine, other, mine_ref, other_ref, width, scale):
    mine_ref[0:width, :] = d_blocks[mine, 0:width, :] * scale
    mine_ref[width:, :] = d_blocks[mine, width:, :]
    other_ref[0:width, :] = (d_blocks[other, 0:width, :] * scale).astype(jnp.bfloat16)
    other_ref[width:, :] = d_blocks[other, width:, :].astype(jnp.bfloat16)


def attention_kernel(
    doc_ref,
    q_rows,
    q_cols,
    do_rows,
    do_cols,
    own_ref,
    near_ref,
    *refs,
    back,
    whole,
    ranks,
    heads,
    width,
    scale,
):
    arrived, far, refs = refs[:back], refs[back : 2 * back], refs[2 * back :]
    out_parts, refs = refs[:ranks], refs[ranks:]
    (lows_ref, scores, top, delta, keys, values, dq_acc), refs = refs[:7], refs[7:]
    d_refs, (o_ref, accum, d_blocks) = refs[:-3], refs[-3:]
    tok = own_ref.shape[0] // 2
    part_rows = tok // ranks
    rank = lax.axis_index("head")
    parity, last, base, own = here(tok, back, whole)
    cut = 2 * (last - 1)
    ones = jnp.ones((width, width), jnp.bfloat16)

    values[:, width:] = jnp.ones_like(values[:, width:])
    for k in range(back + 1):
        pair = last ^ k if whole else last - k
        mine, other = (own_ref, near_ref) if k == 0 else (arrived[k - 1], far[k - 1])
        for ref, place in ((mine, 2 * pair + parity), (other, 2 * pair + 1 - parity)):
            at = pl.ds(pl.multiple_of(place * tok, tok), tok)
            keys[at, :] = ref[0:tok, :]
            values[at, 0:width] = ref[tok:, :]
    d_blocks[...] = jnp.zeros_like(d_blocks)
    top[...] = jnp.full_like(top, NEG_FILL)
    dq_acc[...] = jnp.zeros_like(dq_acc)

    def chunk_step(chunk, carry):
        rows_at = pl.ds(pl.multiple_of(chunk * CHUNK, CHUNK), CHUNK)
        t_first = base + own * TILE + chunk * CHUNK
        t_last = t_first + CHUNK - 1
        t_col = t_first + lax.broadcasted_iota(jnp.int32, (CHUNK, width), 0)
        start_col = starts_in(doc_ref, t_col)
        low = jnp.maximum(starts_in(doc_ref, t_first) - base, 0) // TILE
        lows_ref[chunk] = low
        clear = jnp.clip((starts_in(doc_ref, t_last) - base + TILE - 1) // TILE, low, own)

        def score_tile(i, masked):
            at = pl.ds(pl.multiple_of(i * TILE, TILE), TILE)
            tile = dot_nt(q_rows[chunk], keys[at, :]) * (scale * LOG2_E)
            if masked:
                s_row = base + i * TILE + lax.broadcasted_iota(jnp.int32, (CHUNK, TILE), 1)
                live = (s_row >= twice(start_col)) & (s_row <= twice(t_col))
                tile = jnp.concatenate(
                    [
                        jnp.where(live, tile[j * CHUNK : (j + 1) * CHUNK], NEG_FILL)
                        for j in range(heads)
                    ],
                    axis=0,
                )
            scores[chunk, i] = tile
            top[chunk] = jnp.maximum(top[chunk], jnp.maximum(tile[:, :width], tile[:, width:]))

        def edge_step(n, carry):
            score_tile(jnp.where(n < clear - low, low + n, own), True)
            return carry

        def inner_step(i, carry):
            score_tile(i, False)
            return carry

        lax.fori_loop(0, clear - low + 1, edge_step, 0)
        lax.fori_loop(clear, own, inner_step, 0)
        top[chunk] = jnp.broadcast_to(jnp.max(top[chunk], axis=1, keepdims=True), top.shape[1:])
        accum[...] = jnp.zeros_like(accum)

        def weigh_step(i, carry):
            at = pl.ds(pl.multiple_of(i * TILE, TILE), TILE)
            weights = jnp.exp2(scores[chunk, i] - twice(top[chunk])).astype(jnp.bfloat16)
            accum[...] += dot(weights, values[at, :])
            return carry

        lax.fori_loop(low, own + 1, weigh_step, 0)
        total = accum[:, width:]
        out = (accum[:, 0:width] / total).astype(jnp.bfloat16)
        for j in range(heads):
            o_ref[rows_at, j * width : (j + 1) * width] = out[j * CHUNK : (j + 1) * CHUNK]
        top[chunk] = top[chunk] + jnp.log2(total)
        product = do_rows[chunk].astype(jnp.float32) * out.astype(jnp.float32)
        coarse = product.astype(jnp.bfloat16)
        fine = (product - coarse.astype(jnp.float32)).astype(jnp.bfloat16)
        delta[chunk] = dot(coarse, ones) + dot(fine, ones)

        def back_step(i, carry):
            refs = (
                q_cols, do_rows, do_cols, keys, values, scores, top, delta, dq_acc, d_blocks
            )
            back_tile(i, i, chunk, width, refs)
            return carry

        lax.fori_loop(low, cut, back_step, 0)
        return carry

    lax.fori_loop(0, tok // CHUNK, chunk_step, 0)
    for k in range(ranks):
        at = pl.ds(pl.multiple_of((rank ^ k) * part_rows, part_rows), part_rows)
        out_parts[k][...] = o_ref[at, :]
    for k in range(2, back + 1):
        pair = jnp.maximum(last - k, 0)
        mine, other = 2 * pair + parity, 2 * pair + 1 - parity
        mine_ref, other_ref = (ref.at[k - 2] for ref in d_refs)
        put(d_blocks, mine, other, mine_ref, other_ref, width, scale)


def attend(doc_ends, prepared, own, near, arrived, far, ranks, whole):
    chunks, rows, width = prepared[0].shape
    tok = chunks * CHUNK
    heads = rows // CHUNK
    back = len(arrived)
    tiles = 2 * (back + 1)
    span = tiles * tok
    vmem = pl.BlockSpec(memory_space=pltpu.VMEM)
    smem = pl.BlockSpec(memory_space=pltpu.SMEM)
    out_part = jax.ShapeDtypeStruct((tok // ranks, heads * width), jnp.bfloat16)
    row_state = jax.ShapeDtypeStruct((chunks, rows, width), jnp.float32)
    outputs = pl.pallas_call(
        functools.partial(
            attention_kernel,
            back=back,
            whole=whole,
            ranks=ranks,
            heads=heads,
            width=width,
            scale=1.0 / math.sqrt(width),
        ),
        out_shape=[out_part] * ranks
        + [
            jax.ShapeDtypeStruct((chunks,), jnp.int32),
            jax.ShapeDtypeStruct((chunks, tiles, rows, TILE), jnp.float32),
            row_state,
            row_state,
            jax.ShapeDtypeStruct((span, width), jnp.bfloat16),
            jax.ShapeDtypeStruct((span, 2 * width), jnp.bfloat16),
            row_state,
        ]
        + [
            jax.ShapeDtypeStruct((back - 1, 2 * width, tok), dtype)
            for dtype in (jnp.float32, jnp.bfloat16)
        ],
        in_specs=[smem] + [vmem] * (6 + 2 * back),
        out_specs=[vmem] * ranks + [smem] + [vmem] * 8,
        scratch_shapes=[
            pltpu.VMEM((tok, heads * width), jnp.bfloat16),
            pltpu.VMEM((rows, 2 * width), jnp.float32),
            pltpu.VMEM((tiles, 2 * width, tok), jnp.float32),
        ],
        compiler_params=pltpu.CompilerParams(vmem_limit_bytes=KERNEL_VMEM),
        cost_estimate=pl.CostEstimate(
            flops=14 * tok * heads * width * span,
            bytes_accessed=4 * tok * heads * width * 2 + 4 * span * width * 2,
            transcendentals=tok * heads * span,
        ),
        name="attention",
    )(doc_ends, *prepared, own, near, *arrived, *far)
    return outputs[:ranks], outputs[ranks : ranks + 7], outputs[ranks + 7 :]


def near_kernel(
    q_cols,
    do_rows,
    do_cols,
    lows_ref,
    scores,
    top,
    delta,
    keys,
    values,
    dq_before,
    dq_acc,
    mine_ref,
    other_ref,
    d_blocks,
    *,
    distance,
    back,
    whole,
    width,
    scale,
):
    tok = mine_ref.shape[2]
    parity, last, _, own = here(tok, back, whole)
    first = 2 * (last - distance)
    d_blocks[...] = jnp.zeros_like(d_blocks)
    dq_acc[...] = dq_before[...]

    def chunk_step(chunk, carry):
        def back_step(i, carry):
            refs = (
                q_cols, do_rows, do_cols, keys, values, scores, top, delta, dq_acc, d_blocks
            )
            back_tile(i, i - first, chunk, width, refs)
            return carry

        stop = jnp.minimum(first + 2, own + 1)
        lax.fori_loop(jnp.maximum(lows_ref[chunk], first), stop, back_step, 0)
        return carry

    lax.fori_loop(0, tok // CHUNK, chunk_step, 0)
    put(d_blocks, parity, 1 - parity, mine_ref.at[0], other_ref.at[0], width, scale)


def attend_near(prepared, state, distance, back, whole):
    _, q_cols, do_rows, do_cols = prepared
    chunks, rows, width = do_rows.shape
    tok = chunks * CHUNK
    vmem = pl.BlockSpec(memory_space=pltpu.VMEM)
    smem = pl.BlockSpec(memory_space=pltpu.SMEM)
    return pl.pallas_call(
        functools.partial(
            near_kernel,
            distance=distance,
            back=back,
            whole=whole,
            width=width,
            scale=1.0 / math.sqrt(width),
        ),
        out_shape=[jax.ShapeDtypeStruct((chunks, rows, width), jnp.float32)]
        + [
            jax.ShapeDtypeStruct((1, 2 * width, tok), dtype)
            for dtype in (jnp.float32, jnp.bfloat16)
        ],
        in_specs=[vmem] * 3 + [smem] + [vmem] * 6,
        out_specs=[vmem] * 3,
        scratch_shapes=[pltpu.VMEM((2, 2 * width, tok), jnp.float32)],
        compiler_params=pltpu.CompilerParams(vmem_limit_bytes=KERNEL_VMEM),
        cost_estimate=pl.CostEstimate(
            flops=8 * chunks * rows * width * 2 * tok,
            bytes_accessed=4 * chunks * rows * width * 2,
            transcendentals=2 * chunks * rows * tok,
        ),
        name="near",
    )(q_cols, do_rows, do_cols, *state)


def split_kernel(grad_ref, *part_refs):
    size = part_refs[0].shape[1]
    for k, ref in enumerate(part_refs):
        at = pl.multiple_of((lax.axis_index("head") ^ k) * size, size)
        ref[...] = grad_ref[:, pl.ds(at, size)]


def split(grad_attended, ranks):
    rows, columns = grad_attended.shape
    vmem = pl.BlockSpec(memory_space=pltpu.VMEM)
    part = jax.ShapeDtypeStruct((rows, columns // ranks), grad_attended.dtype)
    return pl.pallas_call(
        split_kernel,
        out_shape=[part] * ranks,
        in_specs=[vmem],
        out_specs=[vmem] * ranks,
        compiler_params=pltpu.CompilerParams(vmem_limit_bytes=SMALL_VMEM),
        name="split",
    )(grad_attended)


def arrange_kernel(q_ref, rows_ref, cols_ref, wide):
    small = unit(q_ref.shape[2])
    wide[...] = q_ref[...].astype(jnp.float32)
    for chunk in range(rows_ref.shape[0]):
        for j in range(q_ref.shape[1]):
            rows_ref[chunk, j * CHUNK : (j + 1) * CHUNK, :] = wide[
                chunk * CHUNK : (chunk + 1) * CHUNK, j, :
            ].astype(jnp.bfloat16)
        cols_ref[chunk] = dot_nt(small, rows_ref[chunk]).astype(jnp.bfloat16)


def arrange_grads_kernel(*refs):
    parts, (rows_ref, cols_ref, grads) = refs[:-3], refs[-3:]
    width = rows_ref.shape[2]
    small = unit(width)
    size = parts[0].shape[0]
    for k, ref in enumerate(parts):
        at = pl.multiple_of((lax.axis_index("head") ^ k) * size, size)
        grads[pl.ds(at, size), :] = ref[...]
    for chunk in range(rows_ref.shape[0]):
        for j in range(rows_ref.shape[1] // CHUNK):
            rows_ref[chunk, j * CHUNK : (j + 1) * CHUNK, :] = grads[
                chunk * CHUNK : (chunk + 1) * CHUNK, j * width : (j + 1) * width
            ]
        cols_ref[chunk] = dot_nt(small, rows_ref[chunk]).astype(jnp.bfloat16)


def arrange(kernel, arrays, shape, scratch):
    tok, heads, width = shape
    vmem = pl.BlockSpec(memory_space=pltpu.VMEM)
    chunks, rows = tok // CHUNK, heads * CHUNK
    return pl.pallas_call(
        kernel,
        out_shape=[
            jax.ShapeDtypeStruct((chunks, rows, width), jnp.bfloat16),
            jax.ShapeDtypeStruct((chunks, width, rows), jnp.bfloat16),
        ],
        in_specs=[vmem] * len(arrays),
        out_specs=[vmem, vmem],
        scratch_shapes=[scratch],
        compiler_params=pltpu.CompilerParams(vmem_limit_bytes=SMALL_VMEM),
        name="arrange",
    )(*arrays)


def join_kernel(*refs):
    parts, (rows_ref, out_ref, dq_ref, wide) = refs[:-4], refs[-4:]
    size = parts[0].shape[1]
    for k, ref in enumerate(parts):
        at = pl.multiple_of((lax.axis_index("head") ^ k) * size, size)
        out_ref[:, pl.ds(at, size)] = ref[...]
    scale = 1.0 / math.sqrt(rows_ref.shape[2])
    for chunk in range(rows_ref.shape[0]):
        for j in range(dq_ref.shape[1]):
            wide[chunk * CHUNK : (chunk + 1) * CHUNK, j, :] = (
                rows_ref[chunk, j * CHUNK : (j + 1) * CHUNK, :] * scale
            )
    dq_ref[...] = wide[...].astype(jnp.bfloat16)


def join(parts, dq_rows, shape):
    rows, size = parts[0].shape
    vmem = pl.BlockSpec(memory_space=pltpu.VMEM)
    return pl.pallas_call(
        join_kernel,
        out_shape=(
            jax.ShapeDtypeStruct((rows, size * len(parts)), parts[0].dtype),
            jax.ShapeDtypeStruct(shape, jnp.bfloat16),
        ),
        in_specs=[vmem] * (len(parts) + 1),
        out_specs=(vmem, vmem),
        scratch_shapes=[pltpu.VMEM(shape, jnp.float32)],
        compiler_params=pltpu.CompilerParams(vmem_limit_bytes=SMALL_VMEM),
        name="join",
    )(*parts, dq_rows)


def merge_kernel(mine_ref, other_ref, *block_refs):
    for k, ref in enumerate(block_refs):
        ref[...] = (mine_ref[k] + other_ref[k].astype(jnp.float32)).astype(ref.dtype)


def merge(mine, other):
    vmem = pl.BlockSpec(memory_space=pltpu.VMEM)
    block = jax.ShapeDtypeStruct(mine.shape[1:], jnp.bfloat16)
    return pl.pallas_call(
        merge_kernel,
        out_shape=[block] * mine.shape[0],
        in_specs=[vmem, vmem],
        out_specs=[vmem] * mine.shape[0],
        compiler_params=pltpu.CompilerParams(vmem_limit_bytes=SMALL_VMEM),
        name="merge",
    )(mine, other)


def finish_kernel(own_ref, *refs):
    arrived = refs[:-2]
    dk_ref, dv_ref = refs[-2:]
    total = own_ref[...]
    for ref in arrived:
        total = total + ref[...].astype(jnp.float32)
    total = total.astype(jnp.bfloat16)
    width = dk_ref.shape[1]
    large = unit(dk_ref.shape[0])
    dk_ref[...] = dot_nt(large, total[:width]).astype(jnp.bfloat16)
    dv_ref[...] = dot_nt(large, total[width:]).astype(jnp.bfloat16)


def finish(own_part, arrived):
    both, tok = own_part.shape
    vmem = pl.BlockSpec(memory_space=pltpu.VMEM)
    shape = jax.ShapeDtypeStruct((tok, both // 2), jnp.bfloat16)
    return pl.pallas_call(
        finish_kernel,
        out_shape=(shape, shape),
        in_specs=[vmem] * (1 + len(arrived)),
        out_specs=(vmem, vmem),
        compiler_params=pltpu.CompilerParams(vmem_limit_bytes=SMALL_VMEM),
        name="finish",
    )(own_part, *arrived)


def shifted(block, by, count):
    pairs = [(i, i + by) for i in range(count) if 0 <= i + by < count]
    return lax.ppermute(block, "ctx", pairs)


def exchanged(block, axis, by):
    return lax.ppermute(block, axis, [(i, i ^ by) for i in range(lax.axis_size(axis))])


def after(value, *others):
    return lax.optimization_barrier((value, *others))


def body(queries, key_states, value_states, doc_lengths, grad_attended):
    tok, heads, width = queries.shape
    count = lax.axis_size("ctx")
    ranks = lax.axis_size("head")
    reach = min((DOC_MOST + tok - 2) // tok, count - 1)
    back = min((reach + 1) // 2, count // 2 - 1)
    whole = count == 8 and back == 3 and ranks == 4
    docs = jnp.arange(doc_lengths.shape[0])
    doc_ends = jnp.sum(jnp.where(docs[None] <= docs[:, None], doc_lengths[None], 0), axis=1)
    own = jnp.concatenate(
        [key_states.reshape(tok, width), value_states.reshape(tok, width)], axis=0
    )
    near = exchanged(own, "ctx", 1)
    if whole:
        beside = exchanged(own, "ctx", 2)
        across = exchanged(own, "ctx", 4)
    else:
        arrived = [shifted(own, 2 * k, count) for k in range(1, back + 1)]
    grads = split(grad_attended, ranks)
    grads = [part if k == 0 else exchanged(part, "head", k) for k, part in enumerate(grads)]
    if whole:
        far_beside = exchanged(beside, "ctx", 1)
        passed = exchanged(across, "ctx", 2)
        far_across = exchanged(across, "ctx", 1)
        passed, doc_ends, far_beside, near, *grads[1:] = after(
            passed, doc_ends, far_beside, near, *grads[1:]
        )
        far_passed = exchanged(passed, "ctx", 1)
        arrived = [beside, across, passed]
        far = [far_beside, far_across, far_passed]
    else:
        far = [exchanged(block, "ctx", 1) for block in arrived]
    prepared = arrange(
        arrange_kernel, [queries], queries.shape, pltpu.VMEM(queries.shape, jnp.float32)
    )
    prepared += arrange(
        arrange_grads_kernel,
        grads,
        queries.shape,
        pltpu.VMEM((tok, heads * width), jnp.bfloat16),
    )
    outs, state, parts = attend(doc_ends, prepared, own, near, arrived, far, ranks, whole)
    outs, (mine_far, other_far) = list(outs), parts
    dq_rows, mine1, other1 = attend_near(prepared, state, 1, back, whole)
    other_far = exchanged(other_far, "ctx", 1)
    outs[1:2] = [exchanged(part, "head", 1) for part in outs[1:2]]
    other1 = exchanged(other1, "ctx", 1)
    outs[2:] = [exchanged(part, "head", k + 2) for k, part in enumerate(outs[2:])]
    other_far, mine1, *outs[1:2] = after(other_far, mine1, *outs[1:2])
    blocks = list(merge(mine_far, other_far))
    returned = [shifted(block, -2 * (k + 2), count) for k, block in enumerate(blocks)]
    dq_rows, returned[-1] = after(dq_rows, returned[-1])
    dq_rows, mine0, other0 = attend_near(prepared, [*state[:-1], dq_rows], 0, back, whole)
    (block,) = merge(mine1, other1)
    returned.append(shifted(block, -2, count))
    other0 = exchanged(other0, "ctx", 1)
    grad_keys, grad_values = finish(mine0[0], returned + [other0[0]])
    attended, grad_queries = join(outs, dq_rows, queries.shape)
    grad_keys = grad_keys.reshape(tok, 1, width)
    grad_values = grad_values.reshape(tok, 1, width)
    return attended, grad_queries, grad_keys, grad_values


def solution(mesh):
    in_specs = (
        P("ctx", "head", None),
        P("ctx", "head", None),
        P("ctx", "head", None),
        P(),
        P(("ctx", "head"), None),
    )
    out_specs = (
        P(("ctx", "head"), None),
        P("ctx", "head", None),
        P("ctx", "head", None),
        P("ctx", "head", None),
    )
    return jax.shard_map(body, mesh=mesh, in_specs=in_specs, out_specs=out_specs, check_vma=False)
```

```python
import functools
import math

import jax
import jax.numpy as jnp
from jax import lax
from jax.experimental import pallas as pl
from jax.experimental.pallas import tpu as pltpu
from jax.sharding import PartitionSpec as P

DOC_MOST = 1792
NEG_FILL = -1e30
TILE = 256
CHUNK = 128
LOG2_E = 1.4426950408889634
SMALL_VMEM = 8 * 1024 * 1024
KERNEL_VMEM = 16 * 1024 * 1024


def dot(a, b):
    return jnp.dot(a, b, preferred_element_type=jnp.float32)


def dot_nt(a, b):
    return lax.dot_general(a, b, (((1,), (1,)), ((), ())), preferred_element_type=jnp.float32)


def unit(size):
    rows = lax.broadcasted_iota(jnp.int32, (size, size), 0)
    return (rows == lax.broadcasted_iota(jnp.int32, (size, size), 1)).astype(jnp.bfloat16)


def twice(column):
    return jnp.concatenate([column, column], axis=1)


def starts_in(doc_ref, positions):
    found = jnp.zeros_like(positions)
    for i in range(doc_ref.shape[0]):
        found = jnp.where(positions >= doc_ref[i], doc_ref[i], found)
    return found


def here(tok, back, whole):
    ctx = lax.axis_index("ctx")
    parity = lax.rem(ctx, 2)
    last = ctx // 2 if whole else back
    base = 0 if whole else (ctx - parity - 2 * back) * tok
    return parity, last, base, 2 * last + parity


def back_tile(i, slot, chunk, width, refs):
    q_cols, do_rows, do_cols, keys, values, scores, top, delta, dq_acc, d_blocks = refs
    at = pl.ds(pl.multiple_of(i * TILE, TILE), TILE)
    probs = jnp.exp2(scores[chunk, i] - twice(top[chunk]))
    d_probs = dot_nt(do_rows[chunk], values[at, 0:width])
    d_scores = (probs * (d_probs - twice(delta[chunk]))).astype(jnp.bfloat16)
    dq_acc[chunk] += dot(d_scores, keys[at, :])
    d_blocks[slot, 0:width, :] += dot(q_cols[chunk], d_scores)
    d_blocks[slot, width:, :] += dot(do_cols[chunk], probs.astype(jnp.bfloat16))


def put(d_blocks, mine, other, mine_ref, other_ref, width, scale):
    mine_ref[0:width, :] = d_blocks[mine, 0:width, :] * scale
    mine_ref[width:, :] = d_blocks[mine, width:, :]
    other_ref[0:width, :] = (d_blocks[other, 0:width, :] * scale).astype(jnp.bfloat16)
    other_ref[width:, :] = d_blocks[other, width:, :].astype(jnp.bfloat16)


def attention_kernel(
    doc_ref,
    q_rows,
    q_cols,
    do_rows,
    do_cols,
    own_ref,
    near_ref,
    *refs,
    back,
    whole,
    ranks,
    heads,
    width,
    scale,
):
    arrived, far, refs = refs[:back], refs[back : 2 * back], refs[2 * back :]
    out_parts, refs = refs[:ranks], refs[ranks:]
    (lows_ref, scores, top, delta, keys, values, dq_acc), refs = refs[:7], refs[7:]
    d_refs, (o_ref, accum, d_blocks) = refs[:-3], refs[-3:]
    tok = own_ref.shape[0] // 2
    part_rows = tok // ranks
    rank = lax.axis_index("head")
    parity, last, base, own = here(tok, back, whole)
    cut = 2 * (last - 1)
    ones = jnp.ones((width, width), jnp.bfloat16)

    values[:, width:] = jnp.ones_like(values[:, width:])
    for k in range(back + 1):
        pair = last ^ k if whole else last - k
        mine, other = (own_ref, near_ref) if k == 0 else (arrived[k - 1], far[k - 1])
        for ref, place in ((mine, 2 * pair + parity), (other, 2 * pair + 1 - parity)):
            at = pl.ds(pl.multiple_of(place * tok, tok), tok)
            keys[at, :] = ref[0:tok, :]
            values[at, 0:width] = ref[tok:, :]
    d_blocks[...] = jnp.zeros_like(d_blocks)
    top[...] = jnp.full_like(top, NEG_FILL)
    dq_acc[...] = jnp.zeros_like(dq_acc)

    def chunk_step(chunk, carry):
        rows_at = pl.ds(pl.multiple_of(chunk * CHUNK, CHUNK), CHUNK)
        t_first = base + own * TILE + chunk * CHUNK
        t_last = t_first + CHUNK - 1
        t_col = t_first + lax.broadcasted_iota(jnp.int32, (CHUNK, width), 0)
        start_col = starts_in(doc_ref, t_col)
        low = jnp.maximum(starts_in(doc_ref, t_first) - base, 0) // TILE
        lows_ref[chunk] = low
        clear = jnp.clip((starts_in(doc_ref, t_last) - base + TILE - 1) // TILE, low, own)

        def score_tile(i, masked):
            at = pl.ds(pl.multiple_of(i * TILE, TILE), TILE)
            tile = dot_nt(q_rows[chunk], keys[at, :]) * (scale * LOG2_E)
            if masked:
                s_row = base + i * TILE + lax.broadcasted_iota(jnp.int32, (CHUNK, TILE), 1)
                live = (s_row >= twice(start_col)) & (s_row <= twice(t_col))
                tile = jnp.concatenate(
                    [
                        jnp.where(live, tile[j * CHUNK : (j + 1) * CHUNK], NEG_FILL)
                        for j in range(heads)
                    ],
                    axis=0,
                )
            scores[chunk, i] = tile
            top[chunk] = jnp.maximum(top[chunk], jnp.maximum(tile[:, :width], tile[:, width:]))

        def edge_step(n, carry):
            score_tile(jnp.where(n < clear - low, low + n, own), True)
            return carry

        def inner_step(i, carry):
            score_tile(i, False)
            return carry

        lax.fori_loop(0, clear - low + 1, edge_step, 0)
        lax.fori_loop(clear, own, inner_step, 0)
        top[chunk] = jnp.broadcast_to(jnp.max(top[chunk], axis=1, keepdims=True), top.shape[1:])
        accum[...] = jnp.zeros_like(accum)

        def weigh_step(i, carry):
            at = pl.ds(pl.multiple_of(i * TILE, TILE), TILE)
            weights = jnp.exp2(scores[chunk, i] - twice(top[chunk])).astype(jnp.bfloat16)
            accum[...] += dot(weights, values[at, :])
            return carry

        lax.fori_loop(low, own + 1, weigh_step, 0)
        total = accum[:, width:]
        out = (accum[:, 0:width] / total).astype(jnp.bfloat16)
        for j in range(heads):
            o_ref[rows_at, j * width : (j + 1) * width] = out[j * CHUNK : (j + 1) * CHUNK]
        top[chunk] = top[chunk] + jnp.log2(total)
        product = do_rows[chunk].astype(jnp.float32) * out.astype(jnp.float32)
        coarse = product.astype(jnp.bfloat16)
        fine = (product - coarse.astype(jnp.float32)).astype(jnp.bfloat16)
        delta[chunk] = dot(coarse, ones) + dot(fine, ones)

        def back_step(i, carry):
            refs = (
                q_cols, do_rows, do_cols, keys, values, scores, top, delta, dq_acc, d_blocks
            )
            back_tile(i, i, chunk, width, refs)
            return carry

        lax.fori_loop(low, cut, back_step, 0)
        return carry

    lax.fori_loop(0, tok // CHUNK, chunk_step, 0)
    for k in range(ranks):
        at = pl.ds(pl.multiple_of((rank ^ k) * part_rows, part_rows), part_rows)
        out_parts[k][...] = o_ref[at, :]
    for k in range(2, back + 1):
        pair = jnp.maximum(last - k, 0)
        mine, other = 2 * pair + parity, 2 * pair + 1 - parity
        mine_ref, other_ref = (ref.at[k - 2] for ref in d_refs)
        put(d_blocks, mine, other, mine_ref, other_ref, width, scale)


def attend(doc_ends, prepared, own, near, arrived, far, ranks, whole):
    chunks, rows, width = prepared[0].shape
    tok = chunks * CHUNK
    heads = rows // CHUNK
    back = len(arrived)
    tiles = 2 * (back + 1)
    span = tiles * tok
    vmem = pl.BlockSpec(memory_space=pltpu.VMEM)
    smem = pl.BlockSpec(memory_space=pltpu.SMEM)
    out_part = jax.ShapeDtypeStruct((tok // ranks, heads * width), jnp.bfloat16)
    row_state = jax.ShapeDtypeStruct((chunks, rows, width), jnp.float32)
    outputs = pl.pallas_call(
        functools.partial(
            attention_kernel,
            back=back,
            whole=whole,
            ranks=ranks,
            heads=heads,
            width=width,
            scale=1.0 / math.sqrt(width),
        ),
        out_shape=[out_part] * ranks
        + [
            jax.ShapeDtypeStruct((chunks,), jnp.int32),
            jax.ShapeDtypeStruct((chunks, tiles, rows, TILE), jnp.float32),
            row_state,
            row_state,
            jax.ShapeDtypeStruct((span, width), jnp.bfloat16),
            jax.ShapeDtypeStruct((span, 2 * width), jnp.bfloat16),
            row_state,
        ]
        + [
            jax.ShapeDtypeStruct((back - 1, 2 * width, tok), dtype)
            for dtype in (jnp.float32, jnp.bfloat16)
        ],
        in_specs=[smem] + [vmem] * (6 + 2 * back),
        out_specs=[vmem] * ranks + [smem] + [vmem] * 8,
        scratch_shapes=[
            pltpu.VMEM((tok, heads * width), jnp.bfloat16),
            pltpu.VMEM((rows, 2 * width), jnp.float32),
            pltpu.VMEM((tiles, 2 * width, tok), jnp.float32),
        ],
        compiler_params=pltpu.CompilerParams(vmem_limit_bytes=KERNEL_VMEM),
        cost_estimate=pl.CostEstimate(
            flops=14 * tok * heads * width * span,
            bytes_accessed=4 * tok * heads * width * 2 + 4 * span * width * 2,
            transcendentals=tok * heads * span,
        ),
        name="attention",
    )(doc_ends, *prepared, own, near, *arrived, *far)
    return outputs[:ranks], outputs[ranks : ranks + 7], outputs[ranks + 7 :]


def near_kernel(
    q_cols,
    do_rows,
    do_cols,
    lows_ref,
    scores,
    top,
    delta,
    keys,
    values,
    dq_before,
    dq_acc,
    mine_ref,
    other_ref,
    d_blocks,
    *,
    distance,
    back,
    whole,
    width,
    scale,
):
    tok = mine_ref.shape[2]
    parity, last, _, own = here(tok, back, whole)
    first = 2 * (last - distance)
    d_blocks[...] = jnp.zeros_like(d_blocks)
    dq_acc[...] = dq_before[...]

    def chunk_step(chunk, carry):
        def back_step(i, carry):
            refs = (
                q_cols, do_rows, do_cols, keys, values, scores, top, delta, dq_acc, d_blocks
            )
            back_tile(i, i - first, chunk, width, refs)
            return carry

        stop = jnp.minimum(first + 2, own + 1)
        lax.fori_loop(jnp.maximum(lows_ref[chunk], first), stop, back_step, 0)
        return carry

    lax.fori_loop(0, tok // CHUNK, chunk_step, 0)
    put(d_blocks, parity, 1 - parity, mine_ref.at[0], other_ref.at[0], width, scale)


def attend_near(prepared, state, distance, back, whole):
    _, q_cols, do_rows, do_cols = prepared
    chunks, rows, width = do_rows.shape
    tok = chunks * CHUNK
    vmem = pl.BlockSpec(memory_space=pltpu.VMEM)
    smem = pl.BlockSpec(memory_space=pltpu.SMEM)
    return pl.pallas_call(
        functools.partial(
            near_kernel,
            distance=distance,
            back=back,
            whole=whole,
            width=width,
            scale=1.0 / math.sqrt(width),
        ),
        out_shape=[jax.ShapeDtypeStruct((chunks, rows, width), jnp.float32)]
        + [
            jax.ShapeDtypeStruct((1, 2 * width, tok), dtype)
            for dtype in (jnp.float32, jnp.bfloat16)
        ],
        in_specs=[vmem] * 3 + [smem] + [vmem] * 6,
        out_specs=[vmem] * 3,
        scratch_shapes=[pltpu.VMEM((2, 2 * width, tok), jnp.float32)],
        compiler_params=pltpu.CompilerParams(vmem_limit_bytes=KERNEL_VMEM),
        cost_estimate=pl.CostEstimate(
            flops=8 * chunks * rows * width * 2 * tok,
            bytes_accessed=4 * chunks * rows * width * 2,
            transcendentals=2 * chunks * rows * tok,
        ),
        name="near",
    )(q_cols, do_rows, do_cols, *state)


def split_kernel(grad_ref, *part_refs):
    size = part_refs[0].shape[1]
    for k, ref in enumerate(part_refs):
        at = pl.multiple_of((lax.axis_index("head") ^ k) * size, size)
        ref[...] = grad_ref[:, pl.ds(at, size)]


def split(grad_attended, ranks):
    rows, columns = grad_attended.shape
    vmem = pl.BlockSpec(memory_space=pltpu.VMEM)
    part = jax.ShapeDtypeStruct((rows, columns // ranks), grad_attended.dtype)
    return pl.pallas_call(
        split_kernel,
        out_shape=[part] * ranks,
        in_specs=[vmem],
        out_specs=[vmem] * ranks,
        compiler_params=pltpu.CompilerParams(vmem_limit_bytes=SMALL_VMEM),
        name="split",
    )(grad_attended)


def arrange_kernel(q_ref, rows_ref, cols_ref, wide):
    small = unit(q_ref.shape[2])
    wide[...] = q_ref[...].astype(jnp.float32)
    for chunk in range(rows_ref.shape[0]):
        for j in range(q_ref.shape[1]):
            rows_ref[chunk, j * CHUNK : (j + 1) * CHUNK, :] = wide[
                chunk * CHUNK : (chunk + 1) * CHUNK, j, :
            ].astype(jnp.bfloat16)
        cols_ref[chunk] = dot_nt(small, rows_ref[chunk]).astype(jnp.bfloat16)


def arrange_grads_kernel(*refs):
    parts, (rows_ref, cols_ref, grads) = refs[:-3], refs[-3:]
    width = rows_ref.shape[2]
    small = unit(width)
    size = parts[0].shape[0]
    for k, ref in enumerate(parts):
        at = pl.multiple_of((lax.axis_index("head") ^ k) * size, size)
        grads[pl.ds(at, size), :] = ref[...]
    for chunk in range(rows_ref.shape[0]):
        for j in range(rows_ref.shape[1] // CHUNK):
            rows_ref[chunk, j * CHUNK : (j + 1) * CHUNK, :] = grads[
                chunk * CHUNK : (chunk + 1) * CHUNK, j * width : (j + 1) * width
            ]
        cols_ref[chunk] = dot_nt(small, rows_ref[chunk]).astype(jnp.bfloat16)


def arrange(kernel, arrays, shape, scratch):
    tok, heads, width = shape
    vmem = pl.BlockSpec(memory_space=pltpu.VMEM)
    chunks, rows = tok // CHUNK, heads * CHUNK
    return pl.pallas_call(
        kernel,
        out_shape=[
            jax.ShapeDtypeStruct((chunks, rows, width), jnp.bfloat16),
            jax.ShapeDtypeStruct((chunks, width, rows), jnp.bfloat16),
        ],
        in_specs=[vmem] * len(arrays),
        out_specs=[vmem, vmem],
        scratch_shapes=[scratch],
        compiler_params=pltpu.CompilerParams(vmem_limit_bytes=SMALL_VMEM),
        name="arrange",
    )(*arrays)


def join_kernel(*refs):
    parts, (rows_ref, out_ref, dq_ref, wide) = refs[:-4], refs[-4:]
    size = parts[0].shape[1]
    for k, ref in enumerate(parts):
        at = pl.multiple_of((lax.axis_index("head") ^ k) * size, size)
        out_ref[:, pl.ds(at, size)] = ref[...]
    scale = 1.0 / math.sqrt(rows_ref.shape[2])
    for chunk in range(rows_ref.shape[0]):
        for j in range(dq_ref.shape[1]):
            wide[chunk * CHUNK : (chunk + 1) * CHUNK, j, :] = (
                rows_ref[chunk, j * CHUNK : (j + 1) * CHUNK, :] * scale
            )
    dq_ref[...] = wide[...].astype(jnp.bfloat16)


def join(parts, dq_rows, shape):
    rows, size = parts[0].shape
    vmem = pl.BlockSpec(memory_space=pltpu.VMEM)
    return pl.pallas_call(
        join_kernel,
        out_shape=(
            jax.ShapeDtypeStruct((rows, size * len(parts)), parts[0].dtype),
            jax.ShapeDtypeStruct(shape, jnp.bfloat16),
        ),
        in_specs=[vmem] * (len(parts) + 1),
        out_specs=(vmem, vmem),
        scratch_shapes=[pltpu.VMEM(shape, jnp.float32)],
        compiler_params=pltpu.CompilerParams(vmem_limit_bytes=SMALL_VMEM),
        name="join",
    )(*parts, dq_rows)


def merge_kernel(mine_ref, other_ref, *block_refs):
    for k, ref in enumerate(block_refs):
        ref[...] = (mine_ref[k] + other_ref[k].astype(jnp.float32)).astype(ref.dtype)


def merge(mine, other):
    vmem = pl.BlockSpec(memory_space=pltpu.VMEM)
    block = jax.ShapeDtypeStruct(mine.shape[1:], jnp.bfloat16)
    return pl.pallas_call(
        merge_kernel,
        out_shape=[block] * mine.shape[0],
        in_specs=[vmem, vmem],
        out_specs=[vmem] * mine.shape[0],
        compiler_params=pltpu.CompilerParams(vmem_limit_bytes=SMALL_VMEM),
        name="merge",
    )(mine, other)


def finish_kernel(own_ref, *refs):
    arrived = refs[:-2]
    dk_ref, dv_ref = refs[-2:]
    total = own_ref[...]
    for ref in arrived:
        total = total + ref[...].astype(jnp.float32)
    total = total.astype(jnp.bfloat16)
    width = dk_ref.shape[1]
    large = unit(dk_ref.shape[0])
    dk_ref[...] = dot_nt(large, total[:width]).astype(jnp.bfloat16)
    dv_ref[...] = dot_nt(large, total[width:]).astype(jnp.bfloat16)


def finish(own_part, arrived):
    both, tok = own_part.shape
    vmem = pl.BlockSpec(memory_space=pltpu.VMEM)
    shape = jax.ShapeDtypeStruct((tok, both // 2), jnp.bfloat16)
    return pl.pallas_call(
        finish_kernel,
        out_shape=(shape, shape),
        in_specs=[vmem] * (1 + len(arrived)),
        out_specs=(vmem, vmem),
        compiler_params=pltpu.CompilerParams(vmem_limit_bytes=SMALL_VMEM),
        name="finish",
    )(own_part, *arrived)


def shifted(block, by, count):
    pairs = [(i, i + by) for i in range(count) if 0 <= i + by < count]
    return lax.ppermute(block, "ctx", pairs)


def exchanged(block, axis, by):
    return lax.ppermute(block, axis, [(i, i ^ by) for i in range(lax.axis_size(axis))])


def after(value, *others):
    return lax.optimization_barrier((value, *others))


def body(queries, key_states, value_states, doc_lengths, grad_attended):
    tok, heads, width = queries.shape
    count = lax.axis_size("ctx")
    ranks = lax.axis_size("head")
    reach = min((DOC_MOST + tok - 2) // tok, count - 1)
    back = min((reach + 1) // 2, count // 2 - 1)
    whole = count == 8 and back == 3 and ranks == 4
    docs = jnp.arange(doc_lengths.shape[0])
    doc_ends = jnp.sum(jnp.where(docs[None] <= docs[:, None], doc_lengths[None], 0), axis=1)
    own = jnp.concatenate(
        [key_states.reshape(tok, width), value_states.reshape(tok, width)], axis=0
    )
    near = exchanged(own, "ctx", 1)
    if whole:
        beside = exchanged(own, "ctx", 2)
        across = exchanged(own, "ctx", 4)
    else:
        arrived = [shifted(own, 2 * k, count) for k in range(1, back + 1)]
    grads = split(grad_attended, ranks)
    grads = [part if k == 0 else exchanged(part, "head", k) for k, part in enumerate(grads)]
    if whole:
        far_beside = exchanged(beside, "ctx", 1)
        passed = exchanged(across, "ctx", 2)
        far_across = exchanged(across, "ctx", 1)
        passed, doc_ends, far_beside, near, *grads[1:] = after(
            passed, doc_ends, far_beside, near, *grads[1:]
        )
        far_passed = exchanged(passed, "ctx", 1)
        arrived = [beside, across, passed]
        far = [far_beside, far_across, far_passed]
    else:
        far = [exchanged(block, "ctx", 1) for block in arrived]
    prepared = arrange(
        arrange_kernel, [queries], queries.shape, pltpu.VMEM(queries.shape, jnp.float32)
    )
    prepared += arrange(
        arrange_grads_kernel,
        grads,
        queries.shape,
        pltpu.VMEM((tok, heads * width), jnp.bfloat16),
    )
    outs, state, parts = attend(doc_ends, prepared, own, near, arrived, far, ranks, whole)
    outs, (mine_far, other_far) = list(outs), parts
    dq_rows, mine1, other1 = attend_near(prepared, state, 1, back, whole)
    other_far = exchanged(other_far, "ctx", 1)
    outs[1:2] = [exchanged(part, "head", 1) for part in outs[1:2]]
    other1 = exchanged(other1, "ctx", 1)
    other_far, mine1, *outs[1:2] = after(other_far, mine1, *outs[1:2])
    blocks = list(merge(mine_far, other_far))
    blocks[-1], *outs[2:] = after(blocks[-1], *outs[2:])
    outs[2:] = [exchanged(part, "head", k + 2) for k, part in enumerate(outs[2:])]
    returned = [shifted(block, -2 * (k + 2), count) for k, block in enumerate(blocks)]
    dq_rows, *outs[2:3] = after(dq_rows, *outs[2:3])
    dq_rows, mine0, other0 = attend_near(prepared, [*state[:-1], dq_rows], 0, back, whole)
    (block,) = merge(mine1, other1)
    returned.append(shifted(block, -2, count))
    other0 = exchanged(other0, "ctx", 1)
    grad_keys, grad_values = finish(mine0[0], returned + [other0[0]])
    attended, grad_queries = join(outs, dq_rows, queries.shape)
    grad_keys = grad_keys.reshape(tok, 1, width)
    grad_values = grad_values.reshape(tok, 1, width)
    return attended, grad_queries, grad_keys, grad_values


def solution(mesh):
    in_specs = (
        P("ctx", "head", None),
        P("ctx", "head", None),
        P("ctx", "head", None),
        P(),
        P(("ctx", "head"), None),
    )
    out_specs = (
        P(("ctx", "head"), None),
        P("ctx", "head", None),
        P("ctx", "head", None),
        P("ctx", "head", None),
    )
    return jax.shard_map(body, mesh=mesh, in_specs=in_specs, out_specs=out_specs, check_vma=False)
```

```python
import functools
import math

import jax
import jax.numpy as jnp
from jax import lax
from jax.experimental import pallas as pl
from jax.experimental.pallas import tpu as pltpu
from jax.sharding import PartitionSpec as P

DOC_MOST = 1792
NEG_FILL = -1e30
TILE = 256
CHUNK = 128
LOG2_E = 1.4426950408889634
SMALL_VMEM = 8 * 1024 * 1024
KERNEL_VMEM = 16 * 1024 * 1024


def dot(a, b):
    return jnp.dot(a, b, preferred_element_type=jnp.float32)


def dot_nt(a, b):
    return lax.dot_general(a, b, (((1,), (1,)), ((), ())), preferred_element_type=jnp.float32)


def unit(size):
    rows = lax.broadcasted_iota(jnp.int32, (size, size), 0)
    return (rows == lax.broadcasted_iota(jnp.int32, (size, size), 1)).astype(jnp.bfloat16)


def twice(column):
    return jnp.concatenate([column, column], axis=1)


def starts_in(doc_ref, positions):
    found = jnp.zeros_like(positions)
    for i in range(doc_ref.shape[0]):
        found = jnp.where(positions >= doc_ref[i], doc_ref[i], found)
    return found


def here(tok, back, whole):
    ctx = lax.axis_index("ctx")
    parity = lax.rem(ctx, 2)
    last = ctx // 2 if whole else back
    base = 0 if whole else (ctx - parity - 2 * back) * tok
    return parity, last, base, 2 * last + parity


def back_tile(i, slot, chunk, width, refs):
    q_cols, do_rows, do_cols, keys, values, scores, top, delta, dq_acc, d_blocks = refs
    at = pl.ds(pl.multiple_of(i * TILE, TILE), TILE)
    probs = jnp.exp2(scores[chunk, i] - twice(top[chunk]))
    d_probs = dot_nt(do_rows[chunk], values[at, 0:width])
    d_scores = (probs * (d_probs - twice(delta[chunk]))).astype(jnp.bfloat16)
    dq_acc[chunk] += dot(d_scores, keys[at, :])
    d_blocks[slot, 0:width, :] += dot(q_cols[chunk], d_scores)
    d_blocks[slot, width:, :] += dot(do_cols[chunk], probs.astype(jnp.bfloat16))


def put(d_blocks, mine, other, mine_ref, other_ref, width, scale):
    mine_ref[0:width, :] = d_blocks[mine, 0:width, :] * scale
    mine_ref[width:, :] = d_blocks[mine, width:, :]
    other_ref[0:width, :] = (d_blocks[other, 0:width, :] * scale).astype(jnp.bfloat16)
    other_ref[width:, :] = d_blocks[other, width:, :].astype(jnp.bfloat16)


def attention_kernel(
    doc_ref,
    q_rows,
    q_cols,
    do_rows,
    do_cols,
    own_ref,
    near_ref,
    *refs,
    back,
    whole,
    ranks,
    heads,
    width,
    scale,
):
    arrived, far, refs = refs[:back], refs[back : 2 * back], refs[2 * back :]
    out_parts, refs = refs[:ranks], refs[ranks:]
    (lows_ref, scores, top, delta, keys, values, dq_acc), refs = refs[:7], refs[7:]
    d_refs, (o_ref, accum, d_blocks) = refs[:-3], refs[-3:]
    tok = own_ref.shape[0] // 2
    part_rows = tok // ranks
    rank = lax.axis_index("head")
    parity, last, base, own = here(tok, back, whole)
    cut = 2 * (last - 1)
    ones = jnp.ones((width, width), jnp.bfloat16)

    values[:, width:] = jnp.ones_like(values[:, width:])
    for k in range(back + 1):
        pair = last ^ k if whole else last - k
        mine, other = (own_ref, near_ref) if k == 0 else (arrived[k - 1], far[k - 1])
        for ref, place in ((mine, 2 * pair + parity), (other, 2 * pair + 1 - parity)):
            at = pl.ds(pl.multiple_of(place * tok, tok), tok)
            keys[at, :] = ref[0:tok, :]
            values[at, 0:width] = ref[tok:, :]
    d_blocks[...] = jnp.zeros_like(d_blocks)
    top[...] = jnp.full_like(top, NEG_FILL)
    dq_acc[...] = jnp.zeros_like(dq_acc)

    def chunk_step(chunk, carry):
        rows_at = pl.ds(pl.multiple_of(chunk * CHUNK, CHUNK), CHUNK)
        t_first = base + own * TILE + chunk * CHUNK
        t_last = t_first + CHUNK - 1
        t_col = t_first + lax.broadcasted_iota(jnp.int32, (CHUNK, width), 0)
        start_col = starts_in(doc_ref, t_col)
        low = jnp.maximum(starts_in(doc_ref, t_first) - base, 0) // TILE
        lows_ref[chunk] = low
        clear = jnp.clip((starts_in(doc_ref, t_last) - base + TILE - 1) // TILE, low, own)

        def score_tile(i, masked):
            at = pl.ds(pl.multiple_of(i * TILE, TILE), TILE)
            tile = dot_nt(q_rows[chunk], keys[at, :]) * (scale * LOG2_E)
            if masked:
                s_row = base + i * TILE + lax.broadcasted_iota(jnp.int32, (CHUNK, TILE), 1)
                live = (s_row >= twice(start_col)) & (s_row <= twice(t_col))
                tile = jnp.concatenate(
                    [
                        jnp.where(live, tile[j * CHUNK : (j + 1) * CHUNK], NEG_FILL)
                        for j in range(heads)
                    ],
                    axis=0,
                )
            scores[chunk, i] = tile
            top[chunk] = jnp.maximum(top[chunk], jnp.maximum(tile[:, :width], tile[:, width:]))

        def edge_step(n, carry):
            score_tile(jnp.where(n < clear - low, low + n, own), True)
            return carry

        def inner_step(i, carry):
            score_tile(i, False)
            return carry

        lax.fori_loop(0, clear - low + 1, edge_step, 0)
        lax.fori_loop(clear, own, inner_step, 0)
        top[chunk] = jnp.broadcast_to(jnp.max(top[chunk], axis=1, keepdims=True), top.shape[1:])
        accum[...] = jnp.zeros_like(accum)

        def weigh_step(i, carry):
            at = pl.ds(pl.multiple_of(i * TILE, TILE), TILE)
            weights = jnp.exp2(scores[chunk, i] - twice(top[chunk])).astype(jnp.bfloat16)
            accum[...] += dot(weights, values[at, :])
            return carry

        lax.fori_loop(low, own + 1, weigh_step, 0)
        total = accum[:, width:]
        out = (accum[:, 0:width] / total).astype(jnp.bfloat16)
        for j in range(heads):
            o_ref[rows_at, j * width : (j + 1) * width] = out[j * CHUNK : (j + 1) * CHUNK]
        top[chunk] = top[chunk] + jnp.log2(total)
        product = do_rows[chunk].astype(jnp.float32) * out.astype(jnp.float32)
        coarse = product.astype(jnp.bfloat16)
        fine = (product - coarse.astype(jnp.float32)).astype(jnp.bfloat16)
        delta[chunk] = dot(coarse, ones) + dot(fine, ones)

        def back_step(i, carry):
            refs = (
                q_cols, do_rows, do_cols, keys, values, scores, top, delta, dq_acc, d_blocks
            )
            back_tile(i, i, chunk, width, refs)
            return carry

        lax.fori_loop(low, cut, back_step, 0)
        return carry

    lax.fori_loop(0, tok // CHUNK, chunk_step, 0)
    for k in range(ranks):
        at = pl.ds(pl.multiple_of((rank ^ k) * part_rows, part_rows), part_rows)
        out_parts[k][...] = o_ref[at, :]
    for k in range(2, back + 1):
        pair = jnp.maximum(last - k, 0)
        mine, other = 2 * pair + parity, 2 * pair + 1 - parity
        mine_ref, other_ref = (ref.at[k - 2] for ref in d_refs)
        put(d_blocks, mine, other, mine_ref, other_ref, width, scale)


def attend(doc_ends, prepared, own, near, arrived, far, ranks, whole):
    chunks, rows, width = prepared[0].shape
    tok = chunks * CHUNK
    heads = rows // CHUNK
    back = len(arrived)
    tiles = 2 * (back + 1)
    span = tiles * tok
    vmem = pl.BlockSpec(memory_space=pltpu.VMEM)
    smem = pl.BlockSpec(memory_space=pltpu.SMEM)
    out_part = jax.ShapeDtypeStruct((tok // ranks, heads * width), jnp.bfloat16)
    row_state = jax.ShapeDtypeStruct((chunks, rows, width), jnp.float32)
    outputs = pl.pallas_call(
        functools.partial(
            attention_kernel,
            back=back,
            whole=whole,
            ranks=ranks,
            heads=heads,
            width=width,
            scale=1.0 / math.sqrt(width),
        ),
        out_shape=[out_part] * ranks
        + [
            jax.ShapeDtypeStruct((chunks,), jnp.int32),
            jax.ShapeDtypeStruct((chunks, tiles, rows, TILE), jnp.float32),
            row_state,
            row_state,
            jax.ShapeDtypeStruct((span, width), jnp.bfloat16),
            jax.ShapeDtypeStruct((span, 2 * width), jnp.bfloat16),
            row_state,
        ]
        + [
            jax.ShapeDtypeStruct((back - 1, 2 * width, tok), dtype)
            for dtype in (jnp.float32, jnp.bfloat16)
        ],
        in_specs=[smem] + [vmem] * (6 + 2 * back),
        out_specs=[vmem] * ranks + [smem] + [vmem] * 8,
        scratch_shapes=[
            pltpu.VMEM((tok, heads * width), jnp.bfloat16),
            pltpu.VMEM((rows, 2 * width), jnp.float32),
            pltpu.VMEM((tiles, 2 * width, tok), jnp.float32),
        ],
        compiler_params=pltpu.CompilerParams(vmem_limit_bytes=KERNEL_VMEM),
        cost_estimate=pl.CostEstimate(
            flops=14 * tok * heads * width * span,
            bytes_accessed=4 * tok * heads * width * 2 + 4 * span * width * 2,
            transcendentals=tok * heads * span,
        ),
        name="attention",
    )(doc_ends, *prepared, own, near, *arrived, *far)
    return outputs[:ranks], outputs[ranks : ranks + 7], outputs[ranks + 7 :]


def near_kernel(
    q_cols,
    do_rows,
    do_cols,
    lows_ref,
    scores,
    top,
    delta,
    keys,
    values,
    dq_before,
    dq_acc,
    mine_ref,
    other_ref,
    d_blocks,
    *,
    distance,
    back,
    whole,
    width,
    scale,
):
    tok = mine_ref.shape[2]
    parity, last, _, own = here(tok, back, whole)
    first = 2 * (last - distance)
    d_blocks[...] = jnp.zeros_like(d_blocks)
    dq_acc[...] = dq_before[...]

    def chunk_step(chunk, carry):
        def back_step(i, carry):
            refs = (
                q_cols, do_rows, do_cols, keys, values, scores, top, delta, dq_acc, d_blocks
            )
            back_tile(i, i - first, chunk, width, refs)
            return carry

        stop = jnp.minimum(first + 2, own + 1)
        lax.fori_loop(jnp.maximum(lows_ref[chunk], first), stop, back_step, 0)
        return carry

    lax.fori_loop(0, tok // CHUNK, chunk_step, 0)
    put(d_blocks, parity, 1 - parity, mine_ref.at[0], other_ref.at[0], width, scale)


def attend_near(prepared, state, distance, back, whole):
    _, q_cols, do_rows, do_cols = prepared
    chunks, rows, width = do_rows.shape
    tok = chunks * CHUNK
    vmem = pl.BlockSpec(memory_space=pltpu.VMEM)
    smem = pl.BlockSpec(memory_space=pltpu.SMEM)
    return pl.pallas_call(
        functools.partial(
            near_kernel,
            distance=distance,
            back=back,
            whole=whole,
            width=width,
            scale=1.0 / math.sqrt(width),
        ),
        out_shape=[jax.ShapeDtypeStruct((chunks, rows, width), jnp.float32)]
        + [
            jax.ShapeDtypeStruct((1, 2 * width, tok), dtype)
            for dtype in (jnp.float32, jnp.bfloat16)
        ],
        in_specs=[vmem] * 3 + [smem] + [vmem] * 6,
        out_specs=[vmem] * 3,
        scratch_shapes=[pltpu.VMEM((2, 2 * width, tok), jnp.float32)],
        compiler_params=pltpu.CompilerParams(vmem_limit_bytes=KERNEL_VMEM),
        cost_estimate=pl.CostEstimate(
            flops=8 * chunks * rows * width * 2 * tok,
            bytes_accessed=4 * chunks * rows * width * 2,
            transcendentals=2 * chunks * rows * tok,
        ),
        name="near",
    )(q_cols, do_rows, do_cols, *state)


def split_kernel(grad_ref, *part_refs):
    size = part_refs[0].shape[1]
    for k, ref in enumerate(part_refs):
        at = pl.multiple_of((lax.axis_index("head") ^ k) * size, size)
        ref[...] = grad_ref[:, pl.ds(at, size)]


def split(grad_attended, ranks):
    rows, columns = grad_attended.shape
    vmem = pl.BlockSpec(memory_space=pltpu.VMEM)
    part = jax.ShapeDtypeStruct((rows, columns // ranks), grad_attended.dtype)
    return pl.pallas_call(
        split_kernel,
        out_shape=[part] * ranks,
        in_specs=[vmem],
        out_specs=[vmem] * ranks,
        compiler_params=pltpu.CompilerParams(vmem_limit_bytes=SMALL_VMEM),
        name="split",
    )(grad_attended)


def arrange_kernel(q_ref, rows_ref, cols_ref, wide):
    small = unit(q_ref.shape[2])
    wide[...] = q_ref[...].astype(jnp.float32)
    for chunk in range(rows_ref.shape[0]):
        for j in range(q_ref.shape[1]):
            rows_ref[chunk, j * CHUNK : (j + 1) * CHUNK, :] = wide[
                chunk * CHUNK : (chunk + 1) * CHUNK, j, :
            ].astype(jnp.bfloat16)
        cols_ref[chunk] = dot_nt(small, rows_ref[chunk]).astype(jnp.bfloat16)


def arrange_grads_kernel(*refs):
    parts, (rows_ref, cols_ref, grads) = refs[:-3], refs[-3:]
    width = rows_ref.shape[2]
    small = unit(width)
    size = parts[0].shape[0]
    for k, ref in enumerate(parts):
        at = pl.multiple_of((lax.axis_index("head") ^ k) * size, size)
        grads[pl.ds(at, size), :] = ref[...]
    for chunk in range(rows_ref.shape[0]):
        for j in range(rows_ref.shape[1] // CHUNK):
            rows_ref[chunk, j * CHUNK : (j + 1) * CHUNK, :] = grads[
                chunk * CHUNK : (chunk + 1) * CHUNK, j * width : (j + 1) * width
            ]
        cols_ref[chunk] = dot_nt(small, rows_ref[chunk]).astype(jnp.bfloat16)


def arrange(kernel, arrays, shape, scratch):
    tok, heads, width = shape
    vmem = pl.BlockSpec(memory_space=pltpu.VMEM)
    chunks, rows = tok // CHUNK, heads * CHUNK
    return pl.pallas_call(
        kernel,
        out_shape=[
            jax.ShapeDtypeStruct((chunks, rows, width), jnp.bfloat16),
            jax.ShapeDtypeStruct((chunks, width, rows), jnp.bfloat16),
        ],
        in_specs=[vmem] * len(arrays),
        out_specs=[vmem, vmem],
        scratch_shapes=[scratch],
        compiler_params=pltpu.CompilerParams(vmem_limit_bytes=SMALL_VMEM),
        name="arrange",
    )(*arrays)


def join_kernel(*refs):
    parts, (rows_ref, out_ref, dq_ref, wide) = refs[:-4], refs[-4:]
    size = parts[0].shape[1]
    for k, ref in enumerate(parts):
        at = pl.multiple_of((lax.axis_index("head") ^ k) * size, size)
        out_ref[:, pl.ds(at, size)] = ref[...]
    scale = 1.0 / math.sqrt(rows_ref.shape[2])
    for chunk in range(rows_ref.shape[0]):
        for j in range(dq_ref.shape[1]):
            wide[chunk * CHUNK : (chunk + 1) * CHUNK, j, :] = (
                rows_ref[chunk, j * CHUNK : (j + 1) * CHUNK, :] * scale
            )
    dq_ref[...] = wide[...].astype(jnp.bfloat16)


def join(parts, dq_rows, shape):
    rows, size = parts[0].shape
    vmem = pl.BlockSpec(memory_space=pltpu.VMEM)
    return pl.pallas_call(
        join_kernel,
        out_shape=(
            jax.ShapeDtypeStruct((rows, size * len(parts)), parts[0].dtype),
            jax.ShapeDtypeStruct(shape, jnp.bfloat16),
        ),
        in_specs=[vmem] * (len(parts) + 1),
        out_specs=(vmem, vmem),
        scratch_shapes=[pltpu.VMEM(shape, jnp.float32)],
        compiler_params=pltpu.CompilerParams(vmem_limit_bytes=SMALL_VMEM),
        name="join",
    )(*parts, dq_rows)


def merge_kernel(mine_ref, other_ref, *block_refs):
    for k, ref in enumerate(block_refs):
        ref[...] = (mine_ref[k] + other_ref[k].astype(jnp.float32)).astype(ref.dtype)


def merge(mine, other):
    vmem = pl.BlockSpec(memory_space=pltpu.VMEM)
    block = jax.ShapeDtypeStruct(mine.shape[1:], jnp.bfloat16)
    return pl.pallas_call(
        merge_kernel,
        out_shape=[block] * mine.shape[0],
        in_specs=[vmem, vmem],
        out_specs=[vmem] * mine.shape[0],
        compiler_params=pltpu.CompilerParams(vmem_limit_bytes=SMALL_VMEM),
        name="merge",
    )(mine, other)


def finish_kernel(own_ref, *refs):
    arrived = refs[:-2]
    dk_ref, dv_ref = refs[-2:]
    total = own_ref[...]
    for ref in arrived:
        total = total + ref[...].astype(jnp.float32)
    total = total.astype(jnp.bfloat16)
    width = dk_ref.shape[1]
    large = unit(dk_ref.shape[0])
    dk_ref[...] = dot_nt(large, total[:width]).astype(jnp.bfloat16)
    dv_ref[...] = dot_nt(large, total[width:]).astype(jnp.bfloat16)


def finish(own_part, arrived):
    both, tok = own_part.shape
    vmem = pl.BlockSpec(memory_space=pltpu.VMEM)
    shape = jax.ShapeDtypeStruct((tok, both // 2), jnp.bfloat16)
    return pl.pallas_call(
        finish_kernel,
        out_shape=(shape, shape),
        in_specs=[vmem] * (1 + len(arrived)),
        out_specs=(vmem, vmem),
        compiler_params=pltpu.CompilerParams(vmem_limit_bytes=SMALL_VMEM),
        name="finish",
    )(own_part, *arrived)


def shifted(block, by, count):
    pairs = [(i, i + by) for i in range(count) if 0 <= i + by < count]
    return lax.ppermute(block, "ctx", pairs)


def exchanged(block, axis, by):
    return lax.ppermute(block, axis, [(i, i ^ by) for i in range(lax.axis_size(axis))])


def after(value, *others):
    return lax.optimization_barrier((value, *others))


def body(queries, key_states, value_states, doc_lengths, grad_attended):
    tok, heads, width = queries.shape
    count = lax.axis_size("ctx")
    ranks = lax.axis_size("head")
    reach = min((DOC_MOST + tok - 2) // tok, count - 1)
    back = min((reach + 1) // 2, count // 2 - 1)
    whole = count == 8 and back == 3 and ranks == 4
    docs = jnp.arange(doc_lengths.shape[0])
    doc_ends = jnp.sum(jnp.where(docs[None] <= docs[:, None], doc_lengths[None], 0), axis=1)
    own = jnp.concatenate(
        [key_states.reshape(tok, width), value_states.reshape(tok, width)], axis=0
    )
    near = exchanged(own, "ctx", 1)
    if whole:
        beside = exchanged(own, "ctx", 2)
        across = exchanged(own, "ctx", 4)
    else:
        arrived = [shifted(own, 2 * k, count) for k in range(1, back + 1)]
    grad_attended, doc_ends = after(grad_attended, doc_ends)
    grads = split(grad_attended, ranks)
    grads = [part if k == 0 else exchanged(part, "head", k) for k, part in enumerate(grads)]
    if whole:
        far_beside = exchanged(beside, "ctx", 1)
        passed = exchanged(across, "ctx", 2)
        far_across = exchanged(across, "ctx", 1)
        passed, far_beside, near, *grads[1:] = after(passed, far_beside, near, *grads[1:])
        far_passed = exchanged(passed, "ctx", 1)
        arrived = [beside, across, passed]
        far = [far_beside, far_across, far_passed]
    else:
        far = [exchanged(block, "ctx", 1) for block in arrived]
    prepared = arrange(
        arrange_kernel, [queries], queries.shape, pltpu.VMEM(queries.shape, jnp.float32)
    )
    prepared += arrange(
        arrange_grads_kernel,
        grads,
        queries.shape,
        pltpu.VMEM((tok, heads * width), jnp.bfloat16),
    )
    outs, state, parts = attend(doc_ends, prepared, own, near, arrived, far, ranks, whole)
    outs, (mine_far, other_far) = list(outs), parts
    dq_rows, mine1, other1 = attend_near(prepared, state, 1, back, whole)
    other_far = exchanged(other_far, "ctx", 1)
    outs[1:2] = [exchanged(part, "head", 1) for part in outs[1:2]]
    other1 = exchanged(other1, "ctx", 1)
    other_far, mine1, *outs[1:2] = after(other_far, mine1, *outs[1:2])
    blocks = list(merge(mine_far, other_far))
    blocks[-1], *outs[2:] = after(blocks[-1], *outs[2:])
    outs[2:] = [exchanged(part, "head", k + 2) for k, part in enumerate(outs[2:])]
    returned = [shifted(block, -2 * (k + 2), count) for k, block in enumerate(blocks)]
    dq_rows, *outs[2:3] = after(dq_rows, *outs[2:3])
    dq_rows, mine0, other0 = attend_near(prepared, [*state[:-1], dq_rows], 0, back, whole)
    (block,) = merge(mine1, other1)
    returned.append(shifted(block, -2, count))
    other0 = exchanged(other0, "ctx", 1)
    grad_keys, grad_values = finish(mine0[0], returned + [other0[0]])
    attended, grad_queries = join(outs, dq_rows, queries.shape)
    grad_keys = grad_keys.reshape(tok, 1, width)
    grad_values = grad_values.reshape(tok, 1, width)
    return attended, grad_queries, grad_keys, grad_values


def solution(mesh):
    in_specs = (
        P("ctx", "head", None),
        P("ctx", "head", None),
        P("ctx", "head", None),
        P(),
        P(("ctx", "head"), None),
    )
    out_specs = (
        P(("ctx", "head"), None),
        P("ctx", "head", None),
        P("ctx", "head", None),
        P("ctx", "head", None),
    )
    return jax.shard_map(body, mesh=mesh, in_specs=in_specs, out_specs=out_specs, check_vma=False)
```

```python
import functools
import math

import jax
import jax.numpy as jnp
from jax import lax
from jax.experimental import pallas as pl
from jax.experimental.pallas import tpu as pltpu
from jax.sharding import PartitionSpec as P

DOC_MOST = 1792
NEG_FILL = -1e30
TILE = 256
CHUNK = 128
LOG2_E = 1.4426950408889634
SMALL_VMEM = 8 * 1024 * 1024
KERNEL_VMEM = 16 * 1024 * 1024


def dot(a, b):
    return jnp.dot(a, b, preferred_element_type=jnp.float32)


def dot_nt(a, b):
    return lax.dot_general(a, b, (((1,), (1,)), ((), ())), preferred_element_type=jnp.float32)


def unit(size):
    rows = lax.broadcasted_iota(jnp.int32, (size, size), 0)
    return (rows == lax.broadcasted_iota(jnp.int32, (size, size), 1)).astype(jnp.bfloat16)


def twice(column):
    return jnp.concatenate([column, column], axis=1)


def starts_in(doc_ref, positions):
    found = jnp.zeros_like(positions)
    for i in range(doc_ref.shape[0]):
        found = jnp.where(positions >= doc_ref[i], doc_ref[i], found)
    return found


def here(tok, back, whole):
    ctx = lax.axis_index("ctx")
    parity = lax.rem(ctx, 2)
    last = ctx // 2 if whole else back
    base = 0 if whole else (ctx - parity - 2 * back) * tok
    return parity, last, base, 2 * last + parity


def back_tile(i, slot, chunk, width, refs):
    q_cols, do_rows, do_cols, keys, values, scores, top, delta, dq_acc, d_blocks = refs
    at = pl.ds(pl.multiple_of(i * TILE, TILE), TILE)
    probs = jnp.exp2(scores[chunk, i] - twice(top[chunk]))
    d_probs = dot_nt(do_rows[chunk], values[at, 0:width])
    d_scores = (probs * (d_probs - twice(delta[chunk]))).astype(jnp.bfloat16)
    dq_acc[chunk] += dot(d_scores, keys[at, :])
    d_blocks[slot, 0:width, :] += dot(q_cols[chunk], d_scores)
    d_blocks[slot, width:, :] += dot(do_cols[chunk], probs.astype(jnp.bfloat16))


def put(d_blocks, mine, other, mine_ref, other_ref, width, scale):
    mine_ref[0:width, :] = d_blocks[mine, 0:width, :] * scale
    mine_ref[width:, :] = d_blocks[mine, width:, :]
    other_ref[0:width, :] = (d_blocks[other, 0:width, :] * scale).astype(jnp.bfloat16)
    other_ref[width:, :] = d_blocks[other, width:, :].astype(jnp.bfloat16)


def attention_kernel(
    doc_ref,
    q_rows,
    q_cols,
    do_rows,
    do_cols,
    own_ref,
    near_ref,
    *refs,
    back,
    whole,
    ranks,
    heads,
    width,
    scale,
):
    arrived, far, refs = refs[:back], refs[back : 2 * back], refs[2 * back :]
    out_parts, refs = refs[:ranks], refs[ranks:]
    (lows_ref, scores, top, delta, keys, values, dq_acc), refs = refs[:7], refs[7:]
    d_refs, (o_ref, accum, d_blocks) = refs[:-3], refs[-3:]
    tok = own_ref.shape[0] // 2
    part_rows = tok // ranks
    rank = lax.axis_index("head")
    parity, last, base, own = here(tok, back, whole)
    cut = 2 * (last - 1)
    ones = jnp.ones((width, width), jnp.bfloat16)

    values[:, width:] = jnp.ones_like(values[:, width:])
    for k in range(back + 1):
        pair = last ^ k if whole else last - k
        mine, other = (own_ref, near_ref) if k == 0 else (arrived[k - 1], far[k - 1])
        for ref, place in ((mine, 2 * pair + parity), (other, 2 * pair + 1 - parity)):
            at = pl.ds(pl.multiple_of(place * tok, tok), tok)
            keys[at, :] = ref[0:tok, :]
            values[at, 0:width] = ref[tok:, :]
    d_blocks[...] = jnp.zeros_like(d_blocks)
    top[...] = jnp.full_like(top, NEG_FILL)
    dq_acc[...] = jnp.zeros_like(dq_acc)

    def chunk_step(chunk, carry):
        rows_at = pl.ds(pl.multiple_of(chunk * CHUNK, CHUNK), CHUNK)
        t_first = base + own * TILE + chunk * CHUNK
        t_last = t_first + CHUNK - 1
        t_col = t_first + lax.broadcasted_iota(jnp.int32, (CHUNK, width), 0)
        start_col = starts_in(doc_ref, t_col)
        low = jnp.maximum(starts_in(doc_ref, t_first) - base, 0) // TILE
        lows_ref[chunk] = low
        clear = jnp.clip((starts_in(doc_ref, t_last) - base + TILE - 1) // TILE, low, own)

        def score_tile(i, masked):
            at = pl.ds(pl.multiple_of(i * TILE, TILE), TILE)
            tile = dot_nt(q_rows[chunk], keys[at, :]) * (scale * LOG2_E)
            if masked:
                s_row = base + i * TILE + lax.broadcasted_iota(jnp.int32, (CHUNK, TILE), 1)
                live = (s_row >= twice(start_col)) & (s_row <= twice(t_col))
                tile = jnp.concatenate(
                    [
                        jnp.where(live, tile[j * CHUNK : (j + 1) * CHUNK], NEG_FILL)
                        for j in range(heads)
                    ],
                    axis=0,
                )
            scores[chunk, i] = tile
            top[chunk] = jnp.maximum(top[chunk], jnp.maximum(tile[:, :width], tile[:, width:]))

        def edge_step(n, carry):
            score_tile(jnp.where(n < clear - low, low + n, own), True)
            return carry

        def inner_step(i, carry):
            score_tile(i, False)
            return carry

        lax.fori_loop(0, clear - low + 1, edge_step, 0)
        lax.fori_loop(clear, own, inner_step, 0)
        top[chunk] = jnp.broadcast_to(jnp.max(top[chunk], axis=1, keepdims=True), top.shape[1:])
        accum[...] = jnp.zeros_like(accum)

        def weigh_step(i, carry):
            at = pl.ds(pl.multiple_of(i * TILE, TILE), TILE)
            weights = jnp.exp2(scores[chunk, i] - twice(top[chunk])).astype(jnp.bfloat16)
            accum[...] += dot(weights, values[at, :])
            return carry

        lax.fori_loop(low, own + 1, weigh_step, 0)
        total = accum[:, width:]
        out = (accum[:, 0:width] / total).astype(jnp.bfloat16)
        for j in range(heads):
            o_ref[rows_at, j * width : (j + 1) * width] = out[j * CHUNK : (j + 1) * CHUNK]
        top[chunk] = top[chunk] + jnp.log2(total)
        product = do_rows[chunk].astype(jnp.float32) * out.astype(jnp.float32)
        coarse = product.astype(jnp.bfloat16)
        fine = (product - coarse.astype(jnp.float32)).astype(jnp.bfloat16)
        delta[chunk] = dot(coarse, ones) + dot(fine, ones)

        def back_step(i, carry):
            refs = (
                q_cols, do_rows, do_cols, keys, values, scores, top, delta, dq_acc, d_blocks
            )
            back_tile(i, i, chunk, width, refs)
            return carry

        lax.fori_loop(low, cut, back_step, 0)
        return carry

    lax.fori_loop(0, tok // CHUNK, chunk_step, 0)
    for k in range(ranks):
        at = pl.ds(pl.multiple_of((rank ^ k) * part_rows, part_rows), part_rows)
        out_parts[k][...] = o_ref[at, :]
    for k in range(2, back + 1):
        pair = jnp.maximum(last - k, 0)
        mine, other = 2 * pair + parity, 2 * pair + 1 - parity
        mine_ref, other_ref = (ref.at[k - 2] for ref in d_refs)
        put(d_blocks, mine, other, mine_ref, other_ref, width, scale)


def attend(doc_ends, prepared, own, near, arrived, far, ranks, whole):
    chunks, rows, width = prepared[0].shape
    tok = chunks * CHUNK
    heads = rows // CHUNK
    back = len(arrived)
    tiles = 2 * (back + 1)
    span = tiles * tok
    vmem = pl.BlockSpec(memory_space=pltpu.VMEM)
    smem = pl.BlockSpec(memory_space=pltpu.SMEM)
    out_part = jax.ShapeDtypeStruct((tok // ranks, heads * width), jnp.bfloat16)
    row_state = jax.ShapeDtypeStruct((chunks, rows, width), jnp.float32)
    outputs = pl.pallas_call(
        functools.partial(
            attention_kernel,
            back=back,
            whole=whole,
            ranks=ranks,
            heads=heads,
            width=width,
            scale=1.0 / math.sqrt(width),
        ),
        out_shape=[out_part] * ranks
        + [
            jax.ShapeDtypeStruct((chunks,), jnp.int32),
            jax.ShapeDtypeStruct((chunks, tiles, rows, TILE), jnp.float32),
            row_state,
            row_state,
            jax.ShapeDtypeStruct((span, width), jnp.bfloat16),
            jax.ShapeDtypeStruct((span, 2 * width), jnp.bfloat16),
            row_state,
        ]
        + [
            jax.ShapeDtypeStruct((back - 1, 2 * width, tok), dtype)
            for dtype in (jnp.float32, jnp.bfloat16)
        ],
        in_specs=[smem] + [vmem] * (6 + 2 * back),
        out_specs=[vmem] * ranks + [smem] + [vmem] * 8,
        scratch_shapes=[
            pltpu.VMEM((tok, heads * width), jnp.bfloat16),
            pltpu.VMEM((rows, 2 * width), jnp.float32),
            pltpu.VMEM((tiles, 2 * width, tok), jnp.float32),
        ],
        compiler_params=pltpu.CompilerParams(vmem_limit_bytes=KERNEL_VMEM),
        cost_estimate=pl.CostEstimate(
            flops=14 * tok * heads * width * span,
            bytes_accessed=4 * tok * heads * width * 2 + 4 * span * width * 2,
            transcendentals=tok * heads * span,
        ),
        name="attention",
    )(doc_ends, *prepared, own, near, *arrived, *far)
    return outputs[:ranks], outputs[ranks : ranks + 7], outputs[ranks + 7 :]


def near_kernel(
    q_cols,
    do_rows,
    do_cols,
    lows_ref,
    scores,
    top,
    delta,
    keys,
    values,
    dq_before,
    dq_acc,
    mine_ref,
    other_ref,
    d_blocks,
    *,
    distance,
    back,
    whole,
    width,
    scale,
):
    tok = mine_ref.shape[2]
    parity, last, _, own = here(tok, back, whole)
    first = 2 * (last - distance)
    d_blocks[...] = jnp.zeros_like(d_blocks)
    dq_acc[...] = dq_before[...]

    def chunk_step(chunk, carry):
        def back_step(i, carry):
            refs = (
                q_cols, do_rows, do_cols, keys, values, scores, top, delta, dq_acc, d_blocks
            )
            back_tile(i, i - first, chunk, width, refs)
            return carry

        stop = jnp.minimum(first + 2, own + 1)
        lax.fori_loop(jnp.maximum(lows_ref[chunk], first), stop, back_step, 0)
        return carry

    lax.fori_loop(0, tok // CHUNK, chunk_step, 0)
    put(d_blocks, parity, 1 - parity, mine_ref.at[0], other_ref.at[0], width, scale)


def attend_near(prepared, state, distance, back, whole):
    _, q_cols, do_rows, do_cols = prepared
    chunks, rows, width = do_rows.shape
    tok = chunks * CHUNK
    vmem = pl.BlockSpec(memory_space=pltpu.VMEM)
    smem = pl.BlockSpec(memory_space=pltpu.SMEM)
    return pl.pallas_call(
        functools.partial(
            near_kernel,
            distance=distance,
            back=back,
            whole=whole,
            width=width,
            scale=1.0 / math.sqrt(width),
        ),
        out_shape=[jax.ShapeDtypeStruct((chunks, rows, width), jnp.float32)]
        + [
            jax.ShapeDtypeStruct((1, 2 * width, tok), dtype)
            for dtype in (jnp.float32, jnp.bfloat16)
        ],
        in_specs=[vmem] * 3 + [smem] + [vmem] * 6,
        out_specs=[vmem] * 3,
        scratch_shapes=[pltpu.VMEM((2, 2 * width, tok), jnp.float32)],
        compiler_params=pltpu.CompilerParams(vmem_limit_bytes=KERNEL_VMEM),
        cost_estimate=pl.CostEstimate(
            flops=8 * chunks * rows * width * 2 * tok,
            bytes_accessed=4 * chunks * rows * width * 2,
            transcendentals=2 * chunks * rows * tok,
        ),
        name="near",
    )(q_cols, do_rows, do_cols, *state)


def split_kernel(grad_ref, *part_refs):
    size = part_refs[0].shape[1]
    for k, ref in enumerate(part_refs):
        at = pl.multiple_of((lax.axis_index("head") ^ k) * size, size)
        ref[...] = grad_ref[:, pl.ds(at, size)]


def split(grad_attended, ranks):
    rows, columns = grad_attended.shape
    vmem = pl.BlockSpec(memory_space=pltpu.VMEM)
    part = jax.ShapeDtypeStruct((rows, columns // ranks), grad_attended.dtype)
    return pl.pallas_call(
        split_kernel,
        out_shape=[part] * ranks,
        in_specs=[vmem],
        out_specs=[vmem] * ranks,
        compiler_params=pltpu.CompilerParams(vmem_limit_bytes=SMALL_VMEM),
        name="split",
    )(grad_attended)


def arrange_kernel(q_ref, rows_ref, cols_ref, wide):
    small = unit(q_ref.shape[2])
    wide[...] = q_ref[...].astype(jnp.float32)
    for chunk in range(rows_ref.shape[0]):
        for j in range(q_ref.shape[1]):
            rows_ref[chunk, j * CHUNK : (j + 1) * CHUNK, :] = wide[
                chunk * CHUNK : (chunk + 1) * CHUNK, j, :
            ].astype(jnp.bfloat16)
        cols_ref[chunk] = dot_nt(small, rows_ref[chunk]).astype(jnp.bfloat16)


def arrange_grads_kernel(*refs):
    parts, (rows_ref, cols_ref, grads) = refs[:-3], refs[-3:]
    width = rows_ref.shape[2]
    small = unit(width)
    size = parts[0].shape[0]
    for k, ref in enumerate(parts):
        at = pl.multiple_of((lax.axis_index("head") ^ k) * size, size)
        grads[pl.ds(at, size), :] = ref[...]
    for chunk in range(rows_ref.shape[0]):
        for j in range(rows_ref.shape[1] // CHUNK):
            rows_ref[chunk, j * CHUNK : (j + 1) * CHUNK, :] = grads[
                chunk * CHUNK : (chunk + 1) * CHUNK, j * width : (j + 1) * width
            ]
        cols_ref[chunk] = dot_nt(small, rows_ref[chunk]).astype(jnp.bfloat16)


def arrange(kernel, arrays, shape, scratch):
    tok, heads, width = shape
    vmem = pl.BlockSpec(memory_space=pltpu.VMEM)
    chunks, rows = tok // CHUNK, heads * CHUNK
    return pl.pallas_call(
        kernel,
        out_shape=[
            jax.ShapeDtypeStruct((chunks, rows, width), jnp.bfloat16),
            jax.ShapeDtypeStruct((chunks, width, rows), jnp.bfloat16),
        ],
        in_specs=[vmem] * len(arrays),
        out_specs=[vmem, vmem],
        scratch_shapes=[scratch],
        compiler_params=pltpu.CompilerParams(vmem_limit_bytes=SMALL_VMEM),
        name="arrange",
    )(*arrays)


def join_kernel(*refs):
    parts, (rows_ref, out_ref, dq_ref, wide) = refs[:-4], refs[-4:]
    size = parts[0].shape[1]
    for k, ref in enumerate(parts):
        at = pl.multiple_of((lax.axis_index("head") ^ k) * size, size)
        out_ref[:, pl.ds(at, size)] = ref[...]
    scale = 1.0 / math.sqrt(rows_ref.shape[2])
    for chunk in range(rows_ref.shape[0]):
        for j in range(dq_ref.shape[1]):
            wide[chunk * CHUNK : (chunk + 1) * CHUNK, j, :] = (
                rows_ref[chunk, j * CHUNK : (j + 1) * CHUNK, :] * scale
            )
    dq_ref[...] = wide[...].astype(jnp.bfloat16)


def join(parts, dq_rows, shape):
    rows, size = parts[0].shape
    vmem = pl.BlockSpec(memory_space=pltpu.VMEM)
    return pl.pallas_call(
        join_kernel,
        out_shape=(
            jax.ShapeDtypeStruct((rows, size * len(parts)), parts[0].dtype),
            jax.ShapeDtypeStruct(shape, jnp.bfloat16),
        ),
        in_specs=[vmem] * (len(parts) + 1),
        out_specs=(vmem, vmem),
        scratch_shapes=[pltpu.VMEM(shape, jnp.float32)],
        compiler_params=pltpu.CompilerParams(vmem_limit_bytes=SMALL_VMEM),
        name="join",
    )(*parts, dq_rows)


def merge_kernel(mine_ref, other_ref, *block_refs):
    for k, ref in enumerate(block_refs):
        ref[...] = (mine_ref[k] + other_ref[k].astype(jnp.float32)).astype(ref.dtype)


def merge(mine, other):
    vmem = pl.BlockSpec(memory_space=pltpu.VMEM)
    block = jax.ShapeDtypeStruct(mine.shape[1:], jnp.bfloat16)
    return pl.pallas_call(
        merge_kernel,
        out_shape=[block] * mine.shape[0],
        in_specs=[vmem, vmem],
        out_specs=[vmem] * mine.shape[0],
        compiler_params=pltpu.CompilerParams(vmem_limit_bytes=SMALL_VMEM),
        name="merge",
    )(mine, other)


def finish_kernel(own_ref, *refs):
    arrived = refs[:-2]
    dk_ref, dv_ref = refs[-2:]
    total = own_ref[...]
    for ref in arrived:
        total = total + ref[...].astype(jnp.float32)
    total = total.astype(jnp.bfloat16)
    width = dk_ref.shape[1]
    large = unit(dk_ref.shape[0])
    dk_ref[...] = dot_nt(large, total[:width]).astype(jnp.bfloat16)
    dv_ref[...] = dot_nt(large, total[width:]).astype(jnp.bfloat16)


def finish(own_part, arrived):
    both, tok = own_part.shape
    vmem = pl.BlockSpec(memory_space=pltpu.VMEM)
    shape = jax.ShapeDtypeStruct((tok, both // 2), jnp.bfloat16)
    return pl.pallas_call(
        finish_kernel,
        out_shape=(shape, shape),
        in_specs=[vmem] * (1 + len(arrived)),
        out_specs=(vmem, vmem),
        compiler_params=pltpu.CompilerParams(vmem_limit_bytes=SMALL_VMEM),
        name="finish",
    )(own_part, *arrived)


def shifted(block, by, count):
    pairs = [(i, i + by) for i in range(count) if 0 <= i + by < count]
    return lax.ppermute(block, "ctx", pairs)


def exchanged(block, axis, by):
    return lax.ppermute(block, axis, [(i, i ^ by) for i in range(lax.axis_size(axis))])


def after(value, *others):
    return lax.optimization_barrier((value, *others))


def body(queries, key_states, value_states, doc_lengths, grad_attended):
    tok, heads, width = queries.shape
    count = lax.axis_size("ctx")
    ranks = lax.axis_size("head")
    reach = min((DOC_MOST + tok - 2) // tok, count - 1)
    back = min((reach + 1) // 2, count // 2 - 1)
    whole = count == 8 and back == 3 and ranks == 4
    docs = jnp.arange(doc_lengths.shape[0])
    doc_ends = jnp.sum(jnp.where(docs[None] <= docs[:, None], doc_lengths[None], 0), axis=1)
    own = jnp.concatenate(
        [key_states.reshape(tok, width), value_states.reshape(tok, width)], axis=0
    )
    near = exchanged(own, "ctx", 1)
    if whole:
        beside = exchanged(own, "ctx", 2)
        across = exchanged(own, "ctx", 4)
    else:
        arrived = [shifted(own, 2 * k, count) for k in range(1, back + 1)]
    grads = split(grad_attended, ranks)
    grads = [part if k == 0 else exchanged(part, "head", k) for k, part in enumerate(grads)]
    if whole:
        far_beside = exchanged(beside, "ctx", 1)
        passed = exchanged(across, "ctx", 2)
        far_across = exchanged(across, "ctx", 1)
        passed, far_beside, near, *grads[1:] = after(passed, far_beside, near, *grads[1:])
        far_passed = exchanged(passed, "ctx", 1)
        arrived = [beside, across, passed]
        far = [far_beside, far_across, far_passed]
    else:
        far = [exchanged(block, "ctx", 1) for block in arrived]
    if whole:
        queries, doc_ends, passed = after(queries, doc_ends, passed)
    prepared = arrange(
        arrange_kernel, [queries], queries.shape, pltpu.VMEM(queries.shape, jnp.float32)
    )
    prepared += arrange(
        arrange_grads_kernel,
        grads,
        queries.shape,
        pltpu.VMEM((tok, heads * width), jnp.bfloat16),
    )
    outs, state, parts = attend(doc_ends, prepared, own, near, arrived, far, ranks, whole)
    outs, (mine_far, other_far) = list(outs), parts
    dq_rows, mine1, other1 = attend_near(prepared, state, 1, back, whole)
    other_far = exchanged(other_far, "ctx", 1)
    outs[1:2] = [exchanged(part, "head", 1) for part in outs[1:2]]
    other1 = exchanged(other1, "ctx", 1)
    other_far, mine1, *outs[1:2] = after(other_far, mine1, *outs[1:2])
    blocks = list(merge(mine_far, other_far))
    blocks[-1], *outs[2:] = after(blocks[-1], *outs[2:])
    outs[2:] = [exchanged(part, "head", k + 2) for k, part in enumerate(outs[2:])]
    returned = [shifted(block, -2 * (k + 2), count) for k, block in enumerate(blocks)]
    dq_rows, *outs[2:3] = after(dq_rows, *outs[2:3])
    dq_rows, mine0, other0 = attend_near(prepared, [*state[:-1], dq_rows], 0, back, whole)
    (block,) = merge(mine1, other1)
    returned.append(shifted(block, -2, count))
    other0 = exchanged(other0, "ctx", 1)
    grad_keys, grad_values = finish(mine0[0], returned + [other0[0]])
    attended, grad_queries = join(outs, dq_rows, queries.shape)
    grad_keys = grad_keys.reshape(tok, 1, width)
    grad_values = grad_values.reshape(tok, 1, width)
    return attended, grad_queries, grad_keys, grad_values


def solution(mesh):
    in_specs = (
        P("ctx", "head", None),
        P("ctx", "head", None),
        P("ctx", "head", None),
        P(),
        P(("ctx", "head"), None),
    )
    out_specs = (
        P(("ctx", "head"), None),
        P("ctx", "head", None),
        P("ctx", "head", None),
        P("ctx", "head", None),
    )
    return jax.shard_map(body, mesh=mesh, in_specs=in_specs, out_specs=out_specs, check_vma=False)
```
